32 devices in a mesh: expert: 8 (over z, x), head: 4 (over y, core).
Axes of the slice: x: 2, y: 2, z: 4, core: 2. Of those that a mesh axis runs over, the one named last changes fastest.
Arguments:
- inputs: bfloat16 [1024, 768], P('expert', 'head'), may hold values from -6 to 6
- out_grad: bfloat16 [1024, 768], P('expert', 'head'), may hold values from -6 to 6
- lengths: int32 [8], P('expert'), may hold values from 1 to 128, 768 in all
- routes: int32 [1024, 1], P('expert'), may hold values from 0 to 7; in each aligned block of 128 rows (0 to 127, 128 to 255, ...) at most 22 rows name the same one
- buckets: int32 [255], replicated, may hold values from 0 to 31
- gain_attn: bfloat16 [768], P('head'), may hold values from 0.25 to 1.75
- w_query: bfloat16 [768, 768], P(None, 'head'), may hold values from -0.21875 to 0.21875
- w_key: bfloat16 [768, 768], P(None, 'head'), may hold values from -0.21875 to 0.21875
- w_value: bfloat16 [768, 768], P(None, 'head'), may hold values from -0.21875 to 0.21875
- w_output: bfloat16 [768, 768], P('head'), may hold values from -1.75 to 1.75
- bias_table: float32 [32, 12], P(None, 'head'), may hold values from -6 to 6
- gain_ffn: bfloat16 [768], P('head'), may hold values from 0.25 to 1.75
- w_router: bfloat16 [768, 8], replicated, may hold values from -0.15625 to 0.15625
- w_in: bfloat16 [8, 768, 3072], P('expert', None, 'head'), may hold values from -0.21875 to 0.21875
- w_out: bfloat16 [8, 3072, 768], P('expert', 'head'), may hold values from -0.875 to 0.875
Outputs:
- block_out: bfloat16 [1024, 768], P('expert', 'head')
- input_grad: float32 [1024, 768], P('expert', 'head')
- aux_loss: float32 [], replicated
- gain_attn_grad: float32 [768], P('head')
- query_weight_grad: float32 [768, 768], P(None, 'head')
- key_weight_grad: float32 [768, 768], P(None, 'head')
- value_weight_grad: float32 [768, 768], P(None, 'head')
- output_weight_grad: float32 [768, 768], P('head')
- table_grad: float32 [32, 12], P(None, 'head')
- gain_ffn_grad: float32 [768], P('head')
- router_grad: float32 [768, 8], replicated
- in_weight_grad: float32 [8, 768, 3072], P('expert', None, 'head')
- out_weight_grad: float32 [8, 3072, 768], P('expert', 'head')
The draws below stay inside these ranges and needn't reach their ends.
Inputs may be any that keep to these rules, and one draw needn't show every extreme that they name: Entry b is the length of the one sequence that starts at row b * 128; the lengths sum to 768, and the largest is 128. `routes`: among the 128 rows of one device no expert is named by more than 22 rows, a bound that some block reaches. `buckets`: entry r is the bucket of relative position r - 127.
All inputs are finite; a program needn't handle non-finite values. No bound on the sum of `lengths` on one device may be relied on, other than what follows from the above.
Results may differ from the reference program's by a relative error of at most 0.017.
Values may be sent and summed in bfloat16 or wider, within the bound.
No kernel may reach another device: no remote copies, remote signals or barrier semaphores. Data moves between devices by JAX's collectives and lax.ppermute only.
A program may use at most 64 MiB of HBM per device.

```python
import math
import jax
import jax.numpy as jnp
import numpy as np
from jax import lax

D = 768
HEADS = 12
HEAD_DIM = 64
FF = 3072
BUCKETS = 32
TOK_DEV = 128
EXPERTS = 8
CAP = 22
TOKENS = 1024
VALID = 768
N_EXPERT = 8


def place_ends(array, stream_key, low, high):
    longest = array.shape.index(max(array.shape))
    spots = []
    for shift in (0, 1):
        where = [jax.random.randint(jax.random.fold_in(stream_key, axis), (), 0, length) for axis, length in enumerate(array.shape)]
        where[longest] = (where[longest] + shift) % array.shape[longest]
        spots.append(tuple(where))
    return array.at[spots[0]].set(low).at[spots[1]].set(high)


def block_scale(own_key, extent, cuts, low, high):
    level = 1.0
    for position, parts in cuts:
        steps = jax.random.uniform(jax.random.fold_in(jax.random.fold_in(own_key, 6), position), (parts,), jnp.float32, low / len(cuts), high / len(cuts))
        level = level * jnp.repeat(jnp.exp(steps), extent[position] // parts).reshape((-1,) + (1,) * (len(extent) - 1 - position))
    return level


def length_profile(amount, total, reach, lean):
    portions = [(1 << 20) // math.isqrt(grade ** lean) + 1 for grade in range(2, amount + 1)]
    rest, given = total - reach - (amount - 1), [1] * (amount - 1)
    while rest > 0:
        candidates = [i for i in range(amount - 1) if given[i] < reach]
        mass, left = sum([portions[i] for i in candidates]), rest
        for i in candidates:
            addition = min(reach - given[i], max(1, left * portions[i] // mass), rest)
            given[i] = given[i] + addition
            rest = rest - addition
    return np.array([reach] + given)


def uneven_parts(key, amount, total, limit, skew):
    if amount == 2:
        one = jax.random.randint(key, (), max(1, total - limit), min(limit, total - 1) + 1)
        return jnp.stack([one, total - one])
    tallies = jnp.asarray(length_profile(amount, total, limit, skew), jnp.int32)
    couples = (amount - 1) // 2
    giver, sink = tallies[1:1 + 2 * couples:2], tallies[2:2 + 2 * couples:2]
    slack = jnp.minimum(giver - 1, limit - sink)
    passed = jax.random.randint(jax.random.fold_in(key, 1), (couples,), 0, 1 << 20) % (slack + 1)
    tallies = tallies.at[1:1 + 2 * couples:2].set(giver - passed).at[2:2 + 2 * couples:2].set(sink + passed)
    return tallies[jax.random.permutation(jax.random.fold_in(key, 2), amount)]


def routed_block(stream_key, own, number, rows, amount, top, bound, skew):
    sequence = jax.random.permutation(stream_key, amount)
    heavy_load, common = load_shares(amount, rows * top, bound, skew, True), load_shares(amount, rows * top, bound, skew, False)
    places = jnp.arange(amount)

    def named(sizes, offset_by):
        used = int((sizes > 0).sum())
        fixed = max(1, used // 4)
        moved = fixed + (places - fixed + offset_by * (used - fixed)) % max(1, amount - fixed)
        return jnp.zeros((amount,), jnp.int32).at[sequence[jnp.where(places < fixed, places, moved)]].set(jnp.asarray(sizes, jnp.int32))

    sizes = jnp.where(number % 4 == 0, named(heavy_load, number // 4), named(common, number - number // 4 - 1))
    mixed = jax.random.permutation(jax.random.fold_in(own, 3), amount)
    donor, taker = mixed[0:amount // 2 * 2:2], mixed[1:amount // 2 * 2:2]
    room = jnp.minimum(sizes[donor] - 1, bound - sizes[taker]) // 2
    room = jnp.where((donor == sequence[0]) | (taker == sequence[0]) | (sizes[taker] == 0), 0, jnp.maximum(room, 0))
    moved = jax.random.randint(jax.random.fold_in(own, 4), (amount // 2,), 0, 1 << 20) % (room + 1)
    sizes = sizes.at[donor].add(-moved).at[taker].add(moved)
    items = jnp.searchsorted(jnp.cumsum(sizes), jnp.arange(rows * top), side="right").astype(jnp.int32)
    grid = items.reshape(top, rows).T
    grid = grid[jax.random.permutation(jax.random.fold_in(own, 1), rows)]
    offset_by = jax.random.randint(jax.random.fold_in(own, 2), (rows, 1), 0, top)
    return jnp.take_along_axis(grid, (jnp.arange(top)[None, :] + offset_by) % top, axis=1)


def load_shares(amount, total, most, slope, full):
    loads = [(1 << 20) // math.isqrt(standing ** slope) + 1 for standing in range(1, amount + 1)]
    largest = most if full else min(most, max(-(-total // amount), total * loads[0] // sum(loads)))
    least = 1 if total - largest >= amount - 1 else 0
    holding, surplus = [largest] + [least] * (amount - 1), total - largest - least * (amount - 1)
    while surplus > 0:
        free = [i for i in range(1, amount) if holding[i] < largest] or [i for i in range(1, amount) if holding[i] < most]
        whole, budget = sum([loads[i] for i in free]), surplus
        for i in free:
            addition = min(most - holding[i], max(1, budget * loads[i] // whole), surplus)
            holding[i] = holding[i] + addition
            surplus = surplus - addition
    return np.array(holding)


def gaussian(rng, extent, spread, bound, cuts=(), kind=jnp.bfloat16):
    loudness = block_scale(rng, extent, cuts, -0.22, 0.18) if cuts else 1.0
    result = jax.random.normal(rng, extent, jnp.float32) * spread * loudness
    return jnp.minimum(jnp.maximum(result, -bound), bound).astype(kind)


def setup_inputs(seed: int = 0) -> dict:
    keys = jax.random.split(jax.random.key(seed), 16)
    inputs = gaussian(keys[0], (TOKENS, D), 1.0, 6.0, ((0, 8), (1, 4)))
    out_grad = gaussian(keys[1], (TOKENS, D), 1.0, 6.0, ((0, 8), (1, 4)))
    lengths = uneven_parts(keys[2], N_EXPERT, VALID, TOK_DEV, 2).astype(jnp.int32)
    routes_keys = jax.random.split(jax.random.fold_in(keys[3], 1), TOKENS // TOK_DEV)
    routes_turns = jax.random.permutation(jax.random.fold_in(keys[3], 3), TOKENS // TOK_DEV)
    routes = jax.vmap(lambda own, number: routed_block(jax.random.fold_in(keys[3], 2), own, number, TOK_DEV, EXPERTS, 1, CAP, 2))(routes_keys, routes_turns).reshape((TOKENS, 1))
    buckets = place_ends(jax.random.randint(keys[4], (2 * TOK_DEV - 1,), 0, BUCKETS), jax.random.fold_in(keys[4], 1), 0, BUCKETS - 1).astype(jnp.int32)
    gain_attn = jnp.clip(1.0 + 0.15 * jax.random.normal(keys[5], (D,), jnp.float32), 0.25, 1.75).astype(jnp.bfloat16)
    w_query = gaussian(keys[6], (D, D), D ** -0.5, 0.21875, ((1, 4),))
    w_key = gaussian(keys[7], (D, D), D ** -0.5, 0.21875, ((1, 4),))
    w_value = gaussian(keys[8], (D, D), D ** -0.5, 0.21875, ((1, 4),))
    w_output = gaussian(keys[9], (D, D), (max(1, D // 64)) ** -0.5, 1.75, ((0, 4),))
    bias_table = gaussian(keys[10], (BUCKETS, HEADS), 1.0, 6.0, ((1, 4),), jnp.float32)
    gain_ffn = jnp.clip(1.0 + 0.15 * jax.random.normal(keys[11], (D,), jnp.float32), 0.25, 1.75).astype(jnp.bfloat16)
    w_router = gaussian(keys[12], (D, EXPERTS), (2 * D) ** -0.5, 0.15625)
    w_in = gaussian(keys[13], (EXPERTS, D, FF), D ** -0.5, 0.21875, ((0, 8), (2, 4)))
    w_out = gaussian(keys[14], (EXPERTS, FF, D), (max(1, FF // (EXPERTS * EXPERTS))) ** -0.5, 0.875, ((0, 8), (1, 4)))
    return dict(inputs=inputs, out_grad=out_grad, lengths=lengths, routes=routes, buckets=buckets, gain_attn=gain_attn, w_query=w_query, w_key=w_key, w_value=w_value, w_output=w_output, bias_table=bias_table, gain_ffn=gain_ffn, w_router=w_router, w_in=w_in, w_out=w_out)


eps = 1e-06
aux_weight = 0.01
highest = lax.Precision.HIGHEST

@jax.custom_vjp
def low(v):
    return lax.optimization_barrier(v.astype(jnp.bfloat16)).astype(jnp.float32)

@jax.custom_vjp
def low_back(v):
    return v

def low_keep(v):
    return (low(v), None)

def low_pass(kept, grad):
    return (grad,)

def back_keep(v):
    return (v, None)

def back_low(kept, grad):
    return (low(grad),)
low.defvjp(low_keep, low_pass)
low_back.defvjp(back_keep, back_low)

def matmul(left, right):
    return jnp.dot(left, right, precision=highest)

def rms_norm(values, gain):
    return values * lax.rsqrt(lax.optimization_barrier(jnp.mean(values * values, axis=-1, keepdims=True)) + eps) * gain

def smooth(values):
    return jax.nn.gelu(values, approximate=True)

def attend(normed_rows, length, w_query, w_key, w_value, offset_bias):
    tok_rows = normed_rows.shape[0]

    def project(weight):
        return low_back(low(matmul(normed_rows, weight))).reshape(tok_rows, HEADS, HEAD_DIM)
    query_heads = project(w_query)
    key_heads = project(w_key)
    value_heads = project(w_value)
    positions = jnp.arange(tok_rows)
    relative = positions[None, :] - positions[:, None] + tok_rows - 1
    bias_full = jnp.transpose(offset_bias[relative], (2, 0, 1))
    scores = jnp.einsum('qhd,khd->hqk', query_heads, key_heads, precision=highest) * HEAD_DIM ** (-0.5) + bias_full
    scores = low_back(scores)
    scores = jnp.where((positions < length)[None, None, :], scores, -1000000000.0)
    weights_low = low(jax.nn.softmax(scores, axis=-1))
    attended = jnp.einsum('hqk,khd->qhd', weights_low, value_heads, precision=highest)
    return low_back(low(attended.reshape(tok_rows, D)))

def expert_block(operands):
    rows, w_first, w_second = operands
    before = low_back(matmul(rows, w_first))
    return matmul(low(smooth(before)), w_second)

def forward(params, lengths, routes, buckets):
    inputs, gain_attn, w_query, w_key, w_value, w_output, bias_table, gain_ffn, w_router, w_in, w_out = params
    normed_one = low(rms_norm(inputs, gain_attn))
    bucket_hot = (buckets[:, None] == jnp.arange(BUCKETS)[None, :]).astype(jnp.float32)
    offset_bias = matmul(bucket_hot, bias_table)
    attend_block = jax.checkpoint(lambda normed_rows, length: attend(normed_rows, length, w_query, w_key, w_value, offset_bias))
    blocks = normed_one.reshape(N_EXPERT, TOK_DEV, D)
    attended = lax.map(lambda operands: attend_block(operands[0], operands[1]), (blocks, lengths))
    branch = low_back(matmul(attended.reshape(TOKENS, D), w_output))
    residual = inputs + branch
    normed_two = low(rms_norm(residual, gain_ffn))
    logits = low_back(matmul(normed_two, w_router))
    router = jax.nn.softmax(logits, axis=-1)
    route_hot = (routes == jnp.arange(EXPERTS)[None, :]).astype(jnp.float32)
    gate_value = lax.optimization_barrier(jnp.sum(router * route_hot, axis=1))
    valid_rows = (jnp.arange(TOK_DEV)[None, :] < lengths[:, None]).reshape(TOKENS).astype(jnp.float32)
    fraction = lax.optimization_barrier(jnp.sum(route_hot * valid_rows[:, None], axis=0)) / VALID
    prob_mean = lax.optimization_barrier(jnp.sum(router * valid_rows[:, None], axis=0)) / VALID
    aux_loss = EXPERTS * jnp.sum(fraction * prob_mean)
    route_int = (routes == jnp.arange(EXPERTS)[None, :]).astype(jnp.int32).reshape(N_EXPERT, TOK_DEV, EXPERTS)
    earlier = jnp.cumsum(route_int, axis=1, dtype=jnp.int32) - route_int
    slot_index = (routes[:, 0].reshape(N_EXPERT, TOK_DEV) * CAP + lax.optimization_barrier(jnp.sum(earlier * route_int, axis=2))).astype(jnp.int32)
    sent = low_back(normed_two).reshape(N_EXPERT, TOK_DEV, D)

    def scatter_rows(rows, where):
        return jnp.zeros((EXPERTS * CAP, D), rows.dtype).at[where].set(rows)
    buffers = jax.vmap(scatter_rows)(sent, slot_index)
    by_expert = jnp.transpose(buffers.reshape(N_EXPERT, EXPERTS, CAP, D), (1, 0, 2, 3)).reshape(EXPERTS, N_EXPERT * CAP, D)
    produced = lax.map(jax.checkpoint(expert_block), (by_expert, w_in, w_out))
    produced = low_back(low(produced))
    back_buffers = jnp.transpose(produced.reshape(EXPERTS, N_EXPERT, CAP, D), (1, 0, 2, 3)).reshape(N_EXPERT, EXPERTS * CAP, D)
    returned = jax.vmap(lambda buffer_rows, where: buffer_rows[where])(back_buffers, slot_index).reshape(TOKENS, D)
    block_out = residual + gate_value[:, None] * returned
    return (block_out, aux_loss)

def reference(inputs, out_grad, lengths, routes, buckets, gain_attn, w_query, w_key, w_value, w_output, bias_table, gain_ffn, w_router, w_in, w_out):
    params = tuple((value.astype(jnp.float32) for value in (inputs, gain_attn, w_query, w_key, w_value, w_output, bias_table, gain_ffn, w_router, w_in, w_out)))
    (block_out, aux_loss), pullback = jax.vjp(lambda values: forward(values, lengths, routes, buckets), params)
    grads = pullback((out_grad.astype(jnp.float32), jnp.ones_like(aux_loss) * aux_weight))[0]
    return (block_out.astype(jnp.bfloat16), grads[0], aux_loss, grads[1], grads[2], grads[3], grads[4], grads[5], grads[6], grads[7], grads[8], grads[9], grads[10])
```

```python
import jax
import jax.numpy as jnp
from jax import lax
from jax.sharding import PartitionSpec as P

eps = 1e-06
aux_weight = 0.01
f32 = jnp.float32
bf16 = jnp.bfloat16


def swap(block, axis, offset):
    size = lax.axis_size(axis)
    return lax.ppermute(block, axis, [(i, i ^ offset) for i in range(size)])


def mm(left, right, dims=((1,), (0,))):
    return lax.dot_general(left, right, (dims, ((), ())), preferred_element_type=f32)


def rms_scale(values):
    return lax.rsqrt(jnp.mean(values * values, axis=-1, keepdims=True) + eps)


def smooth(values):
    return jax.nn.gelu(values, approximate=True)


def gather_head(block):
    size = lax.axis_size("head")
    parts = jnp.stack([block] + [swap(block, "head", k) for k in range(1, size)])
    return parts[jnp.arange(size) ^ lax.axis_index("head")]


def widen(parts):
    count, rows, cols = parts.shape
    return jnp.transpose(parts, (1, 0, 2)).reshape(rows, count * cols)


def column_parts(matrix, count):
    rows, cols = matrix.shape
    return jnp.transpose(matrix.reshape(rows, count, cols // count), (1, 0, 2))


def sum_scatter_head(parts):
    size, me = lax.axis_size("head"), lax.axis_index("head")
    total = parts[me].astype(f32)
    for k in range(1, size):
        total = total + swap(parts[me ^ k].astype(bf16), "head", k).astype(f32)
    return total


def few_experts():
    return lax.axis_size("expert") <= 8


def exchange(blocks):
    if few_experts():
        return jnp.stack([blocks[0]] + [swap(blocks[k], "expert", k) for k in range(1, blocks.shape[0])])
    return lax.all_to_all(blocks, "expert", split_axis=0, concat_axis=0, tiled=True)


def gather_expert(block):
    if few_experts():
        return jnp.stack([block] + [swap(block, "expert", k) for k in range(1, lax.axis_size("expert"))])
    return lax.all_gather(block, "expert", axis=0)


def sum_expert(block):
    if few_experts():
        return jnp.sum(gather_expert(block).astype(f32), axis=0)
    return lax.psum(block.astype(f32), "expert")


def diagonal_spread(offsets, tok_rows):
    heads_here = offsets.shape[1]
    reversed_rows = jnp.transpose(offsets[::-1], (1, 0))
    tiled = jnp.broadcast_to(reversed_rows[:, None, :], (heads_here, tok_rows, 2 * tok_rows - 1))
    flat = tiled.reshape(heads_here, tok_rows * (2 * tok_rows - 1))
    flat = jnp.pad(flat, ((0, 0), (0, tok_rows)))
    skewed = flat.reshape(heads_here, tok_rows, 2 * tok_rows)[:, :, :tok_rows]
    return skewed[:, :, ::-1]


def shards(
    inputs,
    out_grad,
    lengths,
    routes,
    buckets,
    gain_attn,
    w_query,
    w_key,
    w_value,
    w_output,
    bias_table,
    gain_ffn,
    w_router,
    w_in,
    w_out,
):
    tok_rows, col_width = inputs.shape
    heads_here = bias_table.shape[1]
    head_size = w_query.shape[1] // heads_here
    model_width = w_query.shape[0]
    experts = w_router.shape[1]
    bucket_count = bias_table.shape[0]
    head_count = model_width // col_width
    me_head, me_expert = lax.axis_index("head"), lax.axis_index("expert")
    capacity = max(2, (4 * tok_rows + 3 * experts - 1) // (3 * experts))
    slots = -(-capacity // 8) * 8
    valid_total = 3 * tok_rows * lax.axis_size("expert") // 4
    score_scale = head_size ** (-0.5)
    positions = jnp.arange(tok_rows)
    w_in, w_out = w_in[0], w_out[0]

    valid_rows = (positions < lengths[0]).astype(f32)
    expert_ids = jnp.arange(experts)[None, :]
    route_hot = (routes == expert_ids).astype(f32)
    counts = jnp.sum(route_hot * valid_rows[:, None], axis=0)
    fraction = sum_expert(counts) / valid_total
    route_int = (routes == expert_ids).astype(jnp.int32)
    earlier = jnp.cumsum(route_int, axis=0, dtype=jnp.int32) - route_int
    slot = jnp.sum(earlier * route_int, axis=1)
    place = (routes[:, 0] ^ me_expert) if few_experts() else routes[:, 0]
    spots = place * slots + slot
    spot_hot = (spots[:, None] == jnp.arange(experts * slots)[None, :]).astype(bf16)

    packed = jnp.concatenate([inputs, out_grad, gain_attn[None], gain_ffn[None]], axis=0)
    packed = gather_head(packed)
    full_in = widen(packed[:, :tok_rows])
    full_grad = widen(packed[:, tok_rows : 2 * tok_rows])
    gain_one = packed[:, 2 * tok_rows].reshape(1, model_width).astype(f32)
    gain_two = packed[:, 2 * tok_rows + 1].reshape(1, model_width).astype(f32)
    w_output_full = gather_head(w_output).reshape(model_width, model_width)
    all_in = lax.all_gather(inputs, ("expert", "head"), axis=0) if few_experts() else None

    inputs_wide = full_in.astype(f32)
    scale_one = rms_scale(inputs_wide)
    unit_one = inputs_wide * scale_one
    normed_one = (unit_one * gain_one).astype(bf16)
    w_qkv = jnp.concatenate([w_query, w_key, w_value], axis=1)
    qkv = mm(normed_one, w_qkv).astype(bf16)
    query_heads, key_heads, value_heads = (
        qkv[:, i * col_width : (i + 1) * col_width].reshape(tok_rows, heads_here, head_size)
        for i in range(3)
    )
    bucket_hot = (buckets[:, None] == jnp.arange(bucket_count)[None, :]).astype(f32)
    offset_bias = jnp.dot(bucket_hot, bias_table, precision=lax.Precision.HIGHEST)
    bias_full, expand_back = jax.vjp(lambda o: diagonal_spread(o, tok_rows), offset_bias)
    key_mask = (positions < lengths[0])[None, None, :]
    scores = (
        jnp.einsum("qhd,khd->hqk", query_heads, key_heads, preferred_element_type=f32)
        * score_scale
        + bias_full
    )
    scores = jnp.where(key_mask, scores, -1000000000.0)
    raised = jnp.exp(scores - jnp.max(scores, axis=-1, keepdims=True))
    attention_weights = raised / jnp.sum(raised, axis=-1, keepdims=True)
    weights_low = attention_weights.astype(bf16)
    attended = jnp.einsum("hqk,khd->qhd", weights_low, value_heads, preferred_element_type=f32)
    attended = attended.reshape(tok_rows, col_width).astype(bf16)

    attended_parts = gather_head(attended)
    if few_experts():
        all_attended = lax.all_gather(attended, ("expert", "head"), axis=0)
    residual = inputs_wide + mm(widen(attended_parts), w_output_full)
    scale_two = rms_scale(residual)
    unit_two = residual * scale_two
    normed_two = (unit_two * gain_two).astype(bf16)
    logits = mm(normed_two, w_router)
    router_weights = jax.nn.softmax(logits, axis=-1)
    gate_value = jnp.sum(router_weights * route_hot, axis=1)
    prob_sums = jnp.sum(router_weights * valid_rows[:, None], axis=0)

    def dispatch(rows):
        placed = mm(spot_hot, rows, ((0,), (0,))).astype(bf16)
        return exchange(placed.reshape(experts, slots, model_width)).reshape(-1, model_width)

    grad_rows = dispatch(full_grad)
    expert_rows = dispatch(normed_two)
    before_act = mm(expert_rows, w_in)
    act, act_back = jax.vjp(smooth, before_act)
    hidden = act.astype(bf16)
    expert_part = mm(hidden, w_out)
    row_probs = jax.nn.softmax(mm(expert_rows, w_router), axis=-1)
    row_gate = lax.dynamic_slice_in_dim(row_probs, me_expert, 1, 1)
    grad_rows_wide = grad_rows.astype(f32)
    back_rows = (row_gate * grad_rows_wide).astype(bf16)
    gate_part = jnp.sum(grad_rows_wide * expert_part, axis=1, keepdims=True)
    hidden_grad = mm(back_rows, w_out, ((1,), (1,)))
    before_grad = act_back(hidden_grad)[0].astype(bf16)
    rows_part = mm(before_grad, w_in, ((1,), (1,)))
    out_weight_grad = mm(hidden, back_rows, ((0,), (0,)))[None]
    in_weight_grad = mm(expert_rows, before_grad, ((0,), (0,)))[None]

    gate_high = gate_part.astype(bf16).astype(f32)
    gate_low = gate_part - gate_high
    pad = jnp.zeros((experts * slots, 62), f32)
    extra = jnp.concatenate([gate_high, gate_low, pad], axis=1)
    extra = jnp.broadcast_to(extra[None], (head_count,) + extra.shape)
    parts = jnp.concatenate(
        [column_parts(rows_part, head_count), column_parts(expert_part, head_count), extra], axis=2
    )
    own_sum = sum_scatter_head(parts)
    gate_sum = own_sum[:, 2 * col_width : 2 * col_width + 1] + own_sum[:, 2 * col_width + 1 : 2 * col_width + 2]
    gate_high = gate_sum.astype(bf16)
    gate_low = (gate_sum - gate_high.astype(f32)).astype(bf16)
    message = jnp.concatenate(
        [own_sum[:, : 2 * col_width].astype(bf16), gate_high, gate_low, pad.astype(bf16)], axis=1
    )
    came = exchange(message.reshape(experts, slots, -1)).reshape(experts * slots, -1)
    came = mm(spot_hot, came)
    expert_grad_own = came[:, :col_width].astype(bf16)
    returned = came[:, col_width : 2 * col_width]
    gate_grad = came[:, 2 * col_width] + came[:, 2 * col_width + 1]
    expert_grad = widen(gather_head(expert_grad_own)).astype(f32)
    residual_own = lax.dynamic_index_in_dim(column_parts(residual, head_count), me_head, 0, False)
    block_out = (residual_own + gate_value[:, None] * returned).astype(bf16)

    prob_grad = (
        route_hot * gate_grad[:, None]
        + aux_weight * experts * fraction[None, :] * valid_rows[:, None] / valid_total
    )
    logit_grad = (
        router_weights * (prob_grad - jnp.sum(router_weights * prob_grad, axis=1, keepdims=True))
    ).astype(bf16)
    router_grad = mm(logit_grad, normed_two, ((0,), (0,)))
    normed_grad = mm(logit_grad, w_router, ((1,), (1,))) + expert_grad
    gain_two_grad = jnp.sum(normed_grad * unit_two, axis=0)
    unit_grad = normed_grad * gain_two
    residual_grad = full_grad.astype(f32) + scale_two * (
        unit_grad - unit_two * jnp.mean(unit_grad * unit_two, axis=-1, keepdims=True)
    )
    branch_grad = residual_grad.astype(bf16)
    branch_own = lax.dynamic_index_in_dim(column_parts(branch_grad, head_count), me_head, 0, False)

    attended_grad = mm(branch_grad, w_output, ((1,), (1,))).astype(bf16)
    attended_grad = attended_grad.reshape(tok_rows, heads_here, head_size)
    mass_grad = jnp.einsum("qhd,khd->hqk", attended_grad, value_heads, preferred_element_type=f32)
    value_grad = jnp.einsum("hqk,qhd->khd", weights_low, attended_grad, preferred_element_type=f32)
    score_grad = (
        attention_weights
        * (mass_grad - jnp.sum(attention_weights * mass_grad, axis=-1, keepdims=True))
    ).astype(bf16)
    query_grad = (
        jnp.einsum("hqk,khd->qhd", score_grad, key_heads, preferred_element_type=f32) * score_scale
    )
    key_grad = (
        jnp.einsum("hqk,qhd->khd", score_grad, query_heads, preferred_element_type=f32)
        * score_scale
    )
    qkv_grad = jnp.concatenate(
        [g.reshape(tok_rows, col_width).astype(bf16) for g in (query_grad, key_grad, value_grad)],
        axis=1,
    )
    offset_grad = expand_back(score_grad.astype(f32))[0]
    table_part = jnp.dot(bucket_hot.T, offset_grad, precision=lax.Precision.HIGHEST)

    def in_arrival_order(blocks):
        blocks = blocks.reshape((lax.axis_size("expert"), head_count, tok_rows, col_width))
        blocks = blocks[jnp.arange(blocks.shape[0]) ^ me_expert]
        return jnp.transpose(blocks, (0, 2, 1, 3)).reshape(-1, model_width)

    if few_experts():
        all_late = gather_expert(jnp.concatenate([qkv_grad, branch_own], axis=1))
        all_in = in_arrival_order(all_in).astype(f32)
        all_normed = (all_in * rms_scale(all_in) * gain_one).astype(bf16)
        all_late = all_late.reshape(-1, 4 * col_width)
        qkv_weight_grad = mm(all_normed, all_late[:, : 3 * col_width], ((0,), (0,)))
        output_cols = mm(in_arrival_order(all_attended), all_late[:, 3 * col_width :], ((0,), (0,)))
        output_parts = output_cols.astype(bf16).reshape(head_count, col_width, col_width)
        traded = jnp.stack(
            [output_parts[me_head]]
            + [swap(output_parts[me_head ^ k], "head", k) for k in range(1, head_count)]
        )[jnp.arange(head_count) ^ me_head]
        output_grad = widen(traded).astype(f32)
    else:
        qkv_weight_grad = sum_expert(mm(normed_one, qkv_grad, ((0,), (0,))))
        output_grad = sum_expert(mm(attended, branch_grad, ((0,), (0,))))

    first_part = mm(qkv_grad, w_qkv, ((1,), (1,)))
    row_part = jnp.sum(qkv_grad.astype(f32) * qkv.astype(f32), axis=1, keepdims=True)
    row_high = row_part.astype(bf16).astype(f32)
    extra = jnp.concatenate([row_high, row_part - row_high, jnp.zeros((tok_rows, 62), f32)], axis=1)
    extra = jnp.broadcast_to(extra[None], (head_count,) + extra.shape)
    own_first = sum_scatter_head(
        jnp.concatenate([column_parts(first_part, head_count), extra], axis=2)
    )
    first_own = own_first[:, :col_width]
    row_mean = (own_first[:, col_width] + own_first[:, col_width + 1])[:, None] / model_width
    unit_own = inputs.astype(f32) * scale_one
    gain_one_part = jnp.sum(first_own * unit_own, axis=0)
    residual_grad_own = lax.dynamic_index_in_dim(
        column_parts(residual_grad, head_count), me_head, 0, False
    )
    input_grad = residual_grad_own + scale_one * (
        first_own * gain_attn.astype(f32)[None, :] - unit_own * row_mean
    )

    gain_two_own = lax.dynamic_slice_in_dim(gain_two_grad, me_head * col_width, col_width)
    small = jnp.concatenate(
        [prob_sums, gain_two_own, table_part.reshape(-1), router_grad.reshape(-1)]
    )
    small = sum_expert(small)
    prob_sums = small[:experts]
    gain_two_grad = small[experts : experts + col_width]
    at = experts + col_width
    table_grad = small[at : at + table_part.size].reshape(table_part.shape)
    router_grad = small[at + table_part.size :].reshape(experts, model_width).T
    gain_one_grad = sum_expert(gain_one_part)
    aux_loss = experts * jnp.sum(fraction * (prob_sums / valid_total))
    return (
        block_out,
        input_grad,
        aux_loss,
        gain_one_grad,
        qkv_weight_grad[:, :col_width],
        qkv_weight_grad[:, col_width : 2 * col_width],
        qkv_weight_grad[:, 2 * col_width :],
        output_grad,
        table_grad,
        gain_two_grad,
        router_grad,
        in_weight_grad,
        out_weight_grad,
    )


def solution(mesh):
    return jax.shard_map(
        shards,
        mesh=mesh,
        in_specs=(
            P("expert", "head"),
            P("expert", "head"),
            P("expert"),
            P("expert", None),
            P(),
            P("head"),
            P(None, "head"),
            P(None, "head"),
            P(None, "head"),
            P("head", None),
            P(None, "head"),
            P("head"),
            P(),
            P("expert", None, "head"),
            P("expert", "head", None),
        ),
        out_specs=(
            P("expert", "head"),
            P("expert", "head"),
            P(),
            P("head"),
            P(None, "head"),
            P(None, "head"),
            P(None, "head"),
            P("head", None),
            P(None, "head"),
            P("head"),
            P(),
            P("expert", None, "head"),
            P("expert", "head", None),
        ),
        check_vma=False,
    )
```

```python
import functools

import jax
import jax.numpy as jnp
from jax import lax
from jax.experimental import pallas as pl
from jax.experimental.pallas import tpu as pltpu
from jax.sharding import PartitionSpec as P

eps = 1e-06
aux_weight = 0.01
f32 = jnp.float32
bf16 = jnp.bfloat16
gelu_scale = 0.7978845608028654
gelu_cube = 0.044715
scalar_memory = pl.BlockSpec(memory_space=pltpu.SMEM)


def mm(left, right, dims=((1,), (0,)), precision=None):
    return lax.dot_general(left, right, (dims, ((), ())), precision=precision, preferred_element_type=f32)


nt = ((1,), (1,))
tn = ((0,), (0,))


def call(body, outs, *args, scratch=()):
    in_specs = [scalar_memory if a.dtype == jnp.int32 and a.ndim == 1 else pl.BlockSpec() for a in args]
    return pl.pallas_call(
        body,
        out_shape=[jax.ShapeDtypeStruct(shape, kind) for shape, kind in outs],
        in_specs=in_specs,
        scratch_shapes=list(scratch),
        compiler_params=pltpu.CompilerParams(vmem_limit_bytes=40 * 1024 * 1024),
    )(*args)


def wide(ref, first, rows):
    return jnp.concatenate(
        [ref[i, first : first + rows, :].astype(f32) for i in range(ref.shape[0])], axis=1
    )


def row_scale(values):
    return lax.rsqrt(jnp.sum(values * values, axis=1, keepdims=True) * (1.0 / values.shape[1]) + eps)


def lanes(shape):
    return lax.broadcasted_iota(jnp.int32, shape, len(shape) - 1)


def sublanes(shape):
    return lax.broadcasted_iota(jnp.int32, shape, len(shape) - 2)


def side_lanes(rows, width, columns):
    spot = lanes((rows, width))
    out = jnp.zeros((rows, width), f32)
    for i, column in enumerate(columns):
        out = jnp.where(spot == i, column, out)
    return out


def high_low(values, count=2):
    pieces = []
    for _ in range(count):
        piece = values.astype(bf16).astype(f32)
        pieces.append(piece)
        values = values - piece
    return pieces


def softmax(values):
    raised = jnp.exp(values - jnp.max(values, axis=1, keepdims=True))
    return raised / jnp.sum(raised, axis=1, keepdims=True)


def gelu_parts(u):
    t = jnp.tanh(gelu_scale * (u + gelu_cube * u * u * u))
    value = 0.5 * u * (1.0 + t)
    slope = 0.5 * (1.0 + t) + 0.5 * u * (1.0 - t * t) * gelu_scale * (1.0 + 3.0 * gelu_cube * u * u)
    return value, slope


def bucket_hot(buckets_ref, count):
    span = buckets_ref.shape[1]
    return (sublanes((count, span)) == buckets_ref[...]).astype(f32)


def attend_kernel(scale, scalars, packed, wq, wk, wv, buckets, table, qkv_ref, weights_ref, attended_ref, scale_ref):
    tok = weights_ref.shape[1]
    heads = weights_ref.shape[0]
    col = wq.shape[1]
    size = col // heads
    x = wide(packed, 0, tok)
    gain = wide(packed, 2 * tok, 16)[0:1]
    scale_one = row_scale(x)
    scale_ref[...] = scale_one
    normed = (x * scale_one * gain).astype(bf16)
    projected = []
    for i, w in enumerate((wq, wk, wv)):
        rows = mm(normed, w[...]).astype(bf16)
        qkv_ref[:, i * col : (i + 1) * col] = rows
        projected.append(rows)
    query, key, value = projected
    offsets = mm(table[...], bucket_hot(buckets, table.shape[0]), tn, lax.Precision.HIGHEST)
    open_keys = lanes((tok, tok)) < scalars[0]
    outs = []
    for h in range(heads):
        at = slice(h * size, (h + 1) * size)
        spread = jnp.broadcast_to(offsets[h : h + 1, :], (tok, 2 * tok))
        bias = pltpu.roll(spread, tok + 1, 1, stride=1, stride_axis=0)[:, :tok]
        scores = mm(query[:, at], key[:, at], nt) * scale + bias
        weights = softmax(jnp.where(open_keys, scores, -1000000000.0))
        weights_ref[h] = weights
        outs.append(mm(weights.astype(bf16), value[:, at]))
    attended_ref[...] = jnp.concatenate(outs, axis=1).astype(bf16)


def route_kernel(
    capacity, scalars, packed, attended, w_output, routes, w_router,
    residual_ref, own_ref, scale_ref, normed_ref, router_ref, gate_ref, spots_ref, send_ref, parts,
):
    tok = routes.shape[0]
    width = w_router.shape[0]
    experts, slots, _ = send_ref.shape
    heads, _, col = packed.shape
    residual = wide(packed, 0, tok)
    for i in range(heads):
        residual = residual + mm(attended[i], w_output[i])
    residual_ref[...] = residual
    for i in range(heads):
        parts[i] = residual[:, i * col : (i + 1) * col]
    own_ref[...] = parts[scalars[1]]
    gain = wide(packed, 2 * tok, 16)[1:2]
    scale_two = row_scale(residual)
    scale_ref[...] = scale_two
    normed = (residual * scale_two * gain).astype(bf16)
    normed_ref[...] = normed
    router = softmax(mm(normed, w_router[...]))
    router_ref[...] = router
    route_hot = (lanes((tok, experts)) == routes[...]).astype(f32)
    gate_ref[...] = jnp.sum(router * route_hot, axis=1, keepdims=True)
    before = (lanes((tok, tok)) < sublanes((tok, tok))).astype(bf16)
    slot = jnp.sum(mm(before, route_hot.astype(bf16)) * route_hot, axis=1, keepdims=True).astype(jnp.int32)
    spots_ref[...] = routes[...] * slots + slot
    valid = (sublanes((tok, 1)) < scalars[0]).astype(f32)
    counts = jnp.sum(route_hot * valid, axis=0, keepdims=True)
    probs = jnp.sum(router * valid, axis=0, keepdims=True)
    grads = wide(packed, tok, tok).astype(bf16)
    both = jnp.concatenate([normed, grads], axis=1)
    for e in range(experts):
        pick = ((slot == lanes((tok, slots))) & (routes[...] == e)).astype(bf16)
        rows = mm(pick, both, tn)
        send_ref[e, :, :width] = rows[:, :width].astype(bf16)
        stats = side_lanes(1, width, [counts[:, e : e + 1]] + high_low(probs[:, e : e + 1], 3))
        tail = jnp.where(sublanes((slots, width)) == capacity, stats, rows[:, width:])
        send_ref[e, :, width:] = tail.astype(bf16)


def expert_kernel(
    capacity, scalars, rows_ref, w_in, w_out, w_router,
    back_ref, part_ref, hidden_ref, before_ref, grads_ref,
):
    total = rows_ref.shape[0]
    width, experts = w_router.shape
    heads, _, col = part_ref.shape
    slots = total // experts
    rows = rows_ref[:, :width]
    grads = rows_ref[:, width:].astype(f32)
    hidden, slope = gelu_parts(mm(rows, w_in[...]))
    hidden = hidden.astype(bf16)
    hidden_ref[...] = hidden
    produced = mm(hidden, w_out[...])
    for i in range(heads):
        part_ref[i] = produced[:, i * col : (i + 1) * col]
    probs = softmax(mm(rows, w_router[...]))
    gate = jnp.sum(jnp.where(lanes((total, experts)) == scalars[2], probs, 0.0), axis=1, keepdims=True)
    back = (gate * grads).astype(bf16)
    grads_ref[...] = back
    before = (mm(back, w_out[...], nt) * slope).astype(bf16)
    before_ref[...] = before
    rows_grad = mm(before, w_in[...], nt)
    gate_grad = jnp.sum(grads * produced, axis=1, keepdims=True)
    stats = jnp.zeros((1, 128), f32)
    for b in range(experts):
        stats = stats + grads[b * slots + capacity : b * slots + capacity + 1, :128]
    count = stats[:, 0:1]
    prob = stats[:, 1:2] + stats[:, 2:3] + stats[:, 3:4]
    side = side_lanes(
        total, 256 - col, high_low(gate_grad) + high_low(count) + high_low(prob, 3)
    ).astype(bf16)
    rows_grad = rows_grad.astype(bf16).astype(f32)
    for b in range(experts):
        at = slice(b * slots, (b + 1) * slots)
        for i in range(heads):
            back_ref[b * heads + i] = jnp.concatenate(
                [rows_grad[at, i * col : (i + 1) * col], side[at].astype(f32)], axis=1
            ).astype(bf16)


def weights_kernel(rows_ref, hidden, before, grads, in_ref, out_ref):
    width = in_ref.shape[0]
    in_ref[...] = mm(rows_ref[:, :width], before[...], tn)
    out_ref[...] = mm(hidden[...], grads[...], tn)


def collect_kernel(came, spots, grad_ref, gate_ref, stats_ref):
    tok, col = grad_ref.shape
    sources, slots, _ = came.shape
    experts = stats_ref.shape[1]
    heads = sources // experts
    sums = []
    for e in range(experts):
        total = came[e * heads].astype(f32)
        for i in range(1, heads):
            total = total + came[e * heads + i].astype(f32)
        sums.append(total)
    stats = jnp.concatenate([total[0:1, col:] for total in sums], axis=0) * (1.0 / heads)
    sums = jnp.concatenate(sums, axis=0)
    pick = spots[...] == lanes((tok, experts * slots))
    grad_ref[...] = mm(pick.astype(bf16), sums[:, :col].astype(bf16)).astype(bf16)
    gate = mm(pick.astype(f32), sums[:, col:], precision=lax.Precision.HIGHEST)
    gate_ref[...] = gate[:, 0:1] + gate[:, 1:2]
    diagonal = lanes((experts, experts)) == sublanes((experts, experts))
    count = stats[:, 2:3] + stats[:, 3:4]
    prob = stats[:, 4:5] + stats[:, 5:6] + stats[:, 6:7]
    stats_ref[0:1, :] = jnp.sum(jnp.where(diagonal, count, 0.0), axis=0, keepdims=True)
    stats_ref[1:2, :] = jnp.sum(jnp.where(diagonal, prob, 0.0), axis=0, keepdims=True)


def backward_kernel(
    scale, valid_total, scalars, packed, expert_grad, gate_grad, stats, residual_ref, scale_two, normed_two,
    router_ref, routes, w_router, w_output, weights_ref, qkv, wq, wk, wv, scale_one,
    late_ref, first_ref, own_ref, small_ref, parts,
):
    tok = routes.shape[0]
    heads_here = weights_ref.shape[0]
    col = wq.shape[1]
    size = col // heads_here
    width, experts = w_router.shape
    blocks = width // col
    valid = (sublanes((tok, 1)) < scalars[0]).astype(f32)
    route_hot = (lanes((tok, experts)) == routes[...]).astype(f32)
    router = router_ref[...]
    fraction = stats[0:1, :] * (1.0 / valid_total)
    prob_grad = route_hot * gate_grad[...] + aux_weight * experts / valid_total * fraction * valid
    logit_grad = router * (prob_grad - jnp.sum(router * prob_grad, axis=1, keepdims=True))
    logit_grad = logit_grad.astype(bf16)
    small_ref[0:experts, :] = mm(logit_grad, normed_two[...], tn)
    normed_grad = mm(logit_grad, w_router[...], nt) + wide(expert_grad, 0, tok)
    unit = residual_ref[...] * scale_two[...]
    gain_rows = wide(packed, 2 * tok, 16)
    gain_one, gain_two = gain_rows[0:1], gain_rows[1:2]
    small_ref[experts : experts + 1, :] = jnp.sum(normed_grad * unit, axis=0, keepdims=True)
    unit_grad = normed_grad * gain_two
    mean = jnp.sum(unit_grad * unit, axis=1, keepdims=True) * (1.0 / width)
    residual_grad = wide(packed, tok, tok) + scale_two[...] * (unit_grad - unit * mean)
    for i in range(blocks):
        parts[i] = residual_grad[:, i * col : (i + 1) * col]
    own = parts[scalars[1]]
    own_ref[...] = own
    branch = residual_grad.astype(bf16)
    attended_grad = mm(branch, w_output[...], nt).astype(bf16)
    flip = (lanes((tok, tok)) + sublanes((tok, tok)) == tok - 1).astype(bf16)
    query, key, value = (qkv[:, i * col : (i + 1) * col] for i in range(3))
    grads = [[], [], []]
    small_ref[experts + 2 :, :] = jnp.zeros((6, width), f32)
    for h in range(heads_here):
        at = slice(h * size, (h + 1) * size)
        out = attended_grad[:, at]
        weights = weights_ref[h]
        mass = mm(out, value[:, at], nt)
        score = weights * (mass - jnp.sum(weights * mass, axis=1, keepdims=True))
        score = score.astype(bf16)
        grads[0].append(mm(score, key[:, at]) * scale)
        grads[1].append(mm(score, query[:, at], tn) * scale)
        grads[2].append(mm(weights.astype(bf16), out, tn))
        flipped = jnp.concatenate([mm(flip, score), jnp.zeros((tok, tok), f32)], axis=1)
        rolled = pltpu.roll(flipped, 0, 1, stride=1, stride_axis=0)
        small_ref[experts + 2 + h : experts + 3 + h, : 2 * tok] = jnp.sum(rolled, axis=0, keepdims=True)
    first = jnp.zeros((tok, width), f32)
    row = jnp.zeros((tok, 1), f32)
    for i, w in enumerate((wq, wk, wv)):
        grad = jnp.concatenate(grads[i], axis=1)
        low = grad.astype(bf16)
        late_ref[0:tok, i * col : (i + 1) * col] = low
        first = first + mm(low, w[...], nt)
        row = row + jnp.sum(low.astype(f32) * qkv[:, i * col : (i + 1) * col].astype(f32), axis=1, keepdims=True)
    late_ref[0:tok, 3 * col :] = own.astype(bf16)
    unit_one = wide(packed, 0, tok) * scale_one[...]
    small_ref[experts + 1 : experts + 2, :] = jnp.sum(first * unit_one, axis=0, keepdims=True)
    late_ref[tok:, :] = small_ref[...].astype(bf16)
    side = side_lanes(tok, 256 - col, high_low(row))
    for i in range(blocks):
        first_ref[i] = jnp.concatenate([first[:, i * col : (i + 1) * col], side], axis=1).astype(bf16)


def finish_kernel(
    came, first, spots, gate, residual_own, residual_grad_own, inputs, gain, scale_one, block_ref, input_ref
):
    tok, col = inputs.shape
    heads = first.shape[0]
    pick = (spots[...] == lanes((tok, came.shape[0]))).astype(bf16)
    returned = mm(pick, came[...])
    block_ref[...] = (residual_own[...] + gate[...] * returned).astype(bf16)
    total = first[0].astype(f32)
    for i in range(1, heads):
        total = total + first[i].astype(f32)
    mean = (total[:, col : col + 1] + total[:, col + 1 : col + 2]) * (1.0 / (heads * col))
    unit = inputs[...].astype(f32) * scale_one[...]
    input_ref[...] = residual_grad_own[...] + scale_one[...] * (total[:, :col] * gain[...].astype(f32) - unit * mean)


def turn_kernel(all_in, all_attended, packed, tok, normed_ref, turned_ref):
    groups, heads, rows, col = all_in.shape
    gain = wide(packed, 2 * tok, 16)[0:1]
    for b in range(groups):
        x = jnp.concatenate([all_in[b, i].astype(f32) for i in range(heads)], axis=1)
        normed_ref[b * rows : (b + 1) * rows, :] = (x * row_scale(x) * gain).astype(bf16)
        turned_ref[b * rows : (b + 1) * rows, :] = jnp.concatenate(
            [all_attended[b, i].astype(f32) for i in range(heads)], axis=1
        ).astype(bf16)


def products_kernel(late, normed, turned, q_ref, k_ref, v_ref, out_ref, small_ref):
    groups, rows, width = late.shape
    tok = normed.shape[0] // groups
    heads, col = out_ref.shape[0], q_ref.shape[1]
    joined = jnp.concatenate([late[b, :tok, :] for b in range(groups)], axis=0)
    for i, ref in enumerate((q_ref, k_ref, v_ref)):
        ref[...] = mm(normed[...], joined[:, i * col : (i + 1) * col], tn)
    out = mm(turned[...], joined[:, 3 * col :], tn)
    small = late[0, tok:, :].astype(f32)
    for b in range(1, groups):
        small = small + late[b, tok:, :].astype(f32)
    small_ref[...] = small
    spare = rows - tok
    gains = small[spare - 7 : spare - 6, :]
    top = sublanes((16, col)) == 0
    for i in range(heads):
        out_ref[i, 0:col, :] = out[i * col : (i + 1) * col, :].astype(bf16)
        mine = gains[:, i * col : (i + 1) * col]
        high, low = high_low(mine)
        out_ref[i, col:, :] = jnp.where(
            top, high, jnp.where(sublanes((16, col)) == 1, low, 0.0)
        ).astype(bf16)


def few_experts():
    return lax.axis_size("expert") <= 8


def shards(
    inputs,
    out_grad,
    lengths,
    routes,
    buckets,
    gain_attn,
    w_query,
    w_key,
    w_value,
    w_output,
    bias_table,
    gain_ffn,
    w_router,
    w_in,
    w_out,
):
    tok, col = inputs.shape
    heads_here = bias_table.shape[1]
    head_size = w_query.shape[1] // heads_here
    width, experts = w_router.shape
    bucket_count = bias_table.shape[0]
    heads = width // col
    groups = lax.axis_size("expert")
    me_head, me_expert = lax.axis_index("head"), lax.axis_index("expert")
    capacity = max(2, (4 * tok + 3 * experts - 1) // (3 * experts))
    slots = -(-(capacity + 1) // 8) * 8
    valid_total = 3 * tok * groups // 4
    scale = head_size ** (-0.5)
    w_in, w_out = w_in[0], w_out[0]
    scalars = jnp.stack([lengths[0], me_head.astype(jnp.int32), me_expert.astype(jnp.int32)])
    buckets_row = jnp.pad(buckets, (0, 1), constant_values=-1)[None]

    packed = jnp.concatenate(
        [inputs, out_grad, gain_attn[None], gain_ffn[None], jnp.zeros((14, col), bf16)], axis=0
    )
    packed = lax.all_gather(packed, "head")
    w_output_full = lax.all_gather(w_output, "head")
    qkv, weights, attended, scale_one = call(
        functools.partial(attend_kernel, scale),
        [((tok, 3 * col), bf16), ((heads_here, tok, tok), f32), ((tok, col), bf16), ((tok, 1), f32)],
        scalars, packed, w_query, w_key, w_value, buckets_row, bias_table,
    )

    attended_parts = lax.all_gather(attended, "head")
    residual, residual_own, scale_two, normed_two, router, gate, spots, send = call(
        functools.partial(route_kernel, capacity),
        [
            ((tok, width), f32), ((tok, col), f32), ((tok, 1), f32), ((tok, width), bf16),
            ((tok, experts), f32), ((tok, 1), f32), ((tok, 1), jnp.int32),
            ((experts, slots, 2 * width), bf16),
        ],
        scalars, packed, attended_parts, w_output_full, routes, w_router,
        scratch=[pltpu.VMEM((heads, tok, col), f32)],
    )
    rows = lax.all_to_all(send, "expert", split_axis=0, concat_axis=0, tiled=True)
    rows = rows.reshape(experts * slots, 2 * width)

    back, part, hidden, before_grad, back_rows = call(
        functools.partial(expert_kernel, capacity),
        [
            ((experts * heads, slots, 256), bf16), ((heads, experts * slots, col), f32),
            ((experts * slots, width), bf16), ((experts * slots, width), bf16),
            ((experts * slots, width), bf16),
        ],
        scalars, rows, w_in, w_out, w_router,
    )
    produced = lax.psum_scatter(part, "head", scatter_dimension=0)
    came = lax.all_to_all(back, ("expert", "head"), split_axis=0, concat_axis=0, tiled=True)
    grad_own, gate_grad, stats = call(
        collect_kernel,
        [((tok, col), bf16), ((tok, 1), f32), ((8, experts), f32)],
        came, spots,
    )
    expert_grad = lax.all_gather(grad_own, "head")

    late, first, residual_grad_own, small = call(
        functools.partial(backward_kernel, scale, valid_total),
        [
            ((tok + experts + 8, width), bf16), ((heads, tok, 256), bf16), ((tok, col), f32),
            ((experts + 8, width), f32),
        ],
        scalars, packed, expert_grad, gate_grad, stats, residual, scale_two, normed_two, router, routes,
        w_router, w_output, weights, qkv, w_query, w_key, w_value, scale_one,
        scratch=[pltpu.VMEM((heads, tok, col), f32)],
    )
    if few_experts():
        late_all = lax.all_gather(late, "expert")
        all_in = lax.all_gather(inputs, ("expert", "head")).reshape(groups, heads, tok, col)
        all_attended = lax.all_gather(attended, ("expert", "head")).reshape(groups, heads, tok, col)

    first, produced, rows_after, hidden, _ = lax.optimization_barrier((first, produced, rows, hidden, late))
    first = lax.all_to_all(first, "head", split_axis=0, concat_axis=0, tiled=True)
    returned = lax.all_to_all(
        produced.astype(bf16).reshape(experts, slots, col), "expert", split_axis=0, concat_axis=0, tiled=True
    )
    block_out, input_grad = call(
        finish_kernel,
        [((tok, col), bf16), ((tok, col), f32)],
        returned.reshape(experts * slots, col), first, spots, gate, residual_own, residual_grad_own,
        inputs, gain_attn[None], scale_one,
    )
    in_weight_grad, out_weight_grad = call(
        weights_kernel, [((width, width), f32)] * 2, rows_after, hidden, before_grad, back_rows
    )

    if few_experts():
        normed_all, attended_all = call(
            lambda a, b, c, d, e: turn_kernel(a, b, c, tok, d, e),
            [((groups * tok, width), bf16)] * 2,
            all_in, all_attended, packed,
        )
        q_grad, k_grad, v_grad, traded, small = call(
            products_kernel,
            [((width, col), f32)] * 3 + [((heads, col + 16, col), bf16), ((experts + 8, width), f32)],
            late_all, normed_all, attended_all,
        )
        traded = lax.all_to_all(traded, "head", split_axis=0, concat_axis=0, tiled=True)
        output_grad = jnp.transpose(traded[:, :col], (1, 0, 2)).reshape(col, width).astype(f32)
        gain_one_grad = jnp.sum(traded[:, col : col + 2].astype(f32), axis=(0, 1))
    else:
        x = jnp.transpose(packed[:, :tok], (1, 0, 2)).reshape(tok, width).astype(f32)
        normed = (x * scale_one * packed[:, 2 * tok].reshape(1, width).astype(f32)).astype(bf16)
        summed = lax.psum(
            [mm(normed, late[:tok, i * col : (i + 1) * col], tn) for i in range(3)] + [small], "expert"
        )
        q_grad, k_grad, v_grad, small = summed
        branch = lax.all_gather(late[:tok, 3 * col :], "head", axis=1, tiled=True)
        output_grad = lax.psum(mm(attended, branch, tn), "expert")
        gain_one_grad = lax.psum_scatter(small[experts + 1], "head", tiled=True)
    router_grad = small[:experts].T
    gain_two_grad = lax.dynamic_slice_in_dim(small[experts], me_head * col, col)
    offset_grad = small[experts + 2 : experts + 2 + heads_here, : 2 * tok - 1]
    hot = (buckets[None, :] == jnp.arange(bucket_count)[:, None]).astype(f32)
    table_grad = mm(hot, offset_grad, nt, lax.Precision.HIGHEST)
    aux_loss = experts * jnp.sum(stats[0] * stats[1]) / (valid_total * valid_total)
    return (
        block_out,
        input_grad,
        aux_loss,
        gain_one_grad,
        q_grad,
        k_grad,
        v_grad,
        output_grad,
        table_grad,
        gain_two_grad,
        router_grad,
        in_weight_grad[None],
        out_weight_grad[None],
    )


def solution(mesh):
    return jax.shard_map(
        shards,
        mesh=mesh,
        in_specs=(
            P("expert", "head"),
            P("expert", "head"),
            P("expert"),
            P("expert", None),
            P(),
            P("head"),
            P(None, "head"),
            P(None, "head"),
            P(None, "head"),
            P("head", None),
            P(None, "head"),
            P("head"),
            P(),
            P("expert", None, "head"),
            P("expert", "head", None),
        ),
        out_specs=(
            P("expert", "head"),
            P("expert", "head"),
            P(),
            P("head"),
            P(None, "head"),
            P(None, "head"),
            P(None, "head"),
            P("head", None),
            P(None, "head"),
            P("head"),
            P(),
            P("expert", None, "head"),
            P("expert", "head", None),
        ),
        check_vma=False,
    )
```

```python
import functools

import jax
import jax.numpy as jnp
from jax import lax
from jax.experimental import pallas as pl
from jax.experimental.pallas import tpu as pltpu
from jax.sharding import PartitionSpec as P

eps = 1e-06
aux_weight = 0.01
f32 = jnp.float32
bf16 = jnp.bfloat16
gelu_scale = 0.7978845608028654
gelu_cube = 0.044715
highest = lax.Precision.HIGHEST
nt = ((1,), (1,))
tn = ((0,), (0,))


def mm(left, right, dims=((1,), (0,)), precision=None):
    return lax.dot_general(left, right, (dims, ((), ())), precision=precision, preferred_element_type=f32)


def call(body, outs, *args, scratch=()):
    scalar_memory = pl.BlockSpec(memory_space=pltpu.SMEM)
    in_specs = [scalar_memory if a.dtype == jnp.int32 and a.ndim == 1 else pl.BlockSpec() for a in args]
    shapes = []
    for shape, kind, *far in outs:
        shapes.append(pltpu.HBM(shape, kind) if far else jax.ShapeDtypeStruct(shape, kind))
    return pl.pallas_call(
        body,
        out_shape=shapes,
        in_specs=in_specs,
        scratch_shapes=list(scratch),
        compiler_params=pltpu.CompilerParams(vmem_limit_bytes=40 * 1024 * 1024),
    )(*args)


def tall(ref, first, rows):
    return jnp.concatenate([ref[i, first : first + rows, :].astype(f32) for i in range(ref.shape[0])], axis=0)


def gain_columns(block):
    turned = jnp.transpose(block.astype(f32))
    return [jnp.concatenate([turned[:, i : i + 1], turned[:64, i + 1 : i + 2]], axis=0) for i in (0, 2)]


def all_gains(packed):
    first = 2 * packed.shape[2] * 3 // 2
    pairs = [gain_columns(packed[i, first : first + 16, :]) for i in range(packed.shape[0])]
    return [jnp.concatenate([pair[i] for pair in pairs], axis=0) for i in range(2)]


def token_scale(values):
    return lax.rsqrt(jnp.sum(values * values, axis=0, keepdims=True) * (1.0 / values.shape[0]) + eps)


def lanes(shape):
    return lax.broadcasted_iota(jnp.int32, shape, len(shape) - 1)


def sublanes(shape):
    return lax.broadcasted_iota(jnp.int32, shape, len(shape) - 2)


def side_lanes(rows, width, columns):
    spot = lanes((rows, width))
    out = jnp.zeros((rows, width), f32)
    for i, column in enumerate(columns):
        out = jnp.where(spot == i, column, out)
    return out


def side_rows(rows, width, lines):
    spot = sublanes((rows, width))
    out = jnp.zeros((rows, width), f32)
    for i, line in enumerate(lines):
        out = jnp.where(spot == i, line, out)
    return out


def high_low(values, count=2):
    pieces = []
    for _ in range(count):
        piece = values.astype(bf16).astype(f32)
        pieces.append(piece)
        values = values - piece
    return pieces


def softmax(values, axis):
    raised = jnp.exp(values - jnp.max(values, axis=axis, keepdims=True))
    return raised / jnp.sum(raised, axis=axis, keepdims=True)


def gelu_parts(u):
    t = jnp.tanh(gelu_scale * (u + gelu_cube * u * u * u))
    value = 0.5 * u * (1.0 + t)
    slope = 0.5 * (1.0 + t) + 0.5 * u * (1.0 - t * t) * gelu_scale * (1.0 + 3.0 * gelu_cube * u * u)
    return value, slope


def fold_lanes(rows):
    return jnp.concatenate([rows[:, i : i + 128] for i in range(0, rows.shape[1], 128)], axis=0)


def unfold_lanes(rows, pieces):
    size = rows.shape[0] // pieces
    return jnp.concatenate([rows[i * size : (i + 1) * size] for i in range(pieces)], axis=1)


def pick_slots(spots, count):
    return sublanes((count, spots.shape[1])) == spots


def attend_kernel(scale, scalars, packed, wq, wk, wv, buckets, table, qkv_ref, weights_ref, attended_ref):
    heads, tok, _ = weights_ref.shape
    col = wq.shape[0]
    size = col // heads
    x = tall(packed, 0, col)
    normed = (x * token_scale(x) * all_gains(packed)[0]).astype(bf16)
    projected = []
    for i, w in enumerate((wq, wk, wv)):
        rows = mm(w[...], normed).astype(bf16)
        qkv_ref[i] = rows
        projected.append(rows)
    query, key, value = projected
    hot = (sublanes((table.shape[1], 2 * tok)) == buckets[...]).astype(f32)
    offsets = mm(table[...], hot, precision=highest)
    open_keys = lanes((tok, tok)) < scalars[0]
    outs = []
    for h in range(heads):
        at = slice(h * size, (h + 1) * size)
        spread = jnp.broadcast_to(offsets[h : h + 1, :], (tok, 2 * tok))
        bias = pltpu.roll(spread, tok + 1, 1, stride=1, stride_axis=0)[:, :tok]
        scores = mm(query[at], key[at], tn) * scale + bias
        weights = softmax(jnp.where(open_keys, scores, -1000000000.0), 1)
        weights_ref[h] = weights
        outs.append(mm(value[at], weights.astype(bf16), nt))
    attended_ref[...] = jnp.concatenate(outs, axis=0).astype(bf16)


def second_norm(residual, gain, w_router):
    scale = token_scale(residual)
    unit = residual * scale
    normed = (unit * gain).astype(bf16)
    return scale, unit, normed, softmax(mm(w_router, normed), 0)


def route_kernel(capacity, scalars, packed, attended, w_output, routes, w_router, residual_ref, side_ref, send_ref):
    tok = routes.shape[1]
    experts, slots, _ = send_ref.shape
    heads, col, _ = residual_ref.shape
    width = heads * col
    branch = mm(tall(attended, 0, col).astype(bf16), w_output[...], tn)
    residual = tall(packed, 0, col) + jnp.transpose(branch)
    for i in range(heads):
        residual_ref[i] = residual[i * col : (i + 1) * col]
    _, _, normed, router = second_norm(residual, all_gains(packed)[1], w_router[...])
    route_hot = (sublanes((experts, tok)) == routes[...]).astype(f32)
    gate = jnp.sum(router * route_hot, axis=0, keepdims=True)
    before = (sublanes((tok, tok)) < lanes((tok, tok))).astype(bf16)
    slot = jnp.sum(mm(route_hot.astype(bf16), before) * route_hot, axis=0, keepdims=True)
    spots = routes[...].astype(f32) * slots + slot
    side_ref[...] = side_rows(8, tok, [gate, spots])
    valid = (lanes((1, tok)) < scalars[0]).astype(f32)
    counts = jnp.sum(route_hot * valid, axis=1, keepdims=True)
    probs = high_low(jnp.sum(router * valid, axis=1, keepdims=True), 3)
    pick = pick_slots(spots.astype(jnp.int32), experts * slots).astype(bf16)
    rows = mm(pick, normed, nt)
    grads = mm(pick, tall(packed, col, col).astype(bf16), nt)
    for e in range(experts):
        at = slice(e * slots, (e + 1) * slots)
        send_ref[e, :, :width] = rows[at].astype(bf16)
        stats = side_lanes(1, width, [counts[e : e + 1]] + [piece[e : e + 1] for piece in probs])
        filled = jnp.where(sublanes((slots, width)) == capacity, stats, grads[at])
        send_ref[e, :, width:] = filled.astype(bf16)


def expert_kernel(
    capacity, scalars, rows_ref, w_in, w_out, w_router, back_ref, part_ref, hidden_ref, before_ref, grads_ref
):
    total = rows_ref.shape[0]
    experts, width = w_router.shape
    heads = part_ref.shape[0]
    col = width // heads
    slots = total // experts
    half = total // 2
    rows = rows_ref[:, :width]
    grads = rows_ref[:, width:].astype(f32)
    hidden, slope = gelu_parts(mm(rows, w_in[...]))
    hidden = hidden.astype(bf16)
    hidden_ref[...] = hidden
    produced = mm(hidden, w_out[...])
    for i in range(heads):
        mine = produced[:, i * col : (i + 1) * col]
        rest = mine[:, 128:]
        part_ref[i] = jnp.concatenate(
            [mine[:, :128], jnp.concatenate([rest[:half], rest[half:]], axis=1)], axis=0
        ).astype(bf16)
    probs = softmax(mm(rows, w_router[...], nt), 1)
    gate = jnp.sum(jnp.where(lanes((total, experts)) == scalars[2], probs, 0.0), axis=1, keepdims=True)
    back = (gate * grads).astype(bf16)
    grads_ref[...] = back
    before = (mm(back, w_out[...], nt) * slope).astype(bf16)
    before_ref[...] = before
    rows_grad = mm(before, w_in[...], nt)
    gate_grad = jnp.sum(grads * produced, axis=1, keepdims=True)
    stats = jnp.zeros((1, 128), f32)
    for b in range(experts):
        stats = stats + grads[b * slots + capacity : b * slots + capacity + 1, :128]
    prob = stats[:, 1:2] + stats[:, 2:3] + stats[:, 3:4]
    side = side_lanes(
        total, 256 - col, high_low(gate_grad) + high_low(stats[:, 0:1]) + high_low(prob, 3)
    )
    for b in range(experts):
        at = slice(b * slots, (b + 1) * slots)
        for i in range(heads):
            back_ref[b * heads + i] = jnp.concatenate(
                [rows_grad[at, i * col : (i + 1) * col], side[at]], axis=1
            ).astype(bf16)


def weights_kernel(rows_ref, hidden, before, grads, in_ref, out_ref):
    width = in_ref.shape[0]
    in_ref[...] = mm(rows_ref[:, :width], before[...], tn)
    out_ref[...] = mm(hidden[...], grads[...], tn)


def collect_kernel(came, side, grad_ref, gate_ref, stats_ref):
    col, tok = grad_ref.shape
    experts = stats_ref.shape[0]
    sources, slots, _ = came.shape
    heads = sources // experts
    sums = []
    for e in range(experts):
        total = came[e * heads].astype(f32)
        for i in range(1, heads):
            total = total + came[e * heads + i].astype(f32)
        sums.append(total)
    stats = jnp.concatenate([total[0:1, col:] for total in sums], axis=0) * (1.0 / heads)
    sums = jnp.concatenate(sums, axis=0)
    pick = pick_slots(side[1:2, :].astype(jnp.int32), experts * slots)
    grad_ref[...] = mm(sums[:, :col].astype(bf16), pick.astype(bf16), tn).astype(bf16)
    gate = mm(sums[:, col:], pick.astype(f32), tn, highest)
    gate_ref[...] = jnp.broadcast_to(gate[0:1] + gate[1:2], gate_ref.shape)
    count = stats[:, 2:3] + stats[:, 3:4]
    prob = stats[:, 4:5] + stats[:, 5:6] + stats[:, 6:7]
    stats_ref[...] = side_lanes(experts, 128, [count, prob])


def backward_kernel(
    scale, valid_total, scalars, packed, expert_grad, gate_grad, stats, residual_ref, routes, w_router,
    w_output, weights_ref, qkv, wq, wk, wv, attended, part, late_ref, first_ref, own_ref, small_ref, product_ref,
):
    tok = routes.shape[1]
    heads_here = weights_ref.shape[0]
    blocks, col, _ = residual_ref.shape
    experts, width = w_router.shape
    size = col // heads_here
    gain_one, gain_two = all_gains(packed)
    residual = tall(residual_ref, 0, col)
    scale_two, unit, normed, router = second_norm(residual, gain_two, w_router[...])
    valid = (lanes((1, tok)) < scalars[0]).astype(f32)
    route_hot = (sublanes((experts, tok)) == routes[...]).astype(f32)
    fraction = stats[:, 0:1] * (aux_weight * experts / (valid_total * valid_total))
    prob_grad = route_hot * gate_grad[0:1, :] + fraction * valid
    logit_grad = router * (prob_grad - jnp.sum(router * prob_grad, axis=0, keepdims=True))
    logit_grad = logit_grad.astype(bf16)
    normed_grad = mm(w_router[...], logit_grad, tn) + tall(expert_grad, 0, col)
    unit_grad = normed_grad * gain_two
    mean = jnp.sum(unit_grad * unit, axis=0, keepdims=True) * (1.0 / width)
    residual_grad = tall(packed, col, col) + scale_two * (unit_grad - unit * mean)
    branch = residual_grad.astype(bf16)
    attended_grad = mm(w_output[...], branch).astype(bf16)
    flip = (lanes((tok, tok)) + sublanes((tok, tok)) == tok - 1).astype(bf16)
    query, key, value = qkv[0], qkv[1], qkv[2]
    grads = [[], [], []]
    offsets = []
    for h in range(heads_here):
        at = slice(h * size, (h + 1) * size)
        out = attended_grad[at]
        weights = weights_ref[h]
        mass = mm(out, value[at], tn)
        score = weights * (mass - jnp.sum(weights * mass, axis=1, keepdims=True))
        score = score.astype(bf16)
        grads[0].append(mm(key[at], score, nt) * scale)
        grads[1].append(mm(query[at], score) * scale)
        grads[2].append(mm(out, weights.astype(bf16)))
        flipped = jnp.concatenate([mm(flip, score), jnp.zeros((tok, tok), f32)], axis=1)
        rolled = pltpu.roll(flipped, 0, 1, stride=1, stride_axis=0)
        offsets.append(jnp.sum(rolled, axis=0, keepdims=True))
    first = jnp.zeros((width, tok), f32)
    row = jnp.zeros((1, tok), f32)
    for i, w in enumerate((wq, wk, wv)):
        low = jnp.concatenate(grads[i], axis=0).astype(bf16)
        late_ref[i * col : (i + 1) * col, :] = low
        first = first + mm(w[...], low, tn)
        row = row + jnp.sum(low.astype(f32) * qkv[i].astype(f32), axis=0, keepdims=True)
    side = side_rows(16, tok, high_low(row))
    for i in range(blocks):
        at = slice(i * col, (i + 1) * col)
        first_ref[i, : col + 16, :] = jnp.concatenate([first[at], side], axis=0).astype(bf16)
        first_ref[i, col + 16 :, :] = part[i]

    product_ref[...] = mm(attended[...], branch, nt).astype(product_ref.dtype)
    gain_two_grad = jnp.sum(normed_grad * unit, axis=1, keepdims=True)
    gains = jnp.zeros((col, 1), f32)
    own = jnp.zeros((col, tok), f32)
    for i in range(blocks):
        at = slice(i * col, (i + 1) * col)
        gains = jnp.where(scalars[1] == i, gain_two_grad[at], gains)
        own = jnp.where(scalars[1] == i, residual_grad[at], own)
    own_ref[...] = own
    gains = jnp.transpose(side_lanes(col, 128, [gains]))[0:8]
    router_grad = mm(logit_grad, normed, nt)
    offsets = jnp.concatenate(offsets, axis=0)
    offsets = jnp.concatenate([offsets, jnp.zeros((8 - heads_here, 2 * tok), f32)], axis=0)
    gains = jnp.concatenate([gains, jnp.zeros((8, 64), f32)], axis=1)
    small_ref[...] = jnp.concatenate(
        [fold_lanes(router_grad), fold_lanes(offsets), fold_lanes(gains)], axis=0
    )


def first_kernel(joined, scalars, came, packed, own, small, ret_ref, sums_ref, input_ref):
    col, tok = own.shape
    heads = came.shape[0]
    experts = ret_ref.shape[0]
    total = came[0].astype(f32)
    for i in range(1, heads):
        total = total + came[i].astype(f32)
    mean = (total[col : col + 1] + total[col + 1 : col + 2]) * (1.0 / (heads * col))
    scale = token_scale(tall(packed, 0, col))
    mine = packed[scalars[1]].astype(f32)
    unit = mine[:col] * scale
    gain = gain_columns(mine[2 * col : 2 * col + 16])[0]
    input_ref[...] = own[...] + scale * (total[:col] * gain - unit * mean)
    gain_grad = jnp.sum(total[:col] * unit, axis=1, keepdims=True)
    gain_grad = jnp.transpose(side_lanes(col, 128, [jnp.zeros_like(gain_grad), gain_grad]))[0:8]
    gain_grad = jnp.concatenate([gain_grad, jnp.zeros((8, 64), f32)], axis=1)
    kept = small.shape[0] - 16
    sums = jnp.concatenate([small[:kept, :], small[kept:, :] + fold_lanes(gain_grad)], axis=0)
    sums_ref[...] = sums
    produced = total[col + 16 :]
    count = produced.shape[0] * 2 // 3
    half = count // 2
    top = produced[:count]
    rest = jnp.concatenate([produced[count:, :64], produced[count:, 64:]], axis=0)
    rest = jnp.concatenate([rest, jnp.zeros((count, 64), f32)], axis=1)
    slots = count // experts
    for e in range(experts):
        at = slice(e * slots, (e + 1) * slots)
        pieces = [top[at], rest[at]]
        if joined:
            pieces.append(sums)
        ret_ref[e] = jnp.concatenate(pieces, axis=0).astype(bf16)


def last_kernel(slots, scalars, came, side, residual, stats, buckets, *refs):
    block_ref, aux_ref, refs = refs[0], refs[1], refs[2:]
    experts = came.shape[0]
    heads, col, tok = residual.shape
    blocks = [came[e].astype(f32) for e in range(experts)]
    top = jnp.concatenate([block[:slots] for block in blocks], axis=0).astype(bf16)
    rest = jnp.concatenate([block[slots : 2 * slots] for block in blocks], axis=0).astype(bf16)
    pick = pick_slots(side[1:2, :].astype(jnp.int32), experts * slots).astype(bf16)
    returned = jnp.concatenate([mm(top, pick, tn), mm(rest, pick, tn)[: col - 128]], axis=0)
    block_ref[...] = (residual[scalars[1]] + side[0:1, :] * returned).astype(bf16)
    product = stats[:, 0:1] * stats[:, 1:2]
    valid_total = 3 * tok * experts // 4
    aux_ref[...] = jnp.sum(product, axis=0, keepdims=True) * (experts / (valid_total * valid_total))
    if refs:
        router_ref, table_ref, gains_ref = refs
        total = blocks[0][2 * slots :]
        for block in blocks[1:]:
            total = total + block[2 * slots :]
        wide = 6 * experts
        router_ref[...] = unfold_lanes(total[:wide], 6)
        offsets = unfold_lanes(total[wide : wide + 16], 2)
        hot = (sublanes((table_ref.shape[1], 2 * tok)) == buckets[...]).astype(f32)
        table_ref[...] = mm(offsets, hot, nt, highest)[: table_ref.shape[0]]
        gains_ref[...] = unfold_lanes(total[wide + 16 :], 2)


def turn_kernel(all_in, packed, normed_ref):
    groups, heads, col, tok = all_in.shape
    gain = all_gains(packed)[0]
    for b in range(groups):
        x = jnp.concatenate([all_in[b, i].astype(f32) for i in range(heads)], axis=0)
        normed_ref[:, b * tok : (b + 1) * tok] = (x * token_scale(x) * gain).astype(bf16)


def products_kernel(late, normed, q_ref, k_ref, v_ref):
    col = q_ref.shape[0]
    joined = jnp.concatenate([late[b] for b in range(late.shape[0])], axis=1)
    for i, ref in enumerate((q_ref, k_ref, v_ref)):
        ref[...] = mm(joined[i * col : (i + 1) * col], normed[...], nt)


def few_experts():
    return lax.axis_size("expert") <= 8


def shards(
    inputs,
    out_grad,
    lengths,
    routes,
    buckets,
    gain_attn,
    w_query,
    w_key,
    w_value,
    w_output,
    bias_table,
    gain_ffn,
    w_router,
    w_in,
    w_out,
):
    tok, col = inputs.shape
    heads_here = bias_table.shape[1]
    head_size = w_query.shape[1] // heads_here
    width, experts = w_router.shape
    bucket_count = bias_table.shape[0]
    heads = width // col
    groups = lax.axis_size("expert")
    me_head, me_expert = lax.axis_index("head"), lax.axis_index("expert")
    capacity = max(2, (4 * tok + 3 * experts - 1) // (3 * experts))
    slots = -(-(capacity + 1) // 8) * 8
    total = experts * slots
    valid_total = 3 * tok * groups // 4
    scale = head_size ** (-0.5)
    joined = few_experts()
    w_in, w_out = w_in[0], w_out[0]
    wq, wk, wv = w_query.T, w_key.T, w_value.T
    routes_row = routes.T
    router_rows = w_router.T
    scalars = jnp.stack([lengths[0], me_head.astype(jnp.int32), me_expert.astype(jnp.int32)])
    buckets_row = jnp.pad(buckets, (0, 1), constant_values=-1)[None]

    gains = jnp.pad(jnp.stack([gain_attn, gain_ffn]), ((0, 6), (0, 64))).reshape(16, 128)
    packed = lax.all_gather(jnp.concatenate([inputs.T, out_grad.T, gains], axis=0), "head")
    w_output_full = lax.all_gather(w_output, "head", tiled=True)
    if joined:
        all_in = lax.all_gather(inputs.T, ("expert", "head")).reshape(groups, heads, col, tok)
    qkv, weights, attended = call(
        functools.partial(attend_kernel, scale),
        [((3, col, tok), bf16, 1), ((heads_here, tok, tok), f32, 1), ((col, tok), bf16)],
        scalars, packed, wq, wk, wv, buckets_row, bias_table.T,
    )

    attended_parts = lax.all_gather(attended, "head")
    residual, side, send = call(
        functools.partial(route_kernel, capacity),
        [((heads, col, tok), f32, 1), ((8, tok), f32, 1), ((experts, slots, 2 * width), bf16)],
        scalars, packed, attended_parts, w_output_full, routes_row, router_rows,
    )
    rows = lax.all_to_all(send, "expert", split_axis=0, concat_axis=0, tiled=True)
    rows = rows.reshape(total, 2 * width)

    back, part, hidden, before_grad, back_rows = call(
        functools.partial(expert_kernel, capacity),
        [((experts * heads, slots, 256), bf16), ((heads, total * 3 // 2, 128), bf16, 1)]
        + [((total, width), bf16, 1)] * 3,
        scalars, rows, w_in, w_out, router_rows,
    )
    came = lax.all_to_all(back, ("expert", "head"), split_axis=0, concat_axis=0, tiled=True)
    grad_own, gate_grad, stats = call(
        collect_kernel,
        [((col, tok), bf16), ((8, tok), f32, 1), ((experts, 128), f32, 1)],
        came, side,
    )
    expert_grad = lax.all_gather(grad_own, "head")

    late, first, residual_grad_own, small, product = call(
        functools.partial(backward_kernel, scale, valid_total),
        [
            ((3 * col, tok), bf16, 1), ((heads, col + 16 + total * 3 // 2, 128), bf16), ((col, tok), f32, 1),
            ((6 * experts + 32, 128), f32, 1), ((col, width), bf16 if joined else f32, 1),
        ],
        scalars, packed, expert_grad, gate_grad, stats, residual, routes_row, router_rows,
        w_output, weights, qkv, wq, wk, wv, attended, part,
    )

    output_grad = lax.psum(product, "expert").astype(f32)
    if joined:
        late_all = lax.all_gather(late, "expert")

    first = lax.all_to_all(first, "head", split_axis=0, concat_axis=0, tiled=True)
    ret, sums, input_grad = call(
        functools.partial(first_kernel, joined),
        [
            ((experts, 2 * slots + (6 * experts + 32 if joined else 0), 128), bf16),
            ((6 * experts + 32, 128), f32, 1), ((col, tok), f32),
        ],
        scalars, first, packed, residual_grad_own, small,
    )
    ret = lax.all_to_all(ret, "expert", split_axis=0, concat_axis=0, tiled=True)
    out = call(
        functools.partial(last_kernel, slots),
        [((col, tok), bf16), ((1, 1), f32)]
        + ([((experts, width), f32), ((heads_here, bucket_count), f32), ((8, 256), f32)] if joined else []),
        scalars, ret, side, residual, stats, buckets_row,
    )
    block_out, aux_loss = out[:2]
    in_weight_grad, out_weight_grad = call(
        weights_kernel, [((width, width), f32)] * 2, rows, hidden, before_grad, back_rows
    )
    if joined:
        router_grad, table_grad, gain_grads = out[2:]
        normed_all = call(turn_kernel, [((width, groups * tok), bf16)], all_in, packed)[0]
        q_grad, k_grad, v_grad = call(products_kernel, [((col, width), f32)] * 3, late_all, normed_all)
    else:
        gain = packed[:, 2 * col : 2 * col + 2].reshape(heads, 256)[:, :col].reshape(width, 1)
        x = packed[:, :col].reshape(width, tok).astype(f32)
        normed = (x * token_scale(x) * gain.astype(f32)).astype(bf16)
        products = [mm(late[i * col : (i + 1) * col], normed, nt) for i in range(3)]
        q_grad, k_grad, v_grad, sums = lax.psum(products + [sums], "expert")
        wide = 6 * experts
        router_grad = unfold_lanes(sums[:wide], 6)
        offsets = unfold_lanes(sums[wide : wide + 16], 2)[:heads_here, : 2 * tok - 1]
        hot = (buckets[None, :] == jnp.arange(bucket_count)[:, None]).astype(f32)
        table_grad = mm(offsets, hot, nt, highest)
        gain_grads = unfold_lanes(sums[wide + 16 :], 2)
    return (
        block_out.T,
        input_grad.T,
        aux_loss.reshape(()),
        gain_grads[1, :col],
        q_grad.T,
        k_grad.T,
        v_grad.T,
        output_grad,
        table_grad.T,
        gain_grads[0, :col],
        router_grad.T,
        in_weight_grad[None],
        out_weight_grad[None],
    )


def solution(mesh):
    return jax.shard_map(
        shards,
        mesh=mesh,
        in_specs=(
            P("expert", "head"),
            P("expert", "head"),
            P("expert"),
            P("expert", None),
            P(),
            P("head"),
            P(None, "head"),
            P(None, "head"),
            P(None, "head"),
            P("head", None),
            P(None, "head"),
            P("head"),
            P(),
            P("expert", None, "head"),
            P("expert", "head", None),
        ),
        out_specs=(
            P("expert", "head"),
            P("expert", "head"),
            P(),
            P("head"),
            P(None, "head"),
            P(None, "head"),
            P(None, "head"),
            P("head", None),
            P(None, "head"),
            P("head"),
            P(),
            P("expert", None, "head"),
            P("expert", "head", None),
        ),
        check_vma=False,
    )
```

```python
import functools

import jax
import jax.numpy as jnp
from jax import lax
from jax.experimental import pallas as pl
from jax.experimental.pallas import tpu as pltpu
from jax.sharding import PartitionSpec as P

eps = 1e-06
aux_weight = 0.01
f32 = jnp.float32
bf16 = jnp.bfloat16
gelu_scale = 0.7978845608028654
gelu_cube = 0.044715
highest = lax.Precision.HIGHEST
nt = ((1,), (1,))
tn = ((0,), (0,))


def mm(left, right, dims=((1,), (0,)), precision=None):
    return lax.dot_general(left, right, (dims, ((), ())), precision=precision, preferred_element_type=f32)


def call(body, outs, *args, scratch=()):
    scalar_memory = pl.BlockSpec(memory_space=pltpu.SMEM)
    in_specs = [scalar_memory if a.dtype == jnp.int32 and a.ndim == 1 else pl.BlockSpec() for a in args]
    shapes = []
    for shape, kind, *far in outs:
        shapes.append(pltpu.HBM(shape, kind) if far else jax.ShapeDtypeStruct(shape, kind))
    return pl.pallas_call(
        body,
        out_shape=shapes,
        in_specs=in_specs,
        scratch_shapes=list(scratch),
        compiler_params=pltpu.CompilerParams(vmem_limit_bytes=40 * 1024 * 1024),
    )(*args)


def far(array):
    return pltpu.with_memory_space_constraint(array, pltpu.HBM)


def tall(ref, first, rows):
    return jnp.concatenate([ref[i, first : first + rows, :].astype(f32) for i in range(ref.shape[0])], axis=0)


def gain_columns(block):
    turned = jnp.transpose(block.astype(f32))
    return [jnp.concatenate([turned[:, i : i + 1], turned[:64, i + 1 : i + 2]], axis=0) for i in (0, 2)]


def all_gains(packed):
    first = 2 * packed.shape[2] * 3 // 2
    pairs = [gain_columns(packed[i, first : first + 16, :]) for i in range(packed.shape[0])]
    return [jnp.concatenate([pair[i] for pair in pairs], axis=0) for i in range(2)]


def token_scale(values):
    return lax.rsqrt(jnp.sum(values * values, axis=0, keepdims=True) * (1.0 / values.shape[0]) + eps)


def lanes(shape):
    return lax.broadcasted_iota(jnp.int32, shape, len(shape) - 1)


def sublanes(shape):
    return lax.broadcasted_iota(jnp.int32, shape, len(shape) - 2)


def side_lanes(rows, width, columns):
    spot = lanes((rows, width))
    out = jnp.zeros((rows, width), f32)
    for i, column in enumerate(columns):
        out = jnp.where(spot == i, column, out)
    return out


def side_rows(rows, width, lines):
    spot = sublanes((rows, width))
    out = jnp.zeros((rows, width), f32)
    for i, line in enumerate(lines):
        out = jnp.where(spot == i, line, out)
    return out


def high_low(values, count=2):
    pieces = []
    for _ in range(count):
        piece = values.astype(bf16).astype(f32)
        pieces.append(piece)
        values = values - piece
    return pieces


def softmax(values, axis):
    raised = jnp.exp(values - jnp.max(values, axis=axis, keepdims=True))
    return raised / jnp.sum(raised, axis=axis, keepdims=True)


def gelu_parts(u):
    t = jnp.tanh(gelu_scale * (u + gelu_cube * u * u * u))
    value = 0.5 * u * (1.0 + t)
    slope = 0.5 * (1.0 + t) + 0.5 * u * (1.0 - t * t) * gelu_scale * (1.0 + 3.0 * gelu_cube * u * u)
    return value, slope


def fold_lanes(rows):
    return jnp.concatenate([rows[:, i : i + 128] for i in range(0, rows.shape[1], 128)], axis=0)


def unfold_lanes(rows, pieces):
    size = rows.shape[0] // pieces
    return jnp.concatenate([rows[i * size : (i + 1) * size] for i in range(pieces)], axis=1)


def pick_slots(spots, count):
    return sublanes((count, spots.shape[1])) == spots


def attend_kernel(scale, scalars, packed, wq, wk, wv, buckets, table, qkv_ref, weights_ref, attended_ref):
    heads, tok, _ = weights_ref.shape
    col = wq.shape[0]
    size = col // heads
    x = tall(packed, 0, col)
    normed = (x * token_scale(x) * all_gains(packed)[0]).astype(bf16)
    projected = []
    for i, w in enumerate((wq, wk, wv)):
        rows = mm(w[...], normed).astype(bf16)
        qkv_ref[i] = rows
        projected.append(rows)
    query, key, value = projected
    hot = (sublanes((table.shape[1], 2 * tok)) == buckets[...]).astype(f32)
    offsets = mm(table[...], hot, precision=highest)
    open_keys = lanes((tok, tok)) < scalars[0]
    outs = []
    for h in range(heads):
        at = slice(h * size, (h + 1) * size)
        spread = jnp.broadcast_to(offsets[h : h + 1, :], (tok, 2 * tok))
        bias = pltpu.roll(spread, tok + 1, 1, stride=1, stride_axis=0)[:, :tok]
        scores = mm(query[at], key[at], tn) * scale + bias
        weights = softmax(jnp.where(open_keys, scores, -1000000000.0), 1)
        weights_ref[h] = weights
        outs.append(mm(value[at], weights.astype(bf16), nt))
    attended_ref[...] = jnp.concatenate(outs, axis=0).astype(bf16)


def second_norm(residual, gain, w_router):
    scale = token_scale(residual)
    unit = residual * scale
    normed = (unit * gain).astype(bf16)
    return scale, unit, normed, softmax(mm(w_router, normed), 0)


def route_kernel(capacity, scalars, packed, attended, w_output, routes, w_router, residual_ref, side_ref, send_ref):
    tok = routes.shape[1]
    experts, slots, _ = send_ref.shape
    heads, col, _ = residual_ref.shape
    width = heads * col
    branch = mm(tall(attended, 0, col).astype(bf16), w_output[...], tn)
    residual = tall(packed, 0, col) + jnp.transpose(branch)
    for i in range(heads):
        residual_ref[i] = residual[i * col : (i + 1) * col]
    _, _, normed, router = second_norm(residual, all_gains(packed)[1], w_router[...])
    route_hot = (sublanes((experts, tok)) == routes[...]).astype(f32)
    gate = jnp.sum(router * route_hot, axis=0, keepdims=True)
    before = (sublanes((tok, tok)) < lanes((tok, tok))).astype(bf16)
    slot = jnp.sum(mm(route_hot.astype(bf16), before) * route_hot, axis=0, keepdims=True)
    spots = routes[...].astype(f32) * slots + slot
    side_ref[...] = side_rows(8, tok, [gate, spots])
    valid = (lanes((1, tok)) < scalars[0]).astype(f32)
    counts = jnp.sum(route_hot * valid, axis=1, keepdims=True)
    probs = high_low(jnp.sum(router * valid, axis=1, keepdims=True), 3)
    pick = pick_slots(spots.astype(jnp.int32), experts * slots).astype(bf16)
    rows = mm(pick, normed, nt)
    grads = mm(pick, tall(packed, col, col).astype(bf16), nt)
    for e in range(experts):
        at = slice(e * slots, (e + 1) * slots)
        send_ref[e, :, :width] = rows[at].astype(bf16)
        stats = side_lanes(1, width, [counts[e : e + 1]] + [piece[e : e + 1] for piece in probs])
        filled = jnp.where(sublanes((slots, width)) == capacity, stats, grads[at])
        send_ref[e, :, width:] = filled.astype(bf16)


def expert_kernel(
    capacity, scalars, rows_ref, w_in, w_out, w_router, back_ref, part_ref, hidden_ref, before_ref, grads_ref
):
    total = rows_ref.shape[0]
    experts, width = w_router.shape
    heads = part_ref.shape[0]
    col = width // heads
    slots = total // experts
    half = total // 2
    rows = rows_ref[:, :width]
    grads = rows_ref[:, width:].astype(f32)
    hidden, slope = gelu_parts(mm(rows, w_in[...]))
    hidden = hidden.astype(bf16)
    hidden_ref[...] = hidden
    produced = mm(hidden, w_out[...])
    for i in range(heads):
        mine = produced[:, i * col : (i + 1) * col]
        rest = mine[:, 128:]
        part_ref[i] = jnp.concatenate(
            [mine[:, :128], jnp.concatenate([rest[:half], rest[half:]], axis=1)], axis=0
        ).astype(bf16)
    probs = softmax(mm(rows, w_router[...], nt), 1)
    gate = jnp.sum(jnp.where(lanes((total, experts)) == scalars[2], probs, 0.0), axis=1, keepdims=True)
    back = (gate * grads).astype(bf16)
    grads_ref[...] = back
    before = (mm(back, w_out[...], nt) * slope).astype(bf16)
    before_ref[...] = before
    rows_grad = mm(before, w_in[...], nt)
    gate_grad = jnp.sum(grads * produced, axis=1, keepdims=True)
    stats = jnp.zeros((1, 128), f32)
    for b in range(experts):
        stats = stats + grads[b * slots + capacity : b * slots + capacity + 1, :128]
    prob = stats[:, 1:2] + stats[:, 2:3] + stats[:, 3:4]
    side = side_lanes(
        total, 256 - col, high_low(gate_grad) + high_low(stats[:, 0:1]) + high_low(prob, 3)
    )
    for b in range(experts):
        at = slice(b * slots, (b + 1) * slots)
        for i in range(heads):
            back_ref[b * heads + i] = jnp.concatenate(
                [rows_grad[at, i * col : (i + 1) * col], side[at]], axis=1
            ).astype(bf16)


def weights_kernel(rows_ref, hidden, before, grads, in_ref, out_ref):
    width = in_ref.shape[0]
    in_ref[...] = mm(rows_ref[:, :width], before[...], tn)
    out_ref[...] = mm(hidden[...], grads[...], tn)


def collect_kernel(came, side, grad_ref, gate_ref, stats_ref):
    col, tok = grad_ref.shape
    experts = stats_ref.shape[0]
    sources, slots, _ = came.shape
    heads = sources // experts
    sums = []
    for e in range(experts):
        total = came[e * heads].astype(f32)
        for i in range(1, heads):
            total = total + came[e * heads + i].astype(f32)
        sums.append(total)
    stats = jnp.concatenate([total[0:1, col:] for total in sums], axis=0) * (1.0 / heads)
    sums = jnp.concatenate(sums, axis=0)
    pick = pick_slots(side[1:2, :].astype(jnp.int32), experts * slots)
    grad_ref[...] = mm(sums[:, :col].astype(bf16), pick.astype(bf16), tn).astype(bf16)
    gate = mm(sums[:, col:], pick.astype(f32), tn, highest)
    gate_ref[...] = jnp.broadcast_to(gate[0:1] + gate[1:2], gate_ref.shape)
    count = stats[:, 2:3] + stats[:, 3:4]
    prob = stats[:, 4:5] + stats[:, 5:6] + stats[:, 6:7]
    stats_ref[...] = side_lanes(experts, 128, [count, prob])


def backward_kernel(
    scale, valid_total, scalars, packed, expert_grad, gate_grad, stats, residual_ref, routes, w_router,
    w_output, weights_ref, qkv, wq, wk, wv, attended, part, late_ref, first_ref, own_ref, small_ref, product_ref,
):
    tok = routes.shape[1]
    heads_here = weights_ref.shape[0]
    blocks, col, _ = residual_ref.shape
    experts, width = w_router.shape
    size = col // heads_here
    gain_one, gain_two = all_gains(packed)
    residual = tall(residual_ref, 0, col)
    scale_two, unit, normed, router = second_norm(residual, gain_two, w_router[...])
    valid = (lanes((1, tok)) < scalars[0]).astype(f32)
    route_hot = (sublanes((experts, tok)) == routes[...]).astype(f32)
    fraction = stats[:, 0:1] * (aux_weight * experts / (valid_total * valid_total))
    prob_grad = route_hot * gate_grad[0:1, :] + fraction * valid
    logit_grad = router * (prob_grad - jnp.sum(router * prob_grad, axis=0, keepdims=True))
    logit_grad = logit_grad.astype(bf16)
    normed_grad = mm(w_router[...], logit_grad, tn) + tall(expert_grad, 0, col)
    unit_grad = normed_grad * gain_two
    mean = jnp.sum(unit_grad * unit, axis=0, keepdims=True) * (1.0 / width)
    residual_grad = tall(packed, col, col) + scale_two * (unit_grad - unit * mean)
    branch = residual_grad.astype(bf16)
    attended_grad = mm(w_output[...], branch).astype(bf16)
    flip = (lanes((tok, tok)) + sublanes((tok, tok)) == tok - 1).astype(bf16)
    query, key, value = qkv[0], qkv[1], qkv[2]
    grads = [[], [], []]
    offsets = []
    for h in range(heads_here):
        at = slice(h * size, (h + 1) * size)
        out = attended_grad[at]
        weights = weights_ref[h]
        mass = mm(out, value[at], tn)
        score = weights * (mass - jnp.sum(weights * mass, axis=1, keepdims=True))
        score = score.astype(bf16)
        grads[0].append(mm(key[at], score, nt) * scale)
        grads[1].append(mm(query[at], score) * scale)
        grads[2].append(mm(out, weights.astype(bf16)))
        flipped = jnp.concatenate([mm(flip, score), jnp.zeros((tok, tok), f32)], axis=1)
        rolled = pltpu.roll(flipped, 0, 1, stride=1, stride_axis=0)
        offsets.append(jnp.sum(rolled, axis=0, keepdims=True))
    first = jnp.zeros((width, tok), f32)
    row = jnp.zeros((1, tok), f32)
    for i, w in enumerate((wq, wk, wv)):
        low = jnp.concatenate(grads[i], axis=0).astype(bf16)
        late_ref[i * col : (i + 1) * col, :] = low
        first = first + mm(w[...], low, tn)
        row = row + jnp.sum(low.astype(f32) * qkv[i].astype(f32), axis=0, keepdims=True)
    side = side_rows(16, tok, high_low(row))
    for i in range(blocks):
        at = slice(i * col, (i + 1) * col)
        first_ref[i, : col + 16, :] = jnp.concatenate([first[at], side], axis=0).astype(bf16)
        first_ref[i, col + 16 :, :] = part[i]

    product = mm(attended[...], branch, nt)
    pieces = product_ref.shape[0]
    for b in range(pieces):
        at = slice(b * (col // pieces), (b + 1) * (col // pieces))
        product_ref[b] = (product if pieces == 1 else fold_lanes(product[at])).astype(product_ref.dtype)
    gain_two_grad = jnp.sum(normed_grad * unit, axis=1, keepdims=True)
    gains = jnp.zeros((col, 1), f32)
    own = jnp.zeros((col, tok), f32)
    for i in range(blocks):
        at = slice(i * col, (i + 1) * col)
        gains = jnp.where(scalars[1] == i, gain_two_grad[at], gains)
        own = jnp.where(scalars[1] == i, residual_grad[at], own)
    own_ref[...] = own
    gains = jnp.transpose(side_lanes(col, 128, [gains]))[0:8]
    router_grad = mm(logit_grad, normed, nt)
    offsets = jnp.concatenate(offsets, axis=0)
    offsets = jnp.concatenate([offsets, jnp.zeros((8 - heads_here, 2 * tok), f32)], axis=0)
    gains = jnp.concatenate([gains, jnp.zeros((8, 64), f32)], axis=1)
    small_ref[...] = jnp.concatenate(
        [fold_lanes(router_grad), fold_lanes(offsets), fold_lanes(gains)], axis=0
    )


def first_kernel(scalars, came, packed, own, small, *refs):
    product, (ret_ref, sums_ref, input_ref) = refs[:-3], refs[-3:]
    col, tok = own.shape
    heads = came.shape[0]
    experts = ret_ref.shape[0]
    total = came[0].astype(f32)
    for i in range(1, heads):
        total = total + came[i].astype(f32)
    mean = (total[col : col + 1] + total[col + 1 : col + 2]) * (1.0 / (heads * col))
    scale = token_scale(tall(packed, 0, col))
    mine = packed[scalars[1]].astype(f32)
    unit = mine[:col] * scale
    gain = gain_columns(mine[2 * col : 2 * col + 16])[0]
    input_ref[...] = own[...] + scale * (total[:col] * gain - unit * mean)
    gain_grad = jnp.sum(total[:col] * unit, axis=1, keepdims=True)
    gain_grad = jnp.transpose(side_lanes(col, 128, [jnp.zeros_like(gain_grad), gain_grad]))[0:8]
    gain_grad = jnp.concatenate([gain_grad, jnp.zeros((8, 64), f32)], axis=1)
    kept = small.shape[0] - 16
    sums = jnp.concatenate([small[:kept, :], small[kept:, :] + fold_lanes(gain_grad)], axis=0)
    sums_ref[...] = sums
    produced = total[col + 16 :]
    count = produced.shape[0] * 2 // 3
    half = count // 2
    top = produced[:count]
    rest = jnp.concatenate([produced[count:, :64], produced[count:, 64:]], axis=0)
    rest = jnp.concatenate([rest, jnp.zeros((count, 64), f32)], axis=1)
    slots = count // experts
    for e in range(experts):
        at = slice(e * slots, (e + 1) * slots)
        pieces = [top[at], rest[at]]
        if product:
            pieces += [sums, product[0][e].astype(f32)]
        ret_ref[e] = jnp.concatenate(pieces, axis=0).astype(bf16)


def last_kernel(slots, scalars, came, side, residual, stats, buckets, *refs):
    block_ref, aux_ref, refs = refs[0], refs[1], refs[2:]
    experts = came.shape[0]
    heads, col, tok = residual.shape
    blocks = [came[e].astype(f32) for e in range(experts)]
    top = jnp.concatenate([block[:slots] for block in blocks], axis=0).astype(bf16)
    rest = jnp.concatenate([block[slots : 2 * slots] for block in blocks], axis=0).astype(bf16)
    pick = pick_slots(side[1:2, :].astype(jnp.int32), experts * slots).astype(bf16)
    returned = jnp.concatenate([mm(top, pick, tn), mm(rest, pick, tn)[: col - 128]], axis=0)
    block_ref[...] = (residual[scalars[1]] + side[0:1, :] * returned).astype(bf16)
    product = stats[:, 0:1] * stats[:, 1:2]
    valid_total = 3 * tok * experts // 4
    aux_ref[...] = jnp.sum(product, axis=0, keepdims=True) * (experts / (valid_total * valid_total))
    if refs:
        router_ref, table_ref, gains_ref, share_ref = refs
        total = blocks[0][2 * slots :]
        for block in blocks[1:]:
            total = total + block[2 * slots :]
        wide = 6 * experts
        for e in range(experts):
            share_ref[e] = total[wide + 32 :].astype(bf16)
        router_ref[...] = unfold_lanes(total[:wide], 6)
        offsets = unfold_lanes(total[wide : wide + 16], 2)
        hot = (sublanes((table_ref.shape[1], 2 * tok)) == buckets[...]).astype(f32)
        table_ref[...] = mm(offsets, hot, nt, highest)[: table_ref.shape[0]]
        gains_ref[...] = unfold_lanes(total[wide + 16 : wide + 32], 2)


def turn_kernel(all_in, packed, normed_ref):
    groups, heads, col, tok = all_in.shape
    gain = all_gains(packed)[0]
    for b in range(groups):
        x = jnp.concatenate([all_in[b, i].astype(f32) for i in range(heads)], axis=0)
        normed_ref[:, b * tok : (b + 1) * tok] = (x * token_scale(x) * gain).astype(bf16)


def products_kernel(late, normed, shares, q_ref, k_ref, v_ref, out_ref):
    groups = shares.shape[0]
    size = out_ref.shape[0] // groups
    for b in range(groups):
        out_ref[b * size : (b + 1) * size, :] = unfold_lanes(shares[b].astype(f32), 6)
    col = q_ref.shape[0]
    joined = jnp.concatenate([late[b] for b in range(late.shape[0])], axis=1)
    for i, ref in enumerate((q_ref, k_ref, v_ref)):
        ref[...] = mm(joined[i * col : (i + 1) * col], normed[...], nt)


def few_experts():
    return lax.axis_size("expert") <= 8


def shards(
    inputs,
    out_grad,
    lengths,
    routes,
    buckets,
    gain_attn,
    w_query,
    w_key,
    w_value,
    w_output,
    bias_table,
    gain_ffn,
    w_router,
    w_in,
    w_out,
):
    tok, col = inputs.shape
    heads_here = bias_table.shape[1]
    head_size = w_query.shape[1] // heads_here
    width, experts = w_router.shape
    bucket_count = bias_table.shape[0]
    heads = width // col
    groups = lax.axis_size("expert")
    me_head, me_expert = lax.axis_index("head"), lax.axis_index("expert")
    capacity = max(2, (4 * tok + 3 * experts - 1) // (3 * experts))
    slots = -(-(capacity + 1) // 8) * 8
    total = experts * slots
    valid_total = 3 * tok * groups // 4
    scale = head_size ** (-0.5)
    joined = few_experts()
    w_in, w_out = w_in[0], w_out[0]
    wq, wk, wv = w_query.T, w_key.T, w_value.T
    routes_row = routes.T
    router_rows = w_router.T
    scalars = jnp.stack([lengths[0], me_head.astype(jnp.int32), me_expert.astype(jnp.int32)])
    buckets_row = jnp.pad(buckets, (0, 1), constant_values=-1)[None]

    space = jnp.zeros((64,), bf16)
    gains = jnp.concatenate([gain_attn, space, gain_ffn, space, jnp.zeros((1536,), bf16)]).reshape(16, 128)
    packed = lax.all_gather(jnp.concatenate([inputs.T, out_grad.T, gains], axis=0), "head")
    w_output_full = lax.all_gather(w_output, "head", tiled=True)
    if joined:
        all_in = lax.all_gather(inputs.T, ("expert", "head")).reshape(groups, heads, col, tok)
    qkv, weights, attended = call(
        functools.partial(attend_kernel, scale),
        [((3, col, tok), bf16, 1), ((heads_here, tok, tok), f32, 1), ((col, tok), bf16)],
        scalars, packed, far(wq), far(wk), far(wv), far(buckets_row), far(bias_table.T),
    )

    attended_parts = lax.all_gather(attended, "head")
    residual, side, send = call(
        functools.partial(route_kernel, capacity),
        [((heads, col, tok), f32, 1), ((8, tok), f32, 1), ((experts, slots, 2 * width), bf16)],
        scalars, packed, attended_parts, far(w_output_full), far(routes_row), far(router_rows),
    )
    rows = lax.all_to_all(send, "expert", split_axis=0, concat_axis=0, tiled=True)
    rows = rows.reshape(total, 2 * width)

    back, part, hidden, before_grad, back_rows = call(
        functools.partial(expert_kernel, capacity),
        [((experts * heads, slots, 256), bf16), ((heads, total * 3 // 2, 128), bf16, 1)]
        + [((total, width), bf16, 1)] * 3,
        scalars, rows, far(w_in), far(w_out), far(router_rows),
    )
    came = lax.all_to_all(back, ("expert", "head"), split_axis=0, concat_axis=0, tiled=True)
    grad_own, gate_grad, stats = call(
        collect_kernel,
        [((col, tok), bf16), ((8, tok), f32, 1), ((experts, 128), f32, 1)],
        came, far(side),
    )
    expert_grad = lax.all_gather(grad_own, "head")

    late, first, residual_grad_own, small, product = call(
        functools.partial(backward_kernel, scale, valid_total),
        [
            ((3 * col, tok), bf16, 1), ((heads, col + 16 + total * 3 // 2, 128), bf16), ((col, tok), f32, 1),
            ((6 * experts + 32, 128), f32, 1),
            ((groups, col // groups * 6, 128), bf16, 1) if joined else ((1, col, width), f32, 1),
        ],
        scalars, packed, expert_grad, far(gate_grad), far(stats), far(residual), far(routes_row),
        far(router_rows), far(w_output), far(weights), far(qkv), far(wq), far(wk), far(wv), far(attended), far(part),
    )

    if joined:
        late_all = lax.all_gather(late, "expert")

    first = lax.all_to_all(first, "head", split_axis=0, concat_axis=0, tiled=True)
    ret, sums, input_grad = call(
        first_kernel,
        [
            ((experts, 2 * slots + (6 * experts + 32 + product.shape[1] if joined else 0), 128), bf16),
            ((6 * experts + 32, 128), f32, 1), ((col, tok), f32),
        ],
        scalars, first, far(packed), far(residual_grad_own), far(small), *([far(product)] if joined else []),
    )
    ret = lax.all_to_all(ret, "expert", split_axis=0, concat_axis=0, tiled=True)
    out = call(
        functools.partial(last_kernel, slots),
        [((col, tok), bf16), ((1, 1), f32)]
        + ([((experts, width), f32), ((heads_here, bucket_count), f32), ((8, 256), f32), (product.shape, bf16)] if joined else []),
        scalars, ret, far(side), far(residual), far(stats), far(buckets_row),
    )
    block_out, aux_loss = out[:2]
    in_weight_grad, out_weight_grad = call(
        weights_kernel, [((width, width), f32)] * 2, far(rows), far(hidden), far(before_grad), far(back_rows)
    )
    if joined:
        router_grad, table_grad, gain_grads, share = out[2:]
        shares = lax.all_to_all(share, "expert", split_axis=0, concat_axis=0, tiled=True)
        normed_all = call(turn_kernel, [((width, groups * tok), bf16, 1)], far(all_in), far(packed))[0]
        q_grad, k_grad, v_grad, output_grad = call(
            products_kernel, [((col, width), f32, 1)] * 4, far(late_all), far(normed_all), shares
        )
    else:
        gain = packed[:, 2 * col : 2 * col + 2].reshape(heads, 256)[:, :col].reshape(width, 1)
        x = packed[:, :col].reshape(width, tok).astype(f32)
        normed = (x * token_scale(x) * gain.astype(f32)).astype(bf16)
        products = [mm(late[i * col : (i + 1) * col], normed, nt) for i in range(3)]
        q_grad, k_grad, v_grad, sums, output_grad = lax.psum(products + [sums, product[0]], "expert")
        wide = 6 * experts
        router_grad = unfold_lanes(sums[:wide], 6)
        offsets = unfold_lanes(sums[wide : wide + 16], 2)[:heads_here, : 2 * tok - 1]
        hot = (buckets[None, :] == jnp.arange(bucket_count)[:, None]).astype(f32)
        table_grad = mm(offsets, hot, nt, highest)
        gain_grads = unfold_lanes(sums[wide + 16 :], 2)
    return (
        block_out.T,
        input_grad.T,
        aux_loss.reshape(()),
        gain_grads[1, :col],
        q_grad.T,
        k_grad.T,
        v_grad.T,
        output_grad,
        table_grad.T,
        gain_grads[0, :col],
        router_grad.T,
        in_weight_grad[None],
        out_weight_grad[None],
    )


def solution(mesh):
    return jax.shard_map(
        shards,
        mesh=mesh,
        in_specs=(
            P("expert", "head"),
            P("expert", "head"),
            P("expert"),
            P("expert", None),
            P(),
            P("head"),
            P(None, "head"),
            P(None, "head"),
            P(None, "head"),
            P("head", None),
            P(None, "head"),
            P("head"),
            P(),
            P("expert", None, "head"),
            P("expert", "head", None),
        ),
        out_specs=(
            P("expert", "head"),
            P("expert", "head"),
            P(),
            P("head"),
            P(None, "head"),
            P(None, "head"),
            P(None, "head"),
            P("head", None),
            P(None, "head"),
            P("head"),
            P(),
            P("expert", None, "head"),
            P("expert", "head", None),
        ),
        check_vma=False,
    )
```

```python
import functools

import jax
import jax.numpy as jnp
from jax import lax
from jax.experimental import pallas as pl
from jax.experimental.pallas import tpu as pltpu
from jax.sharding import PartitionSpec as P

eps = 1e-06
aux_weight = 0.01
f32 = jnp.float32
bf16 = jnp.bfloat16
gelu_scale = 0.7978845608028654
gelu_cube = 0.044715
highest = lax.Precision.HIGHEST
nt = ((1,), (1,))
tn = ((0,), (0,))


def mm(left, right, dims=((1,), (0,)), precision=None):
    return lax.dot_general(left, right, (dims, ((), ())), precision=precision, preferred_element_type=f32)


class Later:
    def __init__(self, source, space, semaphore):
        self.space, self.shape, self.waited = space, space.shape, False
        self.copy = pltpu.make_async_copy(source, space, semaphore)
        self.copy.start()

    def wait(self):
        if not self.waited:
            self.copy.wait()
            self.waited = True

    def __getitem__(self, index):
        self.wait()
        return self.space[index]


class Sent:
    def __init__(self, space, target, semaphore):
        self.space, self.shape, self.dtype, self.copy = space, space.shape, space.dtype, None
        self.target, self.semaphore = target, semaphore

    def __setitem__(self, index, value):
        self.space[index] = value

    def __getitem__(self, index):
        return self.space[index]

    def send(self):
        if self.copy is None:
            self.copy = pltpu.make_async_copy(self.space, self.target, self.semaphore)
            self.copy.start()


class Lazy:
    def __init__(self, array):
        self.array = array


def lazy(array):
    return Lazy(array)


def call(body, outs, *args):
    hbm = pl.BlockSpec(memory_space=pltpu.HBM)
    in_specs, operands, out_specs, shapes, scratch = [], [], [], [], []
    late_in, late_out = [], []
    for i, a in enumerate(args):
        if isinstance(a, Lazy):
            late_in.append(i)
            in_specs.append(hbm)
            operands.append(far(a.array))
            scratch.append(pltpu.VMEM(a.array.shape, a.array.dtype))
        else:
            whole = a.dtype == jnp.int32 and a.ndim == 1
            in_specs.append(pl.BlockSpec(memory_space=pltpu.SMEM) if whole else pl.BlockSpec())
            operands.append(a)
    for i, (shape, kind, *mode) in enumerate(outs):
        shapes.append(pltpu.HBM(shape, kind) if mode else jax.ShapeDtypeStruct(shape, kind))
        out_specs.append(hbm if mode == [2] else pl.BlockSpec())
        if mode == [2]:
            late_out.append(i)
            scratch.append(pltpu.VMEM(shape, kind))
    count = len(scratch)
    if count:
        scratch.append(pltpu.SemaphoreType.DMA((count,)))

    def run(*refs):
        ins, results, spare = refs[: len(args)], refs[len(args) : len(args) + len(outs)], refs[len(args) + len(outs) :]
        ins, results = list(ins), list(results)
        for k, i in enumerate(late_in):
            ins[i] = Later(ins[i], spare[k], spare[-1].at[k])
        for k, i in enumerate(late_out, len(late_in)):
            results[i] = Sent(spare[k], results[i], spare[-1].at[k])
        body(*ins, *results)
        for i in late_in:
            ins[i].wait()
        for i in late_out:
            results[i].send()
        for i in late_out:
            results[i].copy.wait()

    return pl.pallas_call(
        run,
        out_shape=shapes,
        in_specs=in_specs,
        out_specs=out_specs,
        scratch_shapes=scratch,
        compiler_params=pltpu.CompilerParams(vmem_limit_bytes=40 * 1024 * 1024),
    )(*operands)


def far(array):
    return pltpu.with_memory_space_constraint(array, pltpu.HBM)


def tall(ref, first, rows):
    return jnp.concatenate([ref[i, first : first + rows, :].astype(f32) for i in range(ref.shape[0])], axis=0)


def gain_columns(block):
    turned = jnp.transpose(block.astype(f32))
    return [jnp.concatenate([turned[:, i : i + 1], turned[:64, i + 1 : i + 2]], axis=0) for i in (0, 2)]


def all_gains(packed):
    first = 2 * packed.shape[2] * 3 // 2
    pairs = [gain_columns(packed[i, first : first + 16, :]) for i in range(packed.shape[0])]
    return [jnp.concatenate([pair[i] for pair in pairs], axis=0) for i in range(2)]


def token_scale(values):
    return lax.rsqrt(jnp.sum(values * values, axis=0, keepdims=True) * (1.0 / values.shape[0]) + eps)


def lanes(shape):
    return lax.broadcasted_iota(jnp.int32, shape, len(shape) - 1)


def sublanes(shape):
    return lax.broadcasted_iota(jnp.int32, shape, len(shape) - 2)


def side_lanes(rows, width, columns):
    spot = lanes((rows, width))
    out = jnp.zeros((rows, width), f32)
    for i, column in enumerate(columns):
        out = jnp.where(spot == i, column, out)
    return out


def side_rows(rows, width, lines):
    spot = sublanes((rows, width))
    out = jnp.zeros((rows, width), f32)
    for i, line in enumerate(lines):
        out = jnp.where(spot == i, line, out)
    return out


def high_low(values, count=2):
    pieces = []
    for _ in range(count):
        piece = values.astype(bf16).astype(f32)
        pieces.append(piece)
        values = values - piece
    return pieces


def softmax(values, axis):
    raised = jnp.exp(values - jnp.max(values, axis=axis, keepdims=True))
    return raised / jnp.sum(raised, axis=axis, keepdims=True)


def gelu_parts(u):
    t = jnp.tanh(gelu_scale * (u + gelu_cube * u * u * u))
    value = 0.5 * u * (1.0 + t)
    slope = 0.5 * (1.0 + t) + 0.5 * u * (1.0 - t * t) * gelu_scale * (1.0 + 3.0 * gelu_cube * u * u)
    return value, slope


def fold_lanes(rows):
    return jnp.concatenate([rows[:, i : i + 128] for i in range(0, rows.shape[1], 128)], axis=0)


def unfold_lanes(rows, pieces):
    size = rows.shape[0] // pieces
    return jnp.concatenate([rows[i * size : (i + 1) * size] for i in range(pieces)], axis=1)


def pick_slots(spots, count):
    return sublanes((count, spots.shape[1])) == spots


def attend_kernel(scale, scalars, packed, wq, wk, wv, buckets, table, qkv_ref, weights_ref, attended_ref):
    heads, tok, _ = weights_ref.shape
    col = wq.shape[0]
    size = col // heads
    x = tall(packed, 0, col)
    normed = (x * token_scale(x) * all_gains(packed)[0]).astype(bf16)
    projected = []
    for i, w in enumerate((wq, wk, wv)):
        rows = mm(w[...], normed).astype(bf16)
        qkv_ref[i] = rows
        projected.append(rows)
    query, key, value = projected
    qkv_ref.send()
    hot = (sublanes((table.shape[1], 2 * tok)) == buckets[...]).astype(f32)
    offsets = mm(table[...], hot, precision=highest)
    open_keys = lanes((tok, tok)) < scalars[0]
    outs = []
    for h in range(heads):
        at = slice(h * size, (h + 1) * size)
        spread = jnp.broadcast_to(offsets[h : h + 1, :], (tok, 2 * tok))
        bias = pltpu.roll(spread, tok + 1, 1, stride=1, stride_axis=0)[:, :tok]
        scores = mm(query[at], key[at], tn) * scale + bias
        weights = softmax(jnp.where(open_keys, scores, -1000000000.0), 1)
        weights_ref[h] = weights
        outs.append(mm(value[at], weights.astype(bf16), nt))
    attended_ref[...] = jnp.concatenate(outs, axis=0).astype(bf16)


def second_norm(residual, gain, w_router):
    scale = token_scale(residual)
    unit = residual * scale
    normed = (unit * gain).astype(bf16)
    return scale, unit, normed, softmax(mm(w_router, normed), 0)


def route_kernel(capacity, scalars, packed, attended, w_output, routes, w_router, residual_ref, side_ref, send_ref):
    tok = routes.shape[1]
    experts, slots, _ = send_ref.shape
    heads, col, _ = residual_ref.shape
    width = heads * col
    branch = mm(tall(attended, 0, col).astype(bf16), w_output[...], tn)
    residual = tall(packed, 0, col) + jnp.transpose(branch)
    for i in range(heads):
        residual_ref[i] = residual[i * col : (i + 1) * col]
    residual_ref.send()
    _, _, normed, router = second_norm(residual, all_gains(packed)[1], w_router[...])
    route_hot = (sublanes((experts, tok)) == routes[...]).astype(f32)
    gate = jnp.sum(router * route_hot, axis=0, keepdims=True)
    before = (sublanes((tok, tok)) < lanes((tok, tok))).astype(bf16)
    slot = jnp.sum(mm(route_hot.astype(bf16), before) * route_hot, axis=0, keepdims=True)
    spots = routes[...].astype(f32) * slots + slot
    side_ref[...] = side_rows(8, tok, [gate, spots])
    valid = (lanes((1, tok)) < scalars[0]).astype(f32)
    counts = jnp.sum(route_hot * valid, axis=1, keepdims=True)
    probs = high_low(jnp.sum(router * valid, axis=1, keepdims=True), 3)
    pick = pick_slots(spots.astype(jnp.int32), experts * slots).astype(bf16)
    rows = mm(pick, normed, nt)
    grads = mm(pick, tall(packed, col, col).astype(bf16), nt)
    for e in range(experts):
        at = slice(e * slots, (e + 1) * slots)
        send_ref[e, :, :width] = rows[at].astype(bf16)
        stats = side_lanes(1, width, [counts[e : e + 1]] + [piece[e : e + 1] for piece in probs])
        filled = jnp.where(sublanes((slots, width)) == capacity, stats, grads[at])
        send_ref[e, :, width:] = filled.astype(bf16)


def expert_kernel(
    capacity, scalars, rows_ref, w_in, w_out, w_router, back_ref, part_ref, hidden_ref, before_ref, grads_ref
):
    total = rows_ref.shape[0]
    experts, width = w_router.shape
    heads = part_ref.shape[0]
    col = width // heads
    slots = total // experts
    half = total // 2
    rows = rows_ref[:, :width]
    grads = rows_ref[:, width:].astype(f32)
    hidden, slope = gelu_parts(mm(rows, w_in[...]))
    hidden = hidden.astype(bf16)
    hidden_ref[...] = hidden
    hidden_ref.send()
    produced = mm(hidden, w_out[...])
    for i in range(heads):
        mine = produced[:, i * col : (i + 1) * col]
        rest = mine[:, 128:]
        part_ref[i] = jnp.concatenate(
            [mine[:, :128], jnp.concatenate([rest[:half], rest[half:]], axis=1)], axis=0
        ).astype(bf16)
    part_ref.send()
    probs = softmax(mm(rows, w_router[...], nt), 1)
    gate = jnp.sum(jnp.where(lanes((total, experts)) == scalars[2], probs, 0.0), axis=1, keepdims=True)
    back = (gate * grads).astype(bf16)
    grads_ref[...] = back
    grads_ref.send()
    before = (mm(back, w_out[...], nt) * slope).astype(bf16)
    before_ref[...] = before
    before_ref.send()
    rows_grad = mm(before, w_in[...], nt)
    gate_grad = jnp.sum(grads * produced, axis=1, keepdims=True)
    stats = jnp.zeros((1, 128), f32)
    for b in range(experts):
        stats = stats + grads[b * slots + capacity : b * slots + capacity + 1, :128]
    prob = stats[:, 1:2] + stats[:, 2:3] + stats[:, 3:4]
    side = side_lanes(
        total, 256 - col, high_low(gate_grad) + high_low(stats[:, 0:1]) + high_low(prob, 3)
    )
    for b in range(experts):
        at = slice(b * slots, (b + 1) * slots)
        for i in range(heads):
            back_ref[b * heads + i] = jnp.concatenate(
                [rows_grad[at, i * col : (i + 1) * col], side[at]], axis=1
            ).astype(bf16)


def weights_kernel(rows_ref, hidden, before, grads, in_ref, out_ref):
    width = in_ref.shape[0]
    in_ref[...] = mm(rows_ref[:, :width], before[...], tn)
    in_ref.send()
    out_ref[...] = mm(hidden[...], grads[...], tn)


def collect_kernel(came, side, grad_ref, gate_ref, stats_ref):
    col, tok = grad_ref.shape
    experts = stats_ref.shape[0]
    sources, slots, _ = came.shape
    heads = sources // experts
    sums = []
    for e in range(experts):
        total = came[e * heads].astype(f32)
        for i in range(1, heads):
            total = total + came[e * heads + i].astype(f32)
        sums.append(total)
    stats = jnp.concatenate([total[0:1, col:] for total in sums], axis=0) * (1.0 / heads)
    sums = jnp.concatenate(sums, axis=0)
    pick = pick_slots(side[1:2, :].astype(jnp.int32), experts * slots)
    grad_ref[...] = mm(sums[:, :col].astype(bf16), pick.astype(bf16), tn).astype(bf16)
    gate = mm(sums[:, col:], pick.astype(f32), tn, highest)
    gate_ref[...] = jnp.broadcast_to(gate[0:1] + gate[1:2], gate_ref.shape)
    count = stats[:, 2:3] + stats[:, 3:4]
    prob = stats[:, 4:5] + stats[:, 5:6] + stats[:, 6:7]
    stats_ref[...] = side_lanes(experts, 128, [count, prob])


def backward_kernel(
    scale, valid_total, scalars, packed, expert_grad, gate_grad, stats, residual_ref, routes, w_router,
    w_output, weights_ref, qkv, wq, wk, wv, attended, part, late_ref, first_ref, own_ref, small_ref, product_ref,
):
    tok = routes.shape[1]
    heads_here = weights_ref.shape[0]
    blocks, col, _ = residual_ref.shape
    experts, width = w_router.shape
    size = col // heads_here
    gain_one, gain_two = all_gains(packed)
    residual = tall(residual_ref, 0, col)
    scale_two, unit, normed, router = second_norm(residual, gain_two, w_router[...])
    valid = (lanes((1, tok)) < scalars[0]).astype(f32)
    route_hot = (sublanes((experts, tok)) == routes[...]).astype(f32)
    fraction = stats[:, 0:1] * (aux_weight * experts / (valid_total * valid_total))
    prob_grad = route_hot * gate_grad[0:1, :] + fraction * valid
    logit_grad = router * (prob_grad - jnp.sum(router * prob_grad, axis=0, keepdims=True))
    logit_grad = logit_grad.astype(bf16)
    normed_grad = mm(w_router[...], logit_grad, tn) + tall(expert_grad, 0, col)
    unit_grad = normed_grad * gain_two
    mean = jnp.sum(unit_grad * unit, axis=0, keepdims=True) * (1.0 / width)
    residual_grad = tall(packed, col, col) + scale_two * (unit_grad - unit * mean)
    branch = residual_grad.astype(bf16)
    attended_grad = mm(w_output[...], branch).astype(bf16)
    flip = (lanes((tok, tok)) + sublanes((tok, tok)) == tok - 1).astype(bf16)
    query, key, value = qkv[0], qkv[1], qkv[2]
    grads = [[], [], []]
    offsets = []
    for h in range(heads_here):
        at = slice(h * size, (h + 1) * size)
        out = attended_grad[at]
        weights = weights_ref[h]
        mass = mm(out, value[at], tn)
        score = weights * (mass - jnp.sum(weights * mass, axis=1, keepdims=True))
        score = score.astype(bf16)
        grads[0].append(mm(key[at], score, nt) * scale)
        grads[1].append(mm(query[at], score) * scale)
        grads[2].append(mm(out, weights.astype(bf16)))
        flipped = jnp.concatenate([mm(flip, score), jnp.zeros((tok, tok), f32)], axis=1)
        rolled = pltpu.roll(flipped, 0, 1, stride=1, stride_axis=0)
        offsets.append(jnp.sum(rolled, axis=0, keepdims=True))
    first = jnp.zeros((width, tok), f32)
    row = jnp.zeros((1, tok), f32)
    for i, w in enumerate((wq, wk, wv)):
        low = jnp.concatenate(grads[i], axis=0).astype(bf16)
        late_ref[i * col : (i + 1) * col, :] = low
        first = first + mm(w[...], low, tn)
        row = row + jnp.sum(low.astype(f32) * qkv[i].astype(f32), axis=0, keepdims=True)
    late_ref.send()
    side = side_rows(16, tok, high_low(row))
    for i in range(blocks):
        at = slice(i * col, (i + 1) * col)
        first_ref[i, : col + 16, :] = jnp.concatenate([first[at], side], axis=0).astype(bf16)
        first_ref[i, col + 16 :, :] = part[i]

    product = mm(attended[...], branch, nt)
    pieces = product_ref.shape[0]
    for b in range(pieces):
        at = slice(b * (col // pieces), (b + 1) * (col // pieces))
        product_ref[b] = (product if pieces == 1 else fold_lanes(product[at])).astype(product_ref.dtype)
    gain_two_grad = jnp.sum(normed_grad * unit, axis=1, keepdims=True)
    gains = jnp.zeros((col, 1), f32)
    own = jnp.zeros((col, tok), f32)
    for i in range(blocks):
        at = slice(i * col, (i + 1) * col)
        gains = jnp.where(scalars[1] == i, gain_two_grad[at], gains)
        own = jnp.where(scalars[1] == i, residual_grad[at], own)
    own_ref[...] = own
    gains = jnp.transpose(side_lanes(col, 128, [gains]))[0:8]
    router_grad = mm(logit_grad, normed, nt)
    offsets = jnp.concatenate(offsets, axis=0)
    offsets = jnp.concatenate([offsets, jnp.zeros((8 - heads_here, 2 * tok), f32)], axis=0)
    gains = jnp.concatenate([gains, jnp.zeros((8, 64), f32)], axis=1)
    pieces = [fold_lanes(gains), fold_lanes(offsets), fold_lanes(router_grad)]
    spare = small_ref.shape[0] - 6 * experts - 32
    if spare:
        pieces.append(jnp.zeros((spare, 128), f32))
    small_ref[...] = jnp.concatenate(pieces, axis=0)


def first_kernel(scalars, came, packed, own, small, *refs):
    product, (ret_ref, sums_ref, input_ref) = refs[:-3], refs[-3:]
    col, tok = own.shape
    heads = came.shape[0]
    experts = ret_ref.shape[0]
    total = came[0].astype(f32)
    for i in range(1, heads):
        total = total + came[i].astype(f32)
    mean = (total[col : col + 1] + total[col + 1 : col + 2]) * (1.0 / (heads * col))
    scale = token_scale(tall(packed, 0, col))
    mine = packed[scalars[1]].astype(f32)
    unit = mine[:col] * scale
    gain = gain_columns(mine[2 * col : 2 * col + 16])[0]
    input_ref[...] = own[...] + scale * (total[:col] * gain - unit * mean)
    gain_grad = jnp.sum(total[:col] * unit, axis=1, keepdims=True)
    gain_grad = jnp.transpose(side_lanes(col, 128, [jnp.zeros_like(gain_grad), gain_grad]))[0:8]
    gain_grad = jnp.concatenate([gain_grad, jnp.zeros((8, 64), f32)], axis=1)
    sums = jnp.concatenate([small[:16, :] + fold_lanes(gain_grad), small[16:, :]], axis=0)
    sums_ref[...] = sums
    produced = total[col + 16 :]
    count = produced.shape[0] * 2 // 3
    half = count // 2
    top = produced[:count]
    rest = jnp.concatenate([produced[count:, :64], produced[count:, 64:]], axis=0)
    rest = jnp.concatenate([rest, jnp.zeros((count, 64), f32)], axis=1)
    slots = count // experts
    for e in range(experts):
        at = slice(e * slots, (e + 1) * slots)
        pieces = [top[at], rest[at]]
        if product:
            chunk = sums.shape[0] // experts
            pieces += [sums[e * chunk : (e + 1) * chunk], product[0][e].astype(f32)]
        ret_ref[e] = jnp.concatenate(pieces, axis=0).astype(bf16)


def last_kernel(slots, scalars, came, side, residual, stats, *refs):
    block_ref, aux_ref, refs = refs[0], refs[1], refs[2:]
    experts = came.shape[0]
    heads, col, tok = residual.shape
    blocks = [came[e].astype(f32) for e in range(experts)]
    top = jnp.concatenate([block[:slots] for block in blocks], axis=0).astype(bf16)
    rest = jnp.concatenate([block[slots : 2 * slots] for block in blocks], axis=0).astype(bf16)
    pick = pick_slots(side[1:2, :].astype(jnp.int32), experts * slots).astype(bf16)
    returned = jnp.concatenate([mm(top, pick, tn), mm(rest, pick, tn)[: col - 128]], axis=0)
    block_ref[...] = (residual[scalars[1]] + side[0:1, :] * returned).astype(bf16)
    product = stats[:, 0:1] * stats[:, 1:2]
    valid_total = 3 * tok * experts // 4
    aux_ref[...] = jnp.sum(product, axis=0, keepdims=True) * (experts / (valid_total * valid_total))
    if refs:
        total = blocks[0][2 * slots :]
        for block in blocks[1:]:
            total = total + block[2 * slots :]
        for e in range(experts):
            refs[0][e] = total.astype(bf16)


def turn_kernel(all_in, packed, normed_ref):
    heads, groups, col, tok = all_in.shape
    gain = all_gains(packed)[0]
    for b in range(groups):
        x = jnp.concatenate([all_in[i, b].astype(f32) for i in range(heads)], axis=0)
        normed_ref[:, b * tok : (b + 1) * tok] = (x * token_scale(x) * gain).astype(bf16)


def products_kernel(
    late, normed, shares, buckets, q_ref, k_ref, v_ref, out_ref, router_ref, table_ref, gains_ref
):
    groups = shares.shape[0]
    col = q_ref.shape[0]
    experts = router_ref.shape[0]
    size = col // groups
    blocks = [shares[b].astype(f32) for b in range(groups)]
    chunk = blocks[0].shape[0] - 6 * size
    for b in range(groups):
        out_ref[b * size : (b + 1) * size, :] = unfold_lanes(blocks[b][chunk:], 6)
    out_ref.send()
    joined = jnp.concatenate([late[b] for b in range(groups)], axis=1)
    for i, ref in enumerate((q_ref, k_ref, v_ref)):
        ref[...] = mm(joined[i * col : (i + 1) * col], normed[...], nt)
        ref.send()
    small = jnp.concatenate([block[:chunk] for block in blocks], axis=0)
    gains_ref[...] = unfold_lanes(small[:16], 2)
    hot = (sublanes((table_ref.shape[1], buckets.shape[1])) == buckets[...]).astype(f32)
    table_ref[...] = mm(unfold_lanes(small[16:32], 2), hot, nt, highest)[: table_ref.shape[0]]
    router_ref[...] = unfold_lanes(small[32 : 32 + 6 * experts], 6)


def few_experts():
    return lax.axis_size("expert") <= 8


def shards(
    inputs,
    out_grad,
    lengths,
    routes,
    buckets,
    gain_attn,
    w_query,
    w_key,
    w_value,
    w_output,
    bias_table,
    gain_ffn,
    w_router,
    w_in,
    w_out,
):
    tok, col = inputs.shape
    heads_here = bias_table.shape[1]
    head_size = w_query.shape[1] // heads_here
    width, experts = w_router.shape
    bucket_count = bias_table.shape[0]
    heads = width // col
    groups = lax.axis_size("expert")
    me_head, me_expert = lax.axis_index("head"), lax.axis_index("expert")
    capacity = max(2, (4 * tok + 3 * experts - 1) // (3 * experts))
    slots = -(-(capacity + 1) // 8) * 8
    total = experts * slots
    small_rows = 6 * experts + 32 + (48 if few_experts() else 0)
    valid_total = 3 * tok * groups // 4
    scale = head_size ** (-0.5)
    joined = few_experts()
    w_in, w_out = w_in[0], w_out[0]
    wq, wk, wv = w_query.T, w_key.T, w_value.T
    routes_row = routes.T
    router_rows = w_router.T
    scalars = jnp.stack([lengths[0], me_head.astype(jnp.int32), me_expert.astype(jnp.int32)])
    buckets_row = jnp.pad(buckets, (0, 1), constant_values=-1)[None]

    space = jnp.zeros((64,), bf16)
    gains = jnp.concatenate([gain_attn, space, gain_ffn, space, jnp.zeros((1536,), bf16)]).reshape(16, 128)
    packed = lax.all_gather(jnp.concatenate([inputs.T, out_grad.T, gains], axis=0), "head")
    w_output_full = lax.all_gather(w_output, "head", tiled=True)
    if joined:
        all_in = lax.all_gather(inputs.T, "expert")
    qkv, weights, attended = call(
        functools.partial(attend_kernel, scale),
        [((3, col, tok), bf16, 2), ((heads_here, tok, tok), f32, 2), ((col, tok), bf16)],
        scalars, packed, lazy(wq), lazy(wk), lazy(wv), far(buckets_row), far(bias_table.T),
    )

    attended_parts = lax.all_gather(attended, "head")
    residual, side, send = call(
        functools.partial(route_kernel, capacity),
        [((heads, col, tok), f32, 2), ((8, tok), f32, 1), ((experts, slots, 2 * width), bf16)],
        scalars, packed, attended_parts, lazy(w_output_full), far(routes_row), far(router_rows),
    )
    rows = lax.all_to_all(send, "expert", split_axis=0, concat_axis=0, tiled=True)
    rows = rows.reshape(total, 2 * width)
    if joined:
        rows, all_in = lax.optimization_barrier((rows, all_in))
        all_in = lax.all_gather(all_in, "head")

    back, part, hidden, before_grad, back_rows = call(
        functools.partial(expert_kernel, capacity),
        [((experts * heads, slots, 256), bf16), ((heads, total * 3 // 2, 128), bf16, 2)]
        + [((total, width), bf16, 2)] * 3,
        scalars, rows, lazy(w_in), lazy(w_out), far(router_rows),
    )
    came = lax.all_to_all(back, ("expert", "head"), split_axis=0, concat_axis=0, tiled=True)
    grad_own, gate_grad, stats = call(
        collect_kernel,
        [((col, tok), bf16), ((8, tok), f32, 1), ((experts, 128), f32, 1)],
        came, far(side),
    )
    expert_grad = lax.all_gather(grad_own, "head")

    late, first, residual_grad_own, small, product = call(
        functools.partial(backward_kernel, scale, valid_total),
        [
            ((3 * col, tok), bf16, 2), ((heads, col + 16 + total * 3 // 2, 128), bf16), ((col, tok), f32, 2),
            ((small_rows, 128), f32, 1),
            ((groups, col // groups * 6, 128), bf16, 2) if joined else ((1, col, width), f32, 2),
        ],
        scalars, lazy(packed), expert_grad, far(gate_grad), far(stats), lazy(residual), far(routes_row),
        far(router_rows), lazy(w_output), lazy(weights), lazy(qkv), lazy(wq), lazy(wk), lazy(wv), lazy(attended),
        lazy(part),
    )

    if joined:
        late_all = lax.all_gather(late, "expert")

    first = lax.all_to_all(first, "head", split_axis=0, concat_axis=0, tiled=True)
    ret, sums, input_grad = call(
        first_kernel,
        [
            ((experts, 2 * slots + (small_rows // experts + product.shape[1] if joined else 0), 128), bf16),
            ((small_rows, 128), f32, 1), ((col, tok), f32, 2),
        ],
        scalars, first, lazy(packed), lazy(residual_grad_own), far(small), *([lazy(product)] if joined else []),
    )
    ret = lax.all_to_all(ret, "expert", split_axis=0, concat_axis=0, tiled=True)
    out = call(
        functools.partial(last_kernel, slots),
        [((col, tok), bf16), ((1, 1), f32)]
        + ([((groups, small_rows // groups + product.shape[1], 128), bf16)] if joined else []),
        scalars, ret, far(side), lazy(residual), far(stats),
    )
    block_out, aux_loss = out[:2]
    in_weight_grad, out_weight_grad = call(
        weights_kernel, [((width, width), f32, 2)] * 2, lazy(rows), lazy(hidden), lazy(before_grad), lazy(back_rows)
    )
    if joined:
        shares = lax.all_to_all(out[2], "expert", split_axis=0, concat_axis=0, tiled=True)
        normed_all = call(turn_kernel, [((width, groups * tok), bf16, 1)], lazy(all_in), far(packed))[0]
        q_grad, k_grad, v_grad, output_grad, router_grad, table_grad, gain_grads = call(
            products_kernel,
            [((col, width), f32, 2)] * 4
            + [((experts, width), f32), ((heads_here, bucket_count), f32), ((8, 256), f32)],
            lazy(late_all), lazy(normed_all), shares, far(buckets_row),
        )
    else:
        gain = packed[:, 2 * col : 2 * col + 2].reshape(heads, 256)[:, :col].reshape(width, 1)
        x = packed[:, :col].reshape(width, tok).astype(f32)
        normed = (x * token_scale(x) * gain.astype(f32)).astype(bf16)
        products = [mm(late[i * col : (i + 1) * col], normed, nt) for i in range(3)]
        q_grad, k_grad, v_grad, sums, output_grad = lax.psum(products + [sums, product[0]], "expert")
        router_grad = unfold_lanes(sums[32 : 32 + 6 * experts], 6)
        offsets = unfold_lanes(sums[16:32], 2)[:heads_here, : 2 * tok - 1]
        hot = (buckets[None, :] == jnp.arange(bucket_count)[:, None]).astype(f32)
        table_grad = mm(offsets, hot, nt, highest)
        gain_grads = unfold_lanes(sums[:16], 2)
    return (
        block_out.T,
        input_grad.T,
        aux_loss.reshape(()),
        gain_grads[1, :col],
        q_grad.T,
        k_grad.T,
        v_grad.T,
        output_grad,
        table_grad.T,
        gain_grads[0, :col],
        router_grad.T,
        in_weight_grad[None],
        out_weight_grad[None],
    )


def solution(mesh):
    return jax.shard_map(
        shards,
        mesh=mesh,
        in_specs=(
            P("expert", "head"),
            P("expert", "head"),
            P("expert"),
            P("expert", None),
            P(),
            P("head"),
            P(None, "head"),
            P(None, "head"),
            P(None, "head"),
            P("head", None),
            P(None, "head"),
            P("head"),
            P(),
            P("expert", None, "head"),
            P("expert", "head", None),
        ),
        out_specs=(
            P("expert", "head"),
            P("expert", "head"),
            P(),
            P("head"),
            P(None, "head"),
            P(None, "head"),
            P(None, "head"),
            P("head", None),
            P(None, "head"),
            P("head"),
            P(),
            P("expert", None, "head"),
            P("expert", "head", None),
        ),
        check_vma=False,
    )
```

```python
import functools

import jax
import jax.numpy as jnp
from jax import lax
from jax.experimental import pallas as pl
from jax.experimental.pallas import tpu as pltpu
from jax.sharding import PartitionSpec as P

eps = 1e-06
aux_weight = 0.01
f32 = jnp.float32
bf16 = jnp.bfloat16
gelu_scale = 0.7978845608028654
gelu_cube = 0.044715
highest = lax.Precision.HIGHEST
nt = ((1,), (1,))
tn = ((0,), (0,))


def mm(left, right, dims=((1,), (0,)), precision=None):
    return lax.dot_general(left, right, (dims, ((), ())), precision=precision, preferred_element_type=f32)


def call(body, outs, *args):
    scalar_memory = pl.BlockSpec(memory_space=pltpu.SMEM)
    in_specs = [scalar_memory if a.dtype == jnp.int32 and a.ndim == 1 else pl.BlockSpec() for a in args]
    shapes = []
    for shape, kind, *remote in outs:
        shapes.append(pltpu.HBM(shape, kind) if remote else jax.ShapeDtypeStruct(shape, kind))
    return pl.pallas_call(
        body,
        out_shape=shapes,
        in_specs=in_specs,
        compiler_params=pltpu.CompilerParams(vmem_limit_bytes=40 * 1024 * 1024),
    )(*args)


def far(array):
    return pltpu.with_memory_space_constraint(array, pltpu.HBM)


def tall(ref, first, rows):
    return jnp.concatenate([ref[i, first : first + rows, :].astype(f32) for i in range(ref.shape[0])], axis=0)


def gain_columns(block):
    turned = jnp.transpose(block.astype(f32))
    return [jnp.concatenate([turned[:, i : i + 1], turned[:64, i + 1 : i + 2]], axis=0) for i in (0, 2)]


def all_gains(packed):
    first = 2 * packed.shape[2] * 3 // 2
    pairs = [gain_columns(packed[i, first : first + 16, :]) for i in range(packed.shape[0])]
    return [jnp.concatenate([pair[i] for pair in pairs], axis=0) for i in range(2)]


def token_scale(values):
    return lax.rsqrt(jnp.sum(values * values, axis=0, keepdims=True) * (1.0 / values.shape[0]) + eps)


def lanes(shape):
    return lax.broadcasted_iota(jnp.int32, shape, len(shape) - 1)


def sublanes(shape):
    return lax.broadcasted_iota(jnp.int32, shape, len(shape) - 2)


def side_lanes(rows, width, columns):
    spot = lanes((rows, width))
    out = jnp.zeros((rows, width), f32)
    for i, column in enumerate(columns):
        out = jnp.where(spot == i, column, out)
    return out


def side_rows(rows, width, lines):
    spot = sublanes((rows, width))
    out = jnp.zeros((rows, width), f32)
    for i, line in enumerate(lines):
        out = jnp.where(spot == i, line, out)
    return out


def high_low(values, count=2):
    pieces = []
    for _ in range(count):
        piece = values.astype(bf16).astype(f32)
        pieces.append(piece)
        values = values - piece
    return pieces


def softmax(values, axis):
    raised = jnp.exp(values - jnp.max(values, axis=axis, keepdims=True))
    return raised / jnp.sum(raised, axis=axis, keepdims=True)


def gelu_parts(u):
    t = jnp.tanh(gelu_scale * (u + gelu_cube * u * u * u))
    value = 0.5 * u * (1.0 + t)
    slope = 0.5 * (1.0 + t) + 0.5 * u * (1.0 - t * t) * gelu_scale * (1.0 + 3.0 * gelu_cube * u * u)
    return value, slope


def fold_lanes(rows):
    return jnp.concatenate([rows[:, i : i + 128] for i in range(0, rows.shape[1], 128)], axis=0)


def unfold_lanes(rows, pieces):
    size = rows.shape[0] // pieces
    return jnp.concatenate([rows[i * size : (i + 1) * size] for i in range(pieces)], axis=1)


def pick_slots(spots, count):
    return sublanes((count, spots.shape[1])) == spots


def attend_kernel(
    scale, scalars, packed, wq, wk, wv, w_output, buckets, table, qkv_ref, weights_ref, attended_ref, branch_ref
):
    heads, tok, _ = weights_ref.shape
    col = wq.shape[0]
    size = col // heads
    x = tall(packed, 0, col)
    normed = (x * token_scale(x) * all_gains(packed)[0]).astype(bf16)
    projected = []
    for i, w in enumerate((wq, wk, wv)):
        rows = mm(w[...], normed).astype(bf16)
        qkv_ref[i] = rows
        projected.append(rows)
    query, key, value = projected
    hot = (sublanes((table.shape[1], 2 * tok)) == buckets[...]).astype(f32)
    offsets = mm(table[...], hot, precision=highest)
    open_keys = lanes((tok, tok)) < scalars[0]
    outs = []
    for h in range(heads):
        at = slice(h * size, (h + 1) * size)
        spread = jnp.broadcast_to(offsets[h : h + 1, :], (tok, 2 * tok))
        bias = pltpu.roll(spread, tok + 1, 1, stride=1, stride_axis=0)[:, :tok]
        scores = mm(query[at], key[at], tn) * scale + bias
        weights = softmax(jnp.where(open_keys, scores, -1000000000.0), 1)
        weights_ref[h] = weights
        outs.append(mm(value[at], weights.astype(bf16), nt))
    attended = jnp.concatenate(outs, axis=0).astype(bf16)
    attended_ref[...] = attended
    branch = mm(w_output[...], attended, tn)
    for i in range(branch_ref.shape[0]):
        branch_ref[i] = branch[i * col : (i + 1) * col].astype(bf16)


def second_norm(residual, gain, w_router):
    scale = token_scale(residual)
    unit = residual * scale
    normed = (unit * gain).astype(bf16)
    return scale, unit, normed, softmax(mm(w_router, normed), 0)


def route_kernel(capacity, scalars, came, inputs, out_grad, routes, residual_ref, low_ref, side_ref, send_ref):
    col, tok = inputs.shape
    experts, slots, _ = send_ref.shape
    residual = inputs[...].astype(f32)
    for i in range(came.shape[0]):
        residual = residual + came[i].astype(f32)
    residual_ref[...] = residual
    low = residual.astype(bf16)
    low_ref[...] = low
    route_hot = (sublanes((experts, tok)) == routes[...]).astype(f32)
    before = (sublanes((tok, tok)) < lanes((tok, tok))).astype(bf16)
    slot = jnp.sum(mm(route_hot.astype(bf16), before) * route_hot, axis=0, keepdims=True)
    spots = routes[...].astype(f32) * slots + slot
    side_ref[...] = side_rows(8, tok, [spots])
    valid = (lanes((1, tok)) < scalars[0]).astype(f32)
    counts = jnp.sum(route_hot * valid, axis=1, keepdims=True)
    pick = pick_slots(spots.astype(jnp.int32), experts * slots).astype(bf16)
    rows = mm(pick, jnp.concatenate([low, out_grad[...]], axis=0), nt)
    spare = (sublanes((slots, 2 * col)) == capacity) & (lanes((slots, 2 * col)) == col)
    for e in range(experts):
        block = rows[e * slots : (e + 1) * slots]
        send_ref[e] = jnp.where(spare, counts[e : e + 1], block).astype(bf16)


def gain_row(packed, first, line):
    pieces = []
    for i in range(packed.shape[0]):
        block = packed[i, first : first + 16, :].astype(f32)
        pieces += [block[line : line + 1, :], block[line + 1 : line + 2, :64]]
    return jnp.concatenate(pieces, axis=1)


def expert_kernel(
    capacity, scalars, quarters, packed, w_in, w_out, w_router,
    back_ref, part_ref, hidden_ref, before_ref, grads_ref, rows_ref,
):
    total = rows_ref.shape[0]
    experts, width = w_router.shape
    heads = part_ref.shape[0]
    col = width // heads
    slots = total // experts
    half = total // 2
    parts = [quarters[i].astype(f32) for i in range(heads)]
    residual = jnp.concatenate([block[:, :col] for block in parts], axis=1)
    grads = jnp.concatenate([block[:, col:] for block in parts], axis=1)
    inverse = lax.rsqrt(jnp.sum(residual * residual, axis=1, keepdims=True) * (1.0 / width) + eps)
    rows = (residual * inverse * gain_row(packed, 2 * col, 2)).astype(bf16)
    rows_ref[...] = rows
    hidden, slope = gelu_parts(mm(rows, w_in[...]))
    hidden = hidden.astype(bf16)
    hidden_ref[...] = hidden
    produced = mm(hidden, w_out[...])
    for i in range(heads):
        mine = produced[:, i * col : (i + 1) * col]
        rest = mine[:, 128:]
        part_ref[i] = jnp.concatenate(
            [mine[:, :128], jnp.concatenate([rest[:half], rest[half:]], axis=1)], axis=0
        ).astype(bf16)
    probs = softmax(mm(rows, w_router[...], nt), 1)
    gate = jnp.sum(jnp.where(lanes((total, experts)) == scalars[2], probs, 0.0), axis=1, keepdims=True)
    back = (gate * grads).astype(bf16)
    grads_ref[...] = back
    before = (mm(back, w_out[...], nt) * slope).astype(bf16)
    before_ref[...] = before
    rows_grad = mm(before, w_in[...], nt)
    gate_grad = jnp.sum(grads * produced, axis=1, keepdims=True)
    stats = jnp.zeros((1, 128), f32)
    for b in range(experts):
        stats = stats + grads[b * slots + capacity : b * slots + capacity + 1, :128]
    side = side_lanes(total, 256 - col, high_low(gate_grad) + high_low(stats[:, 0:1]))
    for b in range(experts):
        at = slice(b * slots, (b + 1) * slots)
        for i in range(heads):
            back_ref[b * heads + i] = jnp.concatenate(
                [rows_grad[at, i * col : (i + 1) * col], side[at]], axis=1
            ).astype(bf16)


def weights_kernel(rows_ref, hidden, before, grads, in_ref, out_ref):
    in_ref[...] = mm(rows_ref[...], before[...], tn)
    out_ref[...] = mm(hidden[...], grads[...], tn)


def collect_kernel(came, side, low, grad_ref, gate_ref, stats_ref):
    col, tok = low.shape
    experts = stats_ref.shape[0]
    sources, slots, _ = came.shape
    heads = sources // experts
    sums = []
    for e in range(experts):
        total = came[e * heads].astype(f32)
        for i in range(1, heads):
            total = total + came[e * heads + i].astype(f32)
        sums.append(total)
    stats = jnp.concatenate([total[0:1, col:] for total in sums], axis=0) * (1.0 / heads)
    sums = jnp.concatenate(sums, axis=0)
    pick = pick_slots(side[0:1, :].astype(jnp.int32), experts * slots)
    grad_ref[:col, :] = mm(sums[:, :col].astype(bf16), pick.astype(bf16), tn).astype(bf16)
    grad_ref[col:, :] = low[...]
    gate = mm(sums[:, col:], pick.astype(f32), tn, highest)
    gate_ref[...] = jnp.broadcast_to(gate[0:1] + gate[1:2], gate_ref.shape)
    count = stats[:, 2:3] + stats[:, 3:4]
    stats_ref[...] = side_lanes(experts, 128, [count])


def backward_kernel(
    scale, valid_total, scalars, packed, expert_grad, gate_grad, stats, routes, w_router, w_output, weights_ref,
    qkv, wq, wk, wv, attended, part, late_ref, first_ref, own_ref, small_ref, product_ref, gate_ref,
):
    tok = routes.shape[1]
    heads_here = weights_ref.shape[0]
    blocks, col = packed.shape[0], wq.shape[0]
    experts, width = w_router.shape
    size = col // heads_here
    gain_one, gain_two = all_gains(packed)
    residual = tall(expert_grad, col, col)
    scale_two, unit, normed, router = second_norm(residual, gain_two, w_router[...])
    valid = (lanes((1, tok)) < scalars[0]).astype(f32)
    route_hot = (sublanes((experts, tok)) == routes[...]).astype(f32)
    fraction = stats[:, 0:1] * (aux_weight * experts / (valid_total * valid_total))
    gate = jnp.sum(router * route_hot, axis=0, keepdims=True)
    gate_ref[...] = jnp.broadcast_to(gate, gate_ref.shape)
    prob_grad = route_hot * gate_grad[0:1, :] + fraction * valid
    logit_grad = router * (prob_grad - jnp.sum(router * prob_grad, axis=0, keepdims=True))
    logit_grad = logit_grad.astype(bf16)
    normed_grad = mm(w_router[...], logit_grad, tn) + tall(expert_grad, 0, col)
    unit_grad = normed_grad * gain_two
    mean = jnp.sum(unit_grad * unit, axis=0, keepdims=True) * (1.0 / width)
    residual_grad = tall(packed, col, col) + scale_two * (unit_grad - unit * mean)
    branch = residual_grad.astype(bf16)
    attended_grad = mm(w_output[...], branch).astype(bf16)
    flip = (lanes((tok, tok)) + sublanes((tok, tok)) == tok - 1).astype(bf16)
    query, key, value = qkv[0], qkv[1], qkv[2]
    grads = [[], [], []]
    offsets = []
    for h in range(heads_here):
        at = slice(h * size, (h + 1) * size)
        out = attended_grad[at]
        weights = weights_ref[h]
        mass = mm(out, value[at], tn)
        score = weights * (mass - jnp.sum(weights * mass, axis=1, keepdims=True))
        score = score.astype(bf16)
        grads[0].append(mm(key[at], score, nt) * scale)
        grads[1].append(mm(query[at], score) * scale)
        grads[2].append(mm(out, weights.astype(bf16)))
        flipped = jnp.concatenate([mm(flip, score), jnp.zeros((tok, tok), f32)], axis=1)
        rolled = pltpu.roll(flipped, 0, 1, stride=1, stride_axis=0)
        offsets.append(jnp.sum(rolled, axis=0, keepdims=True))
    first = jnp.zeros((width, tok), f32)
    row = jnp.zeros((1, tok), f32)
    for i, w in enumerate((wq, wk, wv)):
        low = jnp.concatenate(grads[i], axis=0).astype(bf16)
        late_ref[i * col : (i + 1) * col, :] = low
        first = first + mm(w[...], low, tn)
        row = row + jnp.sum(low.astype(f32) * qkv[i].astype(f32), axis=0, keepdims=True)
    side = side_rows(16, tok, high_low(row))
    for i in range(blocks):
        at = slice(i * col, (i + 1) * col)
        first_ref[i, : col + 16, :] = jnp.concatenate([first[at], side], axis=0).astype(bf16)
        first_ref[i, col + 16 :, :] = part[i]

    product = mm(attended[...], branch, nt)
    pieces = product_ref.shape[0]
    for b in range(pieces):
        at = slice(b * (col // pieces), (b + 1) * (col // pieces))
        product_ref[b] = (product if pieces == 1 else fold_lanes(product[at])).astype(product_ref.dtype)
    gain_two_grad = jnp.sum(normed_grad * unit, axis=1, keepdims=True)
    gains = jnp.zeros((col, 1), f32)
    own = jnp.zeros((col, tok), f32)
    for i in range(blocks):
        at = slice(i * col, (i + 1) * col)
        gains = jnp.where(scalars[1] == i, gain_two_grad[at], gains)
        own = jnp.where(scalars[1] == i, residual_grad[at], own)
    own_ref[...] = own
    probs = jnp.sum(router * valid, axis=1, keepdims=True)
    if experts < col:
        probs = jnp.concatenate([probs, jnp.zeros((col - experts, 1), f32)], axis=0)
    gains = jnp.transpose(side_lanes(col, 128, [gains, jnp.zeros_like(gains)] + high_low(probs)))[0:8]
    router_grad = mm(logit_grad, normed, nt)
    offsets = jnp.concatenate(offsets, axis=0)
    offsets = jnp.concatenate([offsets, jnp.zeros((8 - heads_here, 2 * tok), f32)], axis=0)
    gains = jnp.concatenate([gains, jnp.zeros((8, 64), f32)], axis=1)
    pieces = [fold_lanes(gains), fold_lanes(offsets), fold_lanes(router_grad)]
    spare = small_ref.shape[0] - 6 * experts - 32
    if spare:
        pieces.append(jnp.zeros((spare, 128), f32))
    small_ref[...] = jnp.concatenate(pieces, axis=0)


def first_kernel(scalars, came, packed, own, small, *refs):
    product, (ret_ref, sums_ref, input_ref) = refs[:-3], refs[-3:]
    col, tok = own.shape
    heads = came.shape[0]
    experts = ret_ref.shape[0]
    total = came[0].astype(f32)
    for i in range(1, heads):
        total = total + came[i].astype(f32)
    mean = (total[col : col + 1] + total[col + 1 : col + 2]) * (1.0 / (heads * col))
    scale = token_scale(tall(packed, 0, col))
    mine = packed[scalars[1]].astype(f32)
    unit = mine[:col] * scale
    gain = gain_columns(mine[2 * col : 2 * col + 16])[0]
    input_ref[...] = own[...] + scale * (total[:col] * gain - unit * mean)
    gain_grad = jnp.sum(total[:col] * unit, axis=1, keepdims=True)
    gain_grad = jnp.transpose(side_lanes(col, 128, [jnp.zeros_like(gain_grad), gain_grad]))[0:8]
    gain_grad = jnp.concatenate([gain_grad, jnp.zeros((8, 64), f32)], axis=1)
    sums = jnp.concatenate([small[:16, :] + fold_lanes(gain_grad), small[16:, :]], axis=0)
    sums_ref[...] = sums
    produced = total[col + 16 :]
    count = produced.shape[0] * 2 // 3
    half = count // 2
    top = produced[:count]
    rest = jnp.concatenate([produced[count:, :64], produced[count:, 64:]], axis=0)
    rest = jnp.concatenate([rest, jnp.zeros((count, 64), f32)], axis=1)
    slots = count // experts
    for e in range(experts):
        at = slice(e * slots, (e + 1) * slots)
        pieces = [top[at], rest[at]]
        if product:
            chunk = sums.shape[0] // experts
            pieces += [sums[e * chunk : (e + 1) * chunk], product[0][e].astype(f32)]
        ret_ref[e] = jnp.concatenate(pieces, axis=0).astype(bf16)


def last_kernel(slots, came, side, gate, residual, *refs):
    block_ref, refs = refs[0], refs[1:]
    experts = came.shape[0]
    col, tok = residual.shape
    blocks = [came[e].astype(f32) for e in range(experts)]
    top = jnp.concatenate([block[:slots] for block in blocks], axis=0).astype(bf16)
    rest = jnp.concatenate([block[slots : 2 * slots] for block in blocks], axis=0).astype(bf16)
    pick = pick_slots(side[0:1, :].astype(jnp.int32), experts * slots).astype(bf16)
    returned = jnp.concatenate([mm(top, pick, tn), mm(rest, pick, tn)[: col - 128]], axis=0)
    block_ref[...] = (residual[...] + gate[0:1, :] * returned).astype(bf16)
    if refs:
        total = blocks[0][2 * slots :]
        for block in blocks[1:]:
            total = total + block[2 * slots :]
        for e in range(experts):
            refs[0][e] = total.astype(bf16)


def turn_kernel(all_in, packed, normed_ref):
    groups, heads, col, tok = all_in.shape
    gain = all_gains(packed)[0]
    for b in range(groups):
        x = jnp.concatenate([all_in[b, i].astype(f32) for i in range(heads)], axis=0)
        normed_ref[:, b * tok : (b + 1) * tok] = (x * token_scale(x) * gain).astype(bf16)


def products_kernel(
    late, normed, shares, buckets, stats, q_ref, k_ref, v_ref, out_ref, router_ref, table_ref, gains_ref, aux_ref
):
    groups = shares.shape[0]
    col = q_ref.shape[0]
    experts = router_ref.shape[0]
    size = col // groups
    blocks = [shares[b].astype(f32) for b in range(groups)]
    chunk = blocks[0].shape[0] - 6 * size
    for b in range(groups):
        out_ref[b * size : (b + 1) * size, :] = unfold_lanes(blocks[b][chunk:], 6)
    joined = jnp.concatenate([late[b] for b in range(groups)], axis=1)
    for i, ref in enumerate((q_ref, k_ref, v_ref)):
        ref[...] = mm(joined[i * col : (i + 1) * col], normed[...], nt)
    small = jnp.concatenate([block[:chunk] for block in blocks], axis=0)
    gains = unfold_lanes(small[:16], 2)
    gains_ref[...] = gains
    probs = gains[2:3, :experts] + gains[3:4, :experts]
    same = lanes((experts, experts)) == sublanes((experts, experts))
    share = jnp.sum(jnp.where(same, stats[:, 0:1] * probs, 0.0), axis=0, keepdims=True)
    valid_total = 3 * normed.shape[1] // 4
    aux_ref[...] = jnp.sum(share, axis=1, keepdims=True) * (experts / (valid_total * valid_total))
    hot = (sublanes((table_ref.shape[1], buckets.shape[1])) == buckets[...]).astype(f32)
    table_ref[...] = mm(unfold_lanes(small[16:32], 2), hot, nt, highest)[: table_ref.shape[0]]
    router_ref[...] = unfold_lanes(small[32 : 32 + 6 * experts], 6)


def few_experts():
    return lax.axis_size("expert") <= 8


def shards(
    inputs,
    out_grad,
    lengths,
    routes,
    buckets,
    gain_attn,
    w_query,
    w_key,
    w_value,
    w_output,
    bias_table,
    gain_ffn,
    w_router,
    w_in,
    w_out,
):
    tok, col = inputs.shape
    heads_here = bias_table.shape[1]
    head_size = w_query.shape[1] // heads_here
    width, experts = w_router.shape
    bucket_count = bias_table.shape[0]
    heads = width // col
    groups = lax.axis_size("expert")
    me_head, me_expert = lax.axis_index("head"), lax.axis_index("expert")
    capacity = max(2, (4 * tok + 3 * experts - 1) // (3 * experts))
    slots = -(-(capacity + 1) // 8) * 8
    total = experts * slots
    small_rows = 6 * experts + 32 + (48 if few_experts() else 0)
    valid_total = 3 * tok * groups // 4
    scale = head_size ** (-0.5)
    joined = few_experts()
    w_in, w_out = w_in[0], w_out[0]
    wq, wk, wv = w_query.T, w_key.T, w_value.T
    routes_row = routes.T
    router_rows = w_router.T
    scalars = jnp.stack([lengths[0], me_head.astype(jnp.int32), me_expert.astype(jnp.int32)])
    buckets_row = jnp.pad(buckets, (0, 1), constant_values=-1)[None]

    space = jnp.zeros((64,), bf16)
    gains = jnp.concatenate([gain_attn, space, gain_ffn, space, jnp.zeros((1536,), bf16)]).reshape(16, 128)
    packed = lax.all_gather(jnp.concatenate([inputs.T, out_grad.T, gains], axis=0), "head")
    if joined:
        all_in = lax.all_gather(inputs.T, ("expert", "head")).reshape(groups, heads, col, tok)
    qkv, weights, attended, branch = call(
        functools.partial(attend_kernel, scale),
        [
            ((3, col, tok), bf16, 1), ((heads_here, tok, tok), f32, 1), ((col, tok), bf16, 1),
            ((heads, col, tok), bf16),
        ],
        scalars, packed, far(wq), far(wk), far(wv), far(w_output), far(buckets_row), far(bias_table.T),
    )

    branch = lax.all_to_all(branch, "head", split_axis=0, concat_axis=0, tiled=True)
    residual, low, side, send = call(
        functools.partial(route_kernel, capacity),
        [((col, tok), f32, 1), ((col, tok), bf16, 1), ((8, tok), f32, 1), ((experts, slots, 2 * col), bf16)],
        scalars, branch, far(inputs.T), far(out_grad.T), far(routes_row),
    )
    quarter = lax.all_to_all(send, "expert", split_axis=0, concat_axis=0, tiled=True)
    quarters = lax.all_gather(quarter.reshape(total, 2 * col), "head")

    back, part, hidden, before_grad, back_rows, rows = call(
        functools.partial(expert_kernel, capacity),
        [((experts * heads, slots, 256), bf16), ((heads, total * 3 // 2, 128), bf16, 1)]
        + [((total, width), bf16, 1)] * 4,
        scalars, quarters, far(packed), far(w_in), far(w_out), far(router_rows),
    )
    came = lax.all_to_all(back, ("expert", "head"), split_axis=0, concat_axis=0, tiled=True)
    grad_own, gate_grad, stats = call(
        collect_kernel,
        [((2 * col, tok), bf16), ((8, tok), f32, 1), ((experts, 128), f32, 1)],
        came, far(side), far(low),
    )
    expert_grad = lax.all_gather(grad_own, "head")

    late, first, residual_grad_own, small, product, gate = call(
        functools.partial(backward_kernel, scale, valid_total),
        [
            ((3 * col, tok), bf16, 1), ((heads, col + 16 + total * 3 // 2, 128), bf16), ((col, tok), f32, 1),
            ((small_rows, 128), f32, 1),
            ((groups, col // groups * 6, 128), bf16, 1) if joined else ((1, col, width), f32, 1),
            ((8, tok), f32, 1),
        ],
        scalars, far(packed), expert_grad, far(gate_grad), far(stats), far(routes_row),
        far(router_rows), far(w_output), far(weights), far(qkv), far(wq), far(wk), far(wv), far(attended),
        far(part),
    )

    if joined:
        late_all = lax.all_gather(late, "expert")

    first = lax.all_to_all(first, "head", split_axis=0, concat_axis=0, tiled=True)
    ret, sums, input_grad = call(
        first_kernel,
        [
            ((experts, 2 * slots + (small_rows // experts + product.shape[1] if joined else 0), 128), bf16),
            ((small_rows, 128), f32, 1), ((col, tok), f32, 1),
        ],
        scalars, first, far(packed), far(residual_grad_own), far(small), *([far(product)] if joined else []),
    )
    ret = lax.all_to_all(ret, "expert", split_axis=0, concat_axis=0, tiled=True)
    out = call(
        functools.partial(last_kernel, slots),
        [((col, tok), bf16)]
        + ([((groups, small_rows // groups + product.shape[1], 128), bf16)] if joined else []),
        ret, far(side), far(gate), far(residual),
    )
    block_out = out[0]
    in_weight_grad, out_weight_grad = call(
        weights_kernel, [((width, width), f32, 1)] * 2, far(rows), far(hidden), far(before_grad), far(back_rows)
    )
    if joined:
        shares = lax.all_to_all(out[1], "expert", split_axis=0, concat_axis=0, tiled=True)
        normed_all = call(turn_kernel, [((width, groups * tok), bf16, 1)], far(all_in), far(packed))[0]
        q_grad, k_grad, v_grad, output_grad, router_grad, table_grad, gain_grads, aux_loss = call(
            products_kernel,
            [((col, width), f32, 1)] * 4
            + [((experts, width), f32), ((heads_here, bucket_count), f32), ((8, 256), f32), ((1, 1), f32)],
            far(late_all), far(normed_all), shares, far(buckets_row), far(stats),
        )
    else:
        gain = packed[:, 2 * col : 2 * col + 2].reshape(heads, 256)[:, :col].reshape(width, 1)
        x = packed[:, :col].reshape(width, tok).astype(f32)
        normed = (x * token_scale(x) * gain.astype(f32)).astype(bf16)
        products = [mm(late[i * col : (i + 1) * col], normed, nt) for i in range(3)]
        q_grad, k_grad, v_grad, sums, output_grad = lax.psum(products + [sums, product[0]], "expert")
        router_grad = unfold_lanes(sums[32 : 32 + 6 * experts], 6)
        offsets = unfold_lanes(sums[16:32], 2)[:heads_here, : 2 * tok - 1]
        hot = (buckets[None, :] == jnp.arange(bucket_count)[:, None]).astype(f32)
        table_grad = mm(offsets, hot, nt, highest)
        gain_grads = unfold_lanes(sums[:16], 2)
        probs = gain_grads[2, :experts] + gain_grads[3, :experts]
        aux_loss = experts * jnp.sum(stats[:, 0] * probs) / (valid_total * valid_total)
    return (
        block_out.T,
        input_grad.T,
        aux_loss.reshape(()),
        gain_grads[1, :col],
        q_grad.T,
        k_grad.T,
        v_grad.T,
        output_grad,
        table_grad.T,
        gain_grads[0, :col],
        router_grad.T,
        in_weight_grad[None],
        out_weight_grad[None],
    )


def solution(mesh):
    return jax.shard_map(
        shards,
        mesh=mesh,
        in_specs=(
            P("expert", "head"),
            P("expert", "head"),
            P("expert"),
            P("expert", None),
            P(),
            P("head"),
            P(None, "head"),
            P(None, "head"),
            P(None, "head"),
            P("head", None),
            P(None, "head"),
            P("head"),
            P(),
            P("expert", None, "head"),
            P("expert", "head", None),
        ),
        out_specs=(
            P("expert", "head"),
            P("expert", "head"),
            P(),
            P("head"),
            P(None, "head"),
            P(None, "head"),
            P(None, "head"),
            P("head", None),
            P(None, "head"),
            P("head"),
            P(),
            P("expert", None, "head"),
            P("expert", "head", None),
        ),
        check_vma=False,
    )
```

```python
import functools

import jax
import jax.numpy as jnp
from jax import lax
from jax.experimental import pallas as pl
from jax.experimental.pallas import tpu as pltpu
from jax.sharding import PartitionSpec as P

eps = 1e-06
aux_weight = 0.01
f32 = jnp.float32
bf16 = jnp.bfloat16
gelu_scale = 0.7978845608028654
gelu_cube = 0.044715
highest = lax.Precision.HIGHEST
nt = ((1,), (1,))
tn = ((0,), (0,))


def mm(left, right, dims=((1,), (0,)), precision=None):
    return lax.dot_general(left, right, (dims, ((), ())), precision=precision, preferred_element_type=f32)


def call(body, outs, *args):
    scalar_memory = pl.BlockSpec(memory_space=pltpu.SMEM)
    in_specs = [scalar_memory if a.dtype == jnp.int32 and a.ndim == 1 else pl.BlockSpec() for a in args]
    shapes = []
    for shape, kind, *remote in outs:
        shapes.append(pltpu.HBM(shape, kind) if remote else jax.ShapeDtypeStruct(shape, kind))
    return pl.pallas_call(
        body,
        out_shape=shapes,
        in_specs=in_specs,
        compiler_params=pltpu.CompilerParams(vmem_limit_bytes=40 * 1024 * 1024),
    )(*args)


def far(array):
    return pltpu.with_memory_space_constraint(array, pltpu.HBM)


def tall(ref, first, rows):
    return jnp.concatenate([ref[i, first : first + rows, :].astype(f32) for i in range(ref.shape[0])], axis=0)


def gain_columns(block):
    turned = jnp.transpose(block.astype(f32))
    return [jnp.concatenate([turned[:, i : i + 1], turned[:64, i + 1 : i + 2]], axis=0) for i in (0, 2)]


def all_gains(packed):
    first = 2 * packed.shape[2] * 3 // 2
    pairs = [gain_columns(packed[i, first : first + 16, :]) for i in range(packed.shape[0])]
    return [jnp.concatenate([pair[i] for pair in pairs], axis=0) for i in range(2)]


def token_scale(values):
    return lax.rsqrt(jnp.sum(values * values, axis=0, keepdims=True) * (1.0 / values.shape[0]) + eps)


def lanes(shape):
    return lax.broadcasted_iota(jnp.int32, shape, len(shape) - 1)


def sublanes(shape):
    return lax.broadcasted_iota(jnp.int32, shape, len(shape) - 2)


def side_lanes(rows, width, columns):
    spot = lanes((rows, width))
    out = jnp.zeros((rows, width), f32)
    for i, column in enumerate(columns):
        out = jnp.where(spot == i, column, out)
    return out


def side_rows(rows, width, lines):
    spot = sublanes((rows, width))
    out = jnp.zeros((rows, width), f32)
    for i, line in enumerate(lines):
        out = jnp.where(spot == i, line, out)
    return out


def high_low(values, count=2):
    pieces = []
    for _ in range(count):
        piece = values.astype(bf16).astype(f32)
        pieces.append(piece)
        values = values - piece
    return pieces


def softmax(values, axis):
    raised = jnp.exp(values - jnp.max(values, axis=axis, keepdims=True))
    return raised / jnp.sum(raised, axis=axis, keepdims=True)


def gelu_parts(u):
    t = jnp.tanh(gelu_scale * (u + gelu_cube * u * u * u))
    value = 0.5 * u * (1.0 + t)
    slope = 0.5 * (1.0 + t) + 0.5 * u * (1.0 - t * t) * gelu_scale * (1.0 + 3.0 * gelu_cube * u * u)
    return value, slope


def fold_lanes(rows):
    return jnp.concatenate([rows[:, i : i + 128] for i in range(0, rows.shape[1], 128)], axis=0)


def unfold_lanes(rows, pieces):
    size = rows.shape[0] // pieces
    return jnp.concatenate([rows[i * size : (i + 1) * size] for i in range(pieces)], axis=1)


def fold_rest(rest, side):
    groups = [rest[i : i + 8] for i in range(0, rest.shape[0], 8)]
    count = side.shape[1]
    spot = lanes((8, 64))
    last = jnp.zeros((8, 64), f32)
    for g in range(len(groups)):
        for j in range(count):
            last = jnp.where(spot == g * count + j, side[8 * g : 8 * g + 8, j : j + 1], last)
    groups.append(last)
    if len(groups) % 2:
        groups.append(jnp.zeros((8, 64), f32))
    return [jnp.concatenate(groups[i : i + 2], axis=1) for i in range(0, len(groups), 2)]


def unfold_rest(blocks, slots, count):
    halves = []
    for i in range(0, blocks.shape[0], 8):
        halves += [blocks[i : i + 8, :64], blocks[i : i + 8, 64:]]
    number = slots // 8
    side = [halves[number][:, g * count : (g + 1) * count] for g in range(number)]
    return jnp.concatenate(halves[:number], axis=0), jnp.concatenate(side, axis=0)


def folded_rows(slots):
    return slots + 8 * ((slots // 8 + 2) // 2)


def pick_slots(spots, count):
    return sublanes((count, spots.shape[1])) == spots


def attend_kernel(
    scale, scalars, packed, wq, wk, wv, w_output, buckets, table, qkv_ref, weights_ref, attended_ref, branch_ref
):
    heads, tok, _ = weights_ref.shape
    col = wq.shape[0]
    size = col // heads
    x = tall(packed, 0, col)
    normed = (x * token_scale(x) * all_gains(packed)[0]).astype(bf16)
    projected = []
    for i, w in enumerate((wq, wk, wv)):
        rows = mm(w[...], normed).astype(bf16)
        qkv_ref[i] = rows
        projected.append(rows)
    query, key, value = projected
    hot = (sublanes((table.shape[1], 2 * tok - 1)) == buckets[...]).astype(f32)
    offsets = mm(table[...], hot, precision=highest)
    offsets = jnp.concatenate([offsets, jnp.zeros((heads, 1), f32)], axis=1)
    open_keys = lanes((tok, tok)) < scalars[0]
    outs = []
    for h in range(heads):
        at = slice(h * size, (h + 1) * size)
        spread = jnp.broadcast_to(offsets[h : h + 1, :], (tok, 2 * tok))
        bias = pltpu.roll(spread, tok + 1, 1, stride=1, stride_axis=0)[:, :tok]
        scores = mm(query[at], key[at], tn) * scale + bias
        weights = softmax(jnp.where(open_keys, scores, -1000000000.0), 1)
        weights_ref[h] = weights
        outs.append(mm(value[at], weights.astype(bf16), nt))
    attended = jnp.concatenate(outs, axis=0).astype(bf16)
    attended_ref[...] = attended
    branch = mm(w_output[...], attended, tn)
    for i in range(branch_ref.shape[0]):
        branch_ref[i] = branch[i * col : (i + 1) * col].astype(bf16)


def second_norm(residual, gain, w_router):
    scale = token_scale(residual)
    unit = residual * scale
    normed = (unit * gain).astype(bf16)
    return scale, unit, normed, softmax(mm(w_router, normed), 0)


def route_kernel(capacity, scalars, came, inputs, out_grad, routes, residual_ref, low_ref, side_ref, send_ref):
    col, tok = inputs.shape
    experts, slots, _ = send_ref.shape
    residual = inputs[...].astype(f32)
    for i in range(came.shape[0]):
        residual = residual + came[i].astype(f32)
    residual_ref[...] = residual
    low = residual.astype(bf16)
    low_ref[...] = low
    route_hot = (sublanes((experts, tok)) == routes[...]).astype(f32)
    before = (sublanes((tok, tok)) < lanes((tok, tok))).astype(bf16)
    slot = jnp.sum(mm(route_hot.astype(bf16), before) * route_hot, axis=0, keepdims=True)
    spots = routes[...].astype(f32) * slots + slot
    side_ref[...] = side_rows(8, tok, [spots])
    valid = (lanes((1, tok)) < scalars[0]).astype(f32)
    counts = jnp.sum(route_hot * valid, axis=1, keepdims=True)
    pick = pick_slots(spots.astype(jnp.int32), experts * slots).astype(bf16)
    rows = mm(pick, jnp.concatenate([low, out_grad[...]], axis=0), nt)
    spare = (sublanes((slots, 2 * col)) == capacity) & (lanes((slots, 2 * col)) == col)
    for e in range(experts):
        block = rows[e * slots : (e + 1) * slots]
        send_ref[e] = jnp.where(spare, counts[e : e + 1], block).astype(bf16)


def gain_row(packed, first, line):
    pieces = []
    for i in range(packed.shape[0]):
        block = packed[i, first : first + 16, :].astype(f32)
        pieces += [block[line : line + 1, :], block[line + 1 : line + 2, :64]]
    return jnp.concatenate(pieces, axis=1)


def expert_kernel(
    capacity, scalars, quarters, packed, w_in, w_out, w_router,
    back_ref, part_ref, hidden_ref, before_ref, grads_ref, rows_ref,
):
    total = rows_ref.shape[0]
    experts, width = w_router.shape
    heads = part_ref.shape[0]
    col = width // heads
    slots = total // experts
    half = total // 2
    parts = [quarters[i].astype(f32) for i in range(heads)]
    residual = jnp.concatenate([block[:, :col] for block in parts], axis=1)
    grads = jnp.concatenate([block[:, col:] for block in parts], axis=1)
    inverse = lax.rsqrt(jnp.sum(residual * residual, axis=1, keepdims=True) * (1.0 / width) + eps)
    rows = (residual * inverse * gain_row(packed, 2 * col, 2)).astype(bf16)
    rows_ref[...] = rows
    hidden, slope = gelu_parts(mm(rows, w_in[...]))
    hidden = hidden.astype(bf16)
    hidden_ref[...] = hidden
    produced = mm(hidden, w_out[...])
    for i in range(heads):
        mine = produced[:, i * col : (i + 1) * col]
        rest = mine[:, 128:]
        part_ref[i] = jnp.concatenate(
            [mine[:, :128], jnp.concatenate([rest[:half], rest[half:]], axis=1)], axis=0
        ).astype(bf16)
    probs = softmax(mm(rows, w_router[...], nt), 1)
    gate = jnp.sum(jnp.where(lanes((total, experts)) == scalars[2], probs, 0.0), axis=1, keepdims=True)
    back = (gate * grads).astype(bf16)
    grads_ref[...] = back
    before = (mm(back, w_out[...], nt) * slope).astype(bf16)
    before_ref[...] = before
    rows_grad = mm(before, w_in[...], nt)
    gate_grad = jnp.sum(grads * produced, axis=1, keepdims=True)
    stats = jnp.zeros((1, 128), f32)
    for b in range(experts):
        stats = stats + grads[b * slots + capacity : b * slots + capacity + 1, :128]
    side = side_lanes(total, 4, high_low(gate_grad) + high_low(stats[:, 0:1]))
    for b in range(experts):
        at = slice(b * slots, (b + 1) * slots)
        for i in range(heads):
            mine = rows_grad[at, i * col : (i + 1) * col]
            back_ref[b * heads + i] = jnp.concatenate(
                [mine[:, :128]] + fold_rest(mine[:, 128:], side[at]), axis=0
            ).astype(bf16)


def weights_kernel(rows_ref, hidden, before, grads, in_ref, out_ref):
    in_ref[...] = mm(rows_ref[...], before[...], tn)
    out_ref[...] = mm(hidden[...], grads[...], tn)


def collect_kernel(slots, came, side, low, grad_ref, gate_ref, stats_ref):
    col, tok = low.shape
    experts = stats_ref.shape[0]
    heads = came.shape[0] // experts
    tops, rests, scalars = [], [], []
    for e in range(experts):
        total = came[e * heads].astype(f32)
        for i in range(1, heads):
            total = total + came[e * heads + i].astype(f32)
        rest, columns = unfold_rest(total[slots:], slots, 4)
        tops.append(total[:slots])
        rests.append(rest)
        scalars.append(columns)
    counts = jnp.concatenate([columns[0:1] for columns in scalars], axis=0) * (1.0 / heads)
    pick = pick_slots(side[0:1, :].astype(jnp.int32), experts * slots)
    for first, pieces in ((0, tops), (128, rests)):
        block = jnp.concatenate(pieces, axis=0).astype(bf16)
        grad_ref[first : min(first + 128, col), :] = mm(block, pick.astype(bf16), tn).astype(bf16)
    grad_ref[col:, :] = low[...]
    gate = mm(jnp.concatenate(scalars, axis=0), pick.astype(f32), tn, highest)
    gate_ref[...] = jnp.broadcast_to(gate[0:1] + gate[1:2], gate_ref.shape)
    stats_ref[...] = side_lanes(experts, 128, [counts[:, 2:3] + counts[:, 3:4]])


def backward_kernel(
    scale, valid_total, scalars, packed, expert_grad, gate_grad, stats, routes, w_router, w_output, weights_ref,
    qkv, wq, wk, wv, attended, part, late_ref, first_ref, own_ref, gate_ref, *share_refs,
):
    tok = routes.shape[1]
    heads_here = weights_ref.shape[0]
    blocks, col = packed.shape[0], wq.shape[0]
    experts, width = w_router.shape
    size = col // heads_here
    gain_one, gain_two = all_gains(packed)
    residual = tall(expert_grad, col, col)
    scale_two, unit, normed, router = second_norm(residual, gain_two, w_router[...])
    valid = (lanes((1, tok)) < scalars[0]).astype(f32)
    route_hot = (sublanes((experts, tok)) == routes[...]).astype(f32)
    fraction = stats[:, 0:1] * (aux_weight * experts / (valid_total * valid_total))
    gate = jnp.sum(router * route_hot, axis=0, keepdims=True)
    gate_ref[...] = jnp.broadcast_to(gate, gate_ref.shape)
    prob_grad = route_hot * gate_grad[0:1, :] + fraction * valid
    logit_grad = router * (prob_grad - jnp.sum(router * prob_grad, axis=0, keepdims=True))
    logit_grad = logit_grad.astype(bf16)
    normed_grad = mm(w_router[...], logit_grad, tn) + tall(expert_grad, 0, col)
    unit_grad = normed_grad * gain_two
    mean = jnp.sum(unit_grad * unit, axis=0, keepdims=True) * (1.0 / width)
    residual_grad = tall(packed, col, col) + scale_two * (unit_grad - unit * mean)
    branch = residual_grad.astype(bf16)
    attended_grad = mm(w_output[...], branch).astype(bf16)
    flip = (lanes((tok, tok)) + sublanes((tok, tok)) == tok - 1).astype(bf16)
    query, key, value = qkv[0], qkv[1], qkv[2]
    grads = [[], [], []]
    offsets = []
    for h in range(heads_here):
        at = slice(h * size, (h + 1) * size)
        out = attended_grad[at]
        weights = weights_ref[h]
        mass = mm(out, value[at], tn)
        score = weights * (mass - jnp.sum(weights * mass, axis=1, keepdims=True))
        score = score.astype(bf16)
        grads[0].append(mm(key[at], score, nt) * scale)
        grads[1].append(mm(query[at], score) * scale)
        grads[2].append(mm(out, weights.astype(bf16)))
        flipped = jnp.concatenate([mm(flip, score), jnp.zeros((tok, tok), f32)], axis=1)
        rolled = pltpu.roll(flipped, 0, 1, stride=1, stride_axis=0)
        offsets.append(jnp.sum(rolled, axis=0, keepdims=True))
    first = jnp.zeros((width, tok), f32)
    row = jnp.zeros((1, tok), f32)
    for i, w in enumerate((wq, wk, wv)):
        low = jnp.concatenate(grads[i], axis=0).astype(bf16)
        late_ref[i * col : (i + 1) * col, :] = low
        first = first + mm(w[...], low, tn)
        row = row + jnp.sum(low.astype(f32) * qkv[i].astype(f32), axis=0, keepdims=True)
    side = side_rows(16, tok, high_low(row))
    for i in range(blocks):
        at = slice(i * col, (i + 1) * col)
        first_ref[i, : col + 16, :] = jnp.concatenate([first[at], side], axis=0).astype(bf16)
        first_ref[i, col + 16 :, :] = part[i]

    product = mm(attended[...], branch, nt)
    gain_two_grad = jnp.sum(normed_grad * unit, axis=1, keepdims=True)
    gains = jnp.zeros((col, 1), f32)
    own = jnp.zeros((col, tok), f32)
    for i in range(blocks):
        at = slice(i * col, (i + 1) * col)
        gains = jnp.where(scalars[1] == i, gain_two_grad[at], gains)
        own = jnp.where(scalars[1] == i, residual_grad[at], own)
    own_ref[...] = own
    probs = jnp.sum(router * valid, axis=1, keepdims=True)
    if experts < col:
        probs = jnp.concatenate([probs, jnp.zeros((col - experts, 1), f32)], axis=0)
    gains = jnp.transpose(side_lanes(col, 128, [gains] + high_low(probs)))[0:8]
    router_grad = mm(logit_grad, normed, nt)
    offsets = jnp.concatenate(offsets, axis=0)
    offsets = jnp.concatenate([offsets, jnp.zeros((8 - heads_here, 2 * tok), f32)], axis=0)
    gains = jnp.concatenate([gains, jnp.zeros((8, 64), f32)], axis=1)
    pieces = [fold_lanes(gains), fold_lanes(offsets), fold_lanes(router_grad)]
    if len(share_refs) == 2:
        share_refs[0][...] = jnp.concatenate(pieces, axis=0)
        share_refs[1][...] = product
    else:
        share_ref = share_refs[0]
        groups = share_ref.shape[0]
        size = col // groups
        chunk = share_ref.shape[1] - 6 * size
        small = jnp.concatenate(pieces + [jnp.zeros((groups * chunk - 6 * experts - 32, 128), f32)], axis=0)
        for b in range(groups):
            share_ref[b] = jnp.concatenate(
                [small[b * chunk : (b + 1) * chunk], fold_lanes(product[b * size : (b + 1) * size])], axis=0
            ).astype(bf16)


def first_kernel(scalars, came, packed, own, *refs):
    shares, (ret_ref, gain_ref, input_ref) = refs[:-3], refs[-3:]
    col, tok = own.shape
    heads = came.shape[0]
    experts = ret_ref.shape[0]
    total = came[0].astype(f32)
    for i in range(1, heads):
        total = total + came[i].astype(f32)
    mean = (total[col : col + 1] + total[col + 1 : col + 2]) * (1.0 / (heads * col))
    scale = token_scale(tall(packed, 0, col))
    mine = packed[scalars[1]].astype(f32)
    unit = mine[:col] * scale
    gain = gain_columns(mine[2 * col : 2 * col + 16])[0]
    input_ref[...] = own[...] + scale * (total[:col] * gain - unit * mean)
    gain_grad = jnp.sum(total[:col] * unit, axis=1, keepdims=True)
    gain_grad = jnp.transpose(side_lanes(col, 128, [gain_grad]))[0:8]
    gain_grad = fold_lanes(jnp.concatenate([gain_grad, jnp.zeros((8, 64), f32)], axis=1))
    gain_ref[...] = gain_grad
    produced = total[col + 16 :]
    count = produced.shape[0] * 2 // 3
    top = produced[:count]
    rest = jnp.concatenate([produced[count:, :64], produced[count:, 64:]], axis=0)
    rest = jnp.concatenate([rest, jnp.zeros((count, 64), f32)], axis=1)
    slots = count // experts
    joined = []
    if shares:
        share = shares[0][0].astype(f32)
        for e in range(1, experts):
            share = share + shares[0][e].astype(f32)
        joined = [gain_grad, share]
    for e in range(experts):
        at = slice(e * slots, (e + 1) * slots)
        ret_ref[e] = jnp.concatenate([top[at], rest[at]] + joined, axis=0).astype(bf16)


def add_returned(slots, blocks, side, gate, residual):
    col = residual.shape[0]
    top = jnp.concatenate([block[:slots] for block in blocks], axis=0).astype(bf16)
    rest = jnp.concatenate([block[slots : 2 * slots] for block in blocks], axis=0).astype(bf16)
    pick = pick_slots(side[0:1, :].astype(jnp.int32), len(blocks) * slots).astype(bf16)
    returned = jnp.concatenate([mm(top, pick, tn), mm(rest, pick, tn)[: col - 128]], axis=0)
    return (residual[...] + gate[0:1, :] * returned).astype(bf16)


def last_kernel(slots, came, side, gate, residual, block_ref):
    blocks = [came[e].astype(f32) for e in range(came.shape[0])]
    block_ref[...] = add_returned(slots, blocks, side, gate, residual)


def turn_kernel(all_in, packed, normed_ref):
    groups, heads, col, tok = all_in.shape
    gain = all_gains(packed)[0]
    for b in range(groups):
        x = jnp.concatenate([all_in[b, i].astype(f32) for i in range(heads)], axis=0)
        normed_ref[b * tok : (b + 1) * tok, :] = jnp.transpose(x * token_scale(x) * gain).astype(bf16)


def products_kernel(
    slots, late, normed, came, buckets, stats, side, gate, residual,
    q_ref, k_ref, v_ref, out_ref, block_ref, router_ref, table_ref, gains_ref, aux_ref,
):
    groups = came.shape[0]
    col = q_ref.shape[0]
    experts = router_ref.shape[0]
    size = col // groups
    blocks = [came[b].astype(f32) for b in range(groups)]
    block_ref[...] = add_returned(slots, blocks, side, gate, residual)
    gain_one = blocks[0][2 * slots : 2 * slots + 16]
    for block in blocks[1:]:
        gain_one = gain_one + block[2 * slots : 2 * slots + 16]
    shares = [block[2 * slots + 16 :] for block in blocks]
    chunk = shares[0].shape[0] - 6 * size
    for b in range(groups):
        out_ref[b * size : (b + 1) * size, :] = unfold_lanes(shares[b][chunk:], 6)
    joined = jnp.concatenate([late[b] for b in range(groups)], axis=1)
    product = mm(joined, normed[...])
    for i, ref in enumerate((q_ref, k_ref, v_ref)):
        ref[...] = product[i * col : (i + 1) * col]
    small = jnp.concatenate([share[:chunk] for share in shares], axis=0)
    gains = unfold_lanes(small[:16], 2)
    gains_ref[0:8, :] = gains
    gains_ref[8:16, :] = unfold_lanes(gain_one, 2)
    probs = gains[1:2, :experts] + gains[2:3, :experts]
    same = lanes((experts, experts)) == sublanes((experts, experts))
    share = jnp.sum(jnp.where(same, stats[:, 0:1] * probs, 0.0), axis=0, keepdims=True)
    valid_total = 3 * normed.shape[0] // 4
    aux_ref[...] = jnp.sum(share, axis=1, keepdims=True) * (experts / (valid_total * valid_total))
    span = buckets.shape[1]
    hot = (sublanes((table_ref.shape[1], span)) == buckets[...]).astype(f32)
    offsets = unfold_lanes(small[16:32], 2)[:, :span]
    table_ref[...] = mm(offsets, hot, nt, highest)[: table_ref.shape[0]]
    router_ref[...] = unfold_lanes(small[32 : 32 + 6 * experts], 6)


def few_experts():
    return lax.axis_size("expert") <= 8


def shards(
    inputs,
    out_grad,
    lengths,
    routes,
    buckets,
    gain_attn,
    w_query,
    w_key,
    w_value,
    w_output,
    bias_table,
    gain_ffn,
    w_router,
    w_in,
    w_out,
):
    tok, col = inputs.shape
    heads_here = bias_table.shape[1]
    head_size = w_query.shape[1] // heads_here
    width, experts = w_router.shape
    bucket_count = bias_table.shape[0]
    heads = width // col
    groups = lax.axis_size("expert")
    me_head, me_expert = lax.axis_index("head"), lax.axis_index("expert")
    capacity = max(2, (4 * tok + 3 * experts - 1) // (3 * experts))
    slots = -(-(capacity + 1) // 8) * 8
    total = experts * slots
    valid_total = 3 * tok * groups // 4
    scale = head_size ** (-0.5)
    joined = few_experts()
    small_rows = 6 * experts + 32
    chunk = -(-small_rows // (16 * groups)) * 16
    w_in, w_out = w_in[0], w_out[0]
    wq, wk, wv = w_query.T, w_key.T, w_value.T
    routes_row = routes.T
    router_rows = w_router.T
    scalars = jnp.stack([lengths[0], me_head.astype(jnp.int32), me_expert.astype(jnp.int32)])
    buckets_row = buckets[None]

    space = jnp.zeros((64,), bf16)
    gains = jnp.concatenate([gain_attn, space, gain_ffn, space, jnp.zeros((1536,), bf16)]).reshape(16, 128)
    packed = lax.all_gather(jnp.concatenate([inputs.T, out_grad.T, gains], axis=0), "head")
    if joined:
        all_in = lax.all_gather(inputs.T, ("expert", "head")).reshape(groups, heads, col, tok)
    qkv, weights, attended, branch = call(
        functools.partial(attend_kernel, scale),
        [
            ((3, col, tok), bf16, 1), ((heads_here, tok, tok), f32, 1), ((col, tok), bf16, 1),
            ((heads, col, tok), bf16),
        ],
        scalars, packed, far(wq), far(wk), far(wv), far(w_output), far(buckets_row), far(bias_table.T),
    )

    branch = lax.all_to_all(branch, "head", split_axis=0, concat_axis=0, tiled=True)
    residual, low, side, send = call(
        functools.partial(route_kernel, capacity),
        [((col, tok), f32, 1), ((col, tok), bf16, 1), ((8, tok), f32, 1), ((experts, slots, 2 * col), bf16)],
        scalars, branch, far(inputs.T), far(out_grad.T), far(routes_row),
    )
    quarter = lax.all_to_all(send, "expert", split_axis=0, concat_axis=0, tiled=True)
    quarters = lax.all_gather(quarter.reshape(total, 2 * col), "head")

    back, part, hidden, before_grad, back_rows, rows = call(
        functools.partial(expert_kernel, capacity),
        [((experts * heads, folded_rows(slots), 128), bf16), ((heads, total * 3 // 2, 128), bf16, 1)]
        + [((total, width), bf16, 1)] * 4,
        scalars, quarters, far(packed), far(w_in), far(w_out), far(router_rows),
    )
    came = lax.all_to_all(back, ("expert", "head"), split_axis=0, concat_axis=0, tiled=True)
    grad_own, gate_grad, stats = call(
        functools.partial(collect_kernel, slots),
        [((2 * col, tok), bf16), ((8, tok), f32, 1), ((experts, 128), f32, 1)],
        came, far(side), far(low),
    )
    expert_grad = lax.all_gather(grad_own, "head")

    late, first, residual_grad_own, gate, *shares = call(
        functools.partial(backward_kernel, scale, valid_total),
        [
            ((3 * col, tok), bf16, 1), ((heads, col + 16 + total * 3 // 2, 128), bf16), ((col, tok), f32, 1),
            ((8, tok), f32, 1),
        ]
        + (
            [((groups, chunk + 6 * col // groups, 128), bf16)]
            if joined
            else [((small_rows, 128), f32, 1), ((col, width), f32, 1)]
        ),
        scalars, far(packed), expert_grad, far(gate_grad), far(stats), far(routes_row),
        far(router_rows), far(w_output), far(weights), far(qkv), far(wq), far(wk), far(wv), far(attended),
        far(part),
    )

    if joined:
        late_all = lax.all_gather(late, "expert")

    if joined:
        shares = [lax.all_to_all(shares[0], "expert", split_axis=0, concat_axis=0, tiled=True)]
    first = lax.all_to_all(first, "head", split_axis=0, concat_axis=0, tiled=True)
    ret, gain_one_part, input_grad = call(
        first_kernel,
        [
            ((experts, 2 * slots + (16 + shares[0].shape[1] if joined else 0), 128), bf16),
            ((16, 128), f32, 1), ((col, tok), f32, 1),
        ],
        scalars, first, far(packed), far(residual_grad_own), *(shares if joined else []),
    )
    ret = lax.all_to_all(ret, "expert", split_axis=0, concat_axis=0, tiled=True)
    in_weight_grad, out_weight_grad = call(
        weights_kernel, [((width, width), f32, 1)] * 2, far(rows), far(hidden), far(before_grad), far(back_rows)
    )
    if joined:
        normed_all = call(turn_kernel, [((groups * tok, width), bf16, 1)], far(all_in), far(packed))[0]
        q_grad, k_grad, v_grad, output_grad, block_out, router_grad, table_grad, gain_grads, aux_loss = call(
            functools.partial(products_kernel, slots),
            [((col, width), f32, 1)] * 4
            + [((col, tok), bf16), ((experts, width), f32), ((heads_here, bucket_count), f32)]
            + [((16, 256), f32), ((1, 1), f32)],
            far(late_all), far(normed_all), ret, far(buckets_row), far(stats), far(side), far(gate), far(residual),
        )
    else:
        block_out = call(
            functools.partial(last_kernel, slots), [((col, tok), bf16)], ret, far(side), far(gate), far(residual)
        )[0]
        gain = packed[:, 2 * col : 2 * col + 2].reshape(heads, 256)[:, :col].reshape(width, 1)
        x = packed[:, :col].reshape(width, tok).astype(f32)
        normed = (x * token_scale(x) * gain.astype(f32)).astype(bf16)
        products = [mm(late[i * col : (i + 1) * col], normed, nt) for i in range(3)]
        q_grad, k_grad, v_grad, sums, gain_one, output_grad = lax.psum(
            products + [shares[0], gain_one_part, shares[1]], "expert"
        )
        router_grad = unfold_lanes(sums[32 : 32 + 6 * experts], 6)
        offsets = unfold_lanes(sums[16:32], 2)[:heads_here, : 2 * tok - 1]
        hot = (buckets[None, :] == jnp.arange(bucket_count)[:, None]).astype(f32)
        table_grad = mm(offsets, hot, nt, highest)
        gain_grads = jnp.concatenate([unfold_lanes(sums[:16], 2), unfold_lanes(gain_one, 2)], axis=0)
        probs = gain_grads[1, :experts] + gain_grads[2, :experts]
        aux_loss = experts * jnp.sum(stats[:, 0] * probs) / (valid_total * valid_total)
    return (
        block_out.T,
        input_grad.T,
        aux_loss.reshape(()),
        gain_grads[8, :col],
        q_grad.T,
        k_grad.T,
        v_grad.T,
        output_grad,
        table_grad.T,
        gain_grads[0, :col],
        router_grad.T,
        in_weight_grad[None],
        out_weight_grad[None],
    )


def solution(mesh):
    return jax.shard_map(
        shards,
        mesh=mesh,
        in_specs=(
            P("expert", "head"),
            P("expert", "head"),
            P("expert"),
            P("expert", None),
            P(),
            P("head"),
            P(None, "head"),
            P(None, "head"),
            P(None, "head"),
            P("head", None),
            P(None, "head"),
            P("head"),
            P(),
            P("expert", None, "head"),
            P("expert", "head", None),
        ),
        out_specs=(
            P("expert", "head"),
            P("expert", "head"),
            P(),
            P("head"),
            P(None, "head"),
            P(None, "head"),
            P(None, "head"),
            P("head", None),
            P(None, "head"),
            P("head"),
            P(),
            P("expert", None, "head"),
            P("expert", "head", None),
        ),
        check_vma=False,
    )
```

```python
import functools

import jax
import jax.numpy as jnp
from jax import lax
from jax.experimental import pallas as pl
from jax.experimental.pallas import tpu as pltpu
from jax.sharding import PartitionSpec as P

eps = 1e-06
aux_weight = 0.01
f32 = jnp.float32
bf16 = jnp.bfloat16
gelu_scale = 0.7978845608028654
gelu_cube = 0.044715
highest = lax.Precision.HIGHEST
nt = ((1,), (1,))
tn = ((0,), (0,))


def mm(left, right, dims=((1,), (0,)), precision=None):
    return lax.dot_general(left, right, (dims, ((), ())), precision=precision, preferred_element_type=f32)


def call(body, outs, *args):
    scalar_memory = pl.BlockSpec(memory_space=pltpu.SMEM)
    in_specs = [scalar_memory if a.dtype == jnp.int32 and a.ndim == 1 else pl.BlockSpec() for a in args]
    shapes = []
    for shape, kind, *remote in outs:
        shapes.append(pltpu.HBM(shape, kind) if remote else jax.ShapeDtypeStruct(shape, kind))
    return pl.pallas_call(
        body,
        out_shape=shapes,
        in_specs=in_specs,
        compiler_params=pltpu.CompilerParams(vmem_limit_bytes=40 * 1024 * 1024),
    )(*args)


def far(array):
    return pltpu.with_memory_space_constraint(array, pltpu.HBM)


def tall(ref, first, rows):
    return jnp.concatenate([ref[i, first : first + rows, :].astype(f32) for i in range(ref.shape[0])], axis=0)


def gain_columns(block):
    turned = jnp.transpose(block.astype(f32))
    return [jnp.concatenate([turned[:, i : i + 1], turned[:64, i + 1 : i + 2]], axis=0) for i in (0, 2)]


def all_gains(packed):
    first = 2 * packed.shape[2] * 3 // 2
    pairs = [gain_columns(packed[i, first : first + 16, :]) for i in range(packed.shape[0])]
    return [jnp.concatenate([pair[i] for pair in pairs], axis=0) for i in range(2)]


def token_scale(values):
    return lax.rsqrt(jnp.sum(values * values, axis=0, keepdims=True) * (1.0 / values.shape[0]) + eps)


def lanes(shape):
    return lax.broadcasted_iota(jnp.int32, shape, len(shape) - 1)


def sublanes(shape):
    return lax.broadcasted_iota(jnp.int32, shape, len(shape) - 2)


def side_lanes(rows, width, columns):
    spot = lanes((rows, width))
    out = jnp.zeros((rows, width), f32)
    for i, column in enumerate(columns):
        out = jnp.where(spot == i, column, out)
    return out


def side_rows(rows, width, lines):
    spot = sublanes((rows, width))
    out = jnp.zeros((rows, width), f32)
    for i, line in enumerate(lines):
        out = jnp.where(spot == i, line, out)
    return out


def high_low(values, count=2):
    pieces = []
    for _ in range(count):
        piece = values.astype(bf16).astype(f32)
        pieces.append(piece)
        values = values - piece
    return pieces


def softmax(values, axis):
    raised = jnp.exp(values - jnp.max(values, axis=axis, keepdims=True))
    return raised / jnp.sum(raised, axis=axis, keepdims=True)


def gelu_parts(u):
    t = jnp.tanh(gelu_scale * (u + gelu_cube * u * u * u))
    value = 0.5 * u * (1.0 + t)
    slope = 0.5 * (1.0 + t) + 0.5 * u * (1.0 - t * t) * gelu_scale * (1.0 + 3.0 * gelu_cube * u * u)
    return value, slope


def fold_lanes(rows):
    return jnp.concatenate([rows[:, i : i + 128] for i in range(0, rows.shape[1], 128)], axis=0)


def unfold_lanes(rows, pieces):
    size = rows.shape[0] // pieces
    return jnp.concatenate([rows[i * size : (i + 1) * size] for i in range(pieces)], axis=1)


def fold_rest(rest, side):
    groups = [rest[i : i + 8] for i in range(0, rest.shape[0], 8)]
    count = side.shape[1]
    spot = lanes((8, 64))
    last = jnp.zeros((8, 64), f32)
    for g in range(len(groups)):
        for j in range(count):
            last = jnp.where(spot == g * count + j, side[8 * g : 8 * g + 8, j : j + 1], last)
    groups.append(last)
    if len(groups) % 2:
        groups.append(jnp.zeros((8, 64), f32))
    return [jnp.concatenate(groups[i : i + 2], axis=1) for i in range(0, len(groups), 2)]


def unfold_rest(blocks, slots, count):
    halves = []
    for i in range(0, blocks.shape[0], 8):
        halves += [blocks[i : i + 8, :64], blocks[i : i + 8, 64:]]
    number = slots // 8
    side = [halves[number][:, g * count : (g + 1) * count] for g in range(number)]
    return jnp.concatenate(halves[:number], axis=0), jnp.concatenate(side, axis=0)


def folded_rows(slots):
    return slots + 8 * ((slots // 8 + 2) // 2)


def pick_slots(spots, count):
    return sublanes((count, spots.shape[1])) == spots


def attend_kernel(
    scale, scalars, packed, wq, wk, wv, w_output, buckets, table, qkv_ref, weights_ref, attended_ref, branch_ref
):
    heads, tok, _ = weights_ref.shape
    col = wq.shape[0]
    size = col // heads
    x = tall(packed, 0, col)
    normed = (x * token_scale(x) * all_gains(packed)[0]).astype(bf16)
    projected = []
    for i, w in enumerate((wq, wk, wv)):
        rows = mm(w[...], normed).astype(bf16)
        qkv_ref[i] = rows
        projected.append(rows)
    query, key, value = projected
    hot = (sublanes((table.shape[1], 2 * tok - 1)) == buckets[...]).astype(f32)
    offsets = mm(table[...], hot, precision=highest)
    offsets = jnp.concatenate([offsets, jnp.zeros((heads, 1), f32)], axis=1)
    open_keys = lanes((tok, tok)) < scalars[0]
    outs = []
    for h in range(heads):
        at = slice(h * size, (h + 1) * size)
        spread = jnp.broadcast_to(offsets[h : h + 1, :], (tok, 2 * tok))
        bias = pltpu.roll(spread, tok + 1, 1, stride=1, stride_axis=0)[:, :tok]
        scores = mm(query[at], key[at], tn) * scale + bias
        weights = softmax(jnp.where(open_keys, scores, -1000000000.0), 1)
        weights_ref[h] = weights
        outs.append(mm(value[at], weights.astype(bf16), nt))
    attended = jnp.concatenate(outs, axis=0).astype(bf16)
    attended_ref[...] = attended
    branch = mm(w_output[...], attended, tn)
    for i in range(branch_ref.shape[0]):
        branch_ref[i] = branch[i * col : (i + 1) * col].astype(bf16)


def second_norm(residual, gain, w_router):
    scale = token_scale(residual)
    unit = residual * scale
    normed = (unit * gain).astype(bf16)
    return scale, unit, normed, softmax(mm(w_router, normed), 0)


def route_kernel(capacity, scalars, came, inputs, out_grad, routes, residual_ref, low_ref, side_ref, send_ref):
    col, tok = inputs.shape
    experts, slots, _ = send_ref.shape
    residual = inputs[...].astype(f32)
    for i in range(came.shape[0]):
        residual = residual + came[i].astype(f32)
    residual_ref[...] = residual
    low = residual.astype(bf16)
    low_ref[...] = low
    route_hot = (sublanes((experts, tok)) == routes[...]).astype(f32)
    before = (sublanes((tok, tok)) < lanes((tok, tok))).astype(bf16)
    slot = jnp.sum(mm(route_hot.astype(bf16), before) * route_hot, axis=0, keepdims=True)
    spots = routes[...].astype(f32) * slots + slot
    side_ref[...] = side_rows(8, tok, [spots])
    valid = (lanes((1, tok)) < scalars[0]).astype(f32)
    counts = jnp.sum(route_hot * valid, axis=1, keepdims=True)
    pick = pick_slots(spots.astype(jnp.int32), experts * slots).astype(bf16)
    rows = mm(pick, jnp.concatenate([low, out_grad[...]], axis=0), nt)
    spare = (sublanes((slots, 2 * col)) == capacity) & (lanes((slots, 2 * col)) == col)
    for e in range(experts):
        block = rows[e * slots : (e + 1) * slots]
        send_ref[e] = jnp.where(spare, counts[e : e + 1], block).astype(bf16)


def gain_row(packed, first, line):
    pieces = []
    for i in range(packed.shape[0]):
        block = packed[i, first : first + 16, :].astype(f32)
        pieces += [block[line : line + 1, :], block[line + 1 : line + 2, :64]]
    return jnp.concatenate(pieces, axis=1)


def expert_kernel(
    capacity, scalars, quarters, packed, w_in, w_out, w_router,
    back_ref, part_ref, hidden_ref, before_ref, grads_ref, rows_ref,
):
    total = rows_ref.shape[0]
    experts, width = w_router.shape
    heads = part_ref.shape[0]
    col = width // heads
    slots = total // experts
    half = total // 2
    parts = [quarters[i].astype(f32) for i in range(heads)]
    residual = jnp.concatenate([block[:, :col] for block in parts], axis=1)
    grads = jnp.concatenate([block[:, col:] for block in parts], axis=1)
    inverse = lax.rsqrt(jnp.sum(residual * residual, axis=1, keepdims=True) * (1.0 / width) + eps)
    rows = (residual * inverse * gain_row(packed, 2 * col, 2)).astype(bf16)
    rows_ref[...] = rows
    hidden, slope = gelu_parts(mm(rows, w_in[...]))
    hidden = hidden.astype(bf16)
    hidden_ref[...] = hidden
    produced = mm(hidden, w_out[...])
    for i in range(heads):
        mine = produced[:, i * col : (i + 1) * col]
        rest = mine[:, 128:]
        part_ref[i] = jnp.concatenate(
            [mine[:, :128], jnp.concatenate([rest[:half], rest[half:]], axis=1)], axis=0
        ).astype(bf16)
    probs = softmax(mm(rows, w_router[...], nt), 1)
    gate = jnp.sum(jnp.where(lanes((total, experts)) == scalars[2], probs, 0.0), axis=1, keepdims=True)
    back = (gate * grads).astype(bf16)
    grads_ref[...] = back
    before = (mm(back, w_out[...], nt) * slope).astype(bf16)
    before_ref[...] = before
    rows_grad = mm(before, w_in[...], nt)
    gate_grad = jnp.sum(grads * produced, axis=1, keepdims=True)
    stats = jnp.zeros((1, 128), f32)
    for b in range(experts):
        stats = stats + grads[b * slots + capacity : b * slots + capacity + 1, :128]
    side = side_lanes(total, 4, high_low(gate_grad) + high_low(stats[:, 0:1]))
    for b in range(experts):
        at = slice(b * slots, (b + 1) * slots)
        for i in range(heads):
            mine = rows_grad[at, i * col : (i + 1) * col]
            back_ref[b * heads + i] = jnp.concatenate(
                [mine[:, :128]] + fold_rest(mine[:, 128:], side[at]), axis=0
            ).astype(bf16)


def weights_kernel(rows_ref, hidden, before, grads, in_ref, out_ref):
    in_ref[...] = mm(rows_ref[...], before[...], tn)
    out_ref[...] = mm(hidden[...], grads[...], tn)


def collect_kernel(slots, came, side, low, grad_ref, gate_ref, stats_ref):
    col, tok = low.shape
    experts = stats_ref.shape[0]
    heads = came.shape[0] // experts
    tops, rests, scalars = [], [], []
    for e in range(experts):
        total = came[e * heads].astype(f32)
        for i in range(1, heads):
            total = total + came[e * heads + i].astype(f32)
        rest, columns = unfold_rest(total[slots:], slots, 4)
        tops.append(total[:slots])
        rests.append(rest)
        scalars.append(columns)
    counts = jnp.concatenate([columns[0:1] for columns in scalars], axis=0) * (1.0 / heads)
    pick = pick_slots(side[0:1, :].astype(jnp.int32), experts * slots)
    for first, pieces in ((0, tops), (128, rests)):
        block = jnp.concatenate(pieces, axis=0).astype(bf16)
        grad_ref[first : min(first + 128, col), :] = mm(block, pick.astype(bf16), tn).astype(bf16)
    grad_ref[col:, :] = low[...]
    gate = mm(jnp.concatenate(scalars, axis=0), pick.astype(f32), tn, highest)
    gate_ref[...] = jnp.broadcast_to(gate[0:1] + gate[1:2], gate_ref.shape)
    stats_ref[...] = side_lanes(experts, 128, [counts[:, 2:3] + counts[:, 3:4]])


def backward_kernel(
    scale, valid_total, scalars, packed, expert_grad, gate_grad, stats, routes, w_router, w_output, weights_ref,
    qkv, wq, wk, wv, attended, part, late_ref, first_ref, own_ref, gate_ref, *share_refs,
):
    tok = routes.shape[1]
    heads_here = weights_ref.shape[0]
    blocks, col = packed.shape[0], wq.shape[0]
    experts, width = w_router.shape
    size = col // heads_here
    gain_one, gain_two = all_gains(packed)
    residual = tall(expert_grad, col, col)
    scale_two, unit, normed, router = second_norm(residual, gain_two, w_router[...])
    valid = (lanes((1, tok)) < scalars[0]).astype(f32)
    route_hot = (sublanes((experts, tok)) == routes[...]).astype(f32)
    fraction = stats[:, 0:1] * (aux_weight * experts / (valid_total * valid_total))
    gate = jnp.sum(router * route_hot, axis=0, keepdims=True)
    gate_ref[...] = jnp.broadcast_to(gate, gate_ref.shape)
    prob_grad = route_hot * gate_grad[0:1, :] + fraction * valid
    logit_grad = router * (prob_grad - jnp.sum(router * prob_grad, axis=0, keepdims=True))
    logit_grad = logit_grad.astype(bf16)
    normed_grad = mm(w_router[...], logit_grad, tn) + tall(expert_grad, 0, col)
    unit_grad = normed_grad * gain_two
    mean = jnp.sum(unit_grad * unit, axis=0, keepdims=True) * (1.0 / width)
    residual_grad = tall(packed, col, col) + scale_two * (unit_grad - unit * mean)
    branch = residual_grad.astype(bf16)
    attended_grad = mm(w_output[...], branch).astype(bf16)
    flip = (lanes((tok, tok)) + sublanes((tok, tok)) == tok - 1).astype(bf16)
    query, key, value = qkv[0], qkv[1], qkv[2]
    grads = [[], [], []]
    offsets = []
    for h in range(heads_here):
        at = slice(h * size, (h + 1) * size)
        out = attended_grad[at]
        weights = weights_ref[h]
        mass = mm(out, value[at], tn)
        score = weights * (mass - jnp.sum(weights * mass, axis=1, keepdims=True))
        score = score.astype(bf16)
        grads[0].append(mm(key[at], score, nt) * scale)
        grads[1].append(mm(query[at], score) * scale)
        grads[2].append(mm(out, weights.astype(bf16)))
        flipped = jnp.concatenate([mm(flip, score), jnp.zeros((tok, tok), f32)], axis=1)
        rolled = pltpu.roll(flipped, 0, 1, stride=1, stride_axis=0)
        offsets.append(jnp.sum(rolled, axis=0, keepdims=True))
    first = jnp.zeros((width, tok), f32)
    row = jnp.zeros((1, tok), f32)
    for i, w in enumerate((wq, wk, wv)):
        low = jnp.concatenate(grads[i], axis=0).astype(bf16)
        late_ref[i * col : (i + 1) * col, :] = low
        first = first + mm(w[...], low, tn)
        row = row + jnp.sum(low.astype(f32) * qkv[i].astype(f32), axis=0, keepdims=True)
    side = side_rows(16, tok, high_low(row))
    for i in range(blocks):
        at = slice(i * col, (i + 1) * col)
        first_ref[i, : col + 16, :] = jnp.concatenate([first[at], side], axis=0).astype(bf16)
        first_ref[i, col + 16 :, :] = part[i]

    product = mm(attended[...], branch, nt)
    gain_two_grad = jnp.sum(normed_grad * unit, axis=1, keepdims=True)
    gains = jnp.zeros((col, 1), f32)
    own = jnp.zeros((col, tok), f32)
    for i in range(blocks):
        at = slice(i * col, (i + 1) * col)
        gains = jnp.where(scalars[1] == i, gain_two_grad[at], gains)
        own = jnp.where(scalars[1] == i, residual_grad[at], own)
    own_ref[...] = own
    probs = jnp.sum(router * valid, axis=1, keepdims=True)
    if experts < col:
        probs = jnp.concatenate([probs, jnp.zeros((col - experts, 1), f32)], axis=0)
    gains = jnp.transpose(side_lanes(col, 128, [gains] + high_low(probs)))[0:8]
    router_grad = mm(logit_grad, normed, nt)
    offsets = jnp.concatenate(offsets, axis=0)
    offsets = jnp.concatenate([offsets, jnp.zeros((8 - heads_here, 2 * tok), f32)], axis=0)
    gains = jnp.concatenate([gains, jnp.zeros((8, 64), f32)], axis=1)
    pieces = [fold_lanes(gains), fold_lanes(offsets), fold_lanes(router_grad)]
    if len(share_refs) == 2:
        share_refs[0][...] = jnp.concatenate(pieces, axis=0)
        share_refs[1][...] = product
    else:
        share_ref = share_refs[0]
        groups = share_ref.shape[0]
        size = col // groups
        chunk = share_ref.shape[1] - 6 * size
        small = jnp.concatenate(pieces + [jnp.zeros((groups * chunk - 6 * experts - 32, 128), f32)], axis=0)
        for b in range(groups):
            share_ref[b] = jnp.concatenate(
                [small[b * chunk : (b + 1) * chunk], fold_lanes(product[b * size : (b + 1) * size])], axis=0
            ).astype(bf16)


def first_kernel(scalars, came, packed, own, *refs):
    shares, (ret_ref, gain_ref, input_ref) = refs[:-3], refs[-3:]
    col, tok = own.shape
    heads = came.shape[0]
    experts = ret_ref.shape[0]
    total = came[0].astype(f32)
    for i in range(1, heads):
        total = total + came[i].astype(f32)
    mean = (total[col : col + 1] + total[col + 1 : col + 2]) * (1.0 / (heads * col))
    scale = token_scale(tall(packed, 0, col))
    mine = packed[scalars[1]].astype(f32)
    unit = mine[:col] * scale
    gain = gain_columns(mine[2 * col : 2 * col + 16])[0]
    input_ref[...] = own[...] + scale * (total[:col] * gain - unit * mean)
    gain_grad = jnp.sum(total[:col] * unit, axis=1, keepdims=True)
    gain_grad = jnp.transpose(side_lanes(col, 128, [gain_grad]))[0:8]
    gain_grad = fold_lanes(jnp.concatenate([gain_grad, jnp.zeros((8, 64), f32)], axis=1))
    gain_ref[...] = gain_grad
    produced = total[col + 16 :]
    count = produced.shape[0] * 2 // 3
    top = produced[:count]
    rest = jnp.concatenate([produced[count:, :64], produced[count:, 64:]], axis=0)
    rest = jnp.concatenate([rest, jnp.zeros((count, 64), f32)], axis=1)
    slots = count // experts
    joined = []
    if shares:
        share = shares[0][0].astype(f32)
        for e in range(1, experts):
            share = share + shares[0][e].astype(f32)
        joined = [gain_grad, share]
    for e in range(experts):
        at = slice(e * slots, (e + 1) * slots)
        ret_ref[e] = jnp.concatenate([top[at], rest[at]] + joined, axis=0).astype(bf16)


def add_returned(slots, blocks, side, gate, residual):
    col = residual.shape[0]
    top = jnp.concatenate([block[:slots] for block in blocks], axis=0).astype(bf16)
    rest = jnp.concatenate([block[slots : 2 * slots] for block in blocks], axis=0).astype(bf16)
    pick = pick_slots(side[0:1, :].astype(jnp.int32), len(blocks) * slots).astype(bf16)
    returned = jnp.concatenate([mm(top, pick, tn), mm(rest, pick, tn)[: col - 128]], axis=0)
    return (residual[...] + gate[0:1, :] * returned).astype(bf16)


def last_kernel(slots, came, side, gate, residual, block_ref):
    blocks = [came[e].astype(f32) for e in range(came.shape[0])]
    block_ref[...] = add_returned(slots, blocks, side, gate, residual)


def turn_kernel(scalars, all_in, packed, normed_ref):
    groups, heads, col, tok = all_in.shape
    gain = all_gains(packed)[0]
    for b in range(groups):
        x = jnp.concatenate([all_in[b, i].astype(f32) for i in range(heads)], axis=0)
        spot = pl.multiple_of((b ^ (scalars[2] & 1)) * tok, tok)
        normed_ref[pl.ds(spot, tok), :] = jnp.transpose(x * token_scale(x) * gain).astype(bf16)


def products_kernel(
    slots, late, normed, came, buckets, stats, side, gate, residual,
    q_ref, k_ref, v_ref, out_ref, block_ref, router_ref, table_ref, gains_ref, aux_ref,
):
    groups = came.shape[0]
    col = q_ref.shape[0]
    experts = router_ref.shape[0]
    size = col // groups
    blocks = [came[b].astype(f32) for b in range(groups)]
    block_ref[...] = add_returned(slots, blocks, side, gate, residual)
    gain_one = blocks[0][2 * slots : 2 * slots + 16]
    for block in blocks[1:]:
        gain_one = gain_one + block[2 * slots : 2 * slots + 16]
    shares = [block[2 * slots + 16 :] for block in blocks]
    chunk = shares[0].shape[0] - 6 * size
    for b in range(groups):
        out_ref[b * size : (b + 1) * size, :] = unfold_lanes(shares[b][chunk:], 6)
    joined = jnp.concatenate([late[b] for b in range(groups)], axis=1)
    product = mm(joined, normed[...])
    for i, ref in enumerate((q_ref, k_ref, v_ref)):
        ref[...] = product[i * col : (i + 1) * col]
    small = jnp.concatenate([share[:chunk] for share in shares], axis=0)
    gains = unfold_lanes(small[:16], 2)
    gains_ref[0:8, :] = gains
    gains_ref[8:16, :] = unfold_lanes(gain_one, 2)
    probs = gains[1:2, :experts] + gains[2:3, :experts]
    same = lanes((experts, experts)) == sublanes((experts, experts))
    share = jnp.sum(jnp.where(same, stats[:, 0:1] * probs, 0.0), axis=0, keepdims=True)
    valid_total = 3 * normed.shape[0] // 4
    aux_ref[...] = jnp.sum(share, axis=1, keepdims=True) * (experts / (valid_total * valid_total))
    span = buckets.shape[1]
    hot = (sublanes((table_ref.shape[1], span)) == buckets[...]).astype(f32)
    offsets = unfold_lanes(small[16:32], 2)[:, :span]
    table_ref[...] = mm(offsets, hot, nt, highest)[: table_ref.shape[0]]
    router_ref[...] = unfold_lanes(small[32 : 32 + 6 * experts], 6)


def few_experts():
    return lax.axis_size("expert") <= 8


def shards(
    inputs,
    out_grad,
    lengths,
    routes,
    buckets,
    gain_attn,
    w_query,
    w_key,
    w_value,
    w_output,
    bias_table,
    gain_ffn,
    w_router,
    w_in,
    w_out,
):
    tok, col = inputs.shape
    heads_here = bias_table.shape[1]
    head_size = w_query.shape[1] // heads_here
    width, experts = w_router.shape
    bucket_count = bias_table.shape[0]
    heads = width // col
    groups = lax.axis_size("expert")
    me_head, me_expert = lax.axis_index("head"), lax.axis_index("expert")
    capacity = max(2, (4 * tok + 3 * experts - 1) // (3 * experts))
    slots = -(-(capacity + 1) // 8) * 8
    total = experts * slots
    valid_total = 3 * tok * groups // 4
    scale = head_size ** (-0.5)
    joined = few_experts()
    small_rows = 6 * experts + 32
    chunk = -(-small_rows // (16 * groups)) * 16
    w_in, w_out = w_in[0], w_out[0]
    wq, wk, wv = w_query.T, w_key.T, w_value.T
    routes_row = routes.T
    router_rows = w_router.T
    scalars = jnp.stack([lengths[0], me_head.astype(jnp.int32), me_expert.astype(jnp.int32)])
    buckets_row = buckets[None]

    space = jnp.zeros((64,), bf16)
    gains = jnp.concatenate([gain_attn, space, gain_ffn, space, jnp.zeros((1536,), bf16)]).reshape(16, 128)
    packed = lax.all_gather(jnp.concatenate([inputs.T, out_grad.T, gains], axis=0), "head")
    if joined:
        all_in = lax.all_gather(inputs.T, ("expert", "head")).reshape(groups, heads, col, tok)
    qkv, weights, attended, branch = call(
        functools.partial(attend_kernel, scale),
        [
            ((3, col, tok), bf16, 1), ((heads_here, tok, tok), f32, 1), ((col, tok), bf16, 1),
            ((heads, col, tok), bf16),
        ],
        scalars, packed, far(wq), far(wk), far(wv), far(w_output), far(buckets_row), far(bias_table.T),
    )

    branch = lax.all_to_all(branch, "head", split_axis=0, concat_axis=0, tiled=True)
    residual, low, side, send = call(
        functools.partial(route_kernel, capacity),
        [((col, tok), f32, 1), ((col, tok), bf16, 1), ((8, tok), f32, 1), ((experts, slots, 2 * col), bf16)],
        scalars, branch, far(inputs.T), far(out_grad.T), far(routes_row),
    )
    quarter = lax.all_to_all(send, "expert", split_axis=0, concat_axis=0, tiled=True)
    quarters = lax.all_gather(quarter.reshape(total, 2 * col), "head")

    back, part, hidden, before_grad, back_rows, rows = call(
        functools.partial(expert_kernel, capacity),
        [((experts * heads, folded_rows(slots), 128), bf16), ((heads, total * 3 // 2, 128), bf16, 1)]
        + [((total, width), bf16, 1)] * 4,
        scalars, quarters, far(packed), far(w_in), far(w_out), far(router_rows),
    )
    came = lax.all_to_all(back, ("expert", "head"), split_axis=0, concat_axis=0, tiled=True)
    grad_own, gate_grad, stats = call(
        functools.partial(collect_kernel, slots),
        [((2 * col, tok), bf16), ((8, tok), f32, 1), ((experts, 128), f32, 1)],
        came, far(side), far(low),
    )
    expert_grad = lax.all_gather(grad_own, "head")

    late, first, residual_grad_own, gate, *shares = call(
        functools.partial(backward_kernel, scale, valid_total),
        [
            ((3 * col, tok), bf16, 1), ((heads, col + 16 + total * 3 // 2, 128), bf16), ((col, tok), f32, 1),
            ((8, tok), f32, 1),
        ]
        + (
            [((groups, chunk + 6 * col // groups, 128), bf16)]
            if joined
            else [((small_rows, 128), f32, 1), ((col, width), f32, 1)]
        ),
        scalars, far(packed), expert_grad, far(gate_grad), far(stats), far(routes_row),
        far(router_rows), far(w_output), far(weights), far(qkv), far(wq), far(wk), far(wv), far(attended),
        far(part),
    )

    if joined:
        pair = lax.ppermute(late, "expert", [(i, i ^ 1) for i in range(groups)])
        late = jnp.stack([late, pair])
        lines = [[i for i in range(groups) if i % 2 == x] for x in range(2)]
        late_all = lax.all_gather(late, "expert", axis_index_groups=lines).reshape(groups, 3 * col, tok)

    in_weight_grad, out_weight_grad = call(
        weights_kernel, [((width, width), f32, 1)] * 2, far(rows), far(hidden), far(before_grad), far(back_rows)
    )

    if joined:
        shares = [lax.all_to_all(shares[0], "expert", split_axis=0, concat_axis=0, tiled=True)]
    first, late, in_weight_grad, out_weight_grad = lax.optimization_barrier(
        (first, late, in_weight_grad, out_weight_grad)
    )
    first = lax.all_to_all(first, "head", split_axis=0, concat_axis=0, tiled=True)
    ret, gain_one_part, input_grad = call(
        first_kernel,
        [
            ((experts, 2 * slots + (16 + shares[0].shape[1] if joined else 0), 128), bf16),
            ((16, 128), f32, 1), ((col, tok), f32, 1),
        ],
        scalars, first, far(packed), far(residual_grad_own), *(shares if joined else []),
    )
    ret = lax.all_to_all(ret, "expert", split_axis=0, concat_axis=0, tiled=True)
    if joined:
        normed_all = call(turn_kernel, [((groups * tok, width), bf16, 1)], scalars, far(all_in), far(packed))[0]
        q_grad, k_grad, v_grad, output_grad, block_out, router_grad, table_grad, gain_grads, aux_loss = call(
            functools.partial(products_kernel, slots),
            [((col, width), f32, 1)] * 4
            + [((col, tok), bf16), ((experts, width), f32), ((heads_here, bucket_count), f32)]
            + [((16, 256), f32), ((1, 1), f32)],
            far(late_all), far(normed_all), ret, far(buckets_row), far(stats), far(side), far(gate), far(residual),
        )
    else:
        block_out = call(
            functools.partial(last_kernel, slots), [((col, tok), bf16)], ret, far(side), far(gate), far(residual)
        )[0]
        gain = packed[:, 2 * col : 2 * col + 2].reshape(heads, 256)[:, :col].reshape(width, 1)
        x = packed[:, :col].reshape(width, tok).astype(f32)
        normed = (x * token_scale(x) * gain.astype(f32)).astype(bf16)
        products = [mm(late[i * col : (i + 1) * col], normed, nt) for i in range(3)]
        q_grad, k_grad, v_grad, sums, gain_one, output_grad = lax.psum(
            products + [shares[0], gain_one_part, shares[1]], "expert"
        )
        router_grad = unfold_lanes(sums[32 : 32 + 6 * experts], 6)
        offsets = unfold_lanes(sums[16:32], 2)[:heads_here, : 2 * tok - 1]
        hot = (buckets[None, :] == jnp.arange(bucket_count)[:, None]).astype(f32)
        table_grad = mm(offsets, hot, nt, highest)
        gain_grads = jnp.concatenate([unfold_lanes(sums[:16], 2), unfold_lanes(gain_one, 2)], axis=0)
        probs = gain_grads[1, :experts] + gain_grads[2, :experts]
        aux_loss = experts * jnp.sum(stats[:, 0] * probs) / (valid_total * valid_total)
    return (
        block_out.T,
        input_grad.T,
        aux_loss.reshape(()),
        gain_grads[8, :col],
        q_grad.T,
        k_grad.T,
        v_grad.T,
        output_grad,
        table_grad.T,
        gain_grads[0, :col],
        router_grad.T,
        in_weight_grad[None],
        out_weight_grad[None],
    )


def solution(mesh):
    return jax.shard_map(
        shards,
        mesh=mesh,
        in_specs=(
            P("expert", "head"),
            P("expert", "head"),
            P("expert"),
            P("expert", None),
            P(),
            P("head"),
            P(None, "head"),
            P(None, "head"),
            P(None, "head"),
            P("head", None),
            P(None, "head"),
            P("head"),
            P(),
            P("expert", None, "head"),
            P("expert", "head", None),
        ),
        out_specs=(
            P("expert", "head"),
            P("expert", "head"),
            P(),
            P("head"),
            P(None, "head"),
            P(None, "head"),
            P(None, "head"),
            P("head", None),
            P(None, "head"),
            P("head"),
            P(),
            P("expert", None, "head"),
            P("expert", "head", None),
        ),
        check_vma=False,
    )
```

```python
import functools

import jax
import jax.numpy as jnp
from jax import lax
from jax.experimental import pallas as pl
from jax.experimental.pallas import tpu as pltpu
from jax.sharding import PartitionSpec as P

eps = 1e-06
aux_weight = 0.01
f32 = jnp.float32
bf16 = jnp.bfloat16
gelu_scale = 0.7978845608028654
gelu_cube = 0.044715
highest = lax.Precision.HIGHEST
nt = ((1,), (1,))
tn = ((0,), (0,))


def mm(left, right, dims=((1,), (0,)), precision=None):
    return lax.dot_general(left, right, (dims, ((), ())), precision=precision, preferred_element_type=f32)


class Pieces:
    def __init__(self, refs):
        self.refs, self.size = refs, refs[0].shape[0]
        self.shape = (self.size * len(refs),) + tuple(refs[0].shape[1:])

    def __getitem__(self, index):
        if index is Ellipsis:
            return jnp.concatenate([ref[...] for ref in self.refs], axis=0)
        at, rest = (index[0], index[1:]) if isinstance(index, tuple) else (index, ())
        return self.refs[at // self.size][(at % self.size,) + rest]


class Split:
    def __init__(self, array, count):
        self.array, self.count = array, count


def block_of(array, count, i):
    shape = (array.shape[0] // count,) + array.shape[1:]
    return pl.BlockSpec(shape, lambda step: (i,) + (0,) * (array.ndim - 1))


def whole_map(rank):
    return lambda step: (0,) * rank


def call(body, outs, *args):
    in_specs, operands, counts = [], [], []
    for a in args:
        if isinstance(a, Split):
            held = far(a.array)
            in_specs += [block_of(held, a.count, i) for i in range(a.count)]
            operands += [held] * a.count
            counts.append(a.count)
            continue
        whole = a.dtype == jnp.int32 and a.ndim == 1
        in_specs.append(pl.BlockSpec(memory_space=pltpu.SMEM) if whole else pl.BlockSpec())
        operands.append(a)
        counts.append(0)
    shapes = []
    for shape, kind, *remote in outs:
        shapes.append(pltpu.HBM(shape, kind) if remote else jax.ShapeDtypeStruct(shape, kind))

    def run(*refs):
        ins, at = [], 0
        for count in counts:
            ins.append(Pieces(refs[at : at + count]) if count else refs[at])
            at += max(count, 1)
        body(*ins, *refs[at:])

    extra = {}
    if any(counts):
        extra["grid"] = (1,)
        extra["out_specs"] = [pl.BlockSpec(shape.shape, whole_map(len(shape.shape))) for shape in shapes]
        in_specs = [
            pl.BlockSpec(a.shape, whole_map(a.ndim)) if spec.block_shape is None and spec.memory_space is None else spec
            for spec, a in zip(in_specs, operands)
        ]
    return pl.pallas_call(
        run,
        out_shape=shapes,
        in_specs=in_specs,
        **extra,
        compiler_params=pltpu.CompilerParams(vmem_limit_bytes=40 * 1024 * 1024),
    )(*operands)


def far(array):
    return pltpu.with_memory_space_constraint(array, pltpu.HBM)


def tall(ref, first, rows):
    return jnp.concatenate([ref[i, first : first + rows, :].astype(f32) for i in range(ref.shape[0])], axis=0)


def gain_columns(block):
    turned = jnp.transpose(block.astype(f32))
    return [jnp.concatenate([turned[:, i : i + 1], turned[:64, i + 1 : i + 2]], axis=0) for i in (0, 2)]


def all_gains(packed):
    first = 2 * packed.shape[2] * 3 // 2
    pairs = [gain_columns(packed[i, first : first + 16, :]) for i in range(packed.shape[0])]
    return [jnp.concatenate([pair[i] for pair in pairs], axis=0) for i in range(2)]


def token_scale(values):
    return lax.rsqrt(jnp.sum(values * values, axis=0, keepdims=True) * (1.0 / values.shape[0]) + eps)


def lanes(shape):
    return lax.broadcasted_iota(jnp.int32, shape, len(shape) - 1)


def sublanes(shape):
    return lax.broadcasted_iota(jnp.int32, shape, len(shape) - 2)


def side_lanes(rows, width, columns):
    spot = lanes((rows, width))
    out = jnp.zeros((rows, width), f32)
    for i, column in enumerate(columns):
        out = jnp.where(spot == i, column, out)
    return out


def side_rows(rows, width, lines):
    spot = sublanes((rows, width))
    out = jnp.zeros((rows, width), f32)
    for i, line in enumerate(lines):
        out = jnp.where(spot == i, line, out)
    return out


def high_low(values, count=2):
    pieces = []
    for _ in range(count):
        piece = values.astype(bf16).astype(f32)
        pieces.append(piece)
        values = values - piece
    return pieces


def softmax(values, axis):
    raised = jnp.exp(values - jnp.max(values, axis=axis, keepdims=True))
    return raised / jnp.sum(raised, axis=axis, keepdims=True)


def gelu_parts(u):
    t = jnp.tanh(gelu_scale * (u + gelu_cube * u * u * u))
    value = 0.5 * u * (1.0 + t)
    slope = 0.5 * (1.0 + t) + 0.5 * u * (1.0 - t * t) * gelu_scale * (1.0 + 3.0 * gelu_cube * u * u)
    return value, slope


def fold_lanes(rows):
    return jnp.concatenate([rows[:, i : i + 128] for i in range(0, rows.shape[1], 128)], axis=0)


def unfold_lanes(rows, pieces):
    size = rows.shape[0] // pieces
    return jnp.concatenate([rows[i * size : (i + 1) * size] for i in range(pieces)], axis=1)


def fold_rest(rest, side):
    groups = [rest[i : i + 8] for i in range(0, rest.shape[0], 8)]
    count = side.shape[1]
    spot = lanes((8, 64))
    last = jnp.zeros((8, 64), f32)
    for g in range(len(groups)):
        for j in range(count):
            last = jnp.where(spot == g * count + j, side[8 * g : 8 * g + 8, j : j + 1], last)
    groups.append(last)
    if len(groups) % 2:
        groups.append(jnp.zeros((8, 64), f32))
    return [jnp.concatenate(groups[i : i + 2], axis=1) for i in range(0, len(groups), 2)]


def unfold_rest(blocks, slots, count):
    halves = []
    for i in range(0, blocks.shape[0], 8):
        halves += [blocks[i : i + 8, :64], blocks[i : i + 8, 64:]]
    number = slots // 8
    side = [halves[number][:, g * count : (g + 1) * count] for g in range(number)]
    return jnp.concatenate(halves[:number], axis=0), jnp.concatenate(side, axis=0)


def folded_rows(slots):
    return slots + 8 * ((slots // 8 + 2) // 2)


def pick_slots(spots, count):
    return sublanes((count, spots.shape[1])) == spots


def attend_kernel(
    scale, scalars, packed, wq, wk, wv, w_output, buckets, table, qkv_ref, weights_ref, attended_ref, branch_ref
):
    heads, tok, _ = weights_ref.shape
    col = wq.shape[0]
    size = col // heads
    x = tall(packed, 0, col)
    normed = (x * token_scale(x) * all_gains(packed)[0]).astype(bf16)
    projected = []
    for i, w in enumerate((wq, wk, wv)):
        rows = mm(w[...], normed).astype(bf16)
        qkv_ref[i] = rows
        projected.append(rows)
    query, key, value = projected
    hot = (sublanes((table.shape[1], 2 * tok - 1)) == buckets[...]).astype(f32)
    offsets = mm(table[...], hot, precision=highest)
    offsets = jnp.concatenate([offsets, jnp.zeros((heads, 1), f32)], axis=1)
    open_keys = lanes((tok, tok)) < scalars[0]
    outs = []
    for h in range(heads):
        at = slice(h * size, (h + 1) * size)
        spread = jnp.broadcast_to(offsets[h : h + 1, :], (tok, 2 * tok))
        bias = pltpu.roll(spread, tok + 1, 1, stride=1, stride_axis=0)[:, :tok]
        scores = mm(query[at], key[at], tn) * scale + bias
        weights = softmax(jnp.where(open_keys, scores, -1000000000.0), 1)
        weights_ref[h] = weights
        outs.append(mm(value[at], weights.astype(bf16), nt))
    attended = jnp.concatenate(outs, axis=0).astype(bf16)
    attended_ref[...] = attended
    branch = mm(w_output[...], attended, tn)
    for i in range(branch_ref.shape[0]):
        branch_ref[i] = branch[i * col : (i + 1) * col].astype(bf16)


def second_norm(residual, gain, w_router):
    scale = token_scale(residual)
    unit = residual * scale
    normed = (unit * gain).astype(bf16)
    return scale, unit, normed, softmax(mm(w_router, normed), 0)


def route_kernel(capacity, scalars, came, inputs, out_grad, routes, residual_ref, low_ref, side_ref, send_ref):
    col, tok = inputs.shape
    experts, slots, _ = send_ref.shape
    residual = inputs[...].astype(f32)
    for i in range(came.shape[0]):
        residual = residual + came[i].astype(f32)
    residual_ref[...] = residual
    low = residual.astype(bf16)
    low_ref[...] = low
    route_hot = (sublanes((experts, tok)) == routes[...]).astype(f32)
    before = (sublanes((tok, tok)) < lanes((tok, tok))).astype(bf16)
    slot = jnp.sum(mm(route_hot.astype(bf16), before) * route_hot, axis=0, keepdims=True)
    spots = routes[...].astype(f32) * slots + slot
    side_ref[...] = side_rows(8, tok, [spots])
    valid = (lanes((1, tok)) < scalars[0]).astype(f32)
    counts = jnp.sum(route_hot * valid, axis=1, keepdims=True)
    pick = pick_slots(spots.astype(jnp.int32), experts * slots).astype(bf16)
    rows = mm(pick, jnp.concatenate([low, out_grad[...]], axis=0), nt)
    spare = (sublanes((slots, 2 * col)) == capacity) & (lanes((slots, 2 * col)) == col)
    for e in range(experts):
        block = rows[e * slots : (e + 1) * slots]
        send_ref[e] = jnp.where(spare, counts[e : e + 1], block).astype(bf16)


def gain_row(packed, first, line):
    pieces = []
    for i in range(packed.shape[0]):
        block = packed[i, first : first + 16, :].astype(f32)
        pieces += [block[line : line + 1, :], block[line + 1 : line + 2, :64]]
    return jnp.concatenate(pieces, axis=1)


def expert_kernel(
    capacity, scalars, quarters, packed, w_in, w_out, w_router,
    back_ref, part_ref, hidden_ref, before_ref, grads_ref, rows_ref,
):
    total = rows_ref.shape[0]
    experts, width = w_router.shape
    heads = part_ref.shape[0]
    col = width // heads
    slots = total // experts
    half = total // 2
    parts = [quarters[i].astype(f32) for i in range(heads)]
    residual = jnp.concatenate([block[:, :col] for block in parts], axis=1)
    grads = jnp.concatenate([block[:, col:] for block in parts], axis=1)
    inverse = lax.rsqrt(jnp.sum(residual * residual, axis=1, keepdims=True) * (1.0 / width) + eps)
    rows = (residual * inverse * gain_row(packed, 2 * col, 2)).astype(bf16)
    rows_ref[...] = rows
    hidden, slope = gelu_parts(mm(rows, w_in[...]))
    hidden = hidden.astype(bf16)
    hidden_ref[...] = hidden
    produced = mm(hidden, w_out[...])
    for i in range(heads):
        mine = produced[:, i * col : (i + 1) * col]
        rest = mine[:, 128:]
        part_ref[i] = jnp.concatenate(
            [mine[:, :128], jnp.concatenate([rest[:half], rest[half:]], axis=1)], axis=0
        ).astype(bf16)
    probs = softmax(mm(rows, w_router[...], nt), 1)
    gate = jnp.sum(jnp.where(lanes((total, experts)) == scalars[2], probs, 0.0), axis=1, keepdims=True)
    back = (gate * grads).astype(bf16)
    grads_ref[...] = back
    before = (mm(back, w_out[...], nt) * slope).astype(bf16)
    before_ref[...] = before
    rows_grad = mm(before, w_in[...], nt)
    gate_grad = jnp.sum(grads * produced, axis=1, keepdims=True)
    stats = jnp.zeros((1, 128), f32)
    for b in range(experts):
        stats = stats + grads[b * slots + capacity : b * slots + capacity + 1, :128]
    side = side_lanes(total, 4, high_low(gate_grad) + high_low(stats[:, 0:1]))
    for b in range(experts):
        at = slice(b * slots, (b + 1) * slots)
        for i in range(heads):
            mine = rows_grad[at, i * col : (i + 1) * col]
            back_ref[b * heads + i] = jnp.concatenate(
                [mine[:, :128]] + fold_rest(mine[:, 128:], side[at]), axis=0
            ).astype(bf16)


def weights_kernel(rows_ref, hidden, before, grads, in_ref, out_ref):
    in_ref[...] = mm(rows_ref[...], before[...], tn)
    out_ref[...] = mm(hidden[...], grads[...], tn)


def collect_kernel(slots, came, side, low, grad_ref, gate_ref, stats_ref):
    col, tok = low.shape
    experts = stats_ref.shape[0]
    heads = came.shape[0] // experts
    tops, rests, scalars = [], [], []
    for e in range(experts):
        total = came[e * heads].astype(f32)
        for i in range(1, heads):
            total = total + came[e * heads + i].astype(f32)
        rest, columns = unfold_rest(total[slots:], slots, 4)
        tops.append(total[:slots])
        rests.append(rest)
        scalars.append(columns)
    counts = jnp.concatenate([columns[0:1] for columns in scalars], axis=0) * (1.0 / heads)
    pick = pick_slots(side[0:1, :].astype(jnp.int32), experts * slots)
    for first, pieces in ((0, tops), (128, rests)):
        block = jnp.concatenate(pieces, axis=0).astype(bf16)
        grad_ref[first : min(first + 128, col), :] = mm(block, pick.astype(bf16), tn).astype(bf16)
    grad_ref[col:, :] = low[...]
    gate = mm(jnp.concatenate(scalars, axis=0), pick.astype(f32), tn, highest)
    gate_ref[...] = jnp.broadcast_to(gate[0:1] + gate[1:2], gate_ref.shape)
    stats_ref[...] = side_lanes(experts, 128, [counts[:, 2:3] + counts[:, 3:4]])


def backward_kernel(
    scale, valid_total, scalars, packed, expert_grad, gate_grad, stats, routes, w_router, w_output, weights_ref,
    qkv, wq, wk, wv, attended, part, late_ref, first_ref, own_ref, gate_ref, *share_refs,
):
    tok = routes.shape[1]
    heads_here = weights_ref.shape[0]
    blocks, col = packed.shape[0], wq.shape[0]
    experts, width = w_router.shape
    size = col // heads_here
    gain_one, gain_two = all_gains(packed)
    residual = tall(expert_grad, col, col)
    scale_two, unit, normed, router = second_norm(residual, gain_two, w_router[...])
    valid = (lanes((1, tok)) < scalars[0]).astype(f32)
    route_hot = (sublanes((experts, tok)) == routes[...]).astype(f32)
    fraction = stats[:, 0:1] * (aux_weight * experts / (valid_total * valid_total))
    gate = jnp.sum(router * route_hot, axis=0, keepdims=True)
    gate_ref[...] = jnp.broadcast_to(gate, gate_ref.shape)
    prob_grad = route_hot * gate_grad[0:1, :] + fraction * valid
    logit_grad = router * (prob_grad - jnp.sum(router * prob_grad, axis=0, keepdims=True))
    logit_grad = logit_grad.astype(bf16)
    normed_grad = mm(w_router[...], logit_grad, tn) + tall(expert_grad, 0, col)
    unit_grad = normed_grad * gain_two
    mean = jnp.sum(unit_grad * unit, axis=0, keepdims=True) * (1.0 / width)
    residual_grad = tall(packed, col, col) + scale_two * (unit_grad - unit * mean)
    branch = residual_grad.astype(bf16)
    attended_grad = mm(w_output[...], branch).astype(bf16)
    flip = (lanes((tok, tok)) + sublanes((tok, tok)) == tok - 1).astype(bf16)
    query, key, value = qkv[0], qkv[1], qkv[2]
    grads = [[], [], []]
    offsets = []
    for h in range(heads_here):
        at = slice(h * size, (h + 1) * size)
        out = attended_grad[at]
        weights = weights_ref[h]
        mass = mm(out, value[at], tn)
        score = weights * (mass - jnp.sum(weights * mass, axis=1, keepdims=True))
        score = score.astype(bf16)
        grads[0].append(mm(key[at], score, nt) * scale)
        grads[1].append(mm(query[at], score) * scale)
        grads[2].append(mm(out, weights.astype(bf16)))
        flipped = jnp.concatenate([mm(flip, score), jnp.zeros((tok, tok), f32)], axis=1)
        rolled = pltpu.roll(flipped, 0, 1, stride=1, stride_axis=0)
        offsets.append(jnp.sum(rolled, axis=0, keepdims=True))
    first = jnp.zeros((width, tok), f32)
    row = jnp.zeros((1, tok), f32)
    for i, w in enumerate((wq, wk, wv)):
        low = jnp.concatenate(grads[i], axis=0).astype(bf16)
        late_ref[i * col : (i + 1) * col, :] = low
        first = first + mm(w[...], low, tn)
        row = row + jnp.sum(low.astype(f32) * qkv[i].astype(f32), axis=0, keepdims=True)
    side = side_rows(16, tok, high_low(row))
    for i in range(blocks):
        at = slice(i * col, (i + 1) * col)
        first_ref[i, : col + 16, :] = jnp.concatenate([first[at], side], axis=0).astype(bf16)
        first_ref[i, col + 16 :, :] = part[i]

    product = mm(attended[...], branch, nt)
    gain_two_grad = jnp.sum(normed_grad * unit, axis=1, keepdims=True)
    gains = jnp.zeros((col, 1), f32)
    own = jnp.zeros((col, tok), f32)
    for i in range(blocks):
        at = slice(i * col, (i + 1) * col)
        gains = jnp.where(scalars[1] == i, gain_two_grad[at], gains)
        own = jnp.where(scalars[1] == i, residual_grad[at], own)
    own_ref[...] = own
    probs = jnp.sum(router * valid, axis=1, keepdims=True)
    if experts < col:
        probs = jnp.concatenate([probs, jnp.zeros((col - experts, 1), f32)], axis=0)
    gains = jnp.transpose(side_lanes(col, 128, [gains] + high_low(probs)))[0:8]
    router_grad = mm(logit_grad, normed, nt)
    offsets = jnp.concatenate(offsets, axis=0)
    offsets = jnp.concatenate([offsets, jnp.zeros((8 - heads_here, 2 * tok), f32)], axis=0)
    gains = jnp.concatenate([gains, jnp.zeros((8, 64), f32)], axis=1)
    pieces = [fold_lanes(gains), fold_lanes(offsets), fold_lanes(router_grad)]
    if len(share_refs) == 2:
        share_refs[0][...] = jnp.concatenate(pieces, axis=0)
        share_refs[1][...] = product
    else:
        share_ref = share_refs[0]
        groups = share_ref.shape[0]
        size = col // groups
        chunk = share_ref.shape[1] - 6 * size
        small = jnp.concatenate(pieces + [jnp.zeros((groups * chunk - 6 * experts - 32, 128), f32)], axis=0)
        for b in range(groups):
            share_ref[b] = jnp.concatenate(
                [small[b * chunk : (b + 1) * chunk], fold_lanes(product[b * size : (b + 1) * size])], axis=0
            ).astype(bf16)


def first_kernel(scalars, came, packed, own, *refs):
    shares, (ret_ref, gain_ref, input_ref) = refs[:-3], refs[-3:]
    col, tok = own.shape
    heads = came.shape[0]
    experts = ret_ref.shape[0]
    total = came[0].astype(f32)
    for i in range(1, heads):
        total = total + came[i].astype(f32)
    mean = (total[col : col + 1] + total[col + 1 : col + 2]) * (1.0 / (heads * col))
    scale = token_scale(tall(packed, 0, col))
    mine = packed[0].astype(f32)
    for i in range(1, heads):
        mine = jnp.where(scalars[1] == i, packed[i].astype(f32), mine)
    unit = mine[:col] * scale
    gain = gain_columns(mine[2 * col : 2 * col + 16])[0]
    input_ref[...] = own[...] + scale * (total[:col] * gain - unit * mean)
    gain_grad = jnp.sum(total[:col] * unit, axis=1, keepdims=True)
    unused = jnp.zeros_like(gain_grad)
    gain_grad = jnp.transpose(side_lanes(col, 128, [unused, unused, unused, gain_grad]))[0:8]
    gain_grad = fold_lanes(jnp.concatenate([gain_grad, jnp.zeros((8, 64), f32)], axis=1))
    gain_ref[...] = gain_grad
    produced = total[col + 16 :]
    count = produced.shape[0] * 2 // 3
    top = produced[:count]
    rest = jnp.concatenate([produced[count:, :64], produced[count:, 64:]], axis=0)
    rest = jnp.concatenate([rest, jnp.zeros((count, 64), f32)], axis=1)
    slots = count // experts
    for e in range(experts):
        at = slice(e * slots, (e + 1) * slots)
        pieces = [top[at], rest[at]]
        if shares:
            share = shares[0][e].astype(f32)
            if e == 0:
                share = jnp.concatenate([share[:16] + gain_grad, share[16:]], axis=0)
            pieces.append(share)
        ret_ref[e] = jnp.concatenate(pieces, axis=0).astype(bf16)


def share_kernel(slots, came, share_ref):
    total = came[0].astype(f32)
    for e in range(1, came.shape[0]):
        total = total + came[e].astype(f32)
    for e in range(came.shape[0]):
        share_ref[e] = total[2 * slots :].astype(bf16)


def add_returned(slots, blocks, side, gate, residual):
    col = residual.shape[0]
    top = jnp.concatenate([block[:slots] for block in blocks], axis=0).astype(bf16)
    rest = jnp.concatenate([block[slots : 2 * slots] for block in blocks], axis=0).astype(bf16)
    pick = pick_slots(side[0:1, :].astype(jnp.int32), len(blocks) * slots).astype(bf16)
    returned = jnp.concatenate([mm(top, pick, tn), mm(rest, pick, tn)[: col - 128]], axis=0)
    return (residual[...] + gate[0:1, :] * returned).astype(bf16)


def last_kernel(slots, came, side, gate, residual, block_ref):
    blocks = [came[e].astype(f32) for e in range(came.shape[0])]
    block_ref[...] = add_returned(slots, blocks, side, gate, residual)


def turn_kernel(all_in, packed, normed_ref):
    groups, heads, col, tok = all_in.shape
    gain = all_gains(packed)[0]
    for b in range(groups):
        x = jnp.concatenate([all_in[b, i].astype(f32) for i in range(heads)], axis=0)
        normed_ref[b * tok : (b + 1) * tok, :] = jnp.transpose(x * token_scale(x) * gain).astype(bf16)


def products_kernel(
    late, normed, came, buckets, stats, q_ref, k_ref, v_ref, out_ref, router_ref, table_ref, gains_ref, aux_ref,
):
    groups = came.shape[0]
    col = q_ref.shape[0]
    experts = router_ref.shape[0]
    size = col // groups
    shares = [came[b].astype(f32) for b in range(groups)]
    chunk = shares[0].shape[0] - 6 * size
    for b in range(groups):
        out_ref[b * size : (b + 1) * size, :] = unfold_lanes(shares[b][chunk:], 6)
    joined = jnp.concatenate([late[b] for b in range(groups)], axis=1)
    product = mm(joined, normed[...])
    for i, ref in enumerate((q_ref, k_ref, v_ref)):
        ref[...] = product[i * col : (i + 1) * col]
    small = jnp.concatenate([share[:chunk] for share in shares], axis=0)
    gains = unfold_lanes(small[:16], 2)
    gains_ref[...] = gains
    probs = gains[1:2, :experts] + gains[2:3, :experts]
    same = lanes((experts, experts)) == sublanes((experts, experts))
    share = jnp.sum(jnp.where(same, stats[:, 0:1] * probs, 0.0), axis=0, keepdims=True)
    valid_total = 3 * normed.shape[0] // 4
    aux_ref[...] = jnp.sum(share, axis=1, keepdims=True) * (experts / (valid_total * valid_total))
    span = buckets.shape[1]
    hot = (sublanes((table_ref.shape[1], span)) == buckets[...]).astype(f32)
    offsets = unfold_lanes(small[16:32], 2)[:, :span]
    table_ref[...] = mm(offsets, hot, nt, highest)[: table_ref.shape[0]]
    router_ref[...] = unfold_lanes(small[32 : 32 + 6 * experts], 6)


def few_experts():
    return lax.axis_size("expert") <= 8


def shards(
    inputs,
    out_grad,
    lengths,
    routes,
    buckets,
    gain_attn,
    w_query,
    w_key,
    w_value,
    w_output,
    bias_table,
    gain_ffn,
    w_router,
    w_in,
    w_out,
):
    tok, col = inputs.shape
    heads_here = bias_table.shape[1]
    head_size = w_query.shape[1] // heads_here
    width, experts = w_router.shape
    bucket_count = bias_table.shape[0]
    heads = width // col
    groups = lax.axis_size("expert")
    me_head, me_expert = lax.axis_index("head"), lax.axis_index("expert")
    capacity = max(2, (4 * tok + 3 * experts - 1) // (3 * experts))
    slots = -(-(capacity + 1) // 8) * 8
    total = experts * slots
    valid_total = 3 * tok * groups // 4
    scale = head_size ** (-0.5)
    joined = few_experts()
    small_rows = 6 * experts + 32
    chunk = -(-small_rows // (16 * groups)) * 16
    w_in, w_out = w_in[0], w_out[0]
    wq, wk, wv = w_query.T, w_key.T, w_value.T
    routes_row = routes.T
    router_rows = w_router.T
    scalars = jnp.stack([lengths[0], me_head.astype(jnp.int32), me_expert.astype(jnp.int32)])
    buckets_row = buckets[None]

    space = jnp.zeros((64,), bf16)
    gains = jnp.concatenate([gain_attn, space, gain_ffn, space, jnp.zeros((1536,), bf16)]).reshape(16, 128)
    packed = lax.all_gather(jnp.concatenate([inputs.T, out_grad.T, gains], axis=0), "head")
    if joined:
        all_in = lax.all_gather(inputs.T, ("expert", "head")).reshape(groups, heads, col, tok)
    qkv, weights, attended, branch = call(
        functools.partial(attend_kernel, scale),
        [
            ((3, col, tok), bf16, 1), ((heads_here, tok, tok), f32, 1), ((col, tok), bf16, 1),
            ((heads, col, tok), bf16),
        ],
        scalars, packed, far(wq), far(wk), far(wv), far(w_output), far(buckets_row), far(bias_table.T),
    )

    branch = lax.all_to_all(branch, "head", split_axis=0, concat_axis=0, tiled=True)
    residual, low, side, send = call(
        functools.partial(route_kernel, capacity),
        [((col, tok), f32, 1), ((col, tok), bf16, 1), ((8, tok), f32, 1), ((experts, slots, 2 * col), bf16)],
        scalars, branch, far(inputs.T), far(out_grad.T), far(routes_row),
    )
    quarter = lax.all_to_all(send, "expert", split_axis=0, concat_axis=0, tiled=True)
    quarters = lax.all_gather(quarter.reshape(total, 2 * col), "head")

    back, part, hidden, before_grad, back_rows, rows = call(
        functools.partial(expert_kernel, capacity),
        [((experts * heads, folded_rows(slots), 128), bf16), ((heads, total * 3 // 2, 128), bf16, 1)]
        + [((total, width), bf16, 1)] * 4,
        scalars, Split(quarters, heads), far(packed), Split(w_in, 4), Split(w_out, 4), far(router_rows),
    )
    came = lax.all_to_all(back, ("expert", "head"), split_axis=0, concat_axis=0, tiled=True)
    grad_own, gate_grad, stats = call(
        functools.partial(collect_kernel, slots),
        [((2 * col, tok), bf16), ((8, tok), f32, 1), ((experts, 128), f32, 1)],
        came, far(side), far(low),
    )
    expert_grad = lax.all_gather(grad_own, "head")

    late, first, residual_grad_own, gate, *shares = call(
        functools.partial(backward_kernel, scale, valid_total),
        [
            ((3 * col, tok), bf16, 1), ((heads, col + 16 + total * 3 // 2, 128), bf16), ((col, tok), f32, 1),
            ((8, tok), f32, 1),
        ]
        + (
            [((groups, chunk + 6 * col // groups, 128), bf16, 1)]
            if joined
            else [((small_rows, 128), f32, 1), ((col, width), f32, 1)]
        ),
        scalars, far(packed), expert_grad, far(gate_grad), far(stats), far(routes_row),
        far(router_rows), far(w_output), far(weights), far(qkv), far(wq), far(wk), far(wv), far(attended),
        Split(part, heads),
    )

    if joined:
        late_all = lax.all_gather(late, "expert")

    first = lax.all_to_all(first, "head", split_axis=0, concat_axis=0, tiled=True)
    ret, gain_one_part, input_grad = call(
        first_kernel,
        [
            ((experts, 2 * slots + (shares[0].shape[1] if joined else 0), 128), bf16),
            ((16, 128), f32, 1), ((col, tok), f32, 1),
        ],
        scalars, first, Split(packed, heads), far(residual_grad_own), *([Split(shares[0], groups)] if joined else []),
    )
    ret = lax.all_to_all(ret, "expert", split_axis=0, concat_axis=0, tiled=True)
    if joined:
        share = call(
            functools.partial(share_kernel, slots), [(shares[0].shape, bf16)], ret
        )[0]
        share = lax.all_to_all(share, "expert", split_axis=0, concat_axis=0, tiled=True)
    block_out = call(
        functools.partial(last_kernel, slots), [((col, tok), bf16, 1)], far(ret), far(side), far(gate), far(residual)
    )[0]
    in_weight_grad, out_weight_grad = call(
        weights_kernel, [((width, width), f32, 1)] * 2, far(rows), far(hidden), far(before_grad), far(back_rows)
    )
    if joined:
        normed_all = call(turn_kernel, [((groups * tok, width), bf16, 1)], Split(all_in, groups), Split(packed, heads))[0]
        q_grad, k_grad, v_grad, output_grad, router_grad, table_grad, gain_grads, aux_loss = call(
            products_kernel,
            [((col, width), f32, 1)] * 4
            + [((experts, width), f32), ((heads_here, bucket_count), f32), ((8, 256), f32), ((1, 1), f32)],
            Split(late_all, groups), Split(normed_all, groups), share, far(buckets_row), far(stats),
        )
    else:
        gain = packed[:, 2 * col : 2 * col + 2].reshape(heads, 256)[:, :col].reshape(width, 1)
        x = packed[:, :col].reshape(width, tok).astype(f32)
        normed = (x * token_scale(x) * gain.astype(f32)).astype(bf16)
        products = [mm(late[i * col : (i + 1) * col], normed, nt) for i in range(3)]
        q_grad, k_grad, v_grad, sums, gain_one, output_grad = lax.psum(
            products + [shares[0], gain_one_part, shares[1]], "expert"
        )
        router_grad = unfold_lanes(sums[32 : 32 + 6 * experts], 6)
        offsets = unfold_lanes(sums[16:32], 2)[:heads_here, : 2 * tok - 1]
        hot = (buckets[None, :] == jnp.arange(bucket_count)[:, None]).astype(f32)
        table_grad = mm(offsets, hot, nt, highest)
        gain_grads = unfold_lanes(sums[:16] + gain_one, 2)
        probs = gain_grads[1, :experts] + gain_grads[2, :experts]
        aux_loss = experts * jnp.sum(stats[:, 0] * probs) / (valid_total * valid_total)
    return (
        block_out.T,
        input_grad.T,
        aux_loss.reshape(()),
        gain_grads[3, :col],
        q_grad.T,
        k_grad.T,
        v_grad.T,
        output_grad,
        table_grad.T,
        gain_grads[0, :col],
        router_grad.T,
        in_weight_grad[None],
        out_weight_grad[None],
    )


def solution(mesh):
    return jax.shard_map(
        shards,
        mesh=mesh,
        in_specs=(
            P("expert", "head"),
            P("expert", "head"),
            P("expert"),
            P("expert", None),
            P(),
            P("head"),
            P(None, "head"),
            P(None, "head"),
            P(None, "head"),
            P("head", None),
            P(None, "head"),
            P("head"),
            P(),
            P("expert", None, "head"),
            P("expert", "head", None),
        ),
        out_specs=(
            P("expert", "head"),
            P("expert", "head"),
            P(),
            P("head"),
            P(None, "head"),
            P(None, "head"),
            P(None, "head"),
            P("head", None),
            P(None, "head"),
            P("head"),
            P(),
            P("expert", None, "head"),
            P("expert", "head", None),
        ),
        check_vma=False,
    )
```

```python
import functools

import jax
import jax.numpy as jnp
from jax import lax
from jax.experimental import pallas as pl
from jax.experimental.pallas import tpu as pltpu
from jax.sharding import PartitionSpec as P

eps = 1e-06
aux_weight = 0.01
f32 = jnp.float32
bf16 = jnp.bfloat16
gelu_scale = 0.7978845608028654
gelu_cube = 0.044715
highest = lax.Precision.HIGHEST
nt = ((1,), (1,))
tn = ((0,), (0,))


def mm(left, right, dims=((1,), (0,)), precision=None):
    return lax.dot_general(left, right, (dims, ((), ())), precision=precision, preferred_element_type=f32)


def call(body, outs, *args):
    scalar_memory = pl.BlockSpec(memory_space=pltpu.SMEM)
    in_specs = [scalar_memory if a.dtype == jnp.int32 and a.ndim == 1 else pl.BlockSpec() for a in args]
    shapes = []
    for shape, kind, *remote in outs:
        shapes.append(pltpu.HBM(shape, kind) if remote else jax.ShapeDtypeStruct(shape, kind))
    return pl.pallas_call(
        body,
        out_shape=shapes,
        in_specs=in_specs,
        compiler_params=pltpu.CompilerParams(vmem_limit_bytes=40 * 1024 * 1024),
    )(*args)


def grid_call(body, steps, outs, *args):
    def spec(block, along):
        return pl.BlockSpec(block, lambda step: tuple(step if i == along else 0 for i in range(len(block))))

    return pl.pallas_call(
        body,
        grid=(steps,),
        out_shape=[pltpu.HBM(*kind) for kind, _, _ in outs],
        in_specs=[spec(block, along) for _, block, along in args],
        out_specs=[spec(block, along) for _, block, along in outs],
        compiler_params=pltpu.CompilerParams(vmem_limit_bytes=40 * 1024 * 1024),
    )(*(far(array) for array, _, _ in args))


def far(array):
    return pltpu.with_memory_space_constraint(array, pltpu.HBM)


def tall(ref, first, rows):
    return jnp.concatenate([ref[i, first : first + rows, :].astype(f32) for i in range(ref.shape[0])], axis=0)


def gain_columns(block):
    turned = jnp.transpose(block.astype(f32))
    return [
        jnp.concatenate([turned[:, 0:1], turned[:64, 1:2]], axis=0),
        jnp.concatenate([turned[64:, 1:2], turned[:, 2:3]], axis=0),
    ]


def all_gains(packed):
    first = 2 * packed.shape[2] * 3 // 2
    pairs = [gain_columns(packed[i, first : first + 16, :]) for i in range(packed.shape[0])]
    return [jnp.concatenate([pair[i] for pair in pairs], axis=0) for i in range(2)]


def token_scale(values):
    return lax.rsqrt(jnp.sum(values * values, axis=0, keepdims=True) * (1.0 / values.shape[0]) + eps)


def lanes(shape):
    return lax.broadcasted_iota(jnp.int32, shape, len(shape) - 1)


def sublanes(shape):
    return lax.broadcasted_iota(jnp.int32, shape, len(shape) - 2)


def side_lanes(rows, width, columns):
    spot = lanes((rows, width))
    out = jnp.zeros((rows, width), f32)
    for i, column in enumerate(columns):
        out = jnp.where(spot == i, column, out)
    return out


def side_rows(rows, width, lines):
    spot = sublanes((rows, width))
    out = jnp.zeros((rows, width), f32)
    for i, line in enumerate(lines):
        out = jnp.where(spot == i, line, out)
    return out


def high_low(values, count=2):
    pieces = []
    for _ in range(count):
        piece = values.astype(bf16).astype(f32)
        pieces.append(piece)
        values = values - piece
    return pieces


def softmax(values, axis):
    raised = jnp.exp(values - jnp.max(values, axis=axis, keepdims=True))
    return raised / jnp.sum(raised, axis=axis, keepdims=True)


def gelu_parts(u):
    t = jnp.tanh(gelu_scale * (u + gelu_cube * u * u * u))
    value = 0.5 * u * (1.0 + t)
    slope = 0.5 * (1.0 + t) + 0.5 * u * (1.0 - t * t) * gelu_scale * (1.0 + 3.0 * gelu_cube * u * u)
    return value, slope


def fold_lanes(rows):
    return jnp.concatenate([rows[:, i : i + 128] for i in range(0, rows.shape[1], 128)], axis=0)


def unfold_lanes(rows, pieces):
    size = rows.shape[0] // pieces
    return jnp.concatenate([rows[i * size : (i + 1) * size] for i in range(pieces)], axis=1)


def fold_rest(rest, side):
    groups = [rest[i : i + 8] for i in range(0, rest.shape[0], 8)]
    count = side.shape[1]
    spot = lanes((8, 64))
    last = jnp.zeros((8, 64), f32)
    for g in range(len(groups)):
        for j in range(count):
            last = jnp.where(spot == g * count + j, side[8 * g : 8 * g + 8, j : j + 1], last)
    groups.append(last)
    if len(groups) % 2:
        groups.append(jnp.zeros((8, 64), f32))
    return [jnp.concatenate(groups[i : i + 2], axis=1) for i in range(0, len(groups), 2)]


def unfold_rest(blocks, slots, count):
    halves = []
    for i in range(0, blocks.shape[0], 8):
        halves += [blocks[i : i + 8, :64], blocks[i : i + 8, 64:]]
    number = slots // 8
    side = [halves[number][:, g * count : (g + 1) * count] for g in range(number)]
    return jnp.concatenate(halves[:number], axis=0), jnp.concatenate(side, axis=0)


def folded_rows(slots):
    return slots + 8 * ((slots // 8 + 2) // 2)


def pick_slots(spots, count):
    return sublanes((count, spots.shape[1])) == spots


def attend_kernel(
    scale, scalars, packed, wq, wk, wv, w_output, buckets, table, qkv_ref, weights_ref, attended_ref, branch_ref
):
    heads, tok, _ = weights_ref.shape
    col = wq.shape[0]
    size = col // heads
    x = tall(packed, 0, col)
    normed = (x * token_scale(x) * all_gains(packed)[0]).astype(bf16)
    projected = []
    for i, w in enumerate((wq, wk, wv)):
        rows = mm(w[...], normed).astype(bf16)
        qkv_ref[i] = rows
        projected.append(rows)
    query, key, value = projected
    hot = (sublanes((table.shape[1], 2 * tok - 1)) == buckets[...]).astype(f32)
    offsets = mm(table[...], hot, precision=highest)
    offsets = jnp.concatenate([offsets, jnp.zeros((heads, 1), f32)], axis=1)
    open_keys = lanes((tok, tok)) < scalars[0]
    outs = []
    for h in range(heads):
        at = slice(h * size, (h + 1) * size)
        spread = jnp.broadcast_to(offsets[h : h + 1, :], (tok, 2 * tok))
        bias = pltpu.roll(spread, tok + 1, 1, stride=1, stride_axis=0)[:, :tok]
        scores = mm(query[at], key[at], tn) * scale + bias
        weights = softmax(jnp.where(open_keys, scores, -1000000000.0), 1)
        weights_ref[h] = weights
        outs.append(mm(value[at], weights.astype(bf16), nt))
    attended = jnp.concatenate(outs, axis=0).astype(bf16)
    attended_ref[...] = attended
    branch = mm(w_output[...], attended, tn)
    for i in range(branch_ref.shape[0]):
        branch_ref[i] = branch[i * col : (i + 1) * col].astype(bf16)


def second_norm(residual, gain, w_router):
    scale = token_scale(residual)
    unit = residual * scale
    normed = (unit * gain).astype(bf16)
    return scale, unit, normed, softmax(mm(w_router, normed), 0)


def route_kernel(capacity, scalars, came, inputs, out_grad, routes, residual_ref, low_ref, side_ref, send_ref):
    col, tok = inputs.shape
    experts, slots, _ = send_ref.shape
    residual = inputs[...].astype(f32)
    for i in range(came.shape[0]):
        residual = residual + came[i].astype(f32)
    residual_ref[...] = residual
    low = residual.astype(bf16)
    low_ref[...] = low
    route_hot = (sublanes((experts, tok)) == routes[...]).astype(f32)
    before = (sublanes((tok, tok)) < lanes((tok, tok))).astype(bf16)
    slot = jnp.sum(mm(route_hot.astype(bf16), before) * route_hot, axis=0, keepdims=True)
    spots = routes[...].astype(f32) * slots + slot
    side_ref[...] = side_rows(8, tok, [spots])
    valid = (lanes((1, tok)) < scalars[0]).astype(f32)
    counts = jnp.sum(route_hot * valid, axis=1, keepdims=True)
    pick = pick_slots(spots.astype(jnp.int32), experts * slots).astype(bf16)
    rows = mm(pick, jnp.concatenate([low, out_grad[...]], axis=0), nt)
    spare = (sublanes((slots, 2 * col)) == capacity) & (lanes((slots, 2 * col)) == col)
    for e in range(experts):
        block = rows[e * slots : (e + 1) * slots]
        send_ref[e] = jnp.where(spare, counts[e : e + 1], block).astype(bf16)


def second_gain_row(packed, first):
    pieces = []
    for i in range(packed.shape[0]):
        block = packed[i, first : first + 16, :].astype(f32)
        pieces += [block[1:2, 64:], block[2:3, :]]
    return jnp.concatenate(pieces, axis=1)


def expert_kernel(
    capacity, scalars, quarters, packed, w_in, w_out, w_router,
    back_ref, part_ref, hidden_ref, before_ref, grads_ref, rows_ref,
):
    total = rows_ref.shape[0]
    experts, width = w_router.shape
    heads = part_ref.shape[0]
    col = width // heads
    slots = total // experts
    half = total // 2
    parts = [quarters[i].astype(f32) for i in range(heads)]
    residual = jnp.concatenate([block[:, :col] for block in parts], axis=1)
    grads = jnp.concatenate([block[:, col:] for block in parts], axis=1)
    inverse = lax.rsqrt(jnp.sum(residual * residual, axis=1, keepdims=True) * (1.0 / width) + eps)
    rows = (residual * inverse * second_gain_row(packed, 2 * col)).astype(bf16)
    rows_ref[...] = rows
    hidden, slope = gelu_parts(mm(rows, w_in[...]))
    hidden = hidden.astype(bf16)
    hidden_ref[...] = hidden
    produced = mm(hidden, w_out[...])
    for i in range(heads):
        mine = produced[:, i * col : (i + 1) * col]
        rest = mine[:, 128:]
        part_ref[i] = jnp.concatenate(
            [mine[:, :128], jnp.concatenate([rest[:half], rest[half:]], axis=1)], axis=0
        ).astype(bf16)
    probs = softmax(mm(rows, w_router[...], nt), 1)
    gate = jnp.sum(jnp.where(lanes((total, experts)) == scalars[2], probs, 0.0), axis=1, keepdims=True)
    back = (gate * grads).astype(bf16)
    grads_ref[...] = back
    before = (mm(back, w_out[...], nt) * slope).astype(bf16)
    before_ref[...] = before
    rows_grad = mm(before, w_in[...], nt)
    gate_grad = jnp.sum(grads * produced, axis=1, keepdims=True)
    stats = jnp.zeros((1, 128), f32)
    for b in range(experts):
        stats = stats + grads[b * slots + capacity : b * slots + capacity + 1, :128]
    side = side_lanes(total, 4, high_low(gate_grad) + high_low(stats[:, 0:1]))
    for b in range(experts):
        at = slice(b * slots, (b + 1) * slots)
        for i in range(heads):
            mine = rows_grad[at, i * col : (i + 1) * col]
            back_ref[b * heads + i] = jnp.concatenate(
                [mine[:, :128]] + fold_rest(mine[:, 128:], side[at]), axis=0
            ).astype(bf16)


def weights_kernel(rows_ref, hidden, before, grads, in_ref, out_ref):
    in_ref[...] = mm(rows_ref[...], before[...], tn)
    out_ref[...] = mm(hidden[...], grads[...], tn)


def collect_kernel(slots, came, side, low, grad_ref, gate_ref, stats_ref):
    col, tok = low.shape
    experts = stats_ref.shape[0]
    heads = came.shape[0] // experts
    tops, rests, scalars = [], [], []
    for e in range(experts):
        total = came[e * heads].astype(f32)
        for i in range(1, heads):
            total = total + came[e * heads + i].astype(f32)
        rest, columns = unfold_rest(total[slots:], slots, 4)
        tops.append(total[:slots])
        rests.append(rest)
        scalars.append(columns)
    counts = jnp.concatenate([columns[0:1] for columns in scalars], axis=0) * (1.0 / heads)
    pick = pick_slots(side[0:1, :].astype(jnp.int32), experts * slots)
    for first, pieces in ((0, tops), (128, rests)):
        block = jnp.concatenate(pieces, axis=0).astype(bf16)
        grad_ref[first : min(first + 128, col), :] = mm(block, pick.astype(bf16), tn).astype(bf16)
    grad_ref[col:, :] = low[...]
    gate = mm(jnp.concatenate(scalars, axis=0), pick.astype(f32), tn, highest)
    gate_ref[...] = jnp.broadcast_to(gate[0:1] + gate[1:2], gate_ref.shape)
    stats_ref[...] = side_lanes(experts, 128, [counts[:, 2:3] + counts[:, 3:4]])


def backward_kernel(
    scale, valid_total, scalars, packed, expert_grad, gate_grad, stats, routes, w_router, w_output, weights_ref,
    qkv, wq, wk, wv, attended, part, late_ref, first_ref, own_ref, gate_ref, *share_refs,
):
    tok = routes.shape[1]
    heads_here = weights_ref.shape[0]
    blocks, col = packed.shape[0], wq.shape[0]
    experts, width = w_router.shape
    size = col // heads_here
    gain_one, gain_two = all_gains(packed)
    residual = tall(expert_grad, col, col)
    scale_two, unit, normed, router = second_norm(residual, gain_two, w_router[...])
    valid = (lanes((1, tok)) < scalars[0]).astype(f32)
    route_hot = (sublanes((experts, tok)) == routes[...]).astype(f32)
    fraction = stats[:, 0:1] * (aux_weight * experts / (valid_total * valid_total))
    gate = jnp.sum(router * route_hot, axis=0, keepdims=True)
    gate_ref[...] = jnp.broadcast_to(gate, gate_ref.shape)
    prob_grad = route_hot * gate_grad[0:1, :] + fraction * valid
    logit_grad = router * (prob_grad - jnp.sum(router * prob_grad, axis=0, keepdims=True))
    logit_grad = logit_grad.astype(bf16)
    normed_grad = mm(w_router[...], logit_grad, tn) + tall(expert_grad, 0, col)
    unit_grad = normed_grad * gain_two
    mean = jnp.sum(unit_grad * unit, axis=0, keepdims=True) * (1.0 / width)
    residual_grad = tall(packed, col, col) + scale_two * (unit_grad - unit * mean)
    branch = residual_grad.astype(bf16)
    attended_grad = mm(w_output[...], branch).astype(bf16)
    flip = (lanes((tok, tok)) + sublanes((tok, tok)) == tok - 1).astype(bf16)
    query, key, value = qkv[0], qkv[1], qkv[2]
    grads = [[], [], []]
    offsets = []
    for h in range(heads_here):
        at = slice(h * size, (h + 1) * size)
        out = attended_grad[at]
        weights = weights_ref[h]
        mass = mm(out, value[at], tn)
        score = weights * (mass - jnp.sum(weights * mass, axis=1, keepdims=True))
        score = score.astype(bf16)
        grads[0].append(mm(key[at], score, nt) * scale)
        grads[1].append(mm(query[at], score) * scale)
        grads[2].append(mm(out, weights.astype(bf16)))
        flipped = jnp.concatenate([mm(flip, score), jnp.zeros((tok, tok), f32)], axis=1)
        rolled = pltpu.roll(flipped, 0, 1, stride=1, stride_axis=0)
        offsets.append(jnp.sum(rolled, axis=0, keepdims=True))
    first = jnp.zeros((width, tok), f32)
    row = jnp.zeros((1, tok), f32)
    for i, w in enumerate((wq, wk, wv)):
        low = jnp.concatenate(grads[i], axis=0).astype(bf16)
        late_ref[i * col : (i + 1) * col, :] = low
        first = first + mm(w[...], low, tn)
        row = row + jnp.sum(low.astype(f32) * qkv[i].astype(f32), axis=0, keepdims=True)
    side = side_rows(16, tok, high_low(row))
    for i in range(blocks):
        at = slice(i * col, (i + 1) * col)
        first_ref[i, : col + 16, :] = jnp.concatenate([first[at], side], axis=0).astype(bf16)
        first_ref[i, col + 16 :, :] = part[i]

    product = mm(attended[...], branch, nt)
    gain_two_grad = jnp.sum(normed_grad * unit, axis=1, keepdims=True)
    gains = jnp.zeros((col, 1), f32)
    own = jnp.zeros((col, tok), f32)
    for i in range(blocks):
        at = slice(i * col, (i + 1) * col)
        gains = jnp.where(scalars[1] == i, gain_two_grad[at], gains)
        own = jnp.where(scalars[1] == i, residual_grad[at], own)
    own_ref[...] = own
    probs = jnp.sum(router * valid, axis=1, keepdims=True)
    if experts < col:
        probs = jnp.concatenate([probs, jnp.zeros((col - experts, 1), f32)], axis=0)
    gains = jnp.transpose(side_lanes(col, 128, [gains] + high_low(probs)))[0:8]
    router_grad = mm(logit_grad, normed, nt)
    offsets = jnp.concatenate(offsets, axis=0)
    offsets = jnp.concatenate([offsets, jnp.zeros((8 - heads_here, 2 * tok), f32)], axis=0)
    gains = jnp.concatenate([gains, jnp.zeros((8, 64), f32)], axis=1)
    pieces = [fold_lanes(gains), fold_lanes(offsets), fold_lanes(router_grad)]
    if len(share_refs) == 2:
        share_refs[0][...] = jnp.concatenate(pieces, axis=0)
        share_refs[1][...] = product
    else:
        share_ref = share_refs[0]
        groups = share_ref.shape[0]
        size = col // groups
        chunk = share_ref.shape[1] - 6 * size
        small = jnp.concatenate(pieces + [jnp.zeros((groups * chunk - 6 * experts - 32, 128), f32)], axis=0)
        for b in range(groups):
            share_ref[b] = jnp.concatenate(
                [small[b * chunk : (b + 1) * chunk], fold_lanes(product[b * size : (b + 1) * size])], axis=0
            ).astype(bf16)


def first_kernel(scalars, came, packed, own, *refs):
    shares, (ret_ref, gain_ref, input_ref) = refs[:-3], refs[-3:]
    col, tok = own.shape
    heads = came.shape[0]
    experts = ret_ref.shape[0]
    total = came[0].astype(f32)
    for i in range(1, heads):
        total = total + came[i].astype(f32)
    mean = (total[col : col + 1] + total[col + 1 : col + 2]) * (1.0 / (heads * col))
    scale = token_scale(tall(packed, 0, col))
    mine = packed[0].astype(f32)
    for i in range(1, heads):
        mine = jnp.where(scalars[1] == i, packed[i].astype(f32), mine)
    unit = mine[:col] * scale
    gain = gain_columns(mine[2 * col : 2 * col + 16])[0]
    input_ref[...] = own[...] + scale * (total[:col] * gain - unit * mean)
    gain_grad = jnp.sum(total[:col] * unit, axis=1, keepdims=True)
    unused = jnp.zeros_like(gain_grad)
    gain_grad = jnp.transpose(side_lanes(col, 128, [unused, unused, unused, gain_grad]))[0:8]
    gain_grad = fold_lanes(jnp.concatenate([gain_grad, jnp.zeros((8, 64), f32)], axis=1))
    gain_ref[...] = gain_grad
    produced = total[col + 16 :]
    count = produced.shape[0] * 2 // 3
    top = produced[:count]
    rest = jnp.concatenate([produced[count:, :64], produced[count:, 64:]], axis=0)
    rest = jnp.concatenate([rest, jnp.zeros((count, 64), f32)], axis=1)
    slots = count // experts
    for e in range(experts):
        at = slice(e * slots, (e + 1) * slots)
        pieces = [top[at], rest[at]]
        if shares:
            share = shares[0][e].astype(f32)
            if e == 0:
                share = jnp.concatenate([share[:16] + gain_grad, share[16:]], axis=0)
            pieces.append(share)
        ret_ref[e] = jnp.concatenate(pieces, axis=0).astype(bf16)


def share_kernel(slots, came, share_ref):
    total = came[0].astype(f32)
    for e in range(1, came.shape[0]):
        total = total + came[e].astype(f32)
    for e in range(came.shape[0]):
        share_ref[e] = total[2 * slots :].astype(bf16)


def add_returned(slots, blocks, side, gate, residual):
    col = residual.shape[0]
    top = jnp.concatenate([block[:slots] for block in blocks], axis=0).astype(bf16)
    rest = jnp.concatenate([block[slots : 2 * slots] for block in blocks], axis=0).astype(bf16)
    pick = pick_slots(side[0:1, :].astype(jnp.int32), len(blocks) * slots).astype(bf16)
    returned = jnp.concatenate([mm(top, pick, tn), mm(rest, pick, tn)[: col - 128]], axis=0)
    return (residual[...] + gate[0:1, :] * returned).astype(bf16)


def last_kernel(slots, came, side, gate, residual, block_ref):
    blocks = [came[e].astype(f32) for e in range(came.shape[0])]
    block_ref[...] = add_returned(slots, blocks, side, gate, residual)


def turn_kernel(all_in, packed, normed_ref):
    x = jnp.concatenate([all_in[0, i].astype(f32) for i in range(all_in.shape[1])], axis=0)
    gain = all_gains(packed)[0]
    normed_ref[...] = jnp.transpose(x * token_scale(x) * gain).astype(bf16)


def products_kernel(
    late, normed, came, buckets, stats, q_ref, k_ref, v_ref, out_ref, router_ref, table_ref, gains_ref, aux_ref,
):
    groups = came.shape[0]
    col = q_ref.shape[0]
    joined = jnp.concatenate([late[b] for b in range(groups)], axis=1)
    product = mm(joined, normed[...])
    for i, ref in enumerate((q_ref, k_ref, v_ref)):
        ref[...] = product[i * col : (i + 1) * col]

    @pl.when(pl.program_id(0) == 0)
    def _():
        experts = router_ref.shape[0]
        size = col // groups
        shares = [came[b].astype(f32) for b in range(groups)]
        chunk = shares[0].shape[0] - 6 * size
        for b in range(groups):
            out_ref[b * size : (b + 1) * size, :] = unfold_lanes(shares[b][chunk:], 6)
        small = jnp.concatenate([share[:chunk] for share in shares], axis=0)
        gains = unfold_lanes(small[:16], 2)
        gains_ref[...] = gains
        probs = gains[1:2, :experts] + gains[2:3, :experts]
        same = lanes((experts, experts)) == sublanes((experts, experts))
        share = jnp.sum(jnp.where(same, stats[:, 0:1] * probs, 0.0), axis=0, keepdims=True)
        valid_total = 3 * normed.shape[0] // 4
        aux_ref[...] = jnp.sum(share, axis=1, keepdims=True) * (experts / (valid_total * valid_total))
        span = buckets.shape[1]
        hot = (sublanes((table_ref.shape[1], span)) == buckets[...]).astype(f32)
        offsets = unfold_lanes(small[16:32], 2)[:, :span]
        table_ref[...] = mm(offsets, hot, nt, highest)[: table_ref.shape[0]]
        router_ref[...] = unfold_lanes(small[32 : 32 + 6 * experts], 6)


def few_experts():
    return lax.axis_size("expert") <= 8


def shards(
    inputs,
    out_grad,
    lengths,
    routes,
    buckets,
    gain_attn,
    w_query,
    w_key,
    w_value,
    w_output,
    bias_table,
    gain_ffn,
    w_router,
    w_in,
    w_out,
):
    tok, col = inputs.shape
    heads_here = bias_table.shape[1]
    head_size = w_query.shape[1] // heads_here
    width, experts = w_router.shape
    bucket_count = bias_table.shape[0]
    heads = width // col
    groups = lax.axis_size("expert")
    me_head, me_expert = lax.axis_index("head"), lax.axis_index("expert")
    capacity = max(2, (4 * tok + 3 * experts - 1) // (3 * experts))
    slots = -(-(capacity + 1) // 8) * 8
    total = experts * slots
    valid_total = 3 * tok * groups // 4
    scale = head_size ** (-0.5)
    joined = few_experts()
    small_rows = 6 * experts + 32
    chunk = -(-small_rows // (16 * groups)) * 16
    w_in, w_out = w_in[0], w_out[0]
    wq, wk, wv = w_query.T, w_key.T, w_value.T
    routes_row = routes.T
    router_rows = w_router.T
    scalars = jnp.stack([lengths[0], me_head.astype(jnp.int32), me_expert.astype(jnp.int32)])
    buckets_row = buckets[None]

    gains = jnp.concatenate([gain_attn, gain_ffn]).reshape(3, 128)
    gains = jnp.concatenate([inputs.T, out_grad.T, gains, jnp.zeros((13, 128), bf16)], axis=0)
    packed = lax.all_gather(gains, "head")
    if joined:
        all_in = lax.all_gather(inputs.T, ("expert", "head")).reshape(groups, heads, col, tok)
    qkv, weights, attended, branch = call(
        functools.partial(attend_kernel, scale),
        [
            ((3, col, tok), bf16, 1), ((heads_here, tok, tok), f32, 1), ((col, tok), bf16, 1),
            ((heads, col, tok), bf16),
        ],
        scalars, packed, far(wq), far(wk), far(wv), far(w_output), far(buckets_row), far(bias_table.T),
    )

    branch = lax.all_to_all(branch, "head", split_axis=0, concat_axis=0, tiled=True)
    residual, low, side, send = call(
        functools.partial(route_kernel, capacity),
        [((col, tok), f32, 1), ((col, tok), bf16, 1), ((8, tok), f32, 1), ((experts, slots, 2 * col), bf16)],
        scalars, branch, far(inputs.T), far(out_grad.T), far(routes_row),
    )
    quarter = lax.all_to_all(send, "expert", split_axis=0, concat_axis=0, tiled=True)
    quarters = lax.all_gather(quarter.reshape(total, 2 * col), "head")

    back, part, hidden, before_grad, back_rows, rows = call(
        functools.partial(expert_kernel, capacity),
        [((experts * heads, folded_rows(slots), 128), bf16), ((heads, total * 3 // 2, 128), bf16, 1)]
        + [((total, width), bf16, 1)] * 4,
        scalars, quarters, far(packed), far(w_in), far(w_out), far(router_rows),
    )
    came = lax.all_to_all(back, ("expert", "head"), split_axis=0, concat_axis=0, tiled=True)
    grad_own, gate_grad, stats = call(
        functools.partial(collect_kernel, slots),
        [((2 * col, tok), bf16), ((8, tok), f32, 1), ((experts, 128), f32, 1)],
        came, far(side), far(low),
    )
    expert_grad = lax.all_gather(grad_own, "head")

    late, first, residual_grad_own, gate, *shares = call(
        functools.partial(backward_kernel, scale, valid_total),
        [
            ((3 * col, tok), bf16, 1), ((heads, col + 16 + total * 3 // 2, 128), bf16), ((col, tok), f32, 1),
            ((8, tok), f32, 1),
        ]
        + (
            [((groups, chunk + 6 * col // groups, 128), bf16, 1)]
            if joined
            else [((small_rows, 128), f32, 1), ((col, width), f32, 1)]
        ),
        scalars, far(packed), expert_grad, far(gate_grad), far(stats), far(routes_row),
        far(router_rows), far(w_output), far(weights), far(qkv), far(wq), far(wk), far(wv), far(attended),
        far(part),
    )

    if joined:
        late_all = lax.all_gather(late, "expert")

    first = lax.all_to_all(first, "head", split_axis=0, concat_axis=0, tiled=True)
    ret, gain_one_part, input_grad = call(
        first_kernel,
        [
            ((experts, 2 * slots + (shares[0].shape[1] if joined else 0), 128), bf16),
            ((16, 128), f32, 1), ((col, tok), f32, 1),
        ],
        scalars, first, far(packed), far(residual_grad_own), *([far(shares[0])] if joined else []),
    )
    ret = lax.all_to_all(ret, "expert", split_axis=0, concat_axis=0, tiled=True)
    if joined:
        share = call(
            functools.partial(share_kernel, slots), [(shares[0].shape, bf16)], ret
        )[0]
        share = lax.all_to_all(share, "expert", split_axis=0, concat_axis=0, tiled=True)
    block_out = call(
        functools.partial(last_kernel, slots), [((col, tok), bf16, 1)], far(ret), far(side), far(gate), far(residual)
    )[0]
    third = width // 3
    in_weight_grad, out_weight_grad = grid_call(
        weights_kernel,
        3,
        [(((width, width), f32), (third, width), 0)] * 2,
        (rows, (total, third), 1), (hidden, (total, third), 1),
        (before_grad, (total, width), None), (back_rows, (total, width), None),
    )
    if joined:
        (normed_all,) = grid_call(
            turn_kernel,
            groups,
            [(((groups * tok, width), bf16), (tok, width), 0)],
            (all_in, (1, heads, col, tok), 0), (packed, packed.shape, None),
        )
        q_grad, k_grad, v_grad, output_grad, router_grad, table_grad, gain_grads, aux_loss = grid_call(
            products_kernel,
            3,
            [(((col, width), f32), (col, third), 1)] * 3
            + [
                (((col, width), f32), (col, width), None),
                (((experts, width), f32), (experts, width), None),
                (((heads_here, bucket_count), f32), (heads_here, bucket_count), None),
                (((8, 256), f32), (8, 256), None),
                (((1, 1), f32), (1, 1), None),
            ],
            (late_all, late_all.shape, None), (normed_all, (groups * tok, third), 1),
            (share, share.shape, None), (buckets_row, buckets_row.shape, None), (stats, stats.shape, None),
        )
    else:
        gain = packed[:, 2 * col : 2 * col + 3].reshape(heads, 2 * col)[:, :col].reshape(width, 1)
        x = packed[:, :col].reshape(width, tok).astype(f32)
        normed = (x * token_scale(x) * gain.astype(f32)).astype(bf16)
        products = [mm(late[i * col : (i + 1) * col], normed, nt) for i in range(3)]
        q_grad, k_grad, v_grad, sums, gain_one, output_grad = lax.psum(
            products + [shares[0], gain_one_part, shares[1]], "expert"
        )
        router_grad = unfold_lanes(sums[32 : 32 + 6 * experts], 6)
        offsets = unfold_lanes(sums[16:32], 2)[:heads_here, : 2 * tok - 1]
        hot = (buckets[None, :] == jnp.arange(bucket_count)[:, None]).astype(f32)
        table_grad = mm(offsets, hot, nt, highest)
        gain_grads = unfold_lanes(sums[:16] + gain_one, 2)
        probs = gain_grads[1, :experts] + gain_grads[2, :experts]
        aux_loss = experts * jnp.sum(stats[:, 0] * probs) / (valid_total * valid_total)
    return (
        block_out.T,
        input_grad.T,
        aux_loss.reshape(()),
        gain_grads[3, :col],
        q_grad.T,
        k_grad.T,
        v_grad.T,
        output_grad,
        table_grad.T,
        gain_grads[0, :col],
        router_grad.T,
        in_weight_grad[None],
        out_weight_grad[None],
    )


def solution(mesh):
    return jax.shard_map(
        shards,
        mesh=mesh,
        in_specs=(
            P("expert", "head"),
            P("expert", "head"),
            P("expert"),
            P("expert", None),
            P(),
            P("head"),
            P(None, "head"),
            P(None, "head"),
            P(None, "head"),
            P("head", None),
            P(None, "head"),
            P("head"),
            P(),
            P("expert", None, "head"),
            P("expert", "head", None),
        ),
        out_specs=(
            P("expert", "head"),
            P("expert", "head"),
            P(),
            P("head"),
            P(None, "head"),
            P(None, "head"),
            P(None, "head"),
            P("head", None),
            P(None, "head"),
            P("head"),
            P(),
            P("expert", None, "head"),
            P("expert", "head", None),
        ),
        check_vma=False,
    )
```

```python
import functools

import jax
import jax.numpy as jnp
from jax import lax
from jax.experimental import pallas as pl
from jax.experimental.pallas import tpu as pltpu
from jax.sharding import PartitionSpec as P

eps = 1e-06
aux_weight = 0.01
f32 = jnp.float32
bf16 = jnp.bfloat16
gelu_scale = 0.7978845608028654
gelu_cube = 0.044715
highest = lax.Precision.HIGHEST
nt = ((1,), (1,))
tn = ((0,), (0,))


def mm(left, right, dims=((1,), (0,)), precision=None):
    return lax.dot_general(left, right, (dims, ((), ())), precision=precision, preferred_element_type=f32)


def call(body, outs, *args):
    scalar_memory = pl.BlockSpec(memory_space=pltpu.SMEM)
    in_specs = [scalar_memory if a.dtype == jnp.int32 and a.ndim == 1 else pl.BlockSpec() for a in args]
    shapes = []
    for shape, kind, *remote in outs:
        shapes.append(pltpu.HBM(shape, kind) if remote else jax.ShapeDtypeStruct(shape, kind))
    return pl.pallas_call(
        body,
        out_shape=shapes,
        in_specs=in_specs,
        compiler_params=pltpu.CompilerParams(vmem_limit_bytes=40 * 1024 * 1024),
    )(*args)


def far(array):
    return pltpu.with_memory_space_constraint(array, pltpu.HBM)


def tall(ref, first, rows):
    return jnp.concatenate([ref[i, first : first + rows, :].astype(f32) for i in range(ref.shape[0])], axis=0)


def gain_columns(block):
    turned = jnp.transpose(block.astype(f32))
    return [
        jnp.concatenate([turned[:, 0:1], turned[:64, 1:2]], axis=0),
        jnp.concatenate([turned[64:, 1:2], turned[:, 2:3]], axis=0),
    ]


def all_gains(packed):
    first = 2 * packed.shape[2] * 3 // 2
    pairs = [gain_columns(packed[i, first : first + 16, :]) for i in range(packed.shape[0])]
    return [jnp.concatenate([pair[i] for pair in pairs], axis=0) for i in range(2)]


def token_scale(values):
    return lax.rsqrt(jnp.sum(values * values, axis=0, keepdims=True) * (1.0 / values.shape[0]) + eps)


def lanes(shape):
    return lax.broadcasted_iota(jnp.int32, shape, len(shape) - 1)


def sublanes(shape):
    return lax.broadcasted_iota(jnp.int32, shape, len(shape) - 2)


def side_lanes(rows, width, columns):
    spot = lanes((rows, width))
    out = jnp.zeros((rows, width), f32)
    for i, column in enumerate(columns):
        out = jnp.where(spot == i, column, out)
    return out


def side_rows(rows, width, lines):
    spot = sublanes((rows, width))
    out = jnp.zeros((rows, width), f32)
    for i, line in enumerate(lines):
        out = jnp.where(spot == i, line, out)
    return out


def high_low(values, count=2):
    pieces = []
    for _ in range(count):
        piece = values.astype(bf16).astype(f32)
        pieces.append(piece)
        values = values - piece
    return pieces


def softmax(values, axis):
    raised = jnp.exp(values - jnp.max(values, axis=axis, keepdims=True))
    return raised / jnp.sum(raised, axis=axis, keepdims=True)


def gelu_parts(u):
    t = jnp.tanh(gelu_scale * (u + gelu_cube * u * u * u))
    value = 0.5 * u * (1.0 + t)
    slope = 0.5 * (1.0 + t) + 0.5 * u * (1.0 - t * t) * gelu_scale * (1.0 + 3.0 * gelu_cube * u * u)
    return value, slope


def fold_lanes(rows):
    return jnp.concatenate([rows[:, i : i + 128] for i in range(0, rows.shape[1], 128)], axis=0)


def unfold_lanes(rows, pieces):
    size = rows.shape[0] // pieces
    return jnp.concatenate([rows[i * size : (i + 1) * size] for i in range(pieces)], axis=1)


def fold_rest(rest, side):
    groups = [rest[i : i + 8] for i in range(0, rest.shape[0], 8)]
    count = side.shape[1]
    spot = lanes((8, 64))
    last = jnp.zeros((8, 64), f32)
    for g in range(len(groups)):
        for j in range(count):
            last = jnp.where(spot == g * count + j, side[8 * g : 8 * g + 8, j : j + 1], last)
    groups.append(last)
    if len(groups) % 2:
        groups.append(jnp.zeros((8, 64), f32))
    return [jnp.concatenate(groups[i : i + 2], axis=1) for i in range(0, len(groups), 2)]


def unfold_rest(blocks, slots, count):
    halves = []
    for i in range(0, blocks.shape[0], 8):
        halves += [blocks[i : i + 8, :64], blocks[i : i + 8, 64:]]
    number = slots // 8
    side = [halves[number][:, g * count : (g + 1) * count] for g in range(number)]
    return jnp.concatenate(halves[:number], axis=0), jnp.concatenate(side, axis=0)


def folded_rows(slots):
    return slots + 8 * ((slots // 8 + 2) // 2)


def pick_slots(spots, count):
    return sublanes((count, spots.shape[1])) == spots


def attend_kernel(
    scale, scalars, packed, wq, wk, wv, w_output, buckets, table, qkv_ref, weights_ref, attended_ref, branch_ref
):
    heads, tok, _ = weights_ref.shape
    col = wq.shape[0]
    size = col // heads
    x = tall(packed, 0, col)
    normed = (x * token_scale(x) * all_gains(packed)[0]).astype(bf16)
    projected = []
    for i, w in enumerate((wq, wk, wv)):
        rows = mm(w[...], normed).astype(bf16)
        qkv_ref[i] = rows
        projected.append(rows)
    query, key, value = projected
    hot = (sublanes((table.shape[1], 2 * tok - 1)) == buckets[...]).astype(f32)
    offsets = mm(table[...], hot, precision=highest)
    offsets = jnp.concatenate([offsets, jnp.zeros((heads, 1), f32)], axis=1)
    open_keys = lanes((tok, tok)) < scalars[0]
    outs = []
    for h in range(heads):
        at = slice(h * size, (h + 1) * size)
        spread = jnp.broadcast_to(offsets[h : h + 1, :], (tok, 2 * tok))
        bias = pltpu.roll(spread, tok + 1, 1, stride=1, stride_axis=0)[:, :tok]
        scores = mm(query[at], key[at], tn) * scale + bias
        weights = softmax(jnp.where(open_keys, scores, -1000000000.0), 1)
        weights_ref[h] = weights
        outs.append(mm(value[at], weights.astype(bf16), nt))
    attended = jnp.concatenate(outs, axis=0).astype(bf16)
    attended_ref[...] = attended
    branch = mm(w_output[...], attended, tn)
    for i in range(branch_ref.shape[0]):
        branch_ref[i] = branch[i * col : (i + 1) * col].astype(bf16)


def second_norm(residual, gain, w_router):
    scale = token_scale(residual)
    unit = residual * scale
    normed = (unit * gain).astype(bf16)
    return scale, unit, normed, softmax(mm(w_router, normed), 0)


def route_kernel(capacity, scalars, came, inputs, out_grad, routes, residual_ref, low_ref, side_ref, send_ref):
    col, tok = inputs.shape
    experts, slots, _ = send_ref.shape
    residual = inputs[...].astype(f32)
    for i in range(came.shape[0]):
        residual = residual + came[i].astype(f32)
    residual_ref[...] = residual
    low = residual.astype(bf16)
    low_ref[...] = low
    route_hot = (sublanes((experts, tok)) == routes[...]).astype(f32)
    before = (sublanes((tok, tok)) < lanes((tok, tok))).astype(bf16)
    slot = jnp.sum(mm(route_hot.astype(bf16), before) * route_hot, axis=0, keepdims=True)
    spots = routes[...].astype(f32) * slots + slot
    side_ref[...] = side_rows(8, tok, [spots])
    valid = (lanes((1, tok)) < scalars[0]).astype(f32)
    counts = jnp.sum(route_hot * valid, axis=1, keepdims=True)
    pick = pick_slots(spots.astype(jnp.int32), experts * slots).astype(bf16)
    rows = mm(pick, jnp.concatenate([low, out_grad[...]], axis=0), nt)
    spare = (sublanes((slots, 2 * col)) == capacity) & (lanes((slots, 2 * col)) == col)
    for e in range(experts):
        block = rows[e * slots : (e + 1) * slots]
        send_ref[e] = jnp.where(spare, counts[e : e + 1], block).astype(bf16)


def second_gain_row(packed, first):
    pieces = []
    for i in range(packed.shape[0]):
        block = packed[i, first : first + 16, :].astype(f32)
        pieces += [block[1:2, 64:], block[2:3, :]]
    return jnp.concatenate(pieces, axis=1)


def expert_kernel(
    capacity, scalars, quarters, packed, w_in, w_out, w_router,
    back_ref, part_ref, hidden_ref, before_ref, grads_ref, rows_ref,
):
    total = rows_ref.shape[0]
    experts, width = w_router.shape
    heads = part_ref.shape[0]
    col = width // heads
    slots = total // experts
    half = total // 2
    parts = [quarters[i].astype(f32) for i in range(heads)]
    residual = jnp.concatenate([block[:, :col] for block in parts], axis=1)
    grads = jnp.concatenate([block[:, col:] for block in parts], axis=1)
    inverse = lax.rsqrt(jnp.sum(residual * residual, axis=1, keepdims=True) * (1.0 / width) + eps)
    rows = (residual * inverse * second_gain_row(packed, 2 * col)).astype(bf16)
    rows_ref[...] = rows
    hidden, slope = gelu_parts(mm(rows, w_in[...]))
    hidden = hidden.astype(bf16)
    hidden_ref[...] = hidden
    produced = mm(hidden, w_out[...])
    for i in range(heads):
        mine = produced[:, i * col : (i + 1) * col]
        rest = mine[:, 128:]
        part_ref[i] = jnp.concatenate(
            [mine[:, :128], jnp.concatenate([rest[:half], rest[half:]], axis=1)], axis=0
        ).astype(bf16)
    probs = softmax(mm(rows, w_router[...], nt), 1)
    gate = jnp.sum(jnp.where(lanes((total, experts)) == scalars[2], probs, 0.0), axis=1, keepdims=True)
    back = (gate * grads).astype(bf16)
    grads_ref[...] = back
    before = (mm(back, w_out[...], nt) * slope).astype(bf16)
    before_ref[...] = before
    rows_grad = mm(before, w_in[...], nt)
    gate_grad = jnp.sum(grads * produced, axis=1, keepdims=True)
    stats = jnp.zeros((1, 128), f32)
    for b in range(experts):
        stats = stats + grads[b * slots + capacity : b * slots + capacity + 1, :128]
    side = side_lanes(total, 4, high_low(gate_grad) + high_low(stats[:, 0:1]))
    for b in range(experts):
        at = slice(b * slots, (b + 1) * slots)
        for i in range(heads):
            mine = rows_grad[at, i * col : (i + 1) * col]
            back_ref[b * heads + i] = jnp.concatenate(
                [mine[:, :128]] + fold_rest(mine[:, 128:], side[at]), axis=0
            ).astype(bf16)


def weights_kernel(rows_ref, hidden, before, grads, in_ref, out_ref):
    in_ref[...] = mm(rows_ref[...], before[...], tn)
    out_ref[...] = mm(hidden[...], grads[...], tn)


def collect_kernel(slots, came, side, low, grad_ref, gate_ref, stats_ref):
    col, tok = low.shape
    experts = stats_ref.shape[0]
    heads = came.shape[0] // experts
    tops, rests, scalars = [], [], []
    for e in range(experts):
        total = came[e * heads].astype(f32)
        for i in range(1, heads):
            total = total + came[e * heads + i].astype(f32)
        rest, columns = unfold_rest(total[slots:], slots, 4)
        tops.append(total[:slots])
        rests.append(rest)
        scalars.append(columns)
    counts = jnp.concatenate([columns[0:1] for columns in scalars], axis=0) * (1.0 / heads)
    pick = pick_slots(side[0:1, :].astype(jnp.int32), experts * slots)
    for first, pieces in ((0, tops), (128, rests)):
        block = jnp.concatenate(pieces, axis=0).astype(bf16)
        grad_ref[first : min(first + 128, col), :] = mm(block, pick.astype(bf16), tn).astype(bf16)
    grad_ref[col:, :] = low[...]
    gate = mm(jnp.concatenate(scalars, axis=0), pick.astype(f32), tn, highest)
    gate_ref[...] = jnp.broadcast_to(gate[0:1] + gate[1:2], gate_ref.shape)
    stats_ref[...] = side_lanes(experts, 128, [counts[:, 2:3] + counts[:, 3:4]])


def backward_kernel(
    scale, valid_total, scalars, packed, expert_grad, gate_grad, stats, routes, w_router, w_output, weights_ref,
    qkv, wq, wk, wv, attended, part, late_ref, first_ref, own_ref, gate_ref, *share_refs,
):
    tok = routes.shape[1]
    heads_here = weights_ref.shape[0]
    blocks, col = packed.shape[0], wq.shape[0]
    experts, width = w_router.shape
    size = col // heads_here
    gain_one, gain_two = all_gains(packed)
    residual = tall(expert_grad, col, col)
    scale_two, unit, normed, router = second_norm(residual, gain_two, w_router[...])
    valid = (lanes((1, tok)) < scalars[0]).astype(f32)
    route_hot = (sublanes((experts, tok)) == routes[...]).astype(f32)
    fraction = stats[:, 0:1] * (aux_weight * experts / (valid_total * valid_total))
    gate = jnp.sum(router * route_hot, axis=0, keepdims=True)
    gate_ref[...] = jnp.broadcast_to(gate, gate_ref.shape)
    prob_grad = route_hot * gate_grad[0:1, :] + fraction * valid
    logit_grad = router * (prob_grad - jnp.sum(router * prob_grad, axis=0, keepdims=True))
    logit_grad = logit_grad.astype(bf16)
    normed_grad = mm(w_router[...], logit_grad, tn) + tall(expert_grad, 0, col)
    unit_grad = normed_grad * gain_two
    mean = jnp.sum(unit_grad * unit, axis=0, keepdims=True) * (1.0 / width)
    residual_grad = tall(packed, col, col) + scale_two * (unit_grad - unit * mean)
    branch = residual_grad.astype(bf16)
    attended_grad = mm(w_output[...], branch).astype(bf16)
    flip = (lanes((tok, tok)) + sublanes((tok, tok)) == tok - 1).astype(bf16)
    query, key, value = qkv[0], qkv[1], qkv[2]
    grads = [[], [], []]
    offsets = []
    for h in range(heads_here):
        at = slice(h * size, (h + 1) * size)
        out = attended_grad[at]
        weights = weights_ref[h]
        mass = mm(out, value[at], tn)
        score = weights * (mass - jnp.sum(weights * mass, axis=1, keepdims=True))
        score = score.astype(bf16)
        grads[0].append(mm(key[at], score, nt) * scale)
        grads[1].append(mm(query[at], score) * scale)
        grads[2].append(mm(out, weights.astype(bf16)))
        flipped = jnp.concatenate([mm(flip, score), jnp.zeros((tok, tok), f32)], axis=1)
        rolled = pltpu.roll(flipped, 0, 1, stride=1, stride_axis=0)
        offsets.append(jnp.sum(rolled, axis=0, keepdims=True))
    first = jnp.zeros((width, tok), f32)
    row = jnp.zeros((1, tok), f32)
    for i, w in enumerate((wq, wk, wv)):
        low = jnp.concatenate(grads[i], axis=0).astype(bf16)
        late_ref[i * col : (i + 1) * col, :] = low
        first = first + mm(w[...], low, tn)
        row = row + jnp.sum(low.astype(f32) * qkv[i].astype(f32), axis=0, keepdims=True)
    side = side_rows(16, tok, high_low(row))
    for i in range(blocks):
        at = slice(i * col, (i + 1) * col)
        first_ref[i, : col + 16, :] = jnp.concatenate([first[at], side], axis=0).astype(bf16)
        first_ref[i, col + 16 :, :] = part[i]

    product = mm(attended[...], branch, nt)
    gain_two_grad = jnp.sum(normed_grad * unit, axis=1, keepdims=True)
    gains = jnp.zeros((col, 1), f32)
    own = jnp.zeros((col, tok), f32)
    for i in range(blocks):
        at = slice(i * col, (i + 1) * col)
        gains = jnp.where(scalars[1] == i, gain_two_grad[at], gains)
        own = jnp.where(scalars[1] == i, residual_grad[at], own)
    own_ref[...] = own
    probs = jnp.sum(router * valid, axis=1, keepdims=True)
    if experts < col:
        probs = jnp.concatenate([probs, jnp.zeros((col - experts, 1), f32)], axis=0)
    gains = jnp.transpose(side_lanes(col, 128, [gains] + high_low(probs)))[0:8]
    router_grad = mm(logit_grad, normed, nt)
    offsets = jnp.concatenate(offsets, axis=0)
    offsets = jnp.concatenate([offsets, jnp.zeros((8 - heads_here, 2 * tok), f32)], axis=0)
    gains = jnp.concatenate([gains, jnp.zeros((8, 64), f32)], axis=1)
    pieces = [fold_lanes(gains), fold_lanes(offsets), fold_lanes(router_grad)]
    if len(share_refs) == 2:
        share_refs[0][...] = jnp.concatenate(pieces, axis=0)
        share_refs[1][...] = product
    else:
        share_ref = share_refs[0]
        groups = share_ref.shape[0]
        size = col // groups
        chunk = share_ref.shape[1] - 6 * size
        small = jnp.concatenate(pieces + [jnp.zeros((groups * chunk - 6 * experts - 32, 128), f32)], axis=0)
        for b in range(groups):
            share_ref[b] = jnp.concatenate(
                [small[b * chunk : (b + 1) * chunk], fold_lanes(product[b * size : (b + 1) * size])], axis=0
            ).astype(bf16)


def first_kernel(scalars, came, packed, own, *refs):
    shares, (ret_ref, gain_ref, input_ref) = refs[:-3], refs[-3:]
    col, tok = own.shape
    heads = came.shape[0]
    experts = ret_ref.shape[0]
    total = came[0].astype(f32)
    for i in range(1, heads):
        total = total + came[i].astype(f32)
    mean = (total[col : col + 1] + total[col + 1 : col + 2]) * (1.0 / (heads * col))
    scale = token_scale(tall(packed, 0, col))
    mine = packed[0].astype(f32)
    for i in range(1, heads):
        mine = jnp.where(scalars[1] == i, packed[i].astype(f32), mine)
    unit = mine[:col] * scale
    gain = gain_columns(mine[2 * col : 2 * col + 16])[0]
    input_ref[...] = own[...] + scale * (total[:col] * gain - unit * mean)
    gain_grad = jnp.sum(total[:col] * unit, axis=1, keepdims=True)
    unused = jnp.zeros_like(gain_grad)
    gain_grad = jnp.transpose(side_lanes(col, 128, [unused, unused, unused, gain_grad]))[0:8]
    gain_grad = fold_lanes(jnp.concatenate([gain_grad, jnp.zeros((8, 64), f32)], axis=1))
    gain_ref[...] = gain_grad
    produced = total[col + 16 :]
    count = produced.shape[0] * 2 // 3
    top = produced[:count]
    rest = jnp.concatenate([produced[count:, :64], produced[count:, 64:]], axis=0)
    rest = jnp.concatenate([rest, jnp.zeros((count, 64), f32)], axis=1)
    slots = count // experts
    for e in range(experts):
        at = slice(e * slots, (e + 1) * slots)
        pieces = [top[at], rest[at]]
        if shares:
            share = shares[0][e].astype(f32)
            if e == 0:
                share = jnp.concatenate([share[:16] + gain_grad, share[16:]], axis=0)
            pieces.append(share)
        ret_ref[e] = jnp.concatenate(pieces, axis=0).astype(bf16)


def share_kernel(slots, came, share_ref):
    total = came[0].astype(f32)
    for e in range(1, came.shape[0]):
        total = total + came[e].astype(f32)
    for e in range(came.shape[0]):
        share_ref[e] = total[2 * slots :].astype(bf16)


def add_returned(slots, blocks, side, gate, residual):
    col = residual.shape[0]
    top = jnp.concatenate([block[:slots] for block in blocks], axis=0).astype(bf16)
    rest = jnp.concatenate([block[slots : 2 * slots] for block in blocks], axis=0).astype(bf16)
    pick = pick_slots(side[0:1, :].astype(jnp.int32), len(blocks) * slots).astype(bf16)
    returned = jnp.concatenate([mm(top, pick, tn), mm(rest, pick, tn)[: col - 128]], axis=0)
    return (residual[...] + gate[0:1, :] * returned).astype(bf16)


def last_kernel(slots, came, side, gate, residual, block_ref):
    blocks = [came[e].astype(f32) for e in range(came.shape[0])]
    block_ref[...] = add_returned(slots, blocks, side, gate, residual)


def turn_kernel(all_in, packed, normed_ref):
    groups, heads, col, tok = all_in.shape
    gain = all_gains(packed)[0]
    for b in range(groups):
        x = jnp.concatenate([all_in[b, i].astype(f32) for i in range(heads)], axis=0)
        normed_ref[b * tok : (b + 1) * tok, :] = jnp.transpose(x * token_scale(x) * gain).astype(bf16)


def products_kernel(
    late, normed, came, buckets, stats, q_ref, k_ref, v_ref, out_ref, router_ref, table_ref, gains_ref, aux_ref,
):
    groups = came.shape[0]
    col = q_ref.shape[0]
    experts = router_ref.shape[0]
    size = col // groups
    shares = [came[b].astype(f32) for b in range(groups)]
    chunk = shares[0].shape[0] - 6 * size
    for b in range(groups):
        out_ref[b * size : (b + 1) * size, :] = unfold_lanes(shares[b][chunk:], 6)
    joined = jnp.concatenate([late[b] for b in range(groups)], axis=1)
    product = mm(joined, normed[...])
    for i, ref in enumerate((q_ref, k_ref, v_ref)):
        ref[...] = product[i * col : (i + 1) * col]
    small = jnp.concatenate([share[:chunk] for share in shares], axis=0)
    gains = unfold_lanes(small[:16], 2)
    gains_ref[...] = gains
    probs = gains[1:2, :experts] + gains[2:3, :experts]
    same = lanes((experts, experts)) == sublanes((experts, experts))
    share = jnp.sum(jnp.where(same, stats[:, 0:1] * probs, 0.0), axis=0, keepdims=True)
    valid_total = 3 * normed.shape[0] // 4
    aux_ref[...] = jnp.sum(share, axis=1, keepdims=True) * (experts / (valid_total * valid_total))
    span = buckets.shape[1]
    hot = (sublanes((table_ref.shape[1], span)) == buckets[...]).astype(f32)
    offsets = unfold_lanes(small[16:32], 2)[:, :span]
    table_ref[...] = mm(offsets, hot, nt, highest)[: table_ref.shape[0]]
    router_ref[...] = unfold_lanes(small[32 : 32 + 6 * experts], 6)


def few_experts():
    return lax.axis_size("expert") <= 8


def shards(
    inputs,
    out_grad,
    lengths,
    routes,
    buckets,
    gain_attn,
    w_query,
    w_key,
    w_value,
    w_output,
    bias_table,
    gain_ffn,
    w_router,
    w_in,
    w_out,
):
    tok, col = inputs.shape
    heads_here = bias_table.shape[1]
    head_size = w_query.shape[1] // heads_here
    width, experts = w_router.shape
    bucket_count = bias_table.shape[0]
    heads = width // col
    groups = lax.axis_size("expert")
    me_head, me_expert = lax.axis_index("head"), lax.axis_index("expert")
    capacity = max(2, (4 * tok + 3 * experts - 1) // (3 * experts))
    slots = -(-(capacity + 1) // 8) * 8
    total = experts * slots
    valid_total = 3 * tok * groups // 4
    scale = head_size ** (-0.5)
    joined = few_experts()
    small_rows = 6 * experts + 32
    chunk = -(-small_rows // (16 * groups)) * 16
    w_in, w_out = w_in[0], w_out[0]
    wq, wk, wv = w_query.T, w_key.T, w_value.T
    routes_row = routes.T
    router_rows = w_router.T
    scalars = jnp.stack([lengths[0], me_head.astype(jnp.int32), me_expert.astype(jnp.int32)])
    buckets_row = buckets[None]

    gains = jnp.concatenate([gain_attn, gain_ffn]).reshape(3, 128)
    gains = jnp.concatenate([inputs.T, out_grad.T, gains, jnp.zeros((13, 128), bf16)], axis=0)
    packed = lax.all_gather(gains, "head")
    if joined:
        all_in = lax.all_gather(inputs.T, ("expert", "head")).reshape(groups, heads, col, tok)
    qkv, weights, attended, branch = call(
        functools.partial(attend_kernel, scale),
        [
            ((3, col, tok), bf16, 1), ((heads_here, tok, tok), f32, 1), ((col, tok), bf16, 1),
            ((heads, col, tok), bf16),
        ],
        scalars, packed, far(wq), far(wk), far(wv), far(w_output), far(buckets_row), far(bias_table.T),
    )

    branch = lax.all_to_all(branch, "head", split_axis=0, concat_axis=0, tiled=True)
    residual, low, side, send = call(
        functools.partial(route_kernel, capacity),
        [((col, tok), f32, 1), ((col, tok), bf16, 1), ((8, tok), f32, 1), ((experts, slots, 2 * col), bf16)],
        scalars, branch, far(inputs.T), far(out_grad.T), far(routes_row),
    )
    quarter = lax.all_to_all(send, "expert", split_axis=0, concat_axis=0, tiled=True)
    quarters = lax.all_gather(quarter.reshape(total, 2 * col), "head")

    back, part, hidden, before_grad, back_rows, rows = call(
        functools.partial(expert_kernel, capacity),
        [((experts * heads, folded_rows(slots), 128), bf16), ((heads, total * 3 // 2, 128), bf16, 1)]
        + [((total, width), bf16, 1)] * 4,
        scalars, quarters, far(packed), far(w_in), far(w_out), far(router_rows),
    )
    came = lax.all_to_all(back, ("expert", "head"), split_axis=0, concat_axis=0, tiled=True)
    grad_own, gate_grad, stats = call(
        functools.partial(collect_kernel, slots),
        [((2 * col, tok), bf16), ((8, tok), f32, 1), ((experts, 128), f32, 1)],
        came, far(side), far(low),
    )
    expert_grad = lax.all_gather(grad_own, "head")

    late, first, residual_grad_own, gate, *shares = call(
        functools.partial(backward_kernel, scale, valid_total),
        [
            ((3 * col, tok), bf16, 1), ((heads, col + 16 + total * 3 // 2, 128), bf16), ((col, tok), f32, 1),
            ((8, tok), f32, 1),
        ]
        + (
            [((groups, chunk + 6 * col // groups, 128), bf16, 1)]
            if joined
            else [((small_rows, 128), f32, 1), ((col, width), f32, 1)]
        ),
        scalars, far(packed), expert_grad, far(gate_grad), far(stats), far(routes_row),
        far(router_rows), far(w_output), far(weights), far(qkv), far(wq), far(wk), far(wv), far(attended),
        far(part),
    )

    if joined:
        late_all = lax.all_gather(late, "expert")

    first = lax.all_to_all(first, "head", split_axis=0, concat_axis=0, tiled=True)
    in_weight_grad, out_weight_grad = call(
        weights_kernel, [((width, width), f32, 1)] * 2, far(rows), far(hidden), far(before_grad), far(back_rows)
    )
    first, in_weight_grad, out_weight_grad = lax.optimization_barrier((first, in_weight_grad, out_weight_grad))
    ret, gain_one_part, input_grad = call(
        first_kernel,
        [
            ((experts, 2 * slots + (shares[0].shape[1] if joined else 0), 128), bf16),
            ((16, 128), f32, 1), ((col, tok), f32, 1),
        ],
        scalars, first, far(packed), far(residual_grad_own), *([far(shares[0])] if joined else []),
    )
    ret = lax.all_to_all(ret, "expert", split_axis=0, concat_axis=0, tiled=True)
    if joined:
        normed_all = call(turn_kernel, [((groups * tok, width), bf16, 1)], far(all_in), far(packed))[0]
        ret, normed_all = lax.optimization_barrier((ret, normed_all))
        share = call(
            functools.partial(share_kernel, slots), [(shares[0].shape, bf16)], ret
        )[0]
        share = lax.all_to_all(share, "expert", split_axis=0, concat_axis=0, tiled=True)
    block_out = call(
        functools.partial(last_kernel, slots), [((col, tok), bf16, 1)], far(ret), far(side), far(gate), far(residual)
    )[0]
    if joined:
        q_grad, k_grad, v_grad, output_grad, router_grad, table_grad, gain_grads, aux_loss = call(
            products_kernel,
            [((col, width), f32, 1)] * 4
            + [((experts, width), f32), ((heads_here, bucket_count), f32), ((8, 256), f32), ((1, 1), f32)],
            far(late_all), far(normed_all), share, far(buckets_row), far(stats),
        )
    else:
        gain = packed[:, 2 * col : 2 * col + 3].reshape(heads, 2 * col)[:, :col].reshape(width, 1)
        x = packed[:, :col].reshape(width, tok).astype(f32)
        normed = (x * token_scale(x) * gain.astype(f32)).astype(bf16)
        products = [mm(late[i * col : (i + 1) * col], normed, nt) for i in range(3)]
        q_grad, k_grad, v_grad, sums, gain_one, output_grad = lax.psum(
            products + [shares[0], gain_one_part, shares[1]], "expert"
        )
        router_grad = unfold_lanes(sums[32 : 32 + 6 * experts], 6)
        offsets = unfold_lanes(sums[16:32], 2)[:heads_here, : 2 * tok - 1]
        hot = (buckets[None, :] == jnp.arange(bucket_count)[:, None]).astype(f32)
        table_grad = mm(offsets, hot, nt, highest)
        gain_grads = unfold_lanes(sums[:16] + gain_one, 2)
        probs = gain_grads[1, :experts] + gain_grads[2, :experts]
        aux_loss = experts * jnp.sum(stats[:, 0] * probs) / (valid_total * valid_total)
    return (
        block_out.T,
        input_grad.T,
        aux_loss.reshape(()),
        gain_grads[3, :col],
        q_grad.T,
        k_grad.T,
        v_grad.T,
        output_grad,
        table_grad.T,
        gain_grads[0, :col],
        router_grad.T,
        in_weight_grad[None],
        out_weight_grad[None],
    )


def solution(mesh):
    return jax.shard_map(
        shards,
        mesh=mesh,
        in_specs=(
            P("expert", "head"),
            P("expert", "head"),
            P("expert"),
            P("expert", None),
            P(),
            P("head"),
            P(None, "head"),
            P(None, "head"),
            P(None, "head"),
            P("head", None),
            P(None, "head"),
            P("head"),
            P(),
            P("expert", None, "head"),
            P("expert", "head", None),
        ),
        out_specs=(
            P("expert", "head"),
            P("expert", "head"),
            P(),
            P("head"),
            P(None, "head"),
            P(None, "head"),
            P(None, "head"),
            P("head", None),
            P(None, "head"),
            P("head"),
            P(),
            P("expert", None, "head"),
            P("expert", "head", None),
        ),
        check_vma=False,
    )
```

```python
import functools

import jax
import jax.numpy as jnp
from jax import lax
from jax.experimental import pallas as pl
from jax.experimental.pallas import tpu as pltpu
from jax.sharding import PartitionSpec as P

eps = 1e-06
aux_weight = 0.01
f32 = jnp.float32
bf16 = jnp.bfloat16
gelu_scale = 0.7978845608028654
gelu_cube = 0.044715
highest = lax.Precision.HIGHEST
nt = ((1,), (1,))
tn = ((0,), (0,))


def mm(left, right, dims=((1,), (0,)), precision=None):
    return lax.dot_general(left, right, (dims, ((), ())), precision=precision, preferred_element_type=f32)


def call(body, outs, *args):
    scalar_memory = pl.BlockSpec(memory_space=pltpu.SMEM)
    in_specs = [scalar_memory if a.dtype == jnp.int32 and a.ndim == 1 else pl.BlockSpec() for a in args]
    shapes = []
    for shape, kind, *remote in outs:
        shapes.append(pltpu.HBM(shape, kind) if remote else jax.ShapeDtypeStruct(shape, kind))
    return pl.pallas_call(
        body,
        out_shape=shapes,
        in_specs=in_specs,
        compiler_params=pltpu.CompilerParams(vmem_limit_bytes=40 * 1024 * 1024),
    )(*args)


def far(array):
    return pltpu.with_memory_space_constraint(array, pltpu.HBM)


def tall(ref, first, rows):
    return jnp.concatenate([ref[i, first : first + rows, :].astype(f32) for i in range(ref.shape[0])], axis=0)


def gain_columns(block):
    turned = jnp.transpose(block.astype(f32))
    return [
        jnp.concatenate([turned[:, 0:1], turned[:64, 1:2]], axis=0),
        jnp.concatenate([turned[64:, 1:2], turned[:, 2:3]], axis=0),
    ]


def all_gains(packed):
    first = 2 * packed.shape[2] * 3 // 2
    pairs = [gain_columns(packed[i, first : first + 16, :]) for i in range(packed.shape[0])]
    return [jnp.concatenate([pair[i] for pair in pairs], axis=0) for i in range(2)]


def token_scale(values):
    return lax.rsqrt(jnp.sum(values * values, axis=0, keepdims=True) * (1.0 / values.shape[0]) + eps)


def lanes(shape):
    return lax.broadcasted_iota(jnp.int32, shape, len(shape) - 1)


def sublanes(shape):
    return lax.broadcasted_iota(jnp.int32, shape, len(shape) - 2)


def side_lanes(rows, width, columns):
    spot = lanes((rows, width))
    out = jnp.zeros((rows, width), f32)
    for i, column in enumerate(columns):
        out = jnp.where(spot == i, column, out)
    return out


def side_rows(rows, width, lines):
    spot = sublanes((rows, width))
    out = jnp.zeros((rows, width), f32)
    for i, line in enumerate(lines):
        out = jnp.where(spot == i, line, out)
    return out


def high_low(values, count=2):
    pieces = []
    for _ in range(count):
        piece = values.astype(bf16).astype(f32)
        pieces.append(piece)
        values = values - piece
    return pieces


def softmax(values, axis):
    raised = jnp.exp(values - jnp.max(values, axis=axis, keepdims=True))
    return raised / jnp.sum(raised, axis=axis, keepdims=True)


def gelu_parts(u):
    t = jnp.tanh(gelu_scale * (u + gelu_cube * u * u * u))
    value = 0.5 * u * (1.0 + t)
    slope = 0.5 * (1.0 + t) + 0.5 * u * (1.0 - t * t) * gelu_scale * (1.0 + 3.0 * gelu_cube * u * u)
    return value, slope


def fold_lanes(rows):
    return jnp.concatenate([rows[:, i : i + 128] for i in range(0, rows.shape[1], 128)], axis=0)


def unfold_lanes(rows, pieces):
    size = rows.shape[0] // pieces
    return jnp.concatenate([rows[i * size : (i + 1) * size] for i in range(pieces)], axis=1)


def fold_rest(rest, side):
    groups = [rest[i : i + 8] for i in range(0, rest.shape[0], 8)]
    count = side.shape[1]
    spot = lanes((8, 64))
    last = jnp.zeros((8, 64), f32)
    for g in range(len(groups)):
        for j in range(count):
            last = jnp.where(spot == g * count + j, side[8 * g : 8 * g + 8, j : j + 1], last)
    groups.append(last)
    if len(groups) % 2:
        groups.append(jnp.zeros((8, 64), f32))
    return [jnp.concatenate(groups[i : i + 2], axis=1) for i in range(0, len(groups), 2)]


def unfold_rest(blocks, slots, count):
    halves = []
    for i in range(0, blocks.shape[0], 8):
        halves += [blocks[i : i + 8, :64], blocks[i : i + 8, 64:]]
    number = slots // 8
    side = [halves[number][:, g * count : (g + 1) * count] for g in range(number)]
    return jnp.concatenate(halves[:number], axis=0), jnp.concatenate(side, axis=0)


def folded_rows(slots):
    return slots + 8 * ((slots // 8 + 2) // 2)


def pick_slots(spots, count):
    return sublanes((count, spots.shape[1])) == spots


def attend_kernel(
    scale, scalars, packed, wq, wk, wv, w_output, buckets, table, qkv_ref, weights_ref, attended_ref, branch_ref
):
    heads, tok, _ = weights_ref.shape
    col = wq.shape[0]
    size = col // heads
    x = tall(packed, 0, col)
    normed = (x * token_scale(x) * all_gains(packed)[0]).astype(bf16)
    projected = []
    for i, w in enumerate((wq, wk, wv)):
        rows = mm(w[...], normed).astype(bf16)
        qkv_ref[i] = rows
        projected.append(rows)
    query, key, value = projected
    hot = (sublanes((table.shape[1], 2 * tok - 1)) == buckets[...]).astype(f32)
    offsets = mm(table[...], hot, precision=highest)
    offsets = jnp.concatenate([offsets, jnp.zeros((heads, 1), f32)], axis=1)
    open_keys = lanes((tok, tok)) < scalars[0]
    outs = []
    for h in range(heads):
        at = slice(h * size, (h + 1) * size)
        spread = jnp.broadcast_to(offsets[h : h + 1, :], (tok, 2 * tok))
        bias = pltpu.roll(spread, tok + 1, 1, stride=1, stride_axis=0)[:, :tok]
        scores = mm(query[at], key[at], tn) * scale + bias
        weights = softmax(jnp.where(open_keys, scores, -1000000000.0), 1)
        weights_ref[h] = weights
        outs.append(mm(value[at], weights.astype(bf16), nt))
    attended = jnp.concatenate(outs, axis=0).astype(bf16)
    attended_ref[...] = attended
    branch = mm(w_output[...], attended, tn)
    for i in range(branch_ref.shape[0]):
        branch_ref[i] = branch[i * col : (i + 1) * col].astype(bf16)


def second_norm(residual, gain, w_router):
    scale = token_scale(residual)
    unit = residual * scale
    normed = (unit * gain).astype(bf16)
    return scale, unit, normed, softmax(mm(w_router, normed), 0)


def route_kernel(capacity, scalars, came, inputs, out_grad, routes, residual_ref, low_ref, side_ref, send_ref):
    col, tok = inputs.shape
    experts, slots, _ = send_ref.shape
    residual = inputs[...].astype(f32)
    for i in range(came.shape[0]):
        residual = residual + came[i].astype(f32)
    residual_ref[...] = residual
    low = residual.astype(bf16)
    low_ref[...] = low
    route_hot = (sublanes((experts, tok)) == routes[...]).astype(f32)
    before = (sublanes((tok, tok)) < lanes((tok, tok))).astype(bf16)
    slot = jnp.sum(mm(route_hot.astype(bf16), before) * route_hot, axis=0, keepdims=True)
    spots = routes[...].astype(f32) * slots + slot
    side_ref[...] = side_rows(8, tok, [spots])
    valid = (lanes((1, tok)) < scalars[0]).astype(f32)
    counts = jnp.sum(route_hot * valid, axis=1, keepdims=True)
    pick = pick_slots(spots.astype(jnp.int32), experts * slots).astype(bf16)
    rows = mm(pick, jnp.concatenate([low, out_grad[...]], axis=0), nt)
    spare = (sublanes((slots, 2 * col)) == capacity) & (lanes((slots, 2 * col)) == col)
    for e in range(experts):
        block = rows[e * slots : (e + 1) * slots]
        send_ref[e] = jnp.where(spare, counts[e : e + 1], block).astype(bf16)


def second_gain_row(packed, first):
    pieces = []
    for i in range(packed.shape[0]):
        block = packed[i, first : first + 16, :].astype(f32)
        pieces += [block[1:2, 64:], block[2:3, :]]
    return jnp.concatenate(pieces, axis=1)


def expert_kernel(
    capacity, scalars, quarters, packed, w_in, w_out, w_router,
    back_ref, part_ref, hidden_ref, before_ref, grads_ref, rows_ref,
):
    total = rows_ref.shape[0]
    experts, width = w_router.shape
    heads = part_ref.shape[0]
    col = width // heads
    slots = total // experts
    half = total // 2
    parts = [quarters[i].astype(f32) for i in range(heads)]
    residual = jnp.concatenate([block[:, :col] for block in parts], axis=1)
    grads = jnp.concatenate([block[:, col:] for block in parts], axis=1)
    inverse = lax.rsqrt(jnp.sum(residual * residual, axis=1, keepdims=True) * (1.0 / width) + eps)
    rows = (residual * inverse * second_gain_row(packed, 2 * col)).astype(bf16)
    rows_ref[...] = rows
    hidden, slope = gelu_parts(mm(rows, w_in[...]))
    hidden = hidden.astype(bf16)
    hidden_ref[...] = hidden
    produced = mm(hidden, w_out[...])
    for i in range(heads):
        mine = produced[:, i * col : (i + 1) * col]
        rest = mine[:, 128:]
        part_ref[i] = jnp.concatenate(
            [mine[:, :128], jnp.concatenate([rest[:half], rest[half:]], axis=1)], axis=0
        ).astype(bf16)
    probs = softmax(mm(rows, w_router[...], nt), 1)
    gate = jnp.sum(jnp.where(lanes((total, experts)) == scalars[2], probs, 0.0), axis=1, keepdims=True)
    back = (gate * grads).astype(bf16)
    grads_ref[...] = back
    before = (mm(back, w_out[...], nt) * slope).astype(bf16)
    before_ref[...] = before
    rows_grad = mm(before, w_in[...], nt)
    gate_grad = jnp.sum(grads * produced, axis=1, keepdims=True)
    stats = jnp.zeros((1, 128), f32)
    for b in range(experts):
        stats = stats + grads[b * slots + capacity : b * slots + capacity + 1, :128]
    side = side_lanes(total, 4, high_low(gate_grad) + high_low(stats[:, 0:1]))
    for b in range(experts):
        at = slice(b * slots, (b + 1) * slots)
        for i in range(heads):
            mine = rows_grad[at, i * col : (i + 1) * col]
            back_ref[b * heads + i] = jnp.concatenate(
                [mine[:, :128]] + fold_rest(mine[:, 128:], side[at]), axis=0
            ).astype(bf16)


def weights_kernel(rows_ref, hidden, before, grads, in_ref, out_ref):
    in_ref[...] = mm(rows_ref[...], before[...], tn)
    out_ref[...] = mm(hidden[...], grads[...], tn)


def collect_kernel(slots, came, side, low, grad_ref, gate_ref, stats_ref):
    col, tok = low.shape
    experts = stats_ref.shape[0]
    heads = came.shape[0] // experts
    tops, rests, scalars = [], [], []
    for e in range(experts):
        total = came[e * heads].astype(f32)
        for i in range(1, heads):
            total = total + came[e * heads + i].astype(f32)
        rest, columns = unfold_rest(total[slots:], slots, 4)
        tops.append(total[:slots])
        rests.append(rest)
        scalars.append(columns)
    counts = jnp.concatenate([columns[0:1] for columns in scalars], axis=0) * (1.0 / heads)
    pick = pick_slots(side[0:1, :].astype(jnp.int32), experts * slots)
    for first, pieces in ((0, tops), (128, rests)):
        block = jnp.concatenate(pieces, axis=0).astype(bf16)
        grad_ref[first : min(first + 128, col), :] = mm(block, pick.astype(bf16), tn).astype(bf16)
    grad_ref[col:, :] = low[...]
    gate = mm(jnp.concatenate(scalars, axis=0), pick.astype(f32), tn, highest)
    gate_ref[...] = jnp.broadcast_to(gate[0:1] + gate[1:2], gate_ref.shape)
    stats_ref[...] = side_lanes(experts, 128, [counts[:, 2:3] + counts[:, 3:4]])


def backward_kernel(
    scale, valid_total, scalars, packed, expert_grad, gate_grad, stats, routes, w_router, w_output, weights_ref,
    qkv, wq, wk, wv, attended, part, late_ref, first_ref, own_ref, gate_ref, *share_refs,
):
    tok = routes.shape[1]
    heads_here = weights_ref.shape[0]
    blocks, col = packed.shape[0], wq.shape[0]
    experts, width = w_router.shape
    size = col // heads_here
    gain_one, gain_two = all_gains(packed)
    residual = tall(expert_grad, col, col)
    scale_two, unit, normed, router = second_norm(residual, gain_two, w_router[...])
    valid = (lanes((1, tok)) < scalars[0]).astype(f32)
    route_hot = (sublanes((experts, tok)) == routes[...]).astype(f32)
    fraction = stats[:, 0:1] * (aux_weight * experts / (valid_total * valid_total))
    gate = jnp.sum(router * route_hot, axis=0, keepdims=True)
    gate_ref[...] = jnp.broadcast_to(gate, gate_ref.shape)
    prob_grad = route_hot * gate_grad[0:1, :] + fraction * valid
    logit_grad = router * (prob_grad - jnp.sum(router * prob_grad, axis=0, keepdims=True))
    logit_grad = logit_grad.astype(bf16)
    normed_grad = mm(w_router[...], logit_grad, tn) + tall(expert_grad, 0, col)
    unit_grad = normed_grad * gain_two
    mean = jnp.sum(unit_grad * unit, axis=0, keepdims=True) * (1.0 / width)
    residual_grad = tall(packed, col, col) + scale_two * (unit_grad - unit * mean)
    branch = residual_grad.astype(bf16)
    attended_grad = mm(w_output[...], branch).astype(bf16)
    flip = (lanes((tok, tok)) + sublanes((tok, tok)) == tok - 1).astype(bf16)
    query, key, value = qkv[0], qkv[1], qkv[2]
    grads = [[], [], []]
    offsets = []
    for h in range(heads_here):
        at = slice(h * size, (h + 1) * size)
        out = attended_grad[at]
        weights = weights_ref[h]
        mass = mm(out, value[at], tn)
        score = weights * (mass - jnp.sum(weights * mass, axis=1, keepdims=True))
        score = score.astype(bf16)
        grads[0].append(mm(key[at], score, nt) * scale)
        grads[1].append(mm(query[at], score) * scale)
        grads[2].append(mm(out, weights.astype(bf16)))
        flipped = jnp.concatenate([mm(flip, score), jnp.zeros((tok, tok), f32)], axis=1)
        rolled = pltpu.roll(flipped, 0, 1, stride=1, stride_axis=0)
        offsets.append(jnp.sum(rolled, axis=0, keepdims=True))
    first = jnp.zeros((width, tok), f32)
    row = jnp.zeros((1, tok), f32)
    for i, w in enumerate((wq, wk, wv)):
        low = jnp.concatenate(grads[i], axis=0).astype(bf16)
        late_ref[i * col : (i + 1) * col, :] = low
        first = first + mm(w[...], low, tn)
        row = row + jnp.sum(low.astype(f32) * qkv[i].astype(f32), axis=0, keepdims=True)
    side = side_rows(16, tok, high_low(row))
    for i in range(blocks):
        at = slice(i * col, (i + 1) * col)
        first_ref[i, : col + 16, :] = jnp.concatenate([first[at], side], axis=0).astype(bf16)
        first_ref[i, col + 16 :, :] = part[i]

    product = mm(attended[...], branch, nt)
    gain_two_grad = jnp.sum(normed_grad * unit, axis=1, keepdims=True)
    gains = jnp.zeros((col, 1), f32)
    own = jnp.zeros((col, tok), f32)
    for i in range(blocks):
        at = slice(i * col, (i + 1) * col)
        gains = jnp.where(scalars[1] == i, gain_two_grad[at], gains)
        own = jnp.where(scalars[1] == i, residual_grad[at], own)
    own_ref[...] = own
    probs = jnp.sum(router * valid, axis=1, keepdims=True)
    if experts < col:
        probs = jnp.concatenate([probs, jnp.zeros((col - experts, 1), f32)], axis=0)
    gains = jnp.transpose(side_lanes(col, 128, [gains] + high_low(probs)))[0:8]
    router_grad = mm(logit_grad, normed, nt)
    offsets = jnp.concatenate(offsets, axis=0)
    offsets = jnp.concatenate([offsets, jnp.zeros((8 - heads_here, 2 * tok), f32)], axis=0)
    gains = jnp.concatenate([gains, jnp.zeros((8, 64), f32)], axis=1)
    pieces = [fold_lanes(gains), fold_lanes(offsets), fold_lanes(router_grad)]
    if len(share_refs) == 2:
        share_refs[0][...] = jnp.concatenate(pieces, axis=0)
        share_refs[1][...] = product
    else:
        share_ref = share_refs[0]
        groups = share_ref.shape[0]
        size = col // groups
        chunk = share_ref.shape[1] - 6 * size
        small = jnp.concatenate(pieces + [jnp.zeros((groups * chunk - 6 * experts - 32, 128), f32)], axis=0)
        for b in range(groups):
            share_ref[b] = jnp.concatenate(
                [small[b * chunk : (b + 1) * chunk], fold_lanes(product[b * size : (b + 1) * size])], axis=0
            ).astype(bf16)


def first_kernel(scalars, came, packed, own, *refs):
    shares, (ret_ref, gain_ref, input_ref) = refs[:-3], refs[-3:]
    col, tok = own.shape
    heads = came.shape[0]
    experts = ret_ref.shape[0]
    total = came[0].astype(f32)
    for i in range(1, heads):
        total = total + came[i].astype(f32)
    mean = (total[col : col + 1] + total[col + 1 : col + 2]) * (1.0 / (heads * col))
    scale = token_scale(tall(packed, 0, col))
    mine = packed[0].astype(f32)
    for i in range(1, heads):
        mine = jnp.where(scalars[1] == i, packed[i].astype(f32), mine)
    unit = mine[:col] * scale
    gain = gain_columns(mine[2 * col : 2 * col + 16])[0]
    input_ref[...] = own[...] + scale * (total[:col] * gain - unit * mean)
    gain_grad = jnp.sum(total[:col] * unit, axis=1, keepdims=True)
    unused = jnp.zeros_like(gain_grad)
    gain_grad = jnp.transpose(side_lanes(col, 128, [unused, unused, unused, gain_grad]))[0:8]
    gain_grad = fold_lanes(jnp.concatenate([gain_grad, jnp.zeros((8, 64), f32)], axis=1))
    gain_ref[...] = gain_grad
    produced = total[col + 16 :]
    count = produced.shape[0] * 2 // 3
    top = produced[:count]
    rest = jnp.concatenate([produced[count:, :64], produced[count:, 64:]], axis=0)
    rest = jnp.concatenate([rest, jnp.zeros((count, 64), f32)], axis=1)
    slots = count // experts
    for e in range(experts):
        at = slice(e * slots, (e + 1) * slots)
        pieces = [top[at], rest[at]]
        if shares:
            share = shares[0][e].astype(f32)
            if e == 0:
                share = jnp.concatenate([share[:16] + gain_grad, share[16:]], axis=0)
            pieces.append(share)
        ret_ref[e] = jnp.concatenate(pieces, axis=0).astype(bf16)


def share_kernel(slots, came, share_ref):
    total = came[0].astype(f32)
    for e in range(1, came.shape[0]):
        total = total + came[e].astype(f32)
    for e in range(came.shape[0]):
        share_ref[e] = total[2 * slots :].astype(bf16)


def add_returned(slots, blocks, side, gate, residual):
    col = residual.shape[0]
    top = jnp.concatenate([block[:slots] for block in blocks], axis=0).astype(bf16)
    rest = jnp.concatenate([block[slots : 2 * slots] for block in blocks], axis=0).astype(bf16)
    pick = pick_slots(side[0:1, :].astype(jnp.int32), len(blocks) * slots).astype(bf16)
    returned = jnp.concatenate([mm(top, pick, tn), mm(rest, pick, tn)[: col - 128]], axis=0)
    return (residual[...] + gate[0:1, :] * returned).astype(bf16)


def last_kernel(slots, came, side, gate, residual, block_ref):
    blocks = [came[e].astype(f32) for e in range(came.shape[0])]
    block_ref[...] = add_returned(slots, blocks, side, gate, residual)


def products_kernel(late, all_in, packed, q_ref, k_ref, v_ref):
    groups, heads, col, tok = all_in.shape
    gain = all_gains(packed)[0]
    normed = []
    for b in range(groups):
        x = jnp.concatenate([all_in[b, i].astype(f32) for i in range(heads)], axis=0)
        normed.append((x * token_scale(x) * gain).astype(bf16))
    joined = jnp.concatenate([late[b] for b in range(groups)], axis=1)
    product = mm(joined, jnp.concatenate(normed, axis=1), nt)
    for i, ref in enumerate((q_ref, k_ref, v_ref)):
        ref[...] = product[i * col : (i + 1) * col]


def sums_kernel(came, buckets, stats, out_ref, router_ref, table_ref, gains_ref, aux_ref):
    groups, tok = came.shape[0], (buckets.shape[1] + 1) // 2
    experts = router_ref.shape[0]
    size = out_ref.shape[0] // groups
    shares = [came[b].astype(f32) for b in range(groups)]
    chunk = shares[0].shape[0] - 6 * size
    for b in range(groups):
        out_ref[b * size : (b + 1) * size, :] = unfold_lanes(shares[b][chunk:], 6)
    small = jnp.concatenate([share[:chunk] for share in shares], axis=0)
    gains = unfold_lanes(small[:16], 2)
    gains_ref[...] = gains
    probs = gains[1:2, :experts] + gains[2:3, :experts]
    same = lanes((experts, experts)) == sublanes((experts, experts))
    share = jnp.sum(jnp.where(same, stats[:, 0:1] * probs, 0.0), axis=0, keepdims=True)
    valid_total = 3 * tok * groups // 4
    aux_ref[...] = jnp.sum(share, axis=1, keepdims=True) * (experts / (valid_total * valid_total))
    span = buckets.shape[1]
    hot = (sublanes((table_ref.shape[1], span)) == buckets[...]).astype(f32)
    offsets = unfold_lanes(small[16:32], 2)[:, :span]
    table_ref[...] = mm(offsets, hot, nt, highest)[: table_ref.shape[0]]
    router_ref[...] = unfold_lanes(small[32 : 32 + 6 * experts], 6)


def few_experts():
    return lax.axis_size("expert") <= 8


def shards(
    inputs,
    out_grad,
    lengths,
    routes,
    buckets,
    gain_attn,
    w_query,
    w_key,
    w_value,
    w_output,
    bias_table,
    gain_ffn,
    w_router,
    w_in,
    w_out,
):
    tok, col = inputs.shape
    heads_here = bias_table.shape[1]
    head_size = w_query.shape[1] // heads_here
    width, experts = w_router.shape
    bucket_count = bias_table.shape[0]
    heads = width // col
    groups = lax.axis_size("expert")
    me_head, me_expert = lax.axis_index("head"), lax.axis_index("expert")
    capacity = max(2, (4 * tok + 3 * experts - 1) // (3 * experts))
    slots = -(-(capacity + 1) // 8) * 8
    total = experts * slots
    valid_total = 3 * tok * groups // 4
    scale = head_size ** (-0.5)
    joined = few_experts()
    small_rows = 6 * experts + 32
    chunk = -(-small_rows // (16 * groups)) * 16
    w_in, w_out = w_in[0], w_out[0]
    wq, wk, wv = w_query.T, w_key.T, w_value.T
    routes_row = routes.T
    router_rows = w_router.T
    scalars = jnp.stack([lengths[0], me_head.astype(jnp.int32), me_expert.astype(jnp.int32)])
    buckets_row = buckets[None]

    gains = jnp.concatenate([gain_attn, gain_ffn]).reshape(3, 128)
    gains = jnp.concatenate([inputs.T, out_grad.T, gains, jnp.zeros((13, 128), bf16)], axis=0)
    packed = lax.all_gather(gains, "head")
    if joined:
        all_in = lax.all_gather(inputs.T, ("expert", "head")).reshape(groups, heads, col, tok)
    qkv, weights, attended, branch = call(
        functools.partial(attend_kernel, scale),
        [
            ((3, col, tok), bf16, 1), ((heads_here, tok, tok), f32, 1), ((col, tok), bf16, 1),
            ((heads, col, tok), bf16),
        ],
        scalars, packed, far(wq), far(wk), far(wv), far(w_output), far(buckets_row), far(bias_table.T),
    )

    branch = lax.all_to_all(branch, "head", split_axis=0, concat_axis=0, tiled=True)
    residual, low, side, send = call(
        functools.partial(route_kernel, capacity),
        [((col, tok), f32, 1), ((col, tok), bf16, 1), ((8, tok), f32, 1), ((experts, slots, 2 * col), bf16)],
        scalars, branch, far(inputs.T), far(out_grad.T), far(routes_row),
    )
    quarter = lax.all_to_all(send, "expert", split_axis=0, concat_axis=0, tiled=True)
    quarters = lax.all_gather(quarter.reshape(total, 2 * col), "head")

    back, part, hidden, before_grad, back_rows, rows = call(
        functools.partial(expert_kernel, capacity),
        [((experts * heads, folded_rows(slots), 128), bf16), ((heads, total * 3 // 2, 128), bf16, 1)]
        + [((total, width), bf16, 1)] * 4,
        scalars, quarters, far(packed), far(w_in), far(w_out), far(router_rows),
    )
    came = lax.all_to_all(back, ("expert", "head"), split_axis=0, concat_axis=0, tiled=True)
    grad_own, gate_grad, stats = call(
        functools.partial(collect_kernel, slots),
        [((2 * col, tok), bf16), ((8, tok), f32, 1), ((experts, 128), f32, 1)],
        came, far(side), far(low),
    )
    expert_grad = lax.all_gather(grad_own, "head")

    late, first, residual_grad_own, gate, *shares = call(
        functools.partial(backward_kernel, scale, valid_total),
        [
            ((3 * col, tok), bf16, 1), ((heads, col + 16 + total * 3 // 2, 128), bf16), ((col, tok), f32, 1),
            ((8, tok), f32, 1),
        ]
        + (
            [((groups, chunk + 6 * col // groups, 128), bf16, 1)]
            if joined
            else [((small_rows, 128), f32, 1), ((col, width), f32, 1)]
        ),
        scalars, far(packed), expert_grad, far(gate_grad), far(stats), far(routes_row),
        far(router_rows), far(w_output), far(weights), far(qkv), far(wq), far(wk), far(wv), far(attended),
        far(part),
    )

    if joined:
        late_all = lax.all_gather(late, "expert")

    first = lax.all_to_all(first, "head", split_axis=0, concat_axis=0, tiled=True)
    in_weight_grad, out_weight_grad = call(
        weights_kernel, [((width, width), f32, 1)] * 2, far(rows), far(hidden), far(before_grad), far(back_rows)
    )
    first, in_weight_grad, out_weight_grad = lax.optimization_barrier((first, in_weight_grad, out_weight_grad))
    ret, gain_one_part, input_grad = call(
        first_kernel,
        [
            ((experts, 2 * slots + (shares[0].shape[1] if joined else 0), 128), bf16),
            ((16, 128), f32, 1), ((col, tok), f32, 1),
        ],
        scalars, first, far(packed), far(residual_grad_own), *([far(shares[0])] if joined else []),
    )
    ret = lax.all_to_all(ret, "expert", split_axis=0, concat_axis=0, tiled=True)
    if joined:
        share = call(
            functools.partial(share_kernel, slots), [(shares[0].shape, bf16)], ret
        )[0]
        share = lax.all_to_all(share, "expert", split_axis=0, concat_axis=0, tiled=True)
    block_out = call(
        functools.partial(last_kernel, slots), [((col, tok), bf16, 1)], far(ret), far(side), far(gate), far(residual)
    )[0]
    if joined:
        q_grad, k_grad, v_grad = call(
            products_kernel, [((col, width), f32, 1)] * 3, far(late_all), far(all_in), far(packed)
        )
        share, q_grad, k_grad, v_grad, block_out = lax.optimization_barrier(
            (share, q_grad, k_grad, v_grad, block_out)
        )
        output_grad, router_grad, table_grad, gain_grads, aux_loss = call(
            sums_kernel,
            [((col, width), f32, 1), ((experts, width), f32), ((heads_here, bucket_count), f32)]
            + [((8, 256), f32), ((1, 1), f32)],
            share, far(buckets_row), far(stats),
        )
    else:
        gain = packed[:, 2 * col : 2 * col + 3].reshape(heads, 2 * col)[:, :col].reshape(width, 1)
        x = packed[:, :col].reshape(width, tok).astype(f32)
        normed = (x * token_scale(x) * gain.astype(f32)).astype(bf16)
        products = [mm(late[i * col : (i + 1) * col], normed, nt) for i in range(3)]
        q_grad, k_grad, v_grad, sums, gain_one, output_grad = lax.psum(
            products + [shares[0], gain_one_part, shares[1]], "expert"
        )
        router_grad = unfold_lanes(sums[32 : 32 + 6 * experts], 6)
        offsets = unfold_lanes(sums[16:32], 2)[:heads_here, : 2 * tok - 1]
        hot = (buckets[None, :] == jnp.arange(bucket_count)[:, None]).astype(f32)
        table_grad = mm(offsets, hot, nt, highest)
        gain_grads = unfold_lanes(sums[:16] + gain_one, 2)
        probs = gain_grads[1, :experts] + gain_grads[2, :experts]
        aux_loss = experts * jnp.sum(stats[:, 0] * probs) / (valid_total * valid_total)
    return (
        block_out.T,
        input_grad.T,
        aux_loss.reshape(()),
        gain_grads[3, :col],
        q_grad.T,
        k_grad.T,
        v_grad.T,
        output_grad,
        table_grad.T,
        gain_grads[0, :col],
        router_grad.T,
        in_weight_grad[None],
        out_weight_grad[None],
    )


def solution(mesh):
    return jax.shard_map(
        shards,
        mesh=mesh,
        in_specs=(
            P("expert", "head"),
            P("expert", "head"),
            P("expert"),
            P("expert", None),
            P(),
            P("head"),
            P(None, "head"),
            P(None, "head"),
            P(None, "head"),
            P("head", None),
            P(None, "head"),
            P("head"),
            P(),
            P("expert", None, "head"),
            P("expert", "head", None),
        ),
        out_specs=(
            P("expert", "head"),
            P("expert", "head"),
            P(),
            P("head"),
            P(None, "head"),
            P(None, "head"),
            P(None, "head"),
            P("head", None),
            P(None, "head"),
            P("head"),
            P(),
            P("expert", None, "head"),
            P("expert", "head", None),
        ),
        check_vma=False,
    )
```

```python
import functools

import jax
import jax.numpy as jnp
from jax import lax
from jax.experimental import pallas as pl
from jax.experimental.pallas import tpu as pltpu
from jax.sharding import PartitionSpec as P

eps = 1e-06
aux_weight = 0.01
f32 = jnp.float32
bf16 = jnp.bfloat16
gelu_scale = 0.7978845608028654
gelu_cube = 0.044715
highest = lax.Precision.HIGHEST
nt = ((1,), (1,))
tn = ((0,), (0,))


def mm(left, right, dims=((1,), (0,)), precision=None):
    return lax.dot_general(left, right, (dims, ((), ())), precision=precision, preferred_element_type=f32)


def call(body, outs, *args):
    scalar_memory = pl.BlockSpec(memory_space=pltpu.SMEM)
    in_specs = [scalar_memory if a.dtype == jnp.int32 and a.ndim == 1 else pl.BlockSpec() for a in args]
    shapes = []
    for shape, kind, *remote in outs:
        shapes.append(pltpu.HBM(shape, kind) if remote else jax.ShapeDtypeStruct(shape, kind))
    return pl.pallas_call(
        body,
        out_shape=shapes,
        in_specs=in_specs,
        compiler_params=pltpu.CompilerParams(vmem_limit_bytes=40 * 1024 * 1024),
    )(*args)


def far(array):
    return pltpu.with_memory_space_constraint(array, pltpu.HBM)


def tall(ref, first, rows):
    return jnp.concatenate([ref[i, first : first + rows, :].astype(f32) for i in range(ref.shape[0])], axis=0)


def gain_columns(block):
    turned = jnp.transpose(block.astype(f32))
    return [
        jnp.concatenate([turned[:, 0:1], turned[:64, 1:2]], axis=0),
        jnp.concatenate([turned[64:, 1:2], turned[:, 2:3]], axis=0),
    ]


def all_gains(packed):
    first = 2 * packed.shape[2] * 3 // 2
    pairs = [gain_columns(packed[i, first : first + 16, :]) for i in range(packed.shape[0])]
    return [jnp.concatenate([pair[i] for pair in pairs], axis=0) for i in range(2)]


def token_scale(values):
    return lax.rsqrt(jnp.sum(values * values, axis=0, keepdims=True) * (1.0 / values.shape[0]) + eps)


def lanes(shape):
    return lax.broadcasted_iota(jnp.int32, shape, len(shape) - 1)


def sublanes(shape):
    return lax.broadcasted_iota(jnp.int32, shape, len(shape) - 2)


def side_lanes(rows, width, columns):
    spot = lanes((rows, width))
    out = jnp.zeros((rows, width), f32)
    for i, column in enumerate(columns):
        out = jnp.where(spot == i, column, out)
    return out


def side_rows(rows, width, lines):
    spot = sublanes((rows, width))
    out = jnp.zeros((rows, width), f32)
    for i, line in enumerate(lines):
        out = jnp.where(spot == i, line, out)
    return out


def high_low(values, count=2):
    pieces = []
    for _ in range(count):
        piece = values.astype(bf16).astype(f32)
        pieces.append(piece)
        values = values - piece
    return pieces


def softmax(values, axis):
    raised = jnp.exp(values - jnp.max(values, axis=axis, keepdims=True))
    return raised / jnp.sum(raised, axis=axis, keepdims=True)


def gelu_parts(u):
    t = jnp.tanh(gelu_scale * (u + gelu_cube * u * u * u))
    value = 0.5 * u * (1.0 + t)
    slope = 0.5 * (1.0 + t) + 0.5 * u * (1.0 - t * t) * gelu_scale * (1.0 + 3.0 * gelu_cube * u * u)
    return value, slope


def fold_lanes(rows):
    return jnp.concatenate([rows[:, i : i + 128] for i in range(0, rows.shape[1], 128)], axis=0)


def unfold_lanes(rows, pieces):
    size = rows.shape[0] // pieces
    return jnp.concatenate([rows[i * size : (i + 1) * size] for i in range(pieces)], axis=1)


def side_block(side):
    count = side.shape[1]
    spot = lanes((8, 64))
    out = jnp.zeros((8, 64), f32)
    for g in range(side.shape[0] // 8):
        for j in range(count):
            out = jnp.where(spot == g * count + j, side[8 * g : 8 * g + 8, j : j + 1], out)
    return out


def fold_rest(rest, last):
    groups = [rest[i : i + 8] for i in range(0, rest.shape[0], 8)] + [last]
    if len(groups) % 2:
        groups.append(jnp.zeros((8, 64), f32))
    return [jnp.concatenate(groups[i : i + 2], axis=1) for i in range(0, len(groups), 2)]


def unfold_rest(blocks, slots, count):
    halves = []
    for i in range(0, blocks.shape[0], 8):
        halves += [blocks[i : i + 8, :64], blocks[i : i + 8, 64:]]
    number = slots // 8
    side = [halves[number][:, g * count : (g + 1) * count] for g in range(number)]
    return jnp.concatenate(halves[:number], axis=0), jnp.concatenate(side, axis=0)


def folded_rows(slots):
    return slots + 8 * ((slots // 8 + 2) // 2)


def pick_slots(spots, count):
    return sublanes((count, spots.shape[1])) == spots


def attend_kernel(
    scale, scalars, packed, wq, wk, wv, w_output, buckets, table, qkv_ref, weights_ref, attended_ref, branch_ref,
    scale_ref,
):
    heads, tok, _ = weights_ref.shape
    col = wq.shape[0]
    size = col // heads
    x = tall(packed, 0, col)
    scale_one = token_scale(x)
    scale_ref[...] = jnp.broadcast_to(scale_one, scale_ref.shape)
    normed = (x * scale_one * all_gains(packed)[0]).astype(bf16)
    projected = []
    for i, w in enumerate((wq, wk, wv)):
        rows = mm(w[...], normed).astype(bf16)
        qkv_ref[i] = rows
        projected.append(rows)
    query, key, value = projected
    hot = (sublanes((table.shape[1], 2 * tok - 1)) == buckets[...]).astype(f32)
    offsets = mm(table[...], hot, precision=highest)
    offsets = jnp.concatenate([offsets, jnp.zeros((heads, 1), f32)], axis=1)
    open_keys = lanes((tok, tok)) < scalars[0]
    outs = []
    for h in range(heads):
        at = slice(h * size, (h + 1) * size)
        spread = jnp.broadcast_to(offsets[h : h + 1, :], (tok, 2 * tok))
        bias = pltpu.roll(spread, tok + 1, 1, stride=1, stride_axis=0)[:, :tok]
        scores = mm(query[at], key[at], tn) * scale + bias
        weights = softmax(jnp.where(open_keys, scores, -1000000000.0), 1)
        weights_ref[h] = weights
        outs.append(mm(value[at], weights.astype(bf16), nt))
    attended = jnp.concatenate(outs, axis=0).astype(bf16)
    attended_ref[...] = attended
    branch = mm(w_output[...], attended, tn)
    for i in range(branch_ref.shape[0]):
        branch_ref[i] = branch[i * col : (i + 1) * col].astype(bf16)


def second_norm(residual, gain, w_router):
    scale = token_scale(residual)
    unit = residual * scale
    normed = (unit * gain).astype(bf16)
    return scale, unit, normed, softmax(mm(w_router, normed), 0)


def route_kernel(capacity, scalars, came, inputs, out_grad, routes, residual_ref, low_ref, side_ref, send_ref):
    col, tok = inputs.shape
    experts, slots, _ = send_ref.shape
    residual = inputs[...].astype(f32)
    for i in range(came.shape[0]):
        residual = residual + came[i].astype(f32)
    residual_ref[...] = residual
    low = residual.astype(bf16)
    low_ref[...] = low
    route_hot = (sublanes((experts, tok)) == routes[...]).astype(f32)
    before = (sublanes((tok, tok)) < lanes((tok, tok))).astype(bf16)
    slot = jnp.sum(mm(route_hot.astype(bf16), before) * route_hot, axis=0, keepdims=True)
    spots = routes[...].astype(f32) * slots + slot
    side_ref[...] = side_rows(8, tok, [spots])
    valid = (lanes((1, tok)) < scalars[0]).astype(f32)
    counts = jnp.sum(route_hot * valid, axis=1, keepdims=True)
    pick = pick_slots(spots.astype(jnp.int32), experts * slots).astype(bf16)
    rows = mm(pick, jnp.concatenate([low, out_grad[...]], axis=0), nt)
    spare = (sublanes((slots, 2 * col)) == capacity) & (lanes((slots, 2 * col)) == col)
    for e in range(experts):
        block = rows[e * slots : (e + 1) * slots]
        send_ref[e] = jnp.where(spare, counts[e : e + 1], block).astype(bf16)


def second_gain_row(packed, first):
    pieces = []
    for i in range(packed.shape[0]):
        block = packed[i, first : first + 16, :].astype(f32)
        pieces += [block[1:2, 64:], block[2:3, :]]
    return jnp.concatenate(pieces, axis=1)


def expert_kernel(
    capacity, scalars, quarters, packed, w_in, w_out, w_router,
    back_ref, part_ref, hidden_ref, before_ref, grads_ref, rows_ref,
):
    total = rows_ref.shape[0]
    experts, width = w_router.shape
    heads = part_ref.shape[0]
    col = width // heads
    slots = total // experts
    half = total // 2
    parts = [quarters[i].astype(f32) for i in range(heads)]
    residual = jnp.concatenate([block[:, :col] for block in parts], axis=1)
    grads = jnp.concatenate([block[:, col:] for block in parts], axis=1)
    inverse = lax.rsqrt(jnp.sum(residual * residual, axis=1, keepdims=True) * (1.0 / width) + eps)
    rows = (residual * inverse * second_gain_row(packed, 2 * col)).astype(bf16)
    rows_ref[...] = rows
    hidden, slope = gelu_parts(mm(rows, w_in[...]))
    hidden = hidden.astype(bf16)
    hidden_ref[...] = hidden
    produced = mm(hidden, w_out[...])
    for i in range(heads):
        mine = produced[:, i * col : (i + 1) * col]
        rest = mine[:, 128:]
        part_ref[i] = jnp.concatenate(
            [mine[:, :128], jnp.concatenate([rest[:half], rest[half:]], axis=1)], axis=0
        ).astype(bf16)
    probs = softmax(mm(rows, w_router[...], nt), 1)
    gate = jnp.sum(jnp.where(lanes((total, experts)) == scalars[2], probs, 0.0), axis=1, keepdims=True)
    back = (gate * grads).astype(bf16)
    grads_ref[...] = back
    before = (mm(back, w_out[...], nt) * slope).astype(bf16)
    before_ref[...] = before
    rows_grad = mm(before, w_in[...], nt)
    gate_grad = jnp.sum(grads * produced, axis=1, keepdims=True)
    stats = jnp.zeros((1, 128), f32)
    for b in range(experts):
        stats = stats + grads[b * slots + capacity : b * slots + capacity + 1, :128]
    side = side_lanes(total, 4, high_low(gate_grad) + high_low(stats[:, 0:1]))
    for b in range(experts):
        at = slice(b * slots, (b + 1) * slots)
        last = side_block(side[at])
        for i in range(heads):
            mine = rows_grad[at, i * col : (i + 1) * col]
            back_ref[b * heads + i] = jnp.concatenate(
                [mine[:, :128]] + fold_rest(mine[:, 128:], last), axis=0
            ).astype(bf16)


def weights_kernel(rows_ref, hidden, before, grads, in_ref, out_ref):
    in_ref[...] = mm(rows_ref[...], before[...], tn)
    out_ref[...] = mm(hidden[...], grads[...], tn)


def collect_kernel(slots, came, side, low, grad_ref, gate_ref, stats_ref):
    col, tok = low.shape
    experts = stats_ref.shape[0]
    heads = came.shape[0] // experts
    tops, rests, scalars = [], [], []
    for e in range(experts):
        total = came[e * heads].astype(f32)
        for i in range(1, heads):
            total = total + came[e * heads + i].astype(f32)
        rest, columns = unfold_rest(total[slots:], slots, 4)
        tops.append(total[:slots])
        rests.append(rest)
        scalars.append(columns)
    counts = jnp.concatenate([columns[0:1] for columns in scalars], axis=0) * (1.0 / heads)
    pick = pick_slots(side[0:1, :].astype(jnp.int32), experts * slots)
    for first, pieces in ((0, tops), (128, rests)):
        block = jnp.concatenate(pieces, axis=0).astype(bf16)
        grad_ref[first : min(first + 128, col), :] = mm(block, pick.astype(bf16), tn).astype(bf16)
    grad_ref[col:, :] = low[...]
    gate = mm(jnp.concatenate(scalars, axis=0), pick.astype(f32), tn, highest)
    gate_ref[...] = jnp.broadcast_to(gate[0:1] + gate[1:2], gate_ref.shape)
    stats_ref[...] = side_lanes(experts, 128, [counts[:, 2:3] + counts[:, 3:4]])


def backward_kernel(
    scale, valid_total, scalars, packed, expert_grad, gate_grad, stats, routes, w_router, w_output, weights_ref,
    qkv, wq, wk, wv, attended, part, late_ref, first_ref, own_ref, gate_ref, *share_refs,
):
    tok = routes.shape[1]
    heads_here = weights_ref.shape[0]
    blocks, col = packed.shape[0], wq.shape[0]
    experts, width = w_router.shape
    size = col // heads_here
    gain_one, gain_two = all_gains(packed)
    residual = tall(expert_grad, col, col)
    scale_two, unit, normed, router = second_norm(residual, gain_two, w_router[...])
    valid = (lanes((1, tok)) < scalars[0]).astype(f32)
    route_hot = (sublanes((experts, tok)) == routes[...]).astype(f32)
    fraction = stats[:, 0:1] * (aux_weight * experts / (valid_total * valid_total))
    gate = jnp.sum(router * route_hot, axis=0, keepdims=True)
    gate_ref[...] = jnp.broadcast_to(gate, gate_ref.shape)
    prob_grad = route_hot * gate_grad[0:1, :] + fraction * valid
    logit_grad = router * (prob_grad - jnp.sum(router * prob_grad, axis=0, keepdims=True))
    logit_grad = logit_grad.astype(bf16)
    normed_grad = mm(w_router[...], logit_grad, tn) + tall(expert_grad, 0, col)
    unit_grad = normed_grad * gain_two
    mean = jnp.sum(unit_grad * unit, axis=0, keepdims=True) * (1.0 / width)
    residual_grad = tall(packed, col, col) + scale_two * (unit_grad - unit * mean)
    branch = residual_grad.astype(bf16)
    attended_grad = mm(w_output[...], branch).astype(bf16)
    flip = (lanes((tok, tok)) + sublanes((tok, tok)) == tok - 1).astype(bf16)
    query, key, value = qkv[0], qkv[1], qkv[2]
    grads = [[], [], []]
    offsets = []
    for h in range(heads_here):
        at = slice(h * size, (h + 1) * size)
        out = attended_grad[at]
        weights = weights_ref[h]
        mass = mm(out, value[at], tn)
        score = weights * (mass - jnp.sum(weights * mass, axis=1, keepdims=True))
        score = score.astype(bf16)
        grads[0].append(mm(key[at], score, nt) * scale)
        grads[1].append(mm(query[at], score) * scale)
        grads[2].append(mm(out, weights.astype(bf16)))
        flipped = jnp.concatenate([mm(flip, score), jnp.zeros((tok, tok), f32)], axis=1)
        rolled = pltpu.roll(flipped, 0, 1, stride=1, stride_axis=0)
        offsets.append(jnp.sum(rolled, axis=0, keepdims=True))
    first = jnp.zeros((width, tok), f32)
    row = jnp.zeros((1, tok), f32)
    for i, w in enumerate((wq, wk, wv)):
        low = jnp.concatenate(grads[i], axis=0).astype(bf16)
        late_ref[i * col : (i + 1) * col, :] = low
        first = first + mm(w[...], low, tn)
        row = row + jnp.sum(low.astype(f32) * qkv[i].astype(f32), axis=0, keepdims=True)
    side = side_rows(16, tok, high_low(row))
    for i in range(blocks):
        at = slice(i * col, (i + 1) * col)
        first_ref[i, : col + 16, :] = jnp.concatenate([first[at], side], axis=0).astype(bf16)
        first_ref[i, col + 16 :, :] = part[i]

    product = mm(attended[...], branch, nt)
    gain_two_grad = jnp.sum(normed_grad * unit, axis=1, keepdims=True)
    gains = jnp.zeros((col, 1), f32)
    own = jnp.zeros((col, tok), f32)
    for i in range(blocks):
        at = slice(i * col, (i + 1) * col)
        gains = jnp.where(scalars[1] == i, gain_two_grad[at], gains)
        own = jnp.where(scalars[1] == i, residual_grad[at], own)
    own_ref[...] = own
    probs = jnp.sum(router * valid, axis=1, keepdims=True)
    if experts < col:
        probs = jnp.concatenate([probs, jnp.zeros((col - experts, 1), f32)], axis=0)
    gains = jnp.transpose(side_lanes(col, 128, [gains] + high_low(probs)))[0:8]
    router_grad = mm(logit_grad, normed, nt)
    offsets = jnp.concatenate(offsets, axis=0)
    offsets = jnp.concatenate([offsets, jnp.zeros((8 - heads_here, 2 * tok), f32)], axis=0)
    gains = jnp.concatenate([gains, jnp.zeros((8, 64), f32)], axis=1)
    pieces = [fold_lanes(gains), fold_lanes(offsets), fold_lanes(router_grad)]
    if len(share_refs) == 2:
        share_refs[0][...] = jnp.concatenate(pieces, axis=0)
        share_refs[1][...] = product
    else:
        share_ref = share_refs[0]
        groups = share_ref.shape[0]
        size = col // groups
        chunk = share_ref.shape[1] - 6 * size
        small = jnp.concatenate(pieces + [jnp.zeros((groups * chunk - 6 * experts - 32, 128), f32)], axis=0)
        for b in range(groups):
            share_ref[b] = jnp.concatenate(
                [small[b * chunk : (b + 1) * chunk], fold_lanes(product[b * size : (b + 1) * size])], axis=0
            ).astype(bf16)


def first_kernel(came, block, scale_one, own, *refs):
    shares, (ret_ref, gain_ref, input_ref) = refs[:-3], refs[-3:]
    col, tok = own.shape
    heads = came.shape[0]
    experts = ret_ref.shape[0]
    total = came[0].astype(f32)
    for i in range(1, heads):
        total = total + came[i].astype(f32)
    mean = (total[col : col + 1] + total[col + 1 : col + 2]) * (1.0 / (heads * col))
    scale = scale_one[0:1, :]
    mine = block[...].astype(f32)
    unit = mine[:col] * scale
    gain = gain_columns(mine[2 * col : 2 * col + 16])[0]
    input_ref[...] = own[...] + scale * (total[:col] * gain - unit * mean)
    gain_grad = jnp.sum(total[:col] * unit, axis=1, keepdims=True)
    unused = jnp.zeros_like(gain_grad)
    gain_grad = jnp.transpose(side_lanes(col, 128, [unused, unused, unused, gain_grad]))[0:8]
    gain_grad = fold_lanes(jnp.concatenate([gain_grad, jnp.zeros((8, 64), f32)], axis=1))
    gain_ref[...] = gain_grad
    produced = total[col + 16 :]
    count = produced.shape[0] * 2 // 3
    top = produced[:count]
    rest = jnp.concatenate([produced[count:, :64], produced[count:, 64:]], axis=0)
    slots = count // experts
    none = jnp.zeros((8, 64), f32)
    for e in range(experts):
        at = slice(e * slots, (e + 1) * slots)
        pieces = [top[at]] + fold_rest(rest[at], none)
        if shares:
            share = shares[0][e].astype(f32)
            if e == 0:
                share = jnp.concatenate([share[:16] + gain_grad, share[16:]], axis=0)
            pieces.append(share)
        ret_ref[e] = jnp.concatenate(pieces, axis=0).astype(bf16)


def share_kernel(slots, came, share_ref):
    total = came[0].astype(f32)
    for e in range(1, came.shape[0]):
        total = total + came[e].astype(f32)
    for e in range(came.shape[0]):
        share_ref[e] = total[folded_rows(slots) :].astype(bf16)


def add_returned(slots, blocks, side, gate, residual):
    col = residual.shape[0]
    top = jnp.concatenate([block[:slots] for block in blocks], axis=0).astype(bf16)
    rests = [unfold_rest(block[slots : folded_rows(slots)], slots, 1)[0] for block in blocks]
    rest = jnp.concatenate(rests, axis=0).astype(bf16)
    pick = pick_slots(side[0:1, :].astype(jnp.int32), len(blocks) * slots).astype(bf16)
    returned = jnp.concatenate([mm(top, pick, tn), mm(rest, pick, tn)], axis=0)
    return (residual[...] + gate[0:1, :] * returned).astype(bf16)


def last_kernel(slots, came, side, gate, residual, block_ref):
    blocks = [came[e].astype(f32) for e in range(came.shape[0])]
    block_ref[...] = add_returned(slots, blocks, side, gate, residual)


def products_kernel(late, all_in, packed, q_ref, k_ref, v_ref):
    groups, heads, col, tok = all_in.shape
    gain = all_gains(packed)[0]
    normed = []
    for b in range(groups):
        x = jnp.concatenate([all_in[b, i].astype(f32) for i in range(heads)], axis=0)
        normed.append((x * token_scale(x) * gain).astype(bf16))
    joined = jnp.concatenate([late[b] for b in range(groups)], axis=1)
    product = mm(joined, jnp.concatenate(normed, axis=1), nt)
    for i, ref in enumerate((q_ref, k_ref, v_ref)):
        ref[...] = product[i * col : (i + 1) * col]


def sums_kernel(came, buckets, stats, out_ref, router_ref, table_ref, gains_ref, aux_ref):
    groups, tok = came.shape[0], (buckets.shape[1] + 1) // 2
    experts = router_ref.shape[0]
    size = out_ref.shape[0] // groups
    shares = [came[b].astype(f32) for b in range(groups)]
    chunk = shares[0].shape[0] - 6 * size
    for b in range(groups):
        out_ref[b * size : (b + 1) * size, :] = unfold_lanes(shares[b][chunk:], 6)
    small = jnp.concatenate([share[:chunk] for share in shares], axis=0)
    gains = unfold_lanes(small[:16], 2)
    gains_ref[...] = gains
    probs = gains[1:2, :experts] + gains[2:3, :experts]
    same = lanes((experts, experts)) == sublanes((experts, experts))
    share = jnp.sum(jnp.where(same, stats[:, 0:1] * probs, 0.0), axis=0, keepdims=True)
    valid_total = 3 * tok * groups // 4
    aux_ref[...] = jnp.sum(share, axis=1, keepdims=True) * (experts / (valid_total * valid_total))
    span = buckets.shape[1]
    hot = (sublanes((table_ref.shape[1], span)) == buckets[...]).astype(f32)
    offsets = unfold_lanes(small[16:32], 2)[:, :span]
    table_ref[...] = mm(offsets, hot, nt, highest)[: table_ref.shape[0]]
    router_ref[...] = unfold_lanes(small[32 : 32 + 6 * experts], 6)


def few_experts():
    return lax.axis_size("expert") <= 8


def shards(
    inputs,
    out_grad,
    lengths,
    routes,
    buckets,
    gain_attn,
    w_query,
    w_key,
    w_value,
    w_output,
    bias_table,
    gain_ffn,
    w_router,
    w_in,
    w_out,
):
    tok, col = inputs.shape
    heads_here = bias_table.shape[1]
    head_size = w_query.shape[1] // heads_here
    width, experts = w_router.shape
    bucket_count = bias_table.shape[0]
    heads = width // col
    groups = lax.axis_size("expert")
    me_head, me_expert = lax.axis_index("head"), lax.axis_index("expert")
    capacity = max(2, (4 * tok + 3 * experts - 1) // (3 * experts))
    slots = -(-(capacity + 1) // 8) * 8
    total = experts * slots
    valid_total = 3 * tok * groups // 4
    scale = head_size ** (-0.5)
    joined = few_experts()
    small_rows = 6 * experts + 32
    chunk = -(-small_rows // (16 * groups)) * 16
    w_in, w_out = w_in[0], w_out[0]
    wq, wk, wv = w_query.T, w_key.T, w_value.T
    routes_row = routes.T
    router_rows = w_router.T
    scalars = jnp.stack([lengths[0], me_head.astype(jnp.int32), me_expert.astype(jnp.int32)])
    buckets_row = buckets[None]

    gains = jnp.concatenate([gain_attn, gain_ffn]).reshape(3, 128)
    own_block = jnp.concatenate([inputs.T, out_grad.T, gains, jnp.zeros((13, 128), bf16)], axis=0)
    packed = lax.all_gather(own_block, "head")
    if joined:
        all_in = lax.all_gather(inputs.T, ("expert", "head")).reshape(groups, heads, col, tok)
    qkv, weights, attended, branch, scale_one = call(
        functools.partial(attend_kernel, scale),
        [
            ((3, col, tok), bf16, 1), ((heads_here, tok, tok), f32, 1), ((col, tok), bf16, 1),
            ((heads, col, tok), bf16), ((8, tok), f32, 1),
        ],
        scalars, packed, far(wq), far(wk), far(wv), far(w_output), far(buckets_row), far(bias_table.T),
    )

    branch = lax.all_to_all(branch, "head", split_axis=0, concat_axis=0, tiled=True)
    residual, low, side, send = call(
        functools.partial(route_kernel, capacity),
        [((col, tok), f32, 1), ((col, tok), bf16, 1), ((8, tok), f32, 1), ((experts, slots, 2 * col), bf16)],
        scalars, branch, far(inputs.T), far(out_grad.T), far(routes_row),
    )
    quarter = lax.all_to_all(send, "expert", split_axis=0, concat_axis=0, tiled=True)
    quarters = lax.all_gather(quarter.reshape(total, 2 * col), "head")

    back, part, hidden, before_grad, back_rows, rows = call(
        functools.partial(expert_kernel, capacity),
        [((experts * heads, folded_rows(slots), 128), bf16), ((heads, total * 3 // 2, 128), bf16, 1)]
        + [((total, width), bf16, 1)] * 4,
        scalars, quarters, far(packed), far(w_in), far(w_out), far(router_rows),
    )
    came = lax.all_to_all(back, ("expert", "head"), split_axis=0, concat_axis=0, tiled=True)
    grad_own, gate_grad, stats = call(
        functools.partial(collect_kernel, slots),
        [((2 * col, tok), bf16), ((8, tok), f32, 1), ((experts, 128), f32, 1)],
        came, far(side), far(low),
    )
    expert_grad = lax.all_gather(grad_own, "head")

    late, first, residual_grad_own, gate, *shares = call(
        functools.partial(backward_kernel, scale, valid_total),
        [
            ((3 * col, tok), bf16, 1), ((heads, col + 16 + total * 3 // 2, 128), bf16), ((col, tok), f32, 1),
            ((8, tok), f32, 1),
        ]
        + (
            [((groups, chunk + 6 * col // groups, 128), bf16, 1)]
            if joined
            else [((small_rows, 128), f32, 1), ((col, width), f32, 1)]
        ),
        scalars, far(packed), expert_grad, far(gate_grad), far(stats), far(routes_row),
        far(router_rows), far(w_output), far(weights), far(qkv), far(wq), far(wk), far(wv), far(attended),
        far(part),
    )

    if joined:
        late_all = lax.all_gather(late, "expert")

    first = lax.all_to_all(first, "head", split_axis=0, concat_axis=0, tiled=True)
    in_weight_grad, out_weight_grad = call(
        weights_kernel, [((width, width), f32, 1)] * 2, far(rows), far(hidden), far(before_grad), far(back_rows)
    )
    first, in_weight_grad, out_weight_grad = lax.optimization_barrier((first, in_weight_grad, out_weight_grad))
    ret, gain_one_part, input_grad = call(
        first_kernel,
        [
            ((experts, folded_rows(slots) + (shares[0].shape[1] if joined else 0), 128), bf16),
            ((16, 128), f32, 1), ((col, tok), f32, 1),
        ],
        first, far(own_block), far(scale_one), far(residual_grad_own), *([far(shares[0])] if joined else []),
    )
    ret = lax.all_to_all(ret, "expert", split_axis=0, concat_axis=0, tiled=True)
    if joined:
        share = call(
            functools.partial(share_kernel, slots), [(shares[0].shape, bf16)], ret
        )[0]
        share = lax.all_to_all(share, "expert", split_axis=0, concat_axis=0, tiled=True)
    block_out = call(
        functools.partial(last_kernel, slots), [((col, tok), bf16, 1)], far(ret), far(side), far(gate), far(residual)
    )[0]
    if joined:
        q_grad, k_grad, v_grad = call(
            products_kernel, [((col, width), f32, 1)] * 3, far(late_all), far(all_in), far(packed)
        )
        share, q_grad, k_grad, v_grad, block_out = lax.optimization_barrier(
            (share, q_grad, k_grad, v_grad, block_out)
        )
        output_grad, router_grad, table_grad, gain_grads, aux_loss = call(
            sums_kernel,
            [((col, width), f32, 1), ((experts, width), f32), ((heads_here, bucket_count), f32)]
            + [((8, 256), f32), ((1, 1), f32)],
            share, far(buckets_row), far(stats),
        )
    else:
        gain = packed[:, 2 * col : 2 * col + 3].reshape(heads, 2 * col)[:, :col].reshape(width, 1)
        x = packed[:, :col].reshape(width, tok).astype(f32)
        normed = (x * token_scale(x) * gain.astype(f32)).astype(bf16)
        products = [mm(late[i * col : (i + 1) * col], normed, nt) for i in range(3)]
        q_grad, k_grad, v_grad, sums, gain_one, output_grad = lax.psum(
            products + [shares[0], gain_one_part, shares[1]], "expert"
        )
        router_grad = unfold_lanes(sums[32 : 32 + 6 * experts], 6)
        offsets = unfold_lanes(sums[16:32], 2)[:heads_here, : 2 * tok - 1]
        hot = (buckets[None, :] == jnp.arange(bucket_count)[:, None]).astype(f32)
        table_grad = mm(offsets, hot, nt, highest)
        gain_grads = unfold_lanes(sums[:16] + gain_one, 2)
        probs = gain_grads[1, :experts] + gain_grads[2, :experts]
        aux_loss = experts * jnp.sum(stats[:, 0] * probs) / (valid_total * valid_total)
    return (
        block_out.T,
        input_grad.T,
        aux_loss.reshape(()),
        gain_grads[3, :col],
        q_grad.T,
        k_grad.T,
        v_grad.T,
        output_grad,
        table_grad.T,
        gain_grads[0, :col],
        router_grad.T,
        in_weight_grad[None],
        out_weight_grad[None],
    )


def solution(mesh):
    return jax.shard_map(
        shards,
        mesh=mesh,
        in_specs=(
            P("expert", "head"),
            P("expert", "head"),
            P("expert"),
            P("expert", None),
            P(),
            P("head"),
            P(None, "head"),
            P(None, "head"),
            P(None, "head"),
            P("head", None),
            P(None, "head"),
            P("head"),
            P(),
            P("expert", None, "head"),
            P("expert", "head", None),
        ),
        out_specs=(
            P("expert", "head"),
            P("expert", "head"),
            P(),
            P("head"),
            P(None, "head"),
            P(None, "head"),
            P(None, "head"),
            P("head", None),
            P(None, "head"),
            P("head"),
            P(),
            P("expert", None, "head"),
            P("expert", "head", None),
        ),
        check_vma=False,
    )
```

```python
import functools

import jax
import jax.numpy as jnp
from jax import lax
from jax.experimental import pallas as pl
from jax.experimental.pallas import tpu as pltpu
from jax.sharding import PartitionSpec as P

eps = 1e-06
aux_weight = 0.01
f32 = jnp.float32
bf16 = jnp.bfloat16
gelu_scale = 0.7978845608028654
gelu_cube = 0.044715
highest = lax.Precision.HIGHEST
nt = ((1,), (1,))
tn = ((0,), (0,))


def mm(left, right, dims=((1,), (0,)), precision=None):
    return lax.dot_general(left, right, (dims, ((), ())), precision=precision, preferred_element_type=f32)


def call(body, outs, *args):
    scalar_memory = pl.BlockSpec(memory_space=pltpu.SMEM)
    in_specs = [scalar_memory if a.dtype == jnp.int32 and a.ndim == 1 else pl.BlockSpec() for a in args]
    shapes = []
    for shape, kind, *remote in outs:
        shapes.append(pltpu.HBM(shape, kind) if remote else jax.ShapeDtypeStruct(shape, kind))
    return pl.pallas_call(
        body,
        out_shape=shapes,
        in_specs=in_specs,
        compiler_params=pltpu.CompilerParams(vmem_limit_bytes=40 * 1024 * 1024),
    )(*args)


def far(array):
    return pltpu.with_memory_space_constraint(array, pltpu.HBM)


def tall(ref, first, rows):
    return jnp.concatenate([ref[i, first : first + rows, :].astype(f32) for i in range(ref.shape[0])], axis=0)


def gain_columns(block):
    turned = jnp.transpose(block.astype(f32))
    return [
        jnp.concatenate([turned[:, 0:1], turned[:64, 1:2]], axis=0),
        jnp.concatenate([turned[64:, 1:2], turned[:, 2:3]], axis=0),
    ]


def all_gains(packed):
    first = 2 * packed.shape[2] * 3 // 2
    pairs = [gain_columns(packed[i, first : first + 16, :]) for i in range(packed.shape[0])]
    return [jnp.concatenate([pair[i] for pair in pairs], axis=0) for i in range(2)]


def token_scale(values):
    return lax.rsqrt(jnp.sum(values * values, axis=0, keepdims=True) * (1.0 / values.shape[0]) + eps)


def lanes(shape):
    return lax.broadcasted_iota(jnp.int32, shape, len(shape) - 1)


def sublanes(shape):
    return lax.broadcasted_iota(jnp.int32, shape, len(shape) - 2)


def side_lanes(rows, width, columns):
    spot = lanes((rows, width))
    out = jnp.zeros((rows, width), f32)
    for i, column in enumerate(columns):
        out = jnp.where(spot == i, column, out)
    return out


def side_rows(rows, width, lines):
    spot = sublanes((rows, width))
    out = jnp.zeros((rows, width), f32)
    for i, line in enumerate(lines):
        out = jnp.where(spot == i, line, out)
    return out


def high_low(values, count=2):
    pieces = []
    for _ in range(count):
        piece = values.astype(bf16).astype(f32)
        pieces.append(piece)
        values = values - piece
    return pieces


def softmax(values, axis):
    raised = jnp.exp(values - jnp.max(values, axis=axis, keepdims=True))
    return raised / jnp.sum(raised, axis=axis, keepdims=True)


def gelu_parts(u):
    t = jnp.tanh(gelu_scale * (u + gelu_cube * u * u * u))
    value = 0.5 * u * (1.0 + t)
    slope = 0.5 * (1.0 + t) + 0.5 * u * (1.0 - t * t) * gelu_scale * (1.0 + 3.0 * gelu_cube * u * u)
    return value, slope


def fold_lanes(rows):
    return jnp.concatenate([rows[:, i : i + 128] for i in range(0, rows.shape[1], 128)], axis=0)


def unfold_lanes(rows, pieces):
    size = rows.shape[0] // pieces
    return jnp.concatenate([rows[i * size : (i + 1) * size] for i in range(pieces)], axis=1)


def side_block(side):
    count = side.shape[1]
    spot = lanes((8, 64))
    out = jnp.zeros((8, 64), f32)
    for g in range(side.shape[0] // 8):
        for j in range(count):
            out = jnp.where(spot == g * count + j, side[8 * g : 8 * g + 8, j : j + 1], out)
    return out


def fold_rest(rest, last):
    groups = [rest[i : i + 8] for i in range(0, rest.shape[0], 8)] + [last]
    if len(groups) % 2:
        groups.append(jnp.zeros((8, 64), f32))
    return [jnp.concatenate(groups[i : i + 2], axis=1) for i in range(0, len(groups), 2)]


def unfold_rest(blocks, slots, count):
    halves = []
    for i in range(0, blocks.shape[0], 8):
        halves += [blocks[i : i + 8, :64], blocks[i : i + 8, 64:]]
    number = slots // 8
    side = [halves[number][:, g * count : (g + 1) * count] for g in range(number)]
    return jnp.concatenate(halves[:number], axis=0), jnp.concatenate(side, axis=0)


def folded_rows(slots):
    return slots + 8 * ((slots // 8 + 2) // 2)


def pick_slots(spots, count):
    return sublanes((count, spots.shape[1])) == spots


def attend_kernel(
    scale, scalars, packed, wq, wk, wv, w_output, buckets, table, qkv_ref, weights_ref, attended_ref, branch_ref,
    scale_ref,
):
    heads, tok, _ = weights_ref.shape
    col = wq.shape[0]
    size = col // heads
    x = tall(packed, 0, col)
    scale_one = token_scale(x)
    scale_ref[...] = jnp.broadcast_to(scale_one, scale_ref.shape)
    normed = (x * scale_one * all_gains(packed)[0]).astype(bf16)
    projected = []
    for i, w in enumerate((wq, wk, wv)):
        rows = mm(w[...], normed).astype(bf16)
        qkv_ref[i] = rows
        projected.append(rows)
    query, key, value = projected
    hot = (sublanes((table.shape[1], 2 * tok - 1)) == buckets[...]).astype(f32)
    offsets = mm(table[...], hot, precision=highest)
    offsets = jnp.concatenate([offsets, jnp.zeros((heads, 1), f32)], axis=1)
    open_keys = lanes((tok, tok)) < scalars[0]
    outs = []
    for h in range(heads):
        at = slice(h * size, (h + 1) * size)
        spread = jnp.broadcast_to(offsets[h : h + 1, :], (tok, 2 * tok))
        bias = pltpu.roll(spread, tok + 1, 1, stride=1, stride_axis=0)[:, :tok]
        scores = mm(query[at], key[at], tn) * scale + bias
        weights = softmax(jnp.where(open_keys, scores, -1000000000.0), 1)
        weights_ref[h] = weights
        outs.append(mm(value[at], weights.astype(bf16), nt))
    attended = jnp.concatenate(outs, axis=0).astype(bf16)
    attended_ref[...] = attended
    branch = mm(w_output[...], attended, tn)
    for i in range(branch_ref.shape[0]):
        branch_ref[i] = branch[i * col : (i + 1) * col].astype(bf16)


def second_norm(residual, gain, w_router):
    scale = token_scale(residual)
    unit = residual * scale
    normed = (unit * gain).astype(bf16)
    return scale, unit, normed, softmax(mm(w_router, normed), 0)


def route_kernel(capacity, scalars, came, inputs, out_grad, routes, residual_ref, low_ref, side_ref, send_ref):
    col, tok = inputs.shape
    experts, slots, _ = send_ref.shape
    residual = inputs[...].astype(f32)
    for i in range(came.shape[0]):
        residual = residual + came[i].astype(f32)
    residual_ref[...] = residual
    low = residual.astype(bf16)
    low_ref[...] = low
    route_hot = (sublanes((experts, tok)) == routes[...]).astype(f32)
    before = (sublanes((tok, tok)) < lanes((tok, tok))).astype(bf16)
    slot = jnp.sum(mm(route_hot.astype(bf16), before) * route_hot, axis=0, keepdims=True)
    spots = routes[...].astype(f32) * slots + slot
    side_ref[...] = side_rows(8, tok, [spots])
    valid = (lanes((1, tok)) < scalars[0]).astype(f32)
    counts = jnp.sum(route_hot * valid, axis=1, keepdims=True)
    pick = pick_slots(spots.astype(jnp.int32), experts * slots).astype(bf16)
    rows = mm(pick, jnp.concatenate([low, out_grad[...]], axis=0), nt)
    spare = (sublanes((slots, 2 * col)) == capacity) & (lanes((slots, 2 * col)) == col)
    for e in range(experts):
        block = rows[e * slots : (e + 1) * slots]
        send_ref[e] = jnp.where(spare, counts[e : e + 1], block).astype(bf16)


def second_gain_row(packed, first):
    pieces = []
    for i in range(packed.shape[0]):
        block = packed[i, first : first + 16, :].astype(f32)
        pieces += [block[1:2, 64:], block[2:3, :]]
    return jnp.concatenate(pieces, axis=1)


def expert_kernel(
    capacity, scalars, quarters, packed, w_in, w_out, w_router,
    back_ref, part_ref, hidden_ref, before_ref, grads_ref, rows_ref,
):
    total = rows_ref.shape[0]
    experts, width = w_router.shape
    heads = part_ref.shape[0]
    col = width // heads
    slots = total // experts
    half = total // 2
    parts = [quarters[i].astype(f32) for i in range(heads)]
    residual = jnp.concatenate([block[:, :col] for block in parts], axis=1)
    grads = jnp.concatenate([block[:, col:] for block in parts], axis=1)
    inverse = lax.rsqrt(jnp.sum(residual * residual, axis=1, keepdims=True) * (1.0 / width) + eps)
    rows = (residual * inverse * second_gain_row(packed, 2 * col)).astype(bf16)
    rows_ref[...] = rows
    hidden, slope = gelu_parts(mm(rows, w_in[...]))
    hidden = hidden.astype(bf16)
    hidden_ref[...] = hidden
    produced = mm(hidden, w_out[...])
    for i in range(heads):
        mine = produced[:, i * col : (i + 1) * col]
        rest = mine[:, 128:]
        part_ref[i] = jnp.concatenate(
            [mine[:, :128], jnp.concatenate([rest[:half], rest[half:]], axis=1)], axis=0
        ).astype(bf16)
    probs = softmax(mm(rows, w_router[...], nt), 1)
    gate = jnp.sum(jnp.where(lanes((total, experts)) == scalars[2], probs, 0.0), axis=1, keepdims=True)
    back = (gate * grads).astype(bf16)
    grads_ref[...] = back
    before = (mm(back, w_out[...], nt) * slope).astype(bf16)
    before_ref[...] = before
    rows_grad = mm(before, w_in[...], nt)
    gate_grad = jnp.sum(grads * produced, axis=1, keepdims=True)
    stats = jnp.zeros((1, 128), f32)
    for b in range(experts):
        stats = stats + grads[b * slots + capacity : b * slots + capacity + 1, :128]
    side = side_lanes(total, 4, high_low(gate_grad) + high_low(stats[:, 0:1]))
    for b in range(experts):
        at = slice(b * slots, (b + 1) * slots)
        last = side_block(side[at])
        for i in range(heads):
            mine = rows_grad[at, i * col : (i + 1) * col]
            back_ref[b * heads + i] = jnp.concatenate(
                [mine[:, :128]] + fold_rest(mine[:, 128:], last), axis=0
            ).astype(bf16)


def weights_kernel(rows_ref, hidden, before, grads, in_ref, out_ref):
    in_ref[...] = mm(rows_ref[...], before[...], tn)
    out_ref[...] = mm(hidden[...], grads[...], tn)


def collect_kernel(slots, came, side, low, grad_ref, gate_ref, stats_ref):
    col, tok = low.shape
    experts = stats_ref.shape[0]
    heads = came.shape[0] // experts
    tops, rests, scalars = [], [], []
    for e in range(experts):
        total = came[e * heads].astype(f32)
        for i in range(1, heads):
            total = total + came[e * heads + i].astype(f32)
        rest, columns = unfold_rest(total[slots:], slots, 4)
        tops.append(total[:slots])
        rests.append(rest)
        scalars.append(columns)
    counts = jnp.concatenate([columns[0:1] for columns in scalars], axis=0) * (1.0 / heads)
    pick = pick_slots(side[0:1, :].astype(jnp.int32), experts * slots)
    for first, pieces in ((0, tops), (128, rests)):
        block = jnp.concatenate(pieces, axis=0).astype(bf16)
        grad_ref[first : min(first + 128, col), :] = mm(block, pick.astype(bf16), tn).astype(bf16)
    grad_ref[col:, :] = low[...]
    gate = mm(jnp.concatenate(scalars, axis=0), pick.astype(f32), tn, highest)
    gate_ref[...] = jnp.broadcast_to(gate[0:1] + gate[1:2], gate_ref.shape)
    stats_ref[...] = side_lanes(experts, 128, [counts[:, 2:3] + counts[:, 3:4]])


def backward_kernel(
    scale, valid_total, scalars, packed, expert_grad, gate_grad, stats, routes, w_router, w_output, weights_ref,
    qkv, wq, wk, wv, attended, part, late_ref, first_ref, own_ref, gate_ref, *share_refs,
):
    tok = routes.shape[1]
    heads_here = weights_ref.shape[0]
    blocks, col = packed.shape[0], wq.shape[0]
    experts, width = w_router.shape
    size = col // heads_here
    gain_one, gain_two = all_gains(packed)
    residual = tall(expert_grad, col, col)
    scale_two, unit, normed, router = second_norm(residual, gain_two, w_router[...])
    valid = (lanes((1, tok)) < scalars[0]).astype(f32)
    route_hot = (sublanes((experts, tok)) == routes[...]).astype(f32)
    fraction = stats[:, 0:1] * (aux_weight * experts / (valid_total * valid_total))
    gate = jnp.sum(router * route_hot, axis=0, keepdims=True)
    gate_ref[...] = jnp.broadcast_to(gate, gate_ref.shape)
    prob_grad = route_hot * gate_grad[0:1, :] + fraction * valid
    logit_grad = router * (prob_grad - jnp.sum(router * prob_grad, axis=0, keepdims=True))
    logit_grad = logit_grad.astype(bf16)
    normed_grad = mm(w_router[...], logit_grad, tn) + tall(expert_grad, 0, col)
    unit_grad = normed_grad * gain_two
    mean = jnp.sum(unit_grad * unit, axis=0, keepdims=True) * (1.0 / width)
    residual_grad = tall(packed, col, col) + scale_two * (unit_grad - unit * mean)
    branch = residual_grad.astype(bf16)
    attended_grad = mm(w_output[...], branch).astype(bf16)
    flip = (lanes((tok, tok)) + sublanes((tok, tok)) == tok - 1).astype(bf16)
    query, key, value = qkv[0], qkv[1], qkv[2]
    grads = [[], [], []]
    offsets = []
    for h in range(heads_here):
        at = slice(h * size, (h + 1) * size)
        out = attended_grad[at]
        weights = weights_ref[h]
        mass = mm(out, value[at], tn)
        score = weights * (mass - jnp.sum(weights * mass, axis=1, keepdims=True))
        score = score.astype(bf16)
        grads[0].append(mm(key[at], score, nt) * scale)
        grads[1].append(mm(query[at], score) * scale)
        grads[2].append(mm(out, weights.astype(bf16)))
        flipped = jnp.concatenate([mm(flip, score), jnp.zeros((tok, tok), f32)], axis=1)
        rolled = pltpu.roll(flipped, 0, 1, stride=1, stride_axis=0)
        offsets.append(jnp.sum(rolled, axis=0, keepdims=True))
    first = jnp.zeros((width, tok), f32)
    row = jnp.zeros((1, tok), f32)
    for i, w in enumerate((wq, wk, wv)):
        low = jnp.concatenate(grads[i], axis=0).astype(bf16)
        late_ref[i * col : (i + 1) * col, :] = low
        first = first + mm(w[...], low, tn)
        row = row + jnp.sum(low.astype(f32) * qkv[i].astype(f32), axis=0, keepdims=True)
    side = side_rows(16, tok, high_low(row))
    for i in range(blocks):
        at = slice(i * col, (i + 1) * col)
        first_ref[i, : col + 16, :] = jnp.concatenate([first[at], side], axis=0).astype(bf16)
        first_ref[i, col + 16 :, :] = part[i]

    product = mm(attended[...], branch, nt)
    gain_two_grad = jnp.sum(normed_grad * unit, axis=1, keepdims=True)
    gains = jnp.zeros((col, 1), f32)
    own = jnp.zeros((col, tok), f32)
    for i in range(blocks):
        at = slice(i * col, (i + 1) * col)
        gains = jnp.where(scalars[1] == i, gain_two_grad[at], gains)
        own = jnp.where(scalars[1] == i, residual_grad[at], own)
    own_ref[...] = own
    probs = jnp.sum(router * valid, axis=1, keepdims=True)
    if experts < col:
        probs = jnp.concatenate([probs, jnp.zeros((col - experts, 1), f32)], axis=0)
    gains = jnp.transpose(side_lanes(col, 128, [gains] + high_low(probs)))[0:8]
    router_grad = mm(logit_grad, normed, nt)
    offsets = jnp.concatenate(offsets, axis=0)
    offsets = jnp.concatenate([offsets, jnp.zeros((8 - heads_here, 2 * tok), f32)], axis=0)
    gains = jnp.concatenate([gains, jnp.zeros((8, 64), f32)], axis=1)
    pieces = [fold_lanes(gains), fold_lanes(offsets), fold_lanes(router_grad)]
    if len(share_refs) == 2:
        share_refs[0][...] = jnp.concatenate(pieces, axis=0)
        share_refs[1][...] = product
    else:
        share_ref = share_refs[0]
        groups = share_ref.shape[0]
        size = col // groups
        chunk = share_ref.shape[1] - 6 * size
        small = jnp.concatenate(pieces + [jnp.zeros((groups * chunk - 6 * experts - 32, 128), f32)], axis=0)
        for b in range(groups):
            share_ref[b] = jnp.concatenate(
                [small[b * chunk : (b + 1) * chunk], fold_lanes(product[b * size : (b + 1) * size])], axis=0
            ).astype(bf16)


def first_kernel(came, block, scale_one, own, *refs):
    shares, (ret_ref, gain_ref, input_ref) = refs[:-3], refs[-3:]
    col, tok = own.shape
    heads = came.shape[0]
    experts = ret_ref.shape[0]
    total = came[0].astype(f32)
    for i in range(1, heads):
        total = total + came[i].astype(f32)
    mean = (total[col : col + 1] + total[col + 1 : col + 2]) * (1.0 / (heads * col))
    scale = scale_one[0:1, :]
    mine = block[...].astype(f32)
    unit = mine[:col] * scale
    gain = gain_columns(mine[2 * col : 2 * col + 16])[0]
    input_ref[...] = own[...] + scale * (total[:col] * gain - unit * mean)
    gain_grad = jnp.sum(total[:col] * unit, axis=1, keepdims=True)
    unused = jnp.zeros_like(gain_grad)
    gain_grad = jnp.transpose(side_lanes(col, 128, [unused, unused, unused, gain_grad]))[0:8]
    gain_grad = fold_lanes(jnp.concatenate([gain_grad, jnp.zeros((8, 64), f32)], axis=1))
    gain_ref[...] = gain_grad
    produced = total[col + 16 :]
    count = produced.shape[0] * 2 // 3
    top = produced[:count]
    rest = jnp.concatenate([produced[count:, :64], produced[count:, 64:]], axis=0)
    slots = count // experts
    none = jnp.zeros((8, 64), f32)
    for e in range(experts):
        at = slice(e * slots, (e + 1) * slots)
        pieces = [top[at]] + fold_rest(rest[at], none)
        if shares:
            share = shares[0][e].astype(f32)
            if e == 0:
                share = jnp.concatenate([share[:16] + gain_grad, share[16:]], axis=0)
            pieces.append(share)
        ret_ref[e] = jnp.concatenate(pieces, axis=0).astype(bf16)


def share_kernel(slots, came, share_ref):
    total = came[0].astype(f32)
    for e in range(1, came.shape[0]):
        total = total + came[e].astype(f32)
    for e in range(came.shape[0]):
        share_ref[e] = total[folded_rows(slots) :].astype(bf16)


def add_returned(slots, blocks, side, gate, residual):
    col = residual.shape[0]
    top = jnp.concatenate([block[:slots] for block in blocks], axis=0).astype(bf16)
    rests = [unfold_rest(block[slots : folded_rows(slots)], slots, 1)[0] for block in blocks]
    rest = jnp.concatenate(rests, axis=0).astype(bf16)
    pick = pick_slots(side[0:1, :].astype(jnp.int32), len(blocks) * slots).astype(bf16)
    returned = jnp.concatenate([mm(top, pick, tn), mm(rest, pick, tn)], axis=0)
    return (residual[...] + gate[0:1, :] * returned).astype(bf16)


def last_kernel(slots, came, side, gate, residual, block_ref):
    blocks = [came[e].astype(f32) for e in range(came.shape[0])]
    block_ref[...] = add_returned(slots, blocks, side, gate, residual)


def products_kernel(late, all_in, packed, q_ref, k_ref, v_ref):
    groups, heads, col, tok = all_in.shape
    gain = all_gains(packed)[0]
    normed = []
    for b in range(groups):
        x = jnp.concatenate([all_in[b, i].astype(f32) for i in range(heads)], axis=0)
        normed.append((x * token_scale(x) * gain).astype(bf16))
    joined = jnp.concatenate([late[b] for b in range(groups)], axis=1)
    product = mm(joined, jnp.concatenate(normed, axis=1), nt)
    for i, ref in enumerate((q_ref, k_ref, v_ref)):
        ref[...] = product[i * col : (i + 1) * col]


def sums_kernel(came, buckets, stats, out_ref, router_ref, table_ref, gains_ref, aux_ref):
    groups, tok = came.shape[0], (buckets.shape[1] + 1) // 2
    experts = router_ref.shape[0]
    size = out_ref.shape[0] // groups
    shares = [came[b].astype(f32) for b in range(groups)]
    chunk = shares[0].shape[0] - 6 * size
    for b in range(groups):
        out_ref[b * size : (b + 1) * size, :] = unfold_lanes(shares[b][chunk:], 6)
    small = jnp.concatenate([share[:chunk] for share in shares], axis=0)
    gains = unfold_lanes(small[:16], 2)
    gains_ref[...] = gains
    probs = gains[1:2, :experts] + gains[2:3, :experts]
    same = lanes((experts, experts)) == sublanes((experts, experts))
    share = jnp.sum(jnp.where(same, stats[:, 0:1] * probs, 0.0), axis=0, keepdims=True)
    valid_total = 3 * tok * groups // 4
    aux_ref[...] = jnp.sum(share, axis=1, keepdims=True) * (experts / (valid_total * valid_total))
    span = buckets.shape[1]
    hot = (sublanes((table_ref.shape[1], span)) == buckets[...]).astype(f32)
    offsets = unfold_lanes(small[16:32], 2)[:, :span]
    table_ref[...] = mm(offsets, hot, nt, highest)[: table_ref.shape[0]]
    router_ref[...] = unfold_lanes(small[32 : 32 + 6 * experts], 6)


def few_experts():
    return lax.axis_size("expert") <= 8


def shards(
    inputs,
    out_grad,
    lengths,
    routes,
    buckets,
    gain_attn,
    w_query,
    w_key,
    w_value,
    w_output,
    bias_table,
    gain_ffn,
    w_router,
    w_in,
    w_out,
):
    tok, col = inputs.shape
    heads_here = bias_table.shape[1]
    head_size = w_query.shape[1] // heads_here
    width, experts = w_router.shape
    bucket_count = bias_table.shape[0]
    heads = width // col
    groups = lax.axis_size("expert")
    me_head, me_expert = lax.axis_index("head"), lax.axis_index("expert")
    capacity = max(2, (4 * tok + 3 * experts - 1) // (3 * experts))
    slots = -(-(capacity + 1) // 8) * 8
    total = experts * slots
    valid_total = 3 * tok * groups // 4
    scale = head_size ** (-0.5)
    joined = few_experts()
    small_rows = 6 * experts + 32
    chunk = -(-small_rows // (16 * groups)) * 16
    w_in, w_out = w_in[0], w_out[0]
    wq, wk, wv = w_query.T, w_key.T, w_value.T
    routes_row = routes.T
    router_rows = w_router.T
    scalars = jnp.stack([lengths[0], me_head.astype(jnp.int32), me_expert.astype(jnp.int32)])
    buckets_row = buckets[None]

    gains = jnp.concatenate([gain_attn, gain_ffn]).reshape(3, 128)
    own_block = jnp.concatenate([inputs.T, out_grad.T, gains, jnp.zeros((13, 128), bf16)], axis=0)
    packed = lax.all_gather(own_block, "head")
    if joined:
        all_in = lax.all_gather(inputs.T, ("expert", "head")).reshape(groups, heads, col, tok)
    qkv, weights, attended, branch, scale_one = call(
        functools.partial(attend_kernel, scale),
        [
            ((3, col, tok), bf16, 1), ((heads_here, tok, tok), f32, 1), ((col, tok), bf16, 1),
            ((heads, col, tok), bf16), ((8, tok), f32, 1),
        ],
        scalars, packed, far(wq), far(wk), far(wv), far(w_output), far(buckets_row), far(bias_table.T),
    )

    branch = lax.all_to_all(branch, "head", split_axis=0, concat_axis=0, tiled=True)
    residual, low, side, send = call(
        functools.partial(route_kernel, capacity),
        [((col, tok), f32, 1), ((col, tok), bf16, 1), ((8, tok), f32, 1), ((experts, slots, 2 * col), bf16)],
        scalars, branch, far(inputs.T), far(out_grad.T), far(routes_row),
    )
    quarter = lax.all_to_all(send, "expert", split_axis=0, concat_axis=0, tiled=True)
    quarters = lax.all_gather(quarter.reshape(total, 2 * col), "head")

    back, part, hidden, before_grad, back_rows, rows = call(
        functools.partial(expert_kernel, capacity),
        [((experts * heads, folded_rows(slots), 128), bf16), ((heads, total * 3 // 2, 128), bf16, 1)]
        + [((total, width), bf16, 1)] * 4,
        scalars, quarters, far(packed), far(w_in), far(w_out), far(router_rows),
    )
    came = lax.all_to_all(back, ("expert", "head"), split_axis=0, concat_axis=0, tiled=True)
    grad_own, gate_grad, stats = call(
        functools.partial(collect_kernel, slots),
        [((2 * col, tok), bf16), ((8, tok), f32, 1), ((experts, 128), f32, 1)],
        came, far(side), far(low),
    )
    expert_grad = lax.all_gather(grad_own, "head")

    late, first, residual_grad_own, gate, *shares = call(
        functools.partial(backward_kernel, scale, valid_total),
        [
            ((3 * col, tok), bf16, 1), ((heads, col + 16 + total * 3 // 2, 128), bf16), ((col, tok), f32, 1),
            ((8, tok), f32, 1),
        ]
        + (
            [((groups, chunk + 6 * col // groups, 128), bf16, 1)]
            if joined
            else [((small_rows, 128), f32, 1), ((col, width), f32, 1)]
        ),
        scalars, far(packed), expert_grad, far(gate_grad), far(stats), far(routes_row),
        far(router_rows), far(w_output), far(weights), far(qkv), far(wq), far(wk), far(wv), far(attended),
        far(part),
    )

    if joined:
        late_all = lax.all_gather(late, "expert")

    first = lax.all_to_all(first, "head", split_axis=0, concat_axis=0, tiled=True)
    in_weight_grad, out_weight_grad = call(
        weights_kernel, [((width, width), f32, 1)] * 2, far(rows), far(hidden), far(before_grad), far(back_rows)
    )
    ret, gain_one_part, input_grad = call(
        first_kernel,
        [
            ((experts, folded_rows(slots) + (shares[0].shape[1] if joined else 0), 128), bf16),
            ((16, 128), f32, 1), ((col, tok), f32, 1),
        ],
        first, far(own_block), far(scale_one), far(residual_grad_own), *([far(shares[0])] if joined else []),
    )
    ret = lax.all_to_all(ret, "expert", split_axis=0, concat_axis=0, tiled=True)
    ret, in_weight_grad, out_weight_grad = lax.optimization_barrier((ret, in_weight_grad, out_weight_grad))
    if joined:
        share = call(
            functools.partial(share_kernel, slots), [(shares[0].shape, bf16)], ret
        )[0]
        share = lax.all_to_all(share, "expert", split_axis=0, concat_axis=0, tiled=True)
    block_out = call(
        functools.partial(last_kernel, slots), [((col, tok), bf16, 1)], far(ret), far(side), far(gate), far(residual)
    )[0]
    if joined:
        q_grad, k_grad, v_grad = call(
            products_kernel, [((col, width), f32, 1)] * 3, far(late_all), far(all_in), far(packed)
        )
        share, q_grad, k_grad, v_grad, block_out = lax.optimization_barrier(
            (share, q_grad, k_grad, v_grad, block_out)
        )
        output_grad, router_grad, table_grad, gain_grads, aux_loss = call(
            sums_kernel,
            [((col, width), f32, 1), ((experts, width), f32), ((heads_here, bucket_count), f32)]
            + [((8, 256), f32), ((1, 1), f32)],
            share, far(buckets_row), far(stats),
        )
    else:
        gain = packed[:, 2 * col : 2 * col + 3].reshape(heads, 2 * col)[:, :col].reshape(width, 1)
        x = packed[:, :col].reshape(width, tok).astype(f32)
        normed = (x * token_scale(x) * gain.astype(f32)).astype(bf16)
        products = [mm(late[i * col : (i + 1) * col], normed, nt) for i in range(3)]
        q_grad, k_grad, v_grad, sums, gain_one, output_grad = lax.psum(
            products + [shares[0], gain_one_part, shares[1]], "expert"
        )
        router_grad = unfold_lanes(sums[32 : 32 + 6 * experts], 6)
        offsets = unfold_lanes(sums[16:32], 2)[:heads_here, : 2 * tok - 1]
        hot = (buckets[None, :] == jnp.arange(bucket_count)[:, None]).astype(f32)
        table_grad = mm(offsets, hot, nt, highest)
        gain_grads = unfold_lanes(sums[:16] + gain_one, 2)
        probs = gain_grads[1, :experts] + gain_grads[2, :experts]
        aux_loss = experts * jnp.sum(stats[:, 0] * probs) / (valid_total * valid_total)
    return (
        block_out.T,
        input_grad.T,
        aux_loss.reshape(()),
        gain_grads[3, :col],
        q_grad.T,
        k_grad.T,
        v_grad.T,
        output_grad,
        table_grad.T,
        gain_grads[0, :col],
        router_grad.T,
        in_weight_grad[None],
        out_weight_grad[None],
    )


def solution(mesh):
    return jax.shard_map(
        shards,
        mesh=mesh,
        in_specs=(
            P("expert", "head"),
            P("expert", "head"),
            P("expert"),
            P("expert", None),
            P(),
            P("head"),
            P(None, "head"),
            P(None, "head"),
            P(None, "head"),
            P("head", None),
            P(None, "head"),
            P("head"),
            P(),
            P("expert", None, "head"),
            P("expert", "head", None),
        ),
        out_specs=(
            P("expert", "head"),
            P("expert", "head"),
            P(),
            P("head"),
            P(None, "head"),
            P(None, "head"),
            P(None, "head"),
            P("head", None),
            P(None, "head"),
            P("head"),
            P(),
            P("expert", None, "head"),
            P("expert", "head", None),
        ),
        check_vma=False,
    )
```
